128 devices in a mesh: item: 4 (over z), head: 32 (over x, y, core).
Axes of the slice: x: 4, y: 4, z: 4, core: 2. Of those that a mesh axis runs over, the one named last changes fastest.
Arguments:
- tokens: bfloat16 [16384, 2048], P(('item', 'head')), may hold values from -6 to 6
- cotangent: bfloat16 [16384, 2048], P(('item', 'head')), may hold values from -6 to 6
- seg_counts: int32 [8], replicated, may hold values from 0 to 6, as said below
- query_weight: bfloat16 [2048, 2048], P('head'), may hold values from -0.125 to 0.125
- key_weight: bfloat16 [2048, 2048], P('head'), may hold values from -0.125 to 0.125
- value_weight: bfloat16 [2048, 2048], P('head'), may hold values from -0.125 to 0.125
- query_bias: float32 [2048], P('head'), may hold values from -3 to 3
- value_bias: float32 [2048], P('head'), may hold values from -3 to 3
- out_weight: bfloat16 [2048, 2048], P('head'), may hold values from -2 to 2
- out_bias: float32 [2048], replicated, may hold values from -3 to 3
- first_gain: float32 [2048], replicated, may hold values from 0.5 to 1.5
- first_shift: float32 [2048], replicated, may hold values from -3 to 3
- second_gain: float32 [2048], replicated, may hold values from 0.5 to 1.5
- second_shift: float32 [2048], replicated, may hold values from -3 to 3
- up_weight: bfloat16 [8192, 2048], P(('item', 'head')), may hold values from -0.125 to 0.125
- up_bias: float32 [8192], replicated, may hold values from -3 to 3
- down_weight: bfloat16 [8192, 2048], P(('item', 'head')), may hold values from -0.0625 to 0.0625
- down_bias: float32 [2048], replicated, may hold values from -3 to 3
Outputs:
- mixed_out: bfloat16 [16384, 2048], P(('item', 'head'))
- input_grad: float32 [16384, 2048], P(('item', 'head'))
- query_grad: float32 [2048, 2048], P('head')
- key_grad: float32 [2048, 2048], P('head')
- value_grad: float32 [2048, 2048], P('head')
- query_bias_grad: float32 [2048], P('head')
- value_bias_grad: float32 [2048], P('head')
- out_grad: float32 [2048, 2048], P('head')
- out_bias_grad: float32 [2048], replicated
- first_gain_grad: float32 [2048], replicated
- first_shift_grad: float32 [2048], replicated
- second_gain_grad: float32 [2048], replicated
- second_shift_grad: float32 [2048], replicated
- up_grad: float32 [8192, 2048], P(('item', 'head'))
- up_bias_grad: float32 [8192], replicated
- down_grad: float32 [8192, 2048], P(('item', 'head'))
- down_bias_grad: float32 [2048], replicated
The draws below stay inside these ranges and needn't reach their ends.
Inputs may be any that keep to these rules, and one draw needn't show every extreme that they name: `seg_counts`: up to the first zero the entries are the items' lengths in segments, in order along all 8 segments, summing to 8; the rest are 0. Exactly one item has 6 segments, starts within the first 2 segments; every other item has one or two segments.
All inputs are finite; a program needn't handle non-finite values.
Results may differ from the reference program's by a relative error of at most 0.028.
Values may be sent and summed in bfloat16 or wider, within the bound.
No kernel may reach another device: no remote copies, remote signals or barrier semaphores. Data moves between devices by JAX's collectives and lax.ppermute only.
A program may use at most 384 MiB of HBM per device.

```python
from functools import partial
import jax
import jax.numpy as jnp
from jax import lax

D = 2048
H = 32
HD = 64
FF = 8192
NSUM = 50
SEG = 2048
SPG = 2
NSEG = 8
TOKENS = 16384


def draw_seg_counts(key, part):
    key = jax.random.fold_in(key, 11)
    start_key, bit_key = jax.random.split(key)
    places = jnp.arange(NSEG, dtype=jnp.int32)
    longest_run = NSEG - 2 * SPG + 2
    leading = jax.random.randint(start_key, (), 0, SPG)
    closing = leading + longest_run
    coins = jax.random.randint(bit_key, (NSEG,), 0, 2)
    run_first = jnp.where(places < leading, 0, closing)
    parity = (places - run_first) % 2
    inside_long = (places >= leading) & (places < closing)
    opens = jnp.where(inside_long, places == leading, (places == run_first) | (parity == 0) | (coins == 1))
    opens = opens.astype(jnp.int32)
    item_of = jnp.cumsum(opens) - 1
    counts = jnp.sum((item_of[None, :] == places[:, None]).astype(jnp.int32), axis=1)
    return counts.astype(jnp.int32)


def levels(stream_key, extent, cuts, smallest, top_value):
    def one(axis_at, blocks):
        draws = jax.random.uniform(jax.random.fold_in(jax.random.fold_in(stream_key, 6), axis_at), (blocks,), jnp.float32, smallest / len(cuts), top_value / len(cuts))
        return jnp.repeat(jnp.exp(draws), extent[axis_at] // blocks).reshape((-1,) + (1,) * (len(extent) - axis_at - 1))

    factor_of = one(*cuts[0])
    for cut in cuts[1:]:
        factor_of = factor_of * one(*cut)
    return factor_of


def normal_values(key, shape, scale, bound, cuts=(), kind=jnp.bfloat16):
    values = scale * jax.random.normal(key, shape, jnp.float32)
    if cuts:
        values = values * levels(key, shape, cuts, -0.22, 0.18)
    return jnp.clip(values, -bound, bound).astype(kind)


def setup_inputs(seed: int = 0) -> dict:
    streams_of = jax.random.split(jax.random.key(seed), 19)
    tokens = normal_values(streams_of[0], (TOKENS, D), 1.0, 6.0, ((0, 128),))
    cotangent = normal_values(streams_of[1], (TOKENS, D), 1.0, 6.0, ((0, 128),))
    seg_counts = draw_seg_counts(jax.random.fold_in(streams_of[18], 71), 0)
    query_weight = normal_values(streams_of[3], (D, D), D ** -0.5, 0.125, ((0, 32),))
    key_weight = normal_values(streams_of[4], (D, D), D ** -0.5, 0.125, ((0, 32),))
    value_weight = normal_values(streams_of[5], (D, D), D ** -0.5, 0.125, ((0, 32),))
    query_bias = normal_values(streams_of[6], (D,), 0.5, 3.0, ((0, 32),), jnp.float32)
    value_bias = normal_values(streams_of[7], (D,), 0.5, 3.0, ((0, 32),), jnp.float32)
    out_weight = normal_values(streams_of[8], (D, D), (max(D // 256, 2)) ** -0.5, 2.0, ((0, 32),))
    out_bias = normal_values(streams_of[9], (D,), 0.3, 3.0, (), jnp.float32)
    first_gain = jnp.clip(1.0 + 0.1 * jax.random.normal(streams_of[10], (D,), jnp.float32), 0.5, 1.5)
    first_shift = normal_values(streams_of[11], (D,), 0.3, 3.0, (), jnp.float32)
    second_gain = jnp.clip(1.0 + 0.1 * jax.random.normal(streams_of[12], (D,), jnp.float32), 0.5, 1.5)
    second_shift = normal_values(streams_of[13], (D,), 0.3, 3.0, (), jnp.float32)
    up_weight = normal_values(streams_of[14], (FF, D), D ** -0.5, 0.125, ((0, 128),))
    up_bias = normal_values(streams_of[15], (FF,), 0.5, 3.0, (), jnp.float32)
    down_weight = normal_values(streams_of[16], (FF, D), FF ** -0.5, 0.0625, ((0, 128),))
    down_bias = normal_values(streams_of[17], (D,), 0.3, 3.0, (), jnp.float32)
    return {"tokens": tokens, "cotangent": cotangent, "seg_counts": seg_counts, "query_weight": query_weight, "key_weight": key_weight, "value_weight": value_weight, "query_bias": query_bias, "value_bias": value_bias, "out_weight": out_weight, "out_bias": out_bias, "first_gain": first_gain, "first_shift": first_shift, "second_gain": second_gain, "second_shift": second_shift, "up_weight": up_weight, "up_bias": up_bias, "down_weight": down_weight, "down_bias": down_bias}


EPSILON = 1e-05
MASKED = -1e+30

@jax.custom_vjp
def low(v):
    return lax.optimization_barrier(v.astype(jnp.bfloat16)).astype(jnp.float32)

@jax.custom_vjp
def low_back(v):
    return v

def low_keep(v):
    return (low(v), None)

def low_pass(kept, grad):
    return (grad,)

def back_keep(v):
    return (v, None)

def back_low(kept, grad):
    return (low(grad),)
low.defvjp(low_keep, low_pass)
low_back.defvjp(back_keep, back_low)

def both_ways(values):
    return low(low_back(values))

def matmul(left, right):
    return jnp.dot(left, right, precision=lax.Precision.HIGHEST, preferred_element_type=jnp.float32)

def layer_norm(row_data, gain, shift):
    row_mean = lax.optimization_barrier(jnp.mean(row_data, axis=-1, keepdims=True))
    centred = row_data - row_mean
    row_var = lax.optimization_barrier(jnp.mean(centred * centred, axis=-1, keepdims=True))
    return centred * lax.rsqrt(row_var + EPSILON) * gain + shift

def segment_flags(seg_counts):
    total_segs = seg_counts.shape[0]
    openings = jnp.cumsum(seg_counts) - seg_counts
    places = jnp.arange(total_segs, dtype=jnp.int32)
    opens_here = jnp.any((openings[:, None] == places[None, :]) & (seg_counts[:, None] > 0), axis=0)
    opens_before = jnp.concatenate([jnp.ones((1,), dtype=bool), opens_here[:-1]])
    one_back = jnp.logical_not(opens_here)
    two_back = one_back & jnp.logical_not(opens_before)
    return (one_back, two_back)

def attend_block(query_blk, offset, key_seg, value_seg, key_pre, value_pre, visible):
    key_scale = HD ** (-0.5)
    row_count = query_blk.shape[0]
    own = jnp.einsum('qhd,khd->hqk', query_blk, key_seg, precision=lax.Precision.HIGHEST, preferred_element_type=jnp.float32) * key_scale
    prior = jnp.einsum('qhd,khd->hqk', query_blk, key_pre, precision=lax.Precision.HIGHEST, preferred_element_type=jnp.float32) * key_scale
    scores = low_back(jnp.concatenate([own, prior], axis=2))
    query_pos = offset + jnp.arange(row_count, dtype=jnp.int32)
    key_pos = jnp.arange(SEG, dtype=jnp.int32)
    causal = query_pos[:, None] >= key_pos[None, :]
    seen = jnp.concatenate([causal, jnp.broadcast_to(visible[None, :], (row_count, 2 * NSUM))], axis=1)
    scores = jnp.where(seen[None], scores, MASKED)
    row_max = lax.optimization_barrier(jnp.max(scores, axis=2, keepdims=True))
    expd = jnp.exp(scores - row_max)
    probs = low(expd / lax.optimization_barrier(jnp.sum(expd, axis=2, keepdims=True)))
    all_values = jnp.concatenate([value_seg, value_pre], axis=0)
    return jnp.einsum('hqk,khd->qhd', probs, all_values, precision=lax.Precision.HIGHEST, preferred_element_type=jnp.float32)

def attend_segment(pieces):
    query_seg, key_seg, value_seg, key_pre, value_pre, visible = pieces
    span = min(512, SEG)
    blocks = query_seg.reshape(SEG // span, span, H, HD)
    offsets = jnp.arange(SEG // span, dtype=jnp.int32) * span

    def one_block(block_pieces):
        return attend_block(block_pieces[0], block_pieces[1], key_seg, value_seg, key_pre, value_pre, visible)
    result = lax.map(jax.checkpoint(one_block), (blocks, offsets))
    return result.reshape(SEG, H, HD)

def prefix_of(summ):
    padding = jnp.zeros((2,) + summ.shape[1:], jnp.float32)
    padded = jnp.concatenate([padding, summ], axis=0)
    return jnp.concatenate([padded[:-2], padded[1:-1]], axis=1)

def forward(tokens, query_weight, key_weight, value_weight, query_bias, value_bias, out_weight, out_bias, first_gain, first_shift, second_gain, second_shift, up_weight, up_bias, down_weight, down_bias, one_back, two_back):
    inputs_one = low(layer_norm(tokens, first_gain, first_shift))
    queries = both_ways(matmul(inputs_one, query_weight.T) + query_bias)
    keys = both_ways(matmul(inputs_one, key_weight.T))
    values = both_ways(matmul(inputs_one, value_weight.T) + value_bias)
    query_four = queries.reshape(NSEG, SEG, H, HD)
    key_four = keys.reshape(NSEG, SEG, H, HD)
    value_four = values.reshape(NSEG, SEG, H, HD)
    key_pre = prefix_of(key_four[:, SEG - NSUM:])
    value_pre = prefix_of(value_four[:, SEG - NSUM:])
    visible = jnp.concatenate([jnp.repeat(two_back[:, None], NSUM, axis=1), jnp.repeat(one_back[:, None], NSUM, axis=1)], axis=1)
    attended = lax.map(jax.checkpoint(attend_segment), (query_four, key_four, value_four, key_pre, value_pre, visible))
    attended = both_ways(attended.reshape(TOKENS, D))
    resid = tokens + low_back(matmul(attended, out_weight) + out_bias)
    inputs_two = low(layer_norm(resid, second_gain, second_shift))
    pre = low_back(matmul(inputs_two, up_weight.T) + up_bias)
    act = low(jax.nn.gelu(pre, approximate=True))
    return resid + matmul(act, down_weight) + down_bias

def reference(tokens, cotangent, seg_counts, query_weight, key_weight, value_weight, query_bias, value_bias, out_weight, out_bias, first_gain, first_shift, second_gain, second_shift, up_weight, up_bias, down_weight, down_bias):
    one_back, two_back = segment_flags(seg_counts)
    floats = (tokens, query_weight, key_weight, value_weight, query_bias, value_bias, out_weight, out_bias, first_gain, first_shift, second_gain, second_shift, up_weight, up_bias, down_weight, down_bias)
    floats = tuple((item.astype(jnp.float32) for item in floats))
    output, pull = jax.vjp(partial(forward, one_back=one_back, two_back=two_back), *floats)
    grads = pull(cotangent.astype(jnp.float32))
    return (output.astype(jnp.bfloat16), grads[0], grads[1], grads[2], grads[3], grads[4], grads[5], grads[6], grads[7], grads[8], grads[9], grads[10], grads[11], grads[12], grads[13], grads[14], grads[15])
```

```python
from functools import partial

import jax
import jax.numpy as jnp
from jax import lax
from jax.sharding import PartitionSpec as P

HD = 64
NSUM = 50
SEG = 2048


EPSILON = 1e-05
MASKED = -1e30


def shifted(value, axis, steps):
    count = lax.axis_size(axis)
    initial, last = (max(0, -steps), min(count, count - steps))
    return lax.ppermute(value, axis, [(source, source + steps) for source in range(initial, last)])


def layer_norm(row_data, gain, shift):
    row_mean = jnp.mean(row_data, axis=-1, keepdims=True)
    centred = row_data - row_mean
    row_var = jnp.mean(centred * centred, axis=-1, keepdims=True)
    return centred * lax.rsqrt(row_var + EPSILON) * gain + shift


def smooth_gate(values):
    return jax.nn.gelu(values, approximate=True)


def segment_flags(seg_counts):
    total_segs = seg_counts.shape[0]
    openings = jnp.cumsum(seg_counts) - seg_counts
    places = jnp.arange(total_segs, dtype=jnp.int32)
    opens_here = jnp.any((openings[:, None] == places[None, :]) & (seg_counts[:, None] > 0), axis=0)
    opens_before = jnp.concatenate([jnp.ones((1,), dtype=bool), opens_here[:-1]])
    one_back = jnp.logical_not(opens_here)
    two_back = one_back & jnp.logical_not(opens_before)
    return (one_back, two_back)


def block_scores(query_blk, key_own, key_pre, offset, visible):
    key_scale = HD ** (-0.5)
    own = (
        jnp.einsum("qhd,khd->hqk", query_blk, key_own, preferred_element_type=jnp.float32)
        * key_scale
    )
    prior = (
        jnp.einsum("qhd,khd->hqk", query_blk, key_pre, preferred_element_type=jnp.float32)
        * key_scale
    )
    row_count = query_blk.shape[0]
    key_span = key_own.shape[0]
    causal = offset + lax.broadcasted_iota(
        jnp.int32, (row_count, key_span), 0
    ) >= lax.broadcasted_iota(jnp.int32, (row_count, key_span), 1)
    own = jnp.where(causal[None], own, MASKED)
    prior = jnp.where(visible[None, None, :], prior, MASKED)
    return (own, prior)


def attend_forward(pieces, head_feats, heads_here):
    query_seg, kv_seg, prefix_seg, visible = pieces
    span = min(512, SEG)
    key_pre = prefix_seg[:, :head_feats].reshape(2 * NSUM, heads_here, HD)
    value_pre = prefix_seg[:, head_feats:].reshape(2 * NSUM, heads_here, HD)
    results = []
    log_sums = []
    for block_number in range(SEG // span):
        offset = block_number * span
        key_span = offset + span
        query_blk = query_seg[offset:key_span].reshape(span, heads_here, HD)
        key_own = kv_seg[:key_span, :head_feats].reshape(key_span, heads_here, HD)
        value_own = kv_seg[:key_span, head_feats:].reshape(key_span, heads_here, HD)
        own, prior = block_scores(query_blk, key_own, key_pre, offset, visible)
        row_max = jnp.maximum(jnp.max(own, axis=2), jnp.max(prior, axis=2))[..., None]
        own_exp = jnp.exp(own - row_max)
        prior_exp = jnp.exp(prior - row_max)
        summed = jnp.sum(own_exp, axis=2, keepdims=True) + jnp.sum(prior_exp, axis=2, keepdims=True)
        own_probs = (own_exp / summed).astype(jnp.bfloat16)
        prior_probs = (prior_exp / summed).astype(jnp.bfloat16)
        mixed = jnp.einsum("hqk,khd->qhd", own_probs, value_own, preferred_element_type=jnp.float32)
        mixed = mixed + jnp.einsum(
            "hqk,khd->qhd", prior_probs, value_pre, preferred_element_type=jnp.float32
        )
        results.append(mixed.reshape(span, head_feats).astype(jnp.bfloat16))
        log_sums.append((row_max + jnp.log(summed))[..., 0])
    return (jnp.concatenate(results, axis=0), jnp.concatenate(log_sums, axis=1))


def attend_backward(pieces, head_feats, heads_here):
    query_seg, kv_seg, prefix_seg, visible, attended_seg, d_attended_seg, log_sums = pieces
    key_scale = HD ** (-0.5)
    span = min(512, SEG)
    key_pre = prefix_seg[:, :head_feats].reshape(2 * NSUM, heads_here, HD)
    value_pre = prefix_seg[:, head_feats:].reshape(2 * NSUM, heads_here, HD)
    grad_keys = jnp.zeros((SEG, heads_here, HD), jnp.float32)
    grad_values = jnp.zeros((SEG, heads_here, HD), jnp.float32)
    grad_key_pre = jnp.zeros((2 * NSUM, heads_here, HD), jnp.float32)
    grad_value_pre = jnp.zeros((2 * NSUM, heads_here, HD), jnp.float32)
    grad_queries = []
    for block_number in range(SEG // span):
        offset = block_number * span
        key_span = offset + span
        query_blk = query_seg[offset:key_span].reshape(span, heads_here, HD)
        key_own = kv_seg[:key_span, :head_feats].reshape(key_span, heads_here, HD)
        value_own = kv_seg[:key_span, head_feats:].reshape(key_span, heads_here, HD)
        own, prior = block_scores(query_blk, key_own, key_pre, offset, visible)
        block_sums = log_sums[:, offset:key_span][..., None]
        own_probs = jnp.exp(own - block_sums)
        prior_probs = jnp.exp(prior - block_sums)
        d_out_blk = d_attended_seg[offset:key_span].reshape(span, heads_here, HD)
        own_dp = jnp.einsum(
            "qhd,khd->hqk", d_out_blk, value_own, preferred_element_type=jnp.float32
        )
        prior_dp = jnp.einsum(
            "qhd,khd->hqk", d_out_blk, value_pre, preferred_element_type=jnp.float32
        )
        delta = jnp.sum(own_probs * own_dp, axis=2, keepdims=True) + jnp.sum(
            prior_probs * prior_dp, axis=2, keepdims=True
        )
        own_ds = (own_probs * (own_dp - delta)).astype(jnp.bfloat16)
        prior_ds = (prior_probs * (prior_dp - delta)).astype(jnp.bfloat16)
        block_dq = jnp.einsum("hqk,khd->qhd", own_ds, key_own, preferred_element_type=jnp.float32)
        block_dq = (
            block_dq
            + jnp.einsum("hqk,khd->qhd", prior_ds, key_pre, preferred_element_type=jnp.float32)
        ) * key_scale
        grad_queries.append(block_dq.reshape(span, head_feats))
        pad_rows = ((0, SEG - key_span), (0, 0), (0, 0))
        grad_keys = grad_keys + jnp.pad(
            jnp.einsum("hqk,qhd->khd", own_ds, query_blk, preferred_element_type=jnp.float32)
            * key_scale,
            pad_rows,
        )
        grad_values = grad_values + jnp.pad(
            jnp.einsum(
                "hqk,qhd->khd",
                own_probs.astype(jnp.bfloat16),
                d_out_blk,
                preferred_element_type=jnp.float32,
            ),
            pad_rows,
        )
        grad_key_pre = (
            grad_key_pre
            + jnp.einsum("hqk,qhd->khd", prior_ds, query_blk, preferred_element_type=jnp.float32)
            * key_scale
        )
        grad_value_pre = grad_value_pre + jnp.einsum(
            "hqk,qhd->khd",
            prior_probs.astype(jnp.bfloat16),
            d_out_blk,
            preferred_element_type=jnp.float32,
        )
    grad_kv = jnp.concatenate(
        [grad_keys.reshape(SEG, head_feats), grad_values.reshape(SEG, head_feats)], axis=1
    )
    grad_prefix = jnp.concatenate(
        [grad_key_pre.reshape(2 * NSUM, head_feats), grad_value_pre.reshape(2 * NSUM, head_feats)],
        axis=1,
    )
    return (jnp.concatenate(grad_queries, axis=0), grad_kv, grad_prefix)


def all_sum(value, axis):
    count = lax.axis_size(axis)
    step = 1
    while step < count:
        value = value + lax.ppermute(value, axis, [(place, place ^ step) for place in range(count)])
        step *= 2
    return value


def head_swap(value):
    return lax.all_to_all(value, "head", split_axis=0, concat_axis=0, tiled=True)


def local(
    tokens,
    cotangent,
    seg_counts,
    query_weight,
    key_weight,
    value_weight,
    query_bias,
    value_bias,
    out_weight,
    out_bias,
    first_gain,
    first_shift,
    second_gain,
    second_shift,
    up_weight,
    up_bias,
    down_weight,
    down_bias,
):
    local_rows, model_width = tokens.shape
    head_total = lax.axis_size("head")
    item_total = lax.axis_size("item")
    item_place = lax.axis_index("item")
    group_rows = local_rows * head_total
    seg_local = group_rows // SEG
    head_feats = query_weight.shape[0]
    heads_here = head_feats // HD
    hidden_units = up_bias.shape[0]
    hidden_here = hidden_units // item_total
    dims_rows = (((0,), (0,)), ((), ()))
    dims_cols = (((1,), (1,)), ((), ()))
    tokens_f = tokens.astype(jnp.float32)
    inputs_one = layer_norm(tokens_f, first_gain, first_shift).astype(jnp.bfloat16)
    joint_weight = jnp.concatenate([query_weight, key_weight, value_weight], axis=0)
    joint_bias = jnp.concatenate([query_bias, jnp.zeros_like(query_bias), value_bias])
    inputs_all = lax.all_gather(inputs_one, "head", axis=0, tiled=True)
    out_full = lax.all_gather(out_weight, "head", axis=0, tiled=True)
    joint = (
        lax.dot_general(inputs_all, joint_weight, dims_cols, preferred_element_type=jnp.float32)
        + joint_bias
    ).astype(jnp.bfloat16)
    joint_segs = joint.reshape(seg_local, SEG, 3 * head_feats)
    query_segs = joint_segs[:, :, :head_feats]
    kv_segs = joint_segs[:, :, head_feats:]
    own_summ = kv_segs[:, SEG - NSUM :]
    prev_summ = shifted(own_summ, "item", 1)
    table = jnp.concatenate([prev_summ, own_summ], axis=0)
    prefix = jnp.concatenate(
        [table[seg_local - 2 : 2 * seg_local - 2], table[seg_local - 1 : 2 * seg_local - 1]], axis=1
    )
    one_back, two_back = segment_flags(seg_counts)
    one_local = lax.dynamic_slice_in_dim(one_back, item_place * seg_local, seg_local)
    two_local = lax.dynamic_slice_in_dim(two_back, item_place * seg_local, seg_local)
    visible = jnp.concatenate(
        [
            jnp.repeat(two_local[:, None], NSUM, axis=1),
            jnp.repeat(one_local[:, None], NSUM, axis=1),
        ],
        axis=1,
    )
    attended, log_sums = lax.map(
        partial(attend_forward, head_feats=head_feats, heads_here=heads_here),
        (query_segs, kv_segs, prefix, visible),
    )
    attended_rows = attended.reshape(group_rows, head_feats)
    attended_own = head_swap(
        attended_rows.reshape(head_total, local_rows, head_feats).transpose(0, 2, 1)
    ).reshape(model_width, local_rows)
    branch = lax.dot_general(attended_own, out_full, dims_rows, preferred_element_type=jnp.float32)
    resid = tokens_f + branch + out_bias
    inputs_two = layer_norm(resid, second_gain, second_shift).astype(jnp.bfloat16)
    up_block = lax.all_gather(up_weight, "head", axis=0, tiled=True)
    down_block = lax.all_gather(down_weight, "head", axis=0, tiled=True)
    bias_block = lax.dynamic_slice_in_dim(up_bias, item_place * hidden_here, hidden_here)
    cot_rows = lax.all_gather(cotangent, "item", axis=0, tiled=True)
    d_act = lax.dot_general(cot_rows, down_block, dims_cols, preferred_element_type=jnp.float32)
    norm_rows = lax.all_gather(inputs_two, "item", axis=0, tiled=True)
    pre = lax.dot_general(norm_rows, up_block, dims_cols, preferred_element_type=jnp.float32)
    pre = pre + bias_block
    act_f, gate_pull = jax.vjp(smooth_gate, pre)
    act = act_f.astype(jnp.bfloat16)
    slope = gate_pull(d_act)[0].astype(jnp.bfloat16)
    grad_two = lax.psum_scatter(
        jnp.dot(slope, up_block, preferred_element_type=jnp.float32).astype(jnp.bfloat16),
        "item",
        scatter_dimension=0,
        tiled=True,
    ).astype(jnp.float32)
    mixed = lax.psum_scatter(
        jnp.dot(act, down_block, preferred_element_type=jnp.float32).astype(jnp.bfloat16),
        "item",
        scatter_dimension=0,
        tiled=True,
    ).astype(jnp.float32)
    mixed_out = (resid + mixed + down_bias).astype(jnp.bfloat16)
    up_grad = lax.psum_scatter(
        lax.dot_general(slope, norm_rows, dims_rows, preferred_element_type=jnp.float32).astype(
            jnp.bfloat16
        ),
        "head",
        scatter_dimension=0,
        tiled=True,
    ).astype(jnp.float32)
    down_grad = lax.psum_scatter(
        lax.dot_general(act, cot_rows, dims_rows, preferred_element_type=jnp.float32).astype(
            jnp.bfloat16
        ),
        "head",
        scatter_dimension=0,
        tiled=True,
    ).astype(jnp.float32)
    cot_f = cotangent.astype(jnp.float32)
    up_bias_part = lax.dynamic_update_slice_in_dim(
        jnp.zeros((hidden_units,), jnp.float32),
        jnp.sum(slope.astype(jnp.float32), axis=0),
        item_place * hidden_here,
        0,
    )
    down_bias_part = jnp.sum(cot_f, axis=0)
    norm_two_pull = jax.vjp(layer_norm, resid, second_gain, second_shift)[1]
    resid_back, gain_two_part, shift_two_part = norm_two_pull(grad_two)
    d_resid = cot_f + resid_back
    d_branch = d_resid.astype(jnp.bfloat16)
    out_bias_part = jnp.sum(d_branch.astype(jnp.float32), axis=0)
    d_att_own = lax.dot_general(
        out_full, d_branch, dims_cols, preferred_element_type=jnp.float32
    ).astype(jnp.bfloat16)
    d_att = head_swap(d_att_own.reshape(head_total, head_feats, local_rows)).transpose(0, 2, 1)
    d_branch_all = lax.all_gather(d_branch, "head", axis=0, tiled=True)
    out_part = lax.dot_general(
        attended_rows, d_branch_all, dims_rows, preferred_element_type=jnp.float32
    )
    grad_q, grad_kv, grad_prefix = lax.map(
        partial(attend_backward, head_feats=head_feats, heads_here=heads_here),
        (
            query_segs,
            kv_segs,
            prefix,
            visible,
            attended,
            d_att.reshape(seg_local, SEG, head_feats),
            log_sums,
        ),
    )
    spread = jnp.pad(grad_prefix[:, :NSUM], ((seg_local - 2, 2), (0, 0), (0, 0)))
    spread = spread + jnp.pad(grad_prefix[:, NSUM:], ((seg_local - 1, 1), (0, 0), (0, 0)))
    returned = shifted(spread[:seg_local].astype(jnp.bfloat16), "item", -1).astype(jnp.float32)
    summ_grad = spread[seg_local:] + returned
    grad_kv = jnp.concatenate(
        [grad_kv[:, : SEG - NSUM], grad_kv[:, SEG - NSUM :] + summ_grad], axis=1
    )
    joint_grads = (
        jnp.concatenate([grad_q, grad_kv], axis=2)
        .reshape(group_rows, 3 * head_feats)
        .astype(jnp.bfloat16)
    )
    joint_grads_f = joint_grads.astype(jnp.float32)
    bias_parts = jnp.sum(joint_grads_f, axis=0)
    grads_own = head_swap(
        joint_grads.reshape(head_total, local_rows, 3 * head_feats).transpose(0, 2, 1)
    ).reshape(3 * model_width, local_rows)
    joint_full = lax.all_gather(joint_weight, "head", axis=0, tiled=True)
    d_one = lax.dot_general(grads_own, joint_full, dims_rows, preferred_element_type=jnp.float32)
    joint_part = lax.dot_general(
        joint_grads, inputs_all, dims_rows, preferred_element_type=jnp.float32
    )
    norm_one_pull = jax.vjp(layer_norm, tokens_f, first_gain, first_shift)[1]
    tokens_back, gain_one_part, shift_one_part = norm_one_pull(d_one)
    input_grad = d_resid + tokens_back
    joint_grad = lax.psum(joint_part.astype(jnp.bfloat16), "item").astype(jnp.float32)
    out_grad = lax.psum(out_part.astype(jnp.bfloat16), "item").astype(jnp.float32)
    bias_sums = all_sum(bias_parts, "item")
    early = all_sum(
        all_sum(
            jnp.concatenate(
                [up_bias_part, down_bias_part, gain_two_part, shift_two_part, out_bias_part]
            ).reshape(-1, 128),
            "head",
        ),
        "item",
    ).reshape(-1)
    late = all_sum(
        all_sum(jnp.concatenate([gain_one_part, shift_one_part]).reshape(-1, 128), "head"), "item"
    ).reshape(-1)
    up_bias_grad = early[:hidden_units]
    down_bias_grad, gain_two, shift_two, out_bias_grad = early[hidden_units:].reshape(
        4, model_width
    )
    gain_one, shift_one = late.reshape(2, model_width)
    return (
        mixed_out,
        input_grad,
        joint_grad[:head_feats],
        joint_grad[head_feats : 2 * head_feats],
        joint_grad[2 * head_feats :],
        bias_sums[:head_feats],
        bias_sums[2 * head_feats :],
        out_grad,
        out_bias_grad,
        gain_one,
        shift_one,
        gain_two,
        shift_two,
        up_grad,
        up_bias_grad,
        down_grad,
        down_bias_grad,
    )


def solution(mesh):
    placed = (
        P(("item", "head"), None),
        P(("item", "head"), None),
        P(),
        P("head", None),
        P("head", None),
        P("head", None),
        P("head"),
        P("head"),
        P("head", None),
        P(),
        P(),
        P(),
        P(),
        P(),
        P(("item", "head"), None),
        P(),
        P(("item", "head"), None),
        P(),
    )
    return jax.shard_map(
        local,
        mesh=mesh,
        in_specs=placed,
        out_specs=(
            P(("item", "head"), None),
            P(("item", "head"), None),
            P("head", None),
            P("head", None),
            P("head", None),
            P("head"),
            P("head"),
            P("head", None),
            P(),
            P(),
            P(),
            P(),
            P(),
            P(("item", "head"), None),
            P(),
            P(("item", "head"), None),
            P(),
        ),
        check_vma=False,
    )
```

```python
from functools import partial

import jax
import jax.numpy as jnp
from jax import lax
from jax.experimental import pallas as pl
from jax.experimental.pallas import tpu as pltpu
from jax.sharding import Mesh
from jax.sharding import PartitionSpec as P

HD = 64
NSUM = 50
SEG = 2048
SPAN = 512
KEPT = 64
EPSILON = 1e-05
MASKED = -1e30
SCALE = HD ** (-0.5)
MIB = 1 << 20
LOW = jnp.bfloat16


def dot(left, right):
    return jnp.dot(left, right, preferred_element_type=jnp.float32)


def dot_cols(left, right):
    return lax.dot_general(
        left, right, (((1,), (1,)), ((), ())), preferred_element_type=jnp.float32
    )


def turned(value):
    return value.astype(jnp.float32).T


def norm_parts(row_data):
    row_mean = jnp.mean(row_data, axis=-1, keepdims=True)
    centred = row_data - row_mean
    row_var = jnp.mean(centred * centred, axis=-1, keepdims=True)
    scale = lax.rsqrt(row_var + EPSILON)
    return centred * scale, scale


def norm_back(grad, normed, scale, gain):
    scaled = grad * gain
    return scale * (
        scaled
        - jnp.mean(scaled, axis=-1, keepdims=True)
        - normed * jnp.mean(scaled * normed, axis=-1, keepdims=True)
    )


def layer_norm(row_data, gain, shift):
    return norm_parts(row_data)[0] * gain + shift


def run(body, grid, in_specs, out_specs, out_shape, operands, scratch=(), flops=0, vmem=32):
    moved = sum(item.size * item.dtype.itemsize for item in operands)
    moved += sum(item.size * item.dtype.itemsize for item in out_shape)
    return pl.pallas_call(
        body,
        grid=grid,
        in_specs=in_specs,
        out_specs=out_specs,
        out_shape=out_shape,
        scratch_shapes=scratch,
        compiler_params=pltpu.CompilerParams(
            dimension_semantics=("arbitrary",) * len(grid), vmem_limit_bytes=vmem * MIB
        ),
        cost_estimate=pl.CostEstimate(flops=flops, bytes_accessed=moved, transcendentals=0),
    )(*operands)


def shape(dims, kind):
    return jax.ShapeDtypeStruct(dims, kind)


def whole(item):
    return pl.BlockSpec(item.shape, lambda *_: (0,) * len(item.shape))


def project_kernel(rows_ref, weight_ref, bias_ref, query_ref, kv_ref, turned_ref):
    rows = rows_ref[...].reshape(SPAN, rows_ref.shape[2])
    joint = dot_cols(rows, weight_ref[...]) + bias_ref[...]
    query_ref[...] = joint[:, :HD].astype(LOW)
    kv_ref[...] = joint[:, HD:].astype(LOW)
    turned_ref[...] = joint.T.astype(LOW)


def project(gathered, rows_here, weight, bias):
    places, _, width = gathered.shape
    total = places * rows_here
    step = SPAN // rows_here
    return run(
        project_kernel,
        (total // SPAN,),
        [
            pl.BlockSpec((step, rows_here, width), lambda i: (i, 0, 0)),
            whole(weight),
            whole(bias),
        ],
        [
            pl.BlockSpec((SPAN, HD), lambda i: (i, 0)),
            pl.BlockSpec((SPAN, 2 * HD), lambda i: (i, 0)),
            pl.BlockSpec((3 * HD, SPAN), lambda i: (0, i)),
        ],
        [
            shape((total, HD), LOW),
            shape((total, 2 * HD), LOW),
            shape((3 * HD, total), LOW),
        ],
        (gathered, weight, bias),
        flops=2 * total * width * 3 * HD,
    )


def prefix_seen(flags_ref, seg, columns):
    place = lax.broadcasted_iota(jnp.int32, (2 * KEPT, columns), 0)
    older = place < KEPT
    slot = jnp.where(older, place, place - KEPT) >= KEPT - NSUM
    flag = jnp.where(older, flags_ref[2 * seg], flags_ref[2 * seg + 1])
    return slot & (flag > 0)


def causal_seen():
    shape_here = (SPAN, SPAN)
    return lax.broadcasted_iota(jnp.int32, shape_here, 0) <= lax.broadcasted_iota(
        jnp.int32, shape_here, 1
    )


def above(block):
    return jnp.concatenate([block, jnp.zeros_like(block)], axis=0)


def below(block):
    return jnp.concatenate([jnp.zeros_like(block), block], axis=0)


def at_block(index):
    return pl.ds(pl.multiple_of(index * SPAN, SPAN), SPAN)


def attend_kernel(flags_ref, query_ref, turned_ref, kv_ref, prefix_ref, out_ref, log_ref):
    seg, block = pl.program_id(0), pl.program_id(1)
    query = above((query_ref[...].astype(jnp.float32) * SCALE).astype(LOW))
    own = at_block(block)
    scores = dot(kv_ref[own, :], query)
    scores = jnp.where(causal_seen(), scores, MASKED)
    top = jnp.max(scores, axis=0, keepdims=True)
    probs = jnp.exp(scores - top)
    total = jnp.sum(probs, axis=0, keepdims=True)
    mixed = dot(turned_ref[2 * HD :, own], probs.astype(LOW))

    def add(carry, scores, values):
        top, total, mixed = carry
        fresh = jnp.maximum(top, jnp.max(scores, axis=0, keepdims=True))
        fade = jnp.exp(top - fresh)
        probs = jnp.exp(scores - fresh)
        total = total * fade + jnp.sum(probs, axis=0, keepdims=True)
        return fresh, total, mixed * fade + dot(values, probs.astype(LOW))

    prefix = prefix_ref[0]
    scores = jnp.where(prefix_seen(flags_ref, seg, SPAN), dot(prefix, query), MASKED)
    carry = add((top, total, mixed), scores, turned(prefix)[HD:].astype(LOW))

    def step(index, carry):
        here = at_block(index)
        return add(carry, dot(kv_ref[here, :], query), turned_ref[2 * HD :, here])

    top, total, mixed = lax.fori_loop(0, block, step, carry)
    mixed = (mixed / total).astype(LOW)
    rows = out_ref.shape[2]
    for piece in range(SPAN // rows):
        out_ref[piece] = mixed[:, piece * rows : (piece + 1) * rows]
    log_ref[0] = top + jnp.log(total)


def attend(flags, turned_all, kv, prefix, rows_here):
    total = kv.shape[0]
    blocks = SEG // SPAN
    step = SPAN // rows_here
    return run(
        attend_kernel,
        (total // SEG, blocks),
        [
            pl.BlockSpec(memory_space=pltpu.SMEM),
            pl.BlockSpec((HD, SPAN), lambda s, i: (0, s * blocks + i)),
            pl.BlockSpec((3 * HD, SEG), lambda s, i: (0, s)),
            pl.BlockSpec((SEG, 2 * HD), lambda s, i: (s, 0)),
            pl.BlockSpec((1, 2 * KEPT, 2 * HD), lambda s, i: (s, 0, 0)),
        ],
        [
            pl.BlockSpec((step, HD, rows_here), lambda s, i: (s * blocks + i, 0, 0)),
            pl.BlockSpec((1, 1, SPAN), lambda s, i: (s * blocks + i, 0, 0)),
        ],
        [
            shape((total // rows_here, HD, rows_here), LOW),
            shape((total // SPAN, 1, SPAN), jnp.float32),
        ],
        (flags, turned_all, turned_all, kv, prefix),
        flops=total * SEG * HD * 4,
    )


def side_by_side(ref):
    return jnp.concatenate([ref[piece] for piece in range(ref.shape[0])], axis=1)


def beside(block, place):
    zero = jnp.zeros_like(block)
    return jnp.concatenate([block, zero] if place == 0 else [zero, block], axis=1)


def query_side(query_ref, rows_ref, grad_ref, out_ref, log_ref):
    query = above((query_ref[...].astype(jnp.float32) * SCALE).astype(LOW))
    grad = side_by_side(grad_ref)
    mean = jnp.sum(
        grad.astype(jnp.float32) * side_by_side(out_ref).astype(jnp.float32),
        axis=0,
        keepdims=True,
    )
    query_rows = beside((rows_ref[...].astype(jnp.float32) * SCALE).astype(LOW), 0)
    grad_rows = beside(turned(grad).astype(LOW), 1)
    return query, below(grad), mean, log_ref[0], query_rows, grad_rows


def key_side(keys, side, seen):
    query, grad, mean, log_sum, query_rows, grad_rows = side
    probs = jnp.exp(dot(keys, query) - log_sum)
    if seen is not None:
        probs = jnp.where(seen, probs, 0.0)
    d_scores = (probs * (dot(keys, grad) - mean)).astype(LOW)
    return probs.astype(LOW), d_scores


def prefix_back_kernel(
    flags_ref, query_ref, rows_ref, grad_ref, out_ref, log_ref, prefix_ref, sum_ref
):
    seg, block = pl.program_id(0), pl.program_id(1)
    side = query_side(query_ref, rows_ref, grad_ref, out_ref, log_ref)
    probs, d_scores = key_side(prefix_ref[0], side, prefix_seen(flags_ref, seg, SPAN))
    part = dot(d_scores, side[4]) + dot(probs, side[5])

    @pl.when(block == 0)
    def _():
        sum_ref[0] = part

    @pl.when(block > 0)
    def _():
        sum_ref[0] += part


def attend_back_kernel(
    flags_ref,
    query_ref,
    rows_ref,
    grad_ref,
    out_ref,
    log_ref,
    prefix_ref,
    turned_ref,
    kv_ref,
    returned_ref,
    grads_ref,
    kv_grad,
):
    seg, block = pl.program_id(0), pl.program_id(1)

    @pl.when(block == 0)
    def _():
        kv_grad[...] = jnp.zeros_like(kv_grad)
        kv_grad[SEG - KEPT :, :] = returned_ref[0]

    side = query_side(query_ref, rows_ref, grad_ref, out_ref, log_ref)
    prefix = prefix_ref[0]
    _, d_scores = key_side(prefix, side, prefix_seen(flags_ref, seg, SPAN))
    query_grad = dot(turned(prefix)[:HD].astype(LOW), d_scores)

    def add(here, query_grad, seen):
        probs, d_scores = key_side(kv_ref[here, :], side, seen)
        kv_grad[here, :] += dot(d_scores, side[4]) + dot(probs, side[5])
        return query_grad + dot(turned_ref[HD : 2 * HD, here], d_scores)

    query_grad = add(at_block(block), query_grad, causal_seen())
    query_grad = lax.fori_loop(
        0, block, lambda index, grad: add(at_block(index), grad, None), query_grad
    )
    query_grad = (query_grad * SCALE).astype(LOW)
    rows = grads_ref.shape[2]
    step = SPAN // rows
    for piece in range(step):
        grads_ref[block * step + piece, :HD, :] = query_grad[:, piece * rows : (piece + 1) * rows]

    @pl.when(block == pl.num_programs(1) - 1)
    def _():
        for piece in range(SEG // rows):
            grads_ref[piece, HD:, :] = kv_grad[piece * rows : (piece + 1) * rows, :].T.astype(LOW)


def attend_back_specs(rows_here):
    blocks = SEG // SPAN
    step = SPAN // rows_here
    return [
        pl.BlockSpec(memory_space=pltpu.SMEM),
        pl.BlockSpec((HD, SPAN), lambda s, i: (0, s * blocks + i)),
        pl.BlockSpec((SPAN, HD), lambda s, i: (s * blocks + i, 0)),
        pl.BlockSpec((step, HD, rows_here), lambda s, i: (s * blocks + i, 0, 0)),
        pl.BlockSpec((step, HD, rows_here), lambda s, i: (s * blocks + i, 0, 0)),
        pl.BlockSpec((1, 1, SPAN), lambda s, i: (s * blocks + i, 0, 0)),
        pl.BlockSpec((1, 2 * KEPT, 2 * HD), lambda s, i: (s, 0, 0)),
    ]


def prefix_back(flags, turned_all, query, grad, out, log_sums, prefix, rows_here):
    total = query.shape[0]
    return run(
        prefix_back_kernel,
        (total // SEG, SEG // SPAN),
        attend_back_specs(rows_here),
        [pl.BlockSpec((1, 2 * KEPT, 2 * HD), lambda s, i: (s, 0, 0))],
        [shape(prefix.shape, jnp.float32)],
        (flags, turned_all, query, grad, out, log_sums, prefix),
        flops=total * 2 * KEPT * HD * 8,
    )


def attend_back(
    flags, turned_all, query, grad, out, log_sums, prefix, kv, returned, rows_here
):
    total = query.shape[0]
    pieces = SEG // rows_here
    return run(
        attend_back_kernel,
        (total // SEG, SEG // SPAN),
        attend_back_specs(rows_here)
        + [
            pl.BlockSpec((3 * HD, SEG), lambda s, i: (0, s)),
            pl.BlockSpec((SEG, 2 * HD), lambda s, i: (s, 0)),
            pl.BlockSpec((1, KEPT, 2 * HD), lambda s, i: (s, 0, 0)),
        ],
        [pl.BlockSpec((pieces, 3 * HD, rows_here), lambda s, i: (s, 0, 0))],
        [shape((total // rows_here, 3 * HD, rows_here), LOW)],
        (flags, turned_all, query, grad, out, log_sums, prefix, turned_all, kv, returned),
        scratch=[pltpu.VMEM((SEG, 2 * HD), jnp.float32)],
        flops=total * SEG * HD * 10,
    )


def out_kernel(
    part_ref, weight_ref, tokens_ref, bias_ref, gain_ref, shift_ref, resid_ref, two_ref, total
):
    step = pl.program_id(0)
    rows = part_ref.shape[2]
    part = turned(part_ref[...].reshape(-1, rows)).astype(LOW)
    added = dot(part, weight_ref[...].reshape(part.shape[1], -1))

    @pl.when(step == 0)
    def _():
        total[...] = added

    @pl.when(step > 0)
    def _():
        total[...] += added

    @pl.when(step == pl.num_programs(0) - 1)
    def _():
        resid = tokens_ref[...].astype(jnp.float32) + total[...] + bias_ref[...]
        resid_ref[...] = resid
        two_ref[...] = layer_norm(resid, gain_ref[...], shift_ref[...]).astype(LOW)


def out_project(parts, gathered, at, tokens, bias, gain, shift, step=4):
    places, feats, rows = parts.shape
    width = gathered.shape[2]
    return run(
        out_kernel,
        (places // step,),
        [
            pl.BlockSpec((step, feats, rows), lambda i: (i, 0, 0)),
            pl.BlockSpec((step, feats, width), lambda i: (i, at, 0)),
            whole(tokens),
            whole(bias),
            whole(gain),
            whole(shift),
        ],
        [pl.BlockSpec((rows, width), lambda i: (0, 0))] * 2,
        [shape((rows, width), jnp.float32), shape((rows, width), LOW)],
        (parts, gathered, tokens, bias, gain, shift),
        scratch=[pltpu.VMEM((rows, width), jnp.float32)],
        flops=2 * rows * places * feats * width,
    )


def feed_kernel(count, core_ref, *refs):
    norm_refs, cot_refs = refs[:count], refs[count : 2 * count]
    weight_ref, bias_ref = refs[2 * count : 2 * count + 2]
    refs = refs[2 * count + 2 :]
    back_refs, mixed_refs = refs[:count], refs[count : 2 * count]
    keep_ref, send_ref, bias_sum_ref, norms, cots, back, mixed = refs[2 * count :]
    step = pl.program_id(0)
    rows = norm_refs[0].shape[0]

    @pl.when(step == 0)
    def _():
        for place in range(count):
            here = slice(place * rows, (place + 1) * rows)
            norms[here, :] = norm_refs[place][...]
            cots[here, :] = cot_refs[place][...]
        back[...] = jnp.zeros_like(back)
        mixed[...] = jnp.zeros_like(mixed)

    units = weight_ref.shape[1] // 2
    width = weight_ref.shape[2]
    up = weight_ref[:, :units, :].reshape(-1, width)
    down = weight_ref[:, units:, :].reshape(-1, width)
    pre = dot_cols(norms[...], up) + bias_ref[...]
    d_act = dot_cols(cots[...], down)
    square = pre * pre
    bent = jnp.tanh(0.7978845608 * (pre + 0.044715 * (square * pre)))
    half = 0.5 * (1.0 + bent)
    act = pre * half
    slope = half + 0.5 * pre * (1.0 - bent * bent) * (
        0.7978845608 * (1.0 + 3.0 * 0.044715 * square)
    )
    d_pre = (d_act * slope).astype(LOW)
    act = act.astype(LOW)
    bias_sum_ref[0] = jnp.sum(d_pre.astype(jnp.float32), axis=0, keepdims=True)
    back[...] += dot(d_pre, up)
    mixed[...] += dot(act, down)
    up_grad = dot(turned(d_pre).astype(LOW), norms[...]).astype(LOW)
    down_grad = dot(turned(act).astype(LOW), cots[...]).astype(LOW)

    def store(ref, core):
        for pair in range(ref.shape[0]):
            here = slice((2 * pair + core) * units, (2 * pair + core + 1) * units)
            ref[pair, :units, :] = up_grad[here]
            ref[pair, units:, :] = down_grad[here]

    @pl.when(core_ref[0] == 0)
    def _():
        store(keep_ref, 0)
        store(send_ref, 1)

    @pl.when(core_ref[0] == 1)
    def _():
        store(keep_ref, 1)
        store(send_ref, 0)

    @pl.when(step == pl.num_programs(0) - 1)
    def _():
        for place in range(count):
            here = slice(place * rows, (place + 1) * rows)
            back_refs[place][...] = back[here, :].astype(LOW)
            mixed_refs[place][...] = mixed[here, :].astype(LOW)


def feed(core, norms, cots, weights, bias, step=4):
    count = len(norms)
    rows, width = norms[0].shape
    places, both, _ = weights.shape
    units = both // 2
    total = count * rows
    row_spec = pl.BlockSpec((rows, width), lambda i: (0, 0))
    grad_spec = pl.BlockSpec((step // 2, both, width), lambda i: (i, 0, 0))
    results = run(
        partial(feed_kernel, count),
        (places // step,),
        [pl.BlockSpec(memory_space=pltpu.SMEM)]
        + [row_spec] * (2 * count)
        + [
            pl.BlockSpec((step, both, width), lambda i: (i, 0, 0)),
            pl.BlockSpec((1, step * units), lambda i: (0, i)),
        ],
        [row_spec] * (2 * count)
        + [
            grad_spec,
            grad_spec,
            pl.BlockSpec((1, 1, step * units), lambda i: (i, 0, 0)),
        ],
        [shape((rows, width), LOW)] * (2 * count)
        + [
            shape((places // 2, both, width), LOW),
            shape((places // 2, both, width), LOW),
            shape((places // step, 1, step * units), jnp.float32),
        ],
        (core, *norms, *cots, weights, bias),
        scratch=[pltpu.VMEM((total, width), LOW)] * 2
        + [pltpu.VMEM((total, width), jnp.float32)] * 2,
        flops=2 * total * width * places * units * 6,
        vmem=52,
    )
    return results[:count], results[count : 2 * count], results[2 * count :]


def branch_kernel(
    count, resid_ref, cot_ref, gain_ref, weight_ref, *refs
):
    back_refs = refs[:count]
    d_resid_ref, d_branch_ref, sums_ref, parts_ref = refs[count:]

    @pl.when(pl.program_id(0) == 0)
    def _():
        d_two = sum(ref[...].astype(jnp.float32) for ref in back_refs)
        normed, scale = norm_parts(resid_ref[...])
        cot = cot_ref[...].astype(jnp.float32)
        d_resid = cot + norm_back(d_two, normed, scale, gain_ref[...])
        d_branch = d_resid.astype(LOW)
        d_resid_ref[...] = d_resid
        d_branch_ref[...] = d_branch
        sums_ref[0:1, :] = jnp.sum(d_two * normed, axis=0, keepdims=True)
        sums_ref[1:2, :] = jnp.sum(d_two, axis=0, keepdims=True)
        sums_ref[2:3, :] = jnp.sum(d_branch.astype(jnp.float32), axis=0, keepdims=True)
        sums_ref[3:4, :] = jnp.sum(cot, axis=0, keepdims=True)

    width = weight_ref.shape[2]
    part = dot_cols(weight_ref[...].reshape(-1, width), d_branch_ref[...])
    parts_ref[...] = part.reshape(parts_ref.shape).astype(LOW)


def branch_back(resid, cotangent, gain, gathered, at, feats, backs, step=4):
    rows, width = resid.shape
    places = gathered.shape[0]
    row_spec = pl.BlockSpec((rows, width), lambda i: (0, 0))
    return run(
        partial(branch_kernel, len(backs)),
        (places // step,),
        [
            row_spec,
            row_spec,
            whole(gain),
            pl.BlockSpec((step, feats, width), lambda i: (i, at, 0)),
        ]
        + [row_spec] * len(backs),
        [
            row_spec,
            row_spec,
            pl.BlockSpec((4, width), lambda i: (0, 0)),
            pl.BlockSpec((step, feats, rows), lambda i: (i, 0, 0)),
        ],
        [
            shape((rows, width), jnp.float32),
            shape((rows, width), LOW),
            shape((4, width), jnp.float32),
            shape((places, feats, rows), LOW),
        ],
        (resid, cotangent, gain, gathered, *backs),
        flops=2 * rows * places * feats * width,
    )


def weight_grad_kernel(grad_ref, rows_ref, out_ref, total):
    step = pl.program_id(0)
    grads = side_by_side(grad_ref)
    added = dot(grads, rows_ref[...].reshape(grads.shape[1], -1))

    @pl.when(step == 0)
    def _():
        total[...] = added

    @pl.when(step > 0)
    def _():
        total[...] += added

    @pl.when(step == pl.num_programs(0) - 1)
    def _():
        out_ref[...] = total[...].astype(out_ref.dtype)


def weight_grad(grads, gathered, step=4):
    places, feats, rows = grads.shape
    width = gathered.shape[2]
    return run(
        weight_grad_kernel,
        (places // step,),
        [
            pl.BlockSpec((step, feats, rows), lambda i: (i, 0, 0)),
            pl.BlockSpec((step, rows, width), lambda i: (i, 0, 0)),
        ],
        [pl.BlockSpec((feats, width), lambda i: (0, 0))],
        [shape((feats, width), LOW)],
        (grads, gathered),
        scratch=[pltpu.VMEM((feats, width), jnp.float32)],
        flops=2 * places * rows * feats * width,
    )[0]


def joint_grad_kernel(
    grad_ref, rows_ref, weight_ref, gain_ref, shift_ref, out_ref, bias_ref, sums_ref, total, biases
):
    step = pl.program_id(0)
    grads = side_by_side(grad_ref)
    added = dot(grads, rows_ref[...].reshape(grads.shape[1], -1))
    summed = jnp.sum(grads.astype(jnp.float32), axis=1, keepdims=True)

    @pl.when(step == 0)
    def _():
        total[...] = added
        biases[...] = summed

    @pl.when(step > 0)
    def _():
        total[...] += added
        biases[...] += summed

    @pl.when(step == pl.num_programs(0) - 1)
    def _():
        out_ref[...] = total[...].astype(LOW)
        bias_ref[...] = biases[...]
        weight = weight_ref[...].astype(jnp.float32)
        shift_sum = jnp.sum(weight * biases[...], axis=0, keepdims=True)
        product = jnp.sum(weight * total[...], axis=0, keepdims=True)
        sums_ref[0:1, :] = (product - shift_sum * shift_ref[...]) / gain_ref[...]
        sums_ref[1:2, :] = shift_sum


def joint_grad(grads, gathered, weight, gain, shift, step=4):
    places, feats, rows = grads.shape
    width = gathered.shape[2]
    return run(
        joint_grad_kernel,
        (places // step,),
        [
            pl.BlockSpec((step, feats, rows), lambda i: (i, 0, 0)),
            pl.BlockSpec((step, rows, width), lambda i: (i, 0, 0)),
            whole(weight),
            whole(gain),
            whole(shift),
        ],
        [
            pl.BlockSpec((feats, width), lambda i: (0, 0)),
            pl.BlockSpec((feats, 1), lambda i: (0, 0)),
            pl.BlockSpec((2, width), lambda i: (0, 0)),
        ],
        [
            shape((feats, width), LOW),
            shape((feats, 1), jnp.float32),
            shape((2, width), jnp.float32),
        ],
        (grads, gathered, weight, gain, shift),
        scratch=[pltpu.VMEM((feats, width), jnp.float32), pltpu.VMEM((feats, 1), jnp.float32)],
        flops=2 * places * rows * feats * width,
    )


def input_kernel(part_ref, weight_ref, tokens_ref, gain_ref, d_resid_ref, out_ref, total):
    step = pl.program_id(0)
    added = dot(turned(part_ref[...]).astype(LOW), weight_ref[...])

    @pl.when(step == 0)
    def _():
        total[...] = added

    @pl.when(step > 0)
    def _():
        total[...] += added

    @pl.when(step == pl.num_programs(0) - 1)
    def _():
        normed, scale = norm_parts(tokens_ref[...].astype(jnp.float32))
        out_ref[...] = d_resid_ref[...] + norm_back(total[...], normed, scale, gain_ref[...])


def input_back(parts, weights, tokens, gain, d_resid, step=SPAN):
    feats, rows = parts.shape
    width = weights.shape[1]
    return run(
        input_kernel,
        (feats // step,),
        [
            pl.BlockSpec((step, rows), lambda i: (i, 0)),
            pl.BlockSpec((step, width), lambda i: (i, 0)),
            whole(tokens),
            whole(gain),
            whole(d_resid),
        ],
        [pl.BlockSpec((rows, width), lambda i: (0, 0))],
        [shape((rows, width), jnp.float32)],
        (parts, weights, tokens, gain, d_resid),
        scratch=[pltpu.VMEM((rows, width), jnp.float32)],
        flops=2 * feats * rows * width,
    )[0]


ITEM = "z"
HEAD = ("x", "y", "c")
PLANE = ("x", "y")
CORE = "c"


def moved(value, axis, steps):
    count = lax.axis_size(axis)
    return lax.ppermute(value, axis, [(place, (place + steps) % count) for place in range(count)])


def shifted(value, axis, steps):
    count = lax.axis_size(axis)
    initial, last = (max(0, -steps), min(count, count - steps))
    return lax.ppermute(value, axis, [(source, source + steps) for source in range(initial, last)])


def all_sum(value, axes):
    for axis in axes:
        count = lax.axis_size(axis)
        step = 1
        while step < count:
            pairs = [(place, place ^ step) for place in range(count)]
            value = value + lax.ppermute(value, axis, pairs)
            step *= 2
    return value


def around(value, axis):
    return [value] + [moved(value, axis, -step) for step in range(1, lax.axis_size(axis))]


def sum_back(values, axis):
    return [values[0]] + [
        moved(values[step], axis, step) for step in range(1, lax.axis_size(axis))
    ]


def item_sum(value):
    count = lax.axis_size(ITEM)
    place = lax.axis_index(ITEM)
    parts = value.reshape(count, -1, value.shape[1])
    own = [
        lax.dynamic_index_in_dim(parts, (place + step) % count, 0, keepdims=False)
        for step in range(count)
    ]
    block = sum(term.astype(jnp.float32) for term in sum_back(own, ITEM)).astype(LOW)
    blocks = around(block, ITEM)
    twice = jnp.stack(blocks + blocks)
    rows = lax.dynamic_slice_in_dim(twice, (count - place) % count, count, 0)
    return rows.reshape(value.shape).astype(jnp.float32)


def head_swap(value):
    return lax.all_to_all(value, HEAD, split_axis=0, concat_axis=0, tiled=True)


def segment_flags(seg_counts):
    total_segs = seg_counts.shape[0]
    openings = jnp.cumsum(seg_counts) - seg_counts
    places = jnp.arange(total_segs, dtype=jnp.int32)
    opens_here = jnp.any((openings[:, None] == places[None, :]) & (seg_counts[:, None] > 0), axis=0)
    opens_before = jnp.concatenate([jnp.ones((1,), dtype=bool), opens_here[:-1]])
    one_back = jnp.logical_not(opens_here)
    two_back = one_back & jnp.logical_not(opens_before)
    return (one_back, two_back)


def local(
    tokens,
    cotangent,
    seg_counts,
    query_weight,
    key_weight,
    value_weight,
    query_bias,
    value_bias,
    out_weight,
    out_bias,
    first_gain,
    first_shift,
    second_gain,
    second_shift,
    up_weight,
    up_bias,
    down_weight,
    down_bias,
):
    rows, width = tokens.shape
    heads = lax.axis_size(HEAD)
    item_place = lax.axis_index(ITEM)
    group_rows = rows * heads
    seg_local = group_rows // SEG
    feats = query_weight.shape[0]
    units = up_weight.shape[0]
    hidden_units = up_bias.shape[0]
    hidden_here = units * heads

    def row(vector):
        return vector.reshape(1, -1)

    tokens_f = tokens.astype(jnp.float32)
    inputs_one = layer_norm(tokens_f, first_gain, first_shift).astype(LOW)
    first = jnp.concatenate([inputs_one, out_weight], axis=0)
    gathered = lax.all_gather(first, HEAD, axis=0, tiled=True).reshape(heads, -1, width)
    second = jnp.concatenate([up_weight, down_weight], axis=0)
    feed_weights = lax.all_gather(second, HEAD, axis=0, tiled=True).reshape(heads, -1, width)
    cots = around(cotangent, ITEM)
    joint_weight = jnp.concatenate([query_weight, key_weight, value_weight], axis=0)
    joint_bias = jnp.concatenate([query_bias, jnp.zeros_like(query_bias), value_bias])

    one_back, two_back = segment_flags(seg_counts)
    flags = jnp.stack([two_back, one_back], axis=1).astype(jnp.int32)
    flags = lax.dynamic_slice_in_dim(flags, item_place * seg_local, seg_local).reshape(-1)

    query, kv, turned_all = project(gathered, rows, joint_weight, row(joint_bias))
    own_kept = kv.reshape(seg_local, SEG, 2 * HD)[:, SEG - KEPT :]
    table = jnp.concatenate([shifted(own_kept, ITEM, 1), own_kept], axis=0)
    prefix = jnp.concatenate(
        [table[seg_local - 2 : 2 * seg_local - 2], table[seg_local - 1 : 2 * seg_local - 1]], axis=1
    )
    attended, log_sums = attend(flags, turned_all, kv, prefix, rows)
    attended_own = head_swap(attended)
    resid, inputs_two = out_project(
        attended_own, gathered, rows // feats, tokens, row(out_bias), row(second_gain), row(second_shift)
    )

    joint_turn = lax.optimization_barrier((joint_weight, resid))[0]
    joint_full = lax.all_gather(joint_turn, HEAD, axis=0, tiled=True)
    norms = around(inputs_two, ITEM)
    bias_here = lax.dynamic_slice_in_dim(up_bias, item_place * hidden_here, hidden_here)
    core = lax.axis_index(CORE).astype(jnp.int32).reshape(1)
    backs, mixeds, (keep, send, up_bias_part) = feed(
        core, norms, cots, feed_weights, row(bias_here)
    )
    backs = sum_back(backs, ITEM)
    mixeds = sum_back(mixeds, ITEM)
    mixed = sum(part.astype(jnp.float32) for part in mixeds)
    mixed_out = (resid + mixed + down_bias).astype(LOW)

    other = moved(send, CORE, 1)
    grads = (keep.astype(jnp.float32) + other.astype(jnp.float32)).astype(LOW)
    feed_grads = lax.psum_scatter(
        grads.reshape(-1, width), PLANE, scatter_dimension=0, tiled=True
    ).astype(jnp.float32)

    d_resid, d_branch, sums_two, d_parts = branch_back(
        resid, cotangent, row(second_gain), gathered, rows // feats, feats, backs
    )
    d_attended = head_swap(d_parts)
    d_branch_all = lax.all_gather(d_branch, HEAD, axis=0, tiled=True).reshape(heads, rows, width)
    d_prefix = prefix_back(
        flags, turned_all, query, d_attended, attended, log_sums, prefix, rows
    )[0]
    older, newer = d_prefix[:, :KEPT], d_prefix[:, KEPT:]
    spread = jnp.pad(older, ((seg_local - 2, 2), (0, 0), (0, 0)))
    spread = spread + jnp.pad(newer, ((seg_local - 1, 1), (0, 0), (0, 0)))
    returned = spread[seg_local:] + shifted(spread[:seg_local], ITEM, -1)
    joint_grads = attend_back(
        flags, turned_all, query, d_attended, attended, log_sums, prefix, kv, returned, rows
    )[0]
    grads_own = head_swap(joint_grads).reshape(-1, rows)
    joint_part, bias_part, sums_one = joint_grad(
        joint_grads, gathered, joint_weight, row(first_gain), row(first_shift)
    )
    out_part = weight_grad(attended, d_branch_all)
    input_grad = input_back(grads_own, joint_full, tokens, row(first_gain), d_resid)

    joint_sum = item_sum(joint_part)
    out_sum = item_sum(out_part)
    bias_sums = all_sum(bias_part.reshape(-1), (ITEM,))
    early = all_sum(
        jnp.concatenate([up_bias_part.reshape(-1), sums_two.reshape(-1)]).reshape(-1, 128),
        (CORE, "y", "x"),
    ).reshape(-1)
    up_sums = lax.dynamic_update_slice_in_dim(
        jnp.zeros((hidden_units,), jnp.float32), early[:hidden_here], item_place * hidden_here, 0
    )
    early = all_sum(
        jnp.concatenate([up_sums, early[hidden_here:]]).reshape(-1, 128), (ITEM,)
    ).reshape(-1)
    late = all_sum(sums_one.reshape(-1, 128), (CORE, "y", "x", ITEM)).reshape(2, width)
    early_rows = early[hidden_units:].reshape(4, width)
    return (
        mixed_out,
        input_grad,
        joint_sum[:feats],
        joint_sum[feats : 2 * feats],
        joint_sum[2 * feats :],
        bias_sums[:feats],
        bias_sums[2 * feats :],
        out_sum,
        early_rows[2],
        late[0],
        late[1],
        early_rows[0],
        early_rows[1],
        feed_grads[:units],
        early[:hidden_units],
        feed_grads[units:],
        early_rows[3],
    )


def solution(mesh):
    sizes = (mesh.shape["item"], 4, mesh.shape["head"] // 8, 2)
    fine = Mesh(mesh.devices.reshape(sizes), (ITEM, *HEAD))
    split = P((ITEM, *HEAD), None)
    by_head = P(HEAD, None)
    return jax.shard_map(
        local,
        mesh=fine,
        in_specs=(
            split,
            split,
            P(),
            by_head,
            by_head,
            by_head,
            P(HEAD),
            P(HEAD),
            by_head,
            P(),
            P(),
            P(),
            P(),
            P(),
            split,
            P(),
            split,
            P(),
        ),
        out_specs=(
            split,
            split,
            by_head,
            by_head,
            by_head,
            P(HEAD),
            P(HEAD),
            by_head,
            P(),
            P(),
            P(),
            P(),
            P(),
            split,
            P(),
            split,
            P(),
        ),
        check_vma=False,
    )
```

```python
from functools import partial

import jax
import jax.numpy as jnp
from jax import lax
from jax.experimental import pallas as pl
from jax.experimental.pallas import tpu as pltpu
from jax.sharding import Mesh
from jax.sharding import PartitionSpec as P

HD = 64
NSUM = 50
SEG = 2048
SPAN = 512
KEPT = 64
EPSILON = 1e-05
MASKED = -1e30
SCALE = HD ** (-0.5)
MIB = 1 << 20
COST = 1 << 20
LOW = jnp.bfloat16


def dot(left, right):
    return jnp.dot(left, right, preferred_element_type=jnp.float32)


def dot_cols(left, right):
    return lax.dot_general(
        left, right, (((1,), (1,)), ((), ())), preferred_element_type=jnp.float32
    )


def turned(value):
    return value.astype(jnp.float32).T


def norm_parts(row_data):
    row_mean = jnp.mean(row_data, axis=-1, keepdims=True)
    centred = row_data - row_mean
    row_var = jnp.mean(centred * centred, axis=-1, keepdims=True)
    scale = lax.rsqrt(row_var + EPSILON)
    return centred * scale, scale


def norm_back(grad, normed, scale, gain):
    scaled = grad * gain
    return scale * (
        scaled
        - jnp.mean(scaled, axis=-1, keepdims=True)
        - normed * jnp.mean(scaled * normed, axis=-1, keepdims=True)
    )


def layer_norm(row_data, gain, shift):
    return norm_parts(row_data)[0] * gain + shift


def run(body, grid, in_specs, out_specs, out_shape, operands, scratch=(), vmem=32, aliases=None):
    return pl.pallas_call(
        body,
        grid=grid,
        in_specs=in_specs,
        out_specs=out_specs,
        out_shape=out_shape,
        scratch_shapes=scratch,
        compiler_params=pltpu.CompilerParams(
            dimension_semantics=("arbitrary",) * len(grid), vmem_limit_bytes=vmem * MIB
        ),
        input_output_aliases=aliases or {},
        cost_estimate=pl.CostEstimate(flops=COST, bytes_accessed=COST, transcendentals=0),
    )(*operands)


def shape(dims, kind):
    return jax.ShapeDtypeStruct(dims, kind)


def whole(item):
    return pl.BlockSpec(item.shape, lambda *_: (0,) * len(item.shape))


def project_kernel(rows_ref, weight_ref, bias_ref, query_ref, kv_ref, turned_ref):
    rows = rows_ref[...].reshape(SPAN, rows_ref.shape[2])
    joint = dot_cols(rows, weight_ref[...]) + bias_ref[...]
    query_ref[...] = joint[:, :HD].astype(LOW)
    kv_ref[...] = joint[:, HD:].astype(LOW)
    turned_ref[...] = joint.T.astype(LOW)


def project(gathered, rows_here, weight, bias):
    places, _, width = gathered.shape
    total = places * rows_here
    step = SPAN // rows_here
    return run(
        project_kernel,
        (total // SPAN,),
        [
            pl.BlockSpec((step, rows_here, width), lambda i: (i, 0, 0)),
            whole(weight),
            whole(bias),
        ],
        [
            pl.BlockSpec((SPAN, HD), lambda i: (i, 0)),
            pl.BlockSpec((SPAN, 2 * HD), lambda i: (i, 0)),
            pl.BlockSpec((3 * HD, SPAN), lambda i: (0, i)),
        ],
        [
            shape((total, HD), LOW),
            shape((total, 2 * HD), LOW),
            shape((3 * HD, total), LOW),
        ],
        (gathered, weight, bias),
    )


def prefix_seen(flags_ref, seg, columns):
    place = lax.broadcasted_iota(jnp.int32, (2 * KEPT, columns), 0)
    older = place < KEPT
    slot = jnp.where(older, place, place - KEPT) >= KEPT - NSUM
    flag = jnp.where(older, flags_ref[2 * seg], flags_ref[2 * seg + 1])
    return slot & (flag > 0)


def causal_seen():
    shape_here = (SPAN, SPAN)
    return lax.broadcasted_iota(jnp.int32, shape_here, 0) <= lax.broadcasted_iota(
        jnp.int32, shape_here, 1
    )


def above(block):
    return jnp.concatenate([block, jnp.zeros_like(block)], axis=0)


def below(block):
    return jnp.concatenate([jnp.zeros_like(block), block], axis=0)


def at_block(index):
    return pl.ds(pl.multiple_of(index * SPAN, SPAN), SPAN)


def attend_kernel(flags_ref, query_ref, turned_ref, kv_ref, prefix_ref, out_ref, log_ref):
    seg, block = pl.program_id(0), pl.program_id(1)
    query = above((query_ref[...].astype(jnp.float32) * SCALE).astype(LOW))
    own = at_block(block)
    scores = dot(kv_ref[own, :], query)
    scores = jnp.where(causal_seen(), scores, MASKED)
    top = jnp.max(scores, axis=0, keepdims=True)
    probs = jnp.exp(scores - top)
    total = jnp.sum(probs, axis=0, keepdims=True)
    mixed = dot(turned_ref[2 * HD :, own], probs.astype(LOW))

    def add(carry, scores, values):
        top, total, mixed = carry
        fresh = jnp.maximum(top, jnp.max(scores, axis=0, keepdims=True))
        fade = jnp.exp(top - fresh)
        probs = jnp.exp(scores - fresh)
        total = total * fade + jnp.sum(probs, axis=0, keepdims=True)
        return fresh, total, mixed * fade + dot(values, probs.astype(LOW))

    prefix = prefix_ref[0]
    scores = jnp.where(prefix_seen(flags_ref, seg, SPAN), dot(prefix, query), MASKED)
    carry = add((top, total, mixed), scores, turned(prefix)[HD:].astype(LOW))

    def step(index, carry):
        here = at_block(index)
        return add(carry, dot(kv_ref[here, :], query), turned_ref[2 * HD :, here])

    top, total, mixed = lax.fori_loop(0, block, step, carry)
    mixed = (mixed / total).astype(LOW)
    rows = out_ref.shape[2]
    for piece in range(SPAN // rows):
        out_ref[piece] = mixed[:, piece * rows : (piece + 1) * rows]
    log_ref[0] = top + jnp.log(total)


def attend(flags, turned_all, kv, prefix, rows_here):
    total = kv.shape[0]
    blocks = SEG // SPAN
    step = SPAN // rows_here
    return run(
        attend_kernel,
        (total // SEG, blocks),
        [
            pl.BlockSpec(memory_space=pltpu.SMEM),
            pl.BlockSpec((HD, SPAN), lambda s, i: (0, s * blocks + i)),
            pl.BlockSpec((3 * HD, SEG), lambda s, i: (0, s)),
            pl.BlockSpec((SEG, 2 * HD), lambda s, i: (s, 0)),
            pl.BlockSpec((1, 2 * KEPT, 2 * HD), lambda s, i: (s, 0, 0)),
        ],
        [
            pl.BlockSpec((step, HD, rows_here), lambda s, i: (s * blocks + i, 0, 0)),
            pl.BlockSpec((1, 1, SPAN), lambda s, i: (s * blocks + i, 0, 0)),
        ],
        [
            shape((total // rows_here, HD, rows_here), LOW),
            shape((total // SPAN, 1, SPAN), jnp.float32),
        ],
        (flags, turned_all, turned_all, kv, prefix),
    )


def side_by_side(ref):
    return jnp.concatenate([ref[piece] for piece in range(ref.shape[0])], axis=1)


def beside(block, place):
    zero = jnp.zeros_like(block)
    return jnp.concatenate([block, zero] if place == 0 else [zero, block], axis=1)


def query_side(query_ref, rows_ref, grad_ref, out_ref, log_ref):
    query = above((query_ref[...].astype(jnp.float32) * SCALE).astype(LOW))
    grad = side_by_side(grad_ref)
    mean = jnp.sum(
        grad.astype(jnp.float32) * side_by_side(out_ref).astype(jnp.float32),
        axis=0,
        keepdims=True,
    )
    query_rows = beside((rows_ref[...].astype(jnp.float32) * SCALE).astype(LOW), 0)
    grad_rows = beside(turned(grad).astype(LOW), 1)
    return query, below(grad), mean, log_ref[0], query_rows, grad_rows


def key_side(keys, side, seen):
    query, grad, mean, log_sum, query_rows, grad_rows = side
    probs = jnp.exp(dot(keys, query) - log_sum)
    if seen is not None:
        probs = jnp.where(seen, probs, 0.0)
    d_scores = (probs * (dot(keys, grad) - mean)).astype(LOW)
    return probs.astype(LOW), d_scores


def prefix_back_kernel(
    flags_ref, query_ref, rows_ref, grad_ref, out_ref, log_ref, prefix_ref, sum_ref
):
    seg, block = pl.program_id(0), pl.program_id(1)
    side = query_side(query_ref, rows_ref, grad_ref, out_ref, log_ref)
    probs, d_scores = key_side(prefix_ref[0], side, prefix_seen(flags_ref, seg, SPAN))
    part = dot(d_scores, side[4]) + dot(probs, side[5])

    @pl.when(block == 0)
    def _():
        sum_ref[0] = part

    @pl.when(block > 0)
    def _():
        sum_ref[0] += part


def attend_back_kernel(
    flags_ref,
    query_ref,
    rows_ref,
    grad_ref,
    out_ref,
    log_ref,
    prefix_ref,
    turned_ref,
    kv_ref,
    grads_ref,
    kept_ref,
    kv_grad,
):
    seg, block = pl.program_id(0), pl.program_id(1)

    @pl.when(block == 0)
    def _():
        kv_grad[...] = jnp.zeros_like(kv_grad)

    side = query_side(query_ref, rows_ref, grad_ref, out_ref, log_ref)
    prefix = prefix_ref[0]
    _, d_scores = key_side(prefix, side, prefix_seen(flags_ref, seg, SPAN))
    query_grad = dot(turned(prefix)[:HD].astype(LOW), d_scores)

    def add(here, query_grad, seen):
        probs, d_scores = key_side(kv_ref[here, :], side, seen)
        kv_grad[here, :] += dot(d_scores, side[4]) + dot(probs, side[5])
        return query_grad + dot(turned_ref[HD : 2 * HD, here], d_scores)

    query_grad = add(at_block(block), query_grad, causal_seen())
    query_grad = lax.fori_loop(
        0, block, lambda index, grad: add(at_block(index), grad, None), query_grad
    )
    query_grad = (query_grad * SCALE).astype(LOW)
    rows = grads_ref.shape[2]
    step = SPAN // rows
    for piece in range(step):
        grads_ref[block * step + piece, :HD, :] = query_grad[:, piece * rows : (piece + 1) * rows]

    @pl.when(block == pl.num_programs(1) - 1)
    def _():
        for piece in range(SEG // rows):
            grads_ref[piece, HD:, :] = kv_grad[piece * rows : (piece + 1) * rows, :].T.astype(LOW)
        kept_ref[0] = kv_grad[SEG - KEPT :, :]


def attend_back_specs(rows_here):
    blocks = SEG // SPAN
    step = SPAN // rows_here
    return [
        pl.BlockSpec(memory_space=pltpu.SMEM),
        pl.BlockSpec((HD, SPAN), lambda s, i: (0, s * blocks + i)),
        pl.BlockSpec((SPAN, HD), lambda s, i: (s * blocks + i, 0)),
        pl.BlockSpec((step, HD, rows_here), lambda s, i: (s * blocks + i, 0, 0)),
        pl.BlockSpec((step, HD, rows_here), lambda s, i: (s * blocks + i, 0, 0)),
        pl.BlockSpec((1, 1, SPAN), lambda s, i: (s * blocks + i, 0, 0)),
        pl.BlockSpec((1, 2 * KEPT, 2 * HD), lambda s, i: (s, 0, 0)),
    ]


def prefix_back(flags, turned_all, query, grad, out, log_sums, prefix, rows_here):
    total = query.shape[0]
    return run(
        prefix_back_kernel,
        (total // SEG, SEG // SPAN),
        attend_back_specs(rows_here),
        [pl.BlockSpec((1, 2 * KEPT, 2 * HD), lambda s, i: (s, 0, 0))],
        [shape(prefix.shape, jnp.float32)],
        (flags, turned_all, query, grad, out, log_sums, prefix),
    )


def attend_back(flags, turned_all, query, grad, out, log_sums, prefix, kv, rows_here):
    total = query.shape[0]
    pieces = SEG // rows_here
    return run(
        attend_back_kernel,
        (total // SEG, SEG // SPAN),
        attend_back_specs(rows_here)
        + [
            pl.BlockSpec((3 * HD, SEG), lambda s, i: (0, s)),
            pl.BlockSpec((SEG, 2 * HD), lambda s, i: (s, 0)),
        ],
        [
            pl.BlockSpec((pieces, 3 * HD, rows_here), lambda s, i: (s, 0, 0)),
            pl.BlockSpec((1, KEPT, 2 * HD), lambda s, i: (s, 0, 0)),
        ],
        [
            shape((total // rows_here, 3 * HD, rows_here), LOW),
            shape((total // SEG, KEPT, 2 * HD), jnp.float32),
        ],
        (flags, turned_all, query, grad, out, log_sums, prefix, turned_all, kv),
        scratch=[pltpu.VMEM((SEG, 2 * HD), jnp.float32)],
    )


def returned_kernel(grads_ref, kept_ref, returned_ref, out_ref):
    rows = out_ref.shape[2]
    out_ref[0, :, : rows - KEPT] = grads_ref[0, :, : rows - KEPT]
    out_ref[0, :HD, rows - KEPT :] = grads_ref[0, :HD, rows - KEPT :]
    out_ref[0, HD:, rows - KEPT :] = (kept_ref[0] + returned_ref[0]).T.astype(LOW)


def add_returned(grads, kept, returned):
    places, feats, rows = grads.shape
    segs = kept.shape[0]
    last = places // segs
    grad_spec = pl.BlockSpec((1, feats, rows), lambda s: (s * last + last - 1, 0, 0))
    kept_spec = pl.BlockSpec((1, KEPT, 2 * HD), lambda s: (s, 0, 0))
    return run(
        returned_kernel,
        (segs,),
        [grad_spec, kept_spec, kept_spec],
        [grad_spec],
        [shape(grads.shape, LOW)],
        (grads, kept, returned),
        aliases={0: 0},
    )[0]


def out_kernel(
    part_ref, weight_ref, tokens_ref, bias_ref, gain_ref, shift_ref, resid_ref, two_ref, total
):
    step = pl.program_id(0)
    rows = part_ref.shape[2]
    part = turned(part_ref[...].reshape(-1, rows)).astype(LOW)
    added = dot(part, weight_ref[...].reshape(part.shape[1], -1))

    @pl.when(step == 0)
    def _():
        total[...] = added

    @pl.when(step > 0)
    def _():
        total[...] += added

    @pl.when(step == pl.num_programs(0) - 1)
    def _():
        resid = tokens_ref[...].astype(jnp.float32) + total[...] + bias_ref[...]
        resid_ref[...] = resid
        two_ref[...] = layer_norm(resid, gain_ref[...], shift_ref[...]).astype(LOW)


def out_project(parts, gathered, at, tokens, bias, gain, shift, step=4):
    places, feats, rows = parts.shape
    width = gathered.shape[2]
    return run(
        out_kernel,
        (places // step,),
        [
            pl.BlockSpec((step, feats, rows), lambda i: (i, 0, 0)),
            pl.BlockSpec((step, feats, width), lambda i: (i, at, 0)),
            whole(tokens),
            whole(bias),
            whole(gain),
            whole(shift),
        ],
        [pl.BlockSpec((rows, width), lambda i: (0, 0))] * 2,
        [shape((rows, width), jnp.float32), shape((rows, width), LOW)],
        (parts, gathered, tokens, bias, gain, shift),
        scratch=[pltpu.VMEM((rows, width), jnp.float32)],
    )


def owner_maps(chips, at, cores=(0, 1)):
    chips_x, chips_y = chips

    def of(core_step, y_step):
        def index(i, place):
            x = lax.rem(place[1] + i, chips_x)
            y = lax.rem(place[2] + y_step, chips_y)
            return at((x * chips_y + y) * 2 + lax.rem(place[0] + core_step, 2))

        return index

    return [of(core_step, y_step) for core_step in cores for y_step in range(chips_y)]


def own_map(index):
    return lambda i, place: index(i)


def fixed(dims):
    return pl.BlockSpec(
        dims, own_map(lambda i: (0,) * len(dims)), pipeline_mode=pl.Buffered(buffer_count=1)
    )


def feed_run(body, chips, place, in_specs, out_specs, out_shape, operands, scratch, vmem):
    return pl.pallas_call(
        body,
        grid_spec=pltpu.PrefetchScalarGridSpec(
            num_scalar_prefetch=1,
            grid=(chips[0],),
            in_specs=in_specs,
            out_specs=out_specs,
            scratch_shapes=scratch,
        ),
        out_shape=out_shape,
        compiler_params=pltpu.CompilerParams(
            dimension_semantics=("arbitrary",), vmem_limit_bytes=vmem * MIB
        ),
        cost_estimate=pl.CostEstimate(flops=COST, bytes_accessed=COST, transcendentals=0),
    )(place, *operands)


def stacked(refs, axis=0):
    return jnp.concatenate([ref[0] for ref in refs], axis=axis)


def pile(refs, into):
    rows = refs[0].shape[0]
    for at, ref in enumerate(refs):
        into[at * rows : (at + 1) * rows, :] = ref[...]


def spread(source, refs):
    rows = refs[0].shape[0]
    for at, ref in enumerate(refs):
        ref[...] = source[at * rows : (at + 1) * rows, :].astype(ref.dtype)


def take(refs, *counts):
    refs = list(refs)
    return [[refs.pop(0) for _ in range(count)] for count in counts] + [refs]


def d_act_kernel(count, owners, place_ref, *refs):
    cot_refs, weight_refs, (out_ref, cots) = take(refs, count, owners)

    @pl.when(pl.program_id(0) == 0)
    def _():
        pile(cot_refs, cots)

    out_ref[...] = dot_cols(cots[...], stacked(weight_refs))


def feed_d_act(place, chips, cots, weights):
    count = len(cots)
    rows, width = cots[0].shape
    places, both, _ = weights.shape
    units = both // 2
    total = count * rows
    owners = 2 * chips[1]
    step = owners * units
    return feed_run(
        partial(d_act_kernel, count, owners),
        chips,
        place,
        [fixed((rows, width))] * count
        + [
            pl.BlockSpec((1, units, width), at)
            for at in owner_maps(chips, lambda owner: (owner, 1, 0))
        ],
        [pl.BlockSpec((total, step), own_map(lambda i: (0, i)))],
        [shape((total, places * units), jnp.float32)],
        (*cots, *[weights] * owners),
        [pltpu.VMEM((total, width), LOW)],
        32,
    )[0]


def feed_kernel(count, chips, place_ref, *refs):
    owners = 2 * chips[1]
    norm_refs, weight_refs, bias_refs, (d_act_ref,), back_refs, refs = take(
        refs, count, owners, owners, 1, count
    )
    kept_ref, sent_ref, bias_sum_ref, norms, back = refs
    step = pl.program_id(0)

    @pl.when(step == 0)
    def _():
        pile(norm_refs, norms)
        back[...] = jnp.zeros_like(back)

    up = stacked(weight_refs)
    pre = dot_cols(norms[...], up) + stacked(bias_refs, axis=1)
    square = pre * pre
    bent = jnp.tanh(0.7978845608 * (pre + 0.044715 * (square * pre)))
    half = 0.5 * (1.0 + bent)
    slope = half + 0.5 * pre * (1.0 - bent * bent) * (
        0.7978845608 * (1.0 + 3.0 * 0.044715 * square)
    )
    d_pre = (d_act_ref[...] * slope).astype(LOW)
    act = (pre * half).astype(LOW)
    own = act.shape[1] // 2
    kept_ref[0] = act[:, :own]
    kept_ref[1] = d_pre[:, :own]
    sent_ref[0] = act[:, own:]
    sent_ref[1] = d_pre[:, own:]
    bias_sums = jnp.sum(d_pre.astype(jnp.float32), axis=0, keepdims=True)
    units = weight_refs[0].shape[1]
    for at, index in enumerate(owner_maps(chips, lambda owner: owner)):
        bias_sum_ref[index(step, place_ref)] = bias_sums[:, at * units : (at + 1) * units]
    back[...] += dot(d_pre, up)

    @pl.when(step == pl.num_programs(0) - 1)
    def _():
        spread(back, back_refs)


def feed(place, chips, norms, weights, bias, d_act):
    count = len(norms)
    rows, width = norms[0].shape
    places, both, _ = weights.shape
    units = both // 2
    total = count * rows
    owners = 2 * chips[1]
    step = owners * units
    pair_spec = pl.BlockSpec((2, total, step // 2), own_map(lambda i: (0, 0, i)))
    results = feed_run(
        partial(feed_kernel, count, chips),
        chips,
        place,
        [fixed((rows, width))] * count
        + [
            pl.BlockSpec((1, units, width), at)
            for at in owner_maps(chips, lambda owner: (owner, 0, 0))
        ]
        + [
            pl.BlockSpec((1, 1, units), at)
            for at in owner_maps(chips, lambda owner: (owner, 0, 0))
        ]
        + [pl.BlockSpec((total, step), own_map(lambda i: (0, i)))],
        [pl.BlockSpec((rows, width), own_map(lambda i: (0, 0)))] * count
        + [pair_spec, pair_spec, pl.BlockSpec((places, 1, units), own_map(lambda i: (0, 0, 0)))],
        [shape((rows, width), LOW)] * count
        + [shape((2, total, places * units // 2), LOW)] * 2
        + [shape((places, 1, units), jnp.float32)],
        (*norms, *[weights] * owners, *[bias] * owners, d_act),
        [pltpu.VMEM((total, width), LOW), pltpu.VMEM((total, width), jnp.float32)],
        40,
    )
    return results[:count], results[count:]


def feed_grad_kernel(count, owners, turns, place_ref, *refs):
    norm_refs, cot_refs, pair_refs, weight_refs, mixed_refs, x_refs, y_refs, refs = take(
        refs, 2 * count, 2 * count, 3, owners, count, turns, owners // 2
    )
    norms, cots, mixed = refs
    kept_ref, sent_ref, other_ref = pair_refs
    step = pl.program_id(0)
    units = weight_refs[0].shape[1]

    @pl.when(step == 0)
    def _():
        pile(norm_refs, norms)
        pile(cot_refs, cots)
        mixed[...] = jnp.zeros_like(mixed)

    act = jnp.concatenate([kept_ref[0], sent_ref[0]], axis=1)
    mixed[...] += dot(act, stacked(weight_refs))

    def grad(at, rows):
        both = jnp.concatenate([kept_ref[at], other_ref[at]], axis=0)
        return dot(turned(both).astype(LOW), rows[...]).astype(LOW)

    half = units // 2
    down_grad = grad(0, cots)
    up_grad = grad(1, norms)
    for at, ref in enumerate(y_refs):
        ref[0, :half] = up_grad[at * units + half : (at + 1) * units]
        ref[0, half:] = down_grad[at * units : (at + 1) * units]
    for at, ref in enumerate(x_refs):

        @pl.when(step == at)
        def _():
            for turn in range(ref.shape[0]):
                ref[turn] = up_grad[turn * units : turn * units + half]

    @pl.when(step == pl.num_programs(0) - 1)
    def _():
        spread(mixed, mixed_refs)


def feed_grad(place, chips, norms, cots, kept, sent, other, weights):
    count = len(norms) // 2
    rows, width = norms[0].shape
    units = weights.shape[1] // 2
    total = count * rows
    chips_x, chips_y = chips
    owners = 2 * chips_y
    row_spec = pl.BlockSpec((rows, width), own_map(lambda i: (0, 0)))
    pair_spec = pl.BlockSpec((2, total, owners * units // 2), own_map(lambda i: (0, 0, i)))
    results = feed_run(
        partial(feed_grad_kernel, count, owners, chips_x),
        chips,
        place,
        [fixed((rows, width))] * (4 * count)
        + [pair_spec] * 3
        + [
            pl.BlockSpec((1, units, width), at)
            for at in owner_maps(chips, lambda owner: (owner, 1, 0))
        ],
        [row_spec] * count
        + [pl.BlockSpec((chips_y, units // 2, width), own_map(lambda i: (0, 0, 0)))] * chips_x
        + [pl.BlockSpec((1, 3 * units // 2, width), own_map(lambda i: (i, 0, 0)))] * chips_y,
        [shape((rows, width), LOW)] * count
        + [shape((chips_y, units // 2, width), LOW)] * chips_x
        + [shape((chips_x, 3 * units // 2, width), LOW)] * chips_y,
        (*norms, *cots, kept, sent, other, *[weights] * owners),
        [pltpu.VMEM((2 * total, width), LOW)] * 2 + [pltpu.VMEM((total, width), jnp.float32)],
        56,
    )
    return results[:count], results[count : count + chips_x], results[count + chips_x :]


def branch_kernel(
    count, resid_ref, cot_ref, gain_ref, weight_ref, *refs
):
    back_refs = refs[:count]
    d_resid_ref, d_branch_ref, sums_ref, parts_ref = refs[count:]

    @pl.when(pl.program_id(0) == 0)
    def _():
        d_two = sum(ref[...].astype(jnp.float32) for ref in back_refs)
        normed, scale = norm_parts(resid_ref[...])
        cot = cot_ref[...].astype(jnp.float32)
        d_resid = cot + norm_back(d_two, normed, scale, gain_ref[...])
        d_branch = d_resid.astype(LOW)
        d_resid_ref[...] = d_resid
        d_branch_ref[...] = d_branch
        sums_ref[0:1, :] = jnp.sum(d_two * normed, axis=0, keepdims=True)
        sums_ref[1:2, :] = jnp.sum(d_two, axis=0, keepdims=True)
        sums_ref[2:3, :] = jnp.sum(d_branch.astype(jnp.float32), axis=0, keepdims=True)
        sums_ref[3:4, :] = jnp.sum(cot, axis=0, keepdims=True)

    width = weight_ref.shape[2]
    part = dot_cols(weight_ref[...].reshape(-1, width), d_branch_ref[...])
    parts_ref[...] = part.reshape(parts_ref.shape).astype(LOW)


def branch_back(resid, cotangent, gain, gathered, at, feats, backs, step=4):
    rows, width = resid.shape
    places = gathered.shape[0]
    row_spec = pl.BlockSpec((rows, width), lambda i: (0, 0))
    return run(
        partial(branch_kernel, len(backs)),
        (places // step,),
        [
            row_spec,
            row_spec,
            whole(gain),
            pl.BlockSpec((step, feats, width), lambda i: (i, at, 0)),
        ]
        + [row_spec] * len(backs),
        [
            row_spec,
            row_spec,
            pl.BlockSpec((4, width), lambda i: (0, 0)),
            pl.BlockSpec((step, feats, rows), lambda i: (i, 0, 0)),
        ],
        [
            shape((rows, width), jnp.float32),
            shape((rows, width), LOW),
            shape((4, width), jnp.float32),
            shape((places, feats, rows), LOW),
        ],
        (resid, cotangent, gain, gathered, *backs),
    )


def branch_grad_kernel(owners, place_ref, *refs):
    own_refs, other_refs, grad_refs, out_refs = take(refs, owners, owners, 2)
    parts = jnp.concatenate([stacked(own_refs), stacked(other_refs)], axis=1)
    grads = jnp.concatenate([ref[...] for ref in grad_refs], axis=0)
    out = dot(parts, grads).astype(LOW).reshape(out_refs[0].shape)
    for at, ref in enumerate(out_refs):

        @pl.when(pl.program_id(0) == at)
        def _():
            ref[...] = out


def branch_grad(place, chips, own, other, own_grad, other_grad):
    _, feats, rows = own.shape
    width = own_grad.shape[1]
    chips_x, chips_y = chips
    part_specs = [
        pl.BlockSpec((1, feats, rows), at)
        for at in owner_maps(chips, lambda owner: (owner, 0, 0), cores=(0,))
    ]
    return feed_run(
        partial(branch_grad_kernel, chips_y),
        chips,
        place,
        part_specs * 2 + [fixed((rows, width))] * 2,
        [pl.BlockSpec((chips_y, feats, width), own_map(lambda i: (0, 0, 0)))] * chips_x,
        [shape((chips_y, feats, width), LOW)] * chips_x,
        (*[own] * chips_y, *[other] * chips_y, own_grad, other_grad),
        [],
        32,
    )


def joint_grad_kernel(
    grad_ref, rows_ref, weight_ref, gain_ref, shift_ref, out_ref, bias_ref, sums_ref, total, biases
):
    step = pl.program_id(0)
    grads = side_by_side(grad_ref)
    added = dot(grads, rows_ref[...].reshape(grads.shape[1], -1))
    summed = jnp.sum(grads.astype(jnp.float32), axis=1, keepdims=True)

    @pl.when(step == 0)
    def _():
        total[...] = added
        biases[...] = summed

    @pl.when(step > 0)
    def _():
        total[...] += added
        biases[...] += summed

    @pl.when(step == pl.num_programs(0) - 1)
    def _():
        out_ref[...] = total[...].astype(LOW)
        bias_ref[...] = biases[...]
        weight = weight_ref[...].astype(jnp.float32)
        shift_sum = jnp.sum(weight * biases[...], axis=0, keepdims=True)
        product = jnp.sum(weight * total[...], axis=0, keepdims=True)
        sums_ref[0:1, :] = (product - shift_sum * shift_ref[...]) / gain_ref[...]
        sums_ref[1:2, :] = shift_sum


def joint_grad(grads, gathered, weight, gain, shift, step=4):
    places, feats, rows = grads.shape
    width = gathered.shape[2]
    return run(
        joint_grad_kernel,
        (places // step,),
        [
            pl.BlockSpec((step, feats, rows), lambda i: (i, 0, 0)),
            pl.BlockSpec((step, rows, width), lambda i: (i, 0, 0)),
            whole(weight),
            whole(gain),
            whole(shift),
        ],
        [
            pl.BlockSpec((feats, width), lambda i: (0, 0)),
            pl.BlockSpec((feats, 1), lambda i: (0, 0)),
            pl.BlockSpec((2, width), lambda i: (0, 0)),
        ],
        [
            shape((feats, width), LOW),
            shape((feats, 1), jnp.float32),
            shape((2, width), jnp.float32),
        ],
        (grads, gathered, weight, gain, shift),
        scratch=[pltpu.VMEM((feats, width), jnp.float32), pltpu.VMEM((feats, 1), jnp.float32)],
    )


def input_kernel(part_ref, weight_ref, tokens_ref, gain_ref, d_resid_ref, out_ref, total):
    step = pl.program_id(0)
    added = dot(turned(part_ref[...]).astype(LOW), weight_ref[...])

    @pl.when(step == 0)
    def _():
        total[...] = added

    @pl.when(step > 0)
    def _():
        total[...] += added

    @pl.when(step == pl.num_programs(0) - 1)
    def _():
        normed, scale = norm_parts(tokens_ref[...].astype(jnp.float32))
        out_ref[...] = d_resid_ref[...] + norm_back(total[...], normed, scale, gain_ref[...])


def input_back(parts, weights, tokens, gain, d_resid, step=SPAN):
    feats, rows = parts.shape
    width = weights.shape[1]
    return run(
        input_kernel,
        (feats // step,),
        [
            pl.BlockSpec((step, rows), lambda i: (i, 0)),
            pl.BlockSpec((step, width), lambda i: (i, 0)),
            whole(tokens),
            whole(gain),
            whole(d_resid),
        ],
        [pl.BlockSpec((rows, width), lambda i: (0, 0))],
        [shape((rows, width), jnp.float32)],
        (parts, weights, tokens, gain, d_resid),
        scratch=[pltpu.VMEM((rows, width), jnp.float32)],
    )[0]


ITEM = "z"
HEAD = ("x", "y", "c")
CORE = "c"


def moved(value, axis, steps):
    count = lax.axis_size(axis)
    return lax.ppermute(value, axis, [(place, (place + steps) % count) for place in range(count)])


def shifted(value, axis, steps):
    count = lax.axis_size(axis)
    initial, last = (max(0, -steps), min(count, count - steps))
    return lax.ppermute(value, axis, [(source, source + steps) for source in range(initial, last)])


def all_sum(value, axes):
    for axis in axes:
        if lax.axis_size(axis) == 4:
            terms = around(value, axis)
            value = (terms[0] + terms[2]) + (terms[1] + terms[3])
            continue
        step = 1
        while step < lax.axis_size(axis):
            pairs = [(place, place ^ step) for place in range(lax.axis_size(axis))]
            value = value + lax.ppermute(value, axis, pairs)
            step *= 2
    return value


def around(value, axis):
    return [value] + [moved(value, axis, -step) for step in range(1, lax.axis_size(axis))]


def sum_back(values, axis):
    return [values[0]] + [
        moved(values[step], axis, step) for step in range(1, lax.axis_size(axis))
    ]


def item_terms(value):
    count = lax.axis_size(ITEM)
    place = lax.axis_index(ITEM)
    parts = value.reshape(count, -1, value.shape[1])
    own = [
        lax.dynamic_index_in_dim(parts, (place + step) % count, 0, keepdims=False)
        for step in range(count)
    ]
    return sum_back(own, ITEM)


def item_sum(terms):
    count = lax.axis_size(ITEM)
    place = lax.axis_index(ITEM)
    block = sum(term.astype(jnp.float32) for term in terms).astype(LOW)
    blocks = around(block, ITEM)
    rows = lax.dynamic_slice_in_dim(
        jnp.stack(blocks + blocks), (count - place) % count, count, 0
    )
    return rows.reshape(-1, block.shape[1]).astype(jnp.float32)


def chip_terms(terms, axis):
    return sum_back(terms, axis)


def chip_sum(terms, axis):
    terms = [term.astype(jnp.float32) for term in terms]
    terms = [sum(term[step] for term in terms).astype(LOW) for step in range(lax.axis_size(axis))]
    return sum(term.astype(jnp.float32) for term in sum_back(terms, axis))


def head_swap(value):
    return lax.all_to_all(value, HEAD, split_axis=0, concat_axis=0, tiled=True)


def segment_flags(seg_counts):
    total_segs = seg_counts.shape[0]
    openings = jnp.cumsum(seg_counts) - seg_counts
    places = jnp.arange(total_segs, dtype=jnp.int32)
    opens_here = jnp.any((openings[:, None] == places[None, :]) & (seg_counts[:, None] > 0), axis=0)
    opens_before = jnp.concatenate([jnp.ones((1,), dtype=bool), opens_here[:-1]])
    one_back = jnp.logical_not(opens_here)
    two_back = one_back & jnp.logical_not(opens_before)
    return (one_back, two_back)


def local(
    tokens,
    cotangent,
    seg_counts,
    query_weight,
    key_weight,
    value_weight,
    query_bias,
    value_bias,
    out_weight,
    out_bias,
    first_gain,
    first_shift,
    second_gain,
    second_shift,
    up_weight,
    up_bias,
    down_weight,
    down_bias,
):
    rows, width = tokens.shape
    heads = lax.axis_size(HEAD)
    item_place = lax.axis_index(ITEM)
    group_rows = rows * heads
    seg_local = group_rows // SEG
    feats = query_weight.shape[0]
    units = up_weight.shape[0]
    hidden_here = units * heads

    def row(vector):
        return vector.reshape(1, -1)

    tokens_f = tokens.astype(jnp.float32)
    inputs_one = layer_norm(tokens_f, first_gain, first_shift).astype(LOW)
    first = jnp.concatenate([inputs_one, out_weight], axis=0)
    gathered = lax.all_gather(first, HEAD, axis=0, tiled=True).reshape(heads, -1, width)
    second = jnp.concatenate([up_weight, down_weight], axis=0)
    feed_weights = lax.all_gather(second, HEAD, axis=0, tiled=True).reshape(heads, -1, width)
    cots = around(cotangent, ITEM)
    cots = cots + [moved(cot, CORE, 1) for cot in cots]
    joint_weight = jnp.concatenate([query_weight, key_weight, value_weight], axis=0)
    joint_bias = jnp.concatenate([query_bias, jnp.zeros_like(query_bias), value_bias])

    one_back, two_back = segment_flags(seg_counts)
    flags = jnp.stack([two_back, one_back], axis=1).astype(jnp.int32)
    flags = lax.dynamic_slice_in_dim(flags, item_place * seg_local, seg_local).reshape(-1)

    gathered, cots = lax.optimization_barrier((gathered, cots))
    query, kv, turned_all = project(gathered, rows, joint_weight, row(joint_bias))
    own_kept = kv.reshape(seg_local, SEG, 2 * HD)[:, SEG - KEPT :]
    table = jnp.concatenate([shifted(own_kept, ITEM, 1), own_kept], axis=0)
    prefix = jnp.concatenate(
        [table[seg_local - 2 : 2 * seg_local - 2], table[seg_local - 1 : 2 * seg_local - 1]], axis=1
    )
    attended, log_sums = attend(flags, turned_all, kv, prefix, rows)
    attended_own = head_swap(attended)
    attended_other = moved(attended_own, CORE, 1)
    resid, inputs_two = out_project(
        attended_own, gathered, rows // feats, tokens, row(out_bias), row(second_gain), row(second_shift)
    )

    joint_turn = lax.optimization_barrier((joint_weight, resid))[0]
    joint_full = lax.all_gather(joint_turn, HEAD, axis=0, tiled=True)
    norms = around(inputs_two, ITEM)
    chips = (lax.axis_size("x"), lax.axis_size("y"))
    place = jnp.stack([lax.axis_index(axis) for axis in (CORE, "x", "y")]).astype(jnp.int32)
    d_act = feed_d_act(place, chips, cots[: len(cots) // 2], feed_weights)
    bias_here = lax.dynamic_slice_in_dim(up_bias, item_place * hidden_here, hidden_here)
    backs, (kept, sent, up_bias_part) = feed(
        place, chips, norms, feed_weights, bias_here.reshape(heads, 1, units), d_act
    )
    norms = norms + [moved(norm, CORE, 1) for norm in norms]
    backs, norms = lax.optimization_barrier((backs, norms))
    backs = sum_back(backs, ITEM)
    mixeds, grads_x, grads_y = feed_grad(
        place, chips, norms, cots, kept, sent, moved(sent, CORE, 1), feed_weights
    )
    backs, mixeds = lax.optimization_barrier((backs, mixeds))
    mixeds = sum_back(mixeds, ITEM)
    mixed = sum(part.astype(jnp.float32) for part in mixeds)
    mixed_out = (resid + mixed + down_bias).astype(LOW)

    d_resid, d_branch, sums_two, d_parts = branch_back(
        resid, cotangent, row(second_gain), gathered, rows // feats, feats, backs
    )
    d_attended = head_swap(d_parts)

    outs = branch_grad(
        place, chips, attended_own, attended_other, d_branch, moved(d_branch, CORE, 1)
    )
    d_attended, outs = lax.optimization_barrier((d_attended, outs))
    outs = chip_terms(outs, "x")
    grads_x, grads_y = chip_terms(grads_x, "x"), chip_terms(grads_y, "y")

    d_prefix = prefix_back(
        flags, turned_all, query, d_attended, attended, log_sums, prefix, rows
    )[0]
    older, newer = d_prefix[:, :KEPT], d_prefix[:, KEPT:]
    spread = jnp.pad(older, ((seg_local - 2, 2), (0, 0), (0, 0)))
    spread = spread + jnp.pad(newer, ((seg_local - 1, 1), (0, 0), (0, 0)))
    returned = shifted(spread[:seg_local], ITEM, -1)
    joint_grads, kept_grads = attend_back(
        flags, turned_all, query, d_attended, attended, log_sums, prefix, kv, rows
    )
    returned, kept_grads, joint_full = lax.optimization_barrier((returned, kept_grads, joint_full))
    joint_grads = add_returned(joint_grads, kept_grads, spread[seg_local:] + returned)
    grads_own = head_swap(joint_grads).reshape(-1, rows)
    joint_part, bias_part, sums_one = joint_grad(
        joint_grads, gathered, joint_weight, row(first_gain), row(first_shift)
    )
    outs, grads_x, grads_y, joint_part = lax.optimization_barrier(
        (outs, grads_x, grads_y, joint_part)
    )
    out_part = chip_sum(outs, "y").astype(LOW)
    small = [up_bias_part.reshape(-1), sums_two.reshape(-1), sums_one.reshape(-1)]
    small = all_sum(jnp.concatenate(small).reshape(-1, 128), (CORE, "y"))
    grads_own, out_part, small = lax.optimization_barrier((grads_own, out_part, small))
    terms = item_terms(jnp.concatenate([joint_part, out_part], axis=0))
    small = all_sum(small, ("x",))
    grads_x, grads_y = chip_sum(grads_x, "y"), chip_sum(grads_y, "x")
    input_grad = input_back(grads_own, joint_full, tokens, row(first_gain), d_resid)
    input_grad, terms, small = lax.optimization_barrier((input_grad, terms, small))
    item_sums = item_sum(terms)
    up_grad = jnp.concatenate([grads_x, grads_y[: units // 2]], axis=0)
    down_grad = grads_y[units // 2 :]
    small = small.reshape(-1)
    up_bias_sums, small = small[:hidden_here], small[hidden_here:]
    up_bias_sums = lax.dynamic_update_slice_in_dim(
        jnp.zeros(up_bias.shape, jnp.float32), up_bias_sums, item_place * hidden_here, 0
    )
    small = jnp.concatenate([up_bias_sums, small, bias_part.reshape(-1)])
    small = all_sum(jnp.pad(small, (0, -small.size % 128)).reshape(-1, 128), (ITEM,)).reshape(-1)
    up_bias_grad, small = small[: up_bias.size], small[up_bias.size :]
    early_rows, late = small[: 4 * width].reshape(4, width), small[4 * width : 6 * width]
    late = late.reshape(2, width)
    bias_sums = small[6 * width : 6 * width + 3 * feats]
    return (
        mixed_out,
        input_grad,
        item_sums[:feats],
        item_sums[feats : 2 * feats],
        item_sums[2 * feats : 3 * feats],
        bias_sums[:feats],
        bias_sums[2 * feats :],
        item_sums[3 * feats :],
        early_rows[2],
        late[0],
        late[1],
        early_rows[0],
        early_rows[1],
        up_grad,
        up_bias_grad,
        down_grad,
        early_rows[3],
    )


def solution(mesh):
    sizes = (mesh.shape["item"], 4, mesh.shape["head"] // 8, 2)
    fine = Mesh(mesh.devices.reshape(sizes), (ITEM, *HEAD))
    split = P((ITEM, *HEAD), None)
    by_head = P(HEAD, None)
    return jax.shard_map(
        local,
        mesh=fine,
        in_specs=(
            split,
            split,
            P(),
            by_head,
            by_head,
            by_head,
            P(HEAD),
            P(HEAD),
            by_head,
            P(),
            P(),
            P(),
            P(),
            P(),
            split,
            P(),
            split,
            P(),
        ),
        out_specs=(
            split,
            split,
            by_head,
            by_head,
            by_head,
            P(HEAD),
            P(HEAD),
            by_head,
            P(),
            P(),
            P(),
            P(),
            P(),
            split,
            P(),
            split,
            P(),
        ),
        check_vma=False,
    )
```

```python
from functools import partial

import jax
import jax.numpy as jnp
from jax import lax
from jax.experimental import pallas as pl
from jax.experimental.pallas import tpu as pltpu
from jax.sharding import Mesh
from jax.sharding import PartitionSpec as P

HD = 64
NSUM = 50
SEG = 2048
SPAN = 512
KEPT = 64
EPSILON = 1e-05
MASKED = -1e30
SCALE = HD ** (-0.5)
MIB = 1 << 20
COST = 1 << 20
LOW = jnp.bfloat16


def dot(left, right):
    return jnp.dot(left, right, preferred_element_type=jnp.float32)


def dot_cols(left, right):
    return lax.dot_general(
        left, right, (((1,), (1,)), ((), ())), preferred_element_type=jnp.float32
    )


def turned(value):
    return value.astype(jnp.float32).T


def norm_parts(row_data):
    row_mean = jnp.mean(row_data, axis=-1, keepdims=True)
    centred = row_data - row_mean
    row_var = jnp.mean(centred * centred, axis=-1, keepdims=True)
    scale = lax.rsqrt(row_var + EPSILON)
    return centred * scale, scale


def norm_back(grad, normed, scale, gain):
    scaled = grad * gain
    return scale * (
        scaled
        - jnp.mean(scaled, axis=-1, keepdims=True)
        - normed * jnp.mean(scaled * normed, axis=-1, keepdims=True)
    )


def layer_norm(row_data, gain, shift):
    return norm_parts(row_data)[0] * gain + shift


def run(body, grid, in_specs, out_specs, out_shape, operands, scratch=(), vmem=32, aliases=None):
    return pl.pallas_call(
        body,
        grid=grid,
        in_specs=in_specs,
        out_specs=out_specs,
        out_shape=out_shape,
        scratch_shapes=scratch,
        compiler_params=pltpu.CompilerParams(
            dimension_semantics=("arbitrary",) * len(grid), vmem_limit_bytes=vmem * MIB
        ),
        input_output_aliases=aliases or {},
        cost_estimate=pl.CostEstimate(flops=COST, bytes_accessed=COST, transcendentals=0),
    )(*operands)


def shape(dims, kind):
    return jax.ShapeDtypeStruct(dims, kind)


def whole(item):
    return pl.BlockSpec(item.shape, lambda *_: (0,) * len(item.shape))


def project_kernel(rows_ref, weight_ref, bias_ref, query_ref, kv_ref, turned_ref):
    rows = rows_ref[...].reshape(SPAN, rows_ref.shape[2])
    joint = dot_cols(rows, weight_ref[...]) + bias_ref[...]
    query_ref[...] = joint[:, :HD].astype(LOW)
    kv_ref[...] = joint[:, HD:].astype(LOW)
    turned_ref[...] = joint.T.astype(LOW)


def project(gathered, rows_here, weight, bias):
    places, _, width = gathered.shape
    total = places * rows_here
    step = SPAN // rows_here
    return run(
        project_kernel,
        (total // SPAN,),
        [
            pl.BlockSpec((step, rows_here, width), lambda i: (i, 0, 0)),
            whole(weight),
            whole(bias),
        ],
        [
            pl.BlockSpec((SPAN, HD), lambda i: (i, 0)),
            pl.BlockSpec((SPAN, 2 * HD), lambda i: (i, 0)),
            pl.BlockSpec((3 * HD, SPAN), lambda i: (0, i)),
        ],
        [
            shape((total, HD), LOW),
            shape((total, 2 * HD), LOW),
            shape((3 * HD, total), LOW),
        ],
        (gathered, weight, bias),
    )


def prefix_seen(flags_ref, seg, columns):
    place = lax.broadcasted_iota(jnp.int32, (2 * KEPT, columns), 0)
    older = place < KEPT
    slot = jnp.where(older, place, place - KEPT) >= KEPT - NSUM
    flag = jnp.where(older, flags_ref[2 * seg], flags_ref[2 * seg + 1])
    return slot & (flag > 0)


def causal_seen():
    shape_here = (SPAN, SPAN)
    return lax.broadcasted_iota(jnp.int32, shape_here, 0) <= lax.broadcasted_iota(
        jnp.int32, shape_here, 1
    )


def above(block):
    return jnp.concatenate([block, jnp.zeros_like(block)], axis=0)


def below(block):
    return jnp.concatenate([jnp.zeros_like(block), block], axis=0)


def at_block(index):
    return pl.ds(pl.multiple_of(index * SPAN, SPAN), SPAN)


def attend_kernel(flags_ref, query_ref, turned_ref, kv_ref, prefix_ref, out_ref, log_ref):
    seg, block = pl.program_id(0), pl.program_id(1)
    query = above((query_ref[...].astype(jnp.float32) * SCALE).astype(LOW))
    own = at_block(block)
    scores = dot(kv_ref[own, :], query)
    scores = jnp.where(causal_seen(), scores, MASKED)
    top = jnp.max(scores, axis=0, keepdims=True)
    probs = jnp.exp(scores - top)
    total = jnp.sum(probs, axis=0, keepdims=True)
    mixed = dot(turned_ref[2 * HD :, own], probs.astype(LOW))

    def add(carry, scores, values):
        top, total, mixed = carry
        fresh = jnp.maximum(top, jnp.max(scores, axis=0, keepdims=True))
        fade = jnp.exp(top - fresh)
        probs = jnp.exp(scores - fresh)
        total = total * fade + jnp.sum(probs, axis=0, keepdims=True)
        return fresh, total, mixed * fade + dot(values, probs.astype(LOW))

    prefix = prefix_ref[0]
    scores = jnp.where(prefix_seen(flags_ref, seg, SPAN), dot(prefix, query), MASKED)
    carry = add((top, total, mixed), scores, turned(prefix)[HD:].astype(LOW))

    def step(index, carry):
        here = at_block(index)
        return add(carry, dot(kv_ref[here, :], query), turned_ref[2 * HD :, here])

    top, total, mixed = lax.fori_loop(0, block, step, carry)
    mixed = (mixed / total).astype(LOW)
    rows = out_ref.shape[2]
    for piece in range(SPAN // rows):
        out_ref[piece] = mixed[:, piece * rows : (piece + 1) * rows]
    log_ref[0] = top + jnp.log(total)


def attend(flags, turned_all, kv, prefix, rows_here):
    total = kv.shape[0]
    blocks = SEG // SPAN
    step = SPAN // rows_here
    return run(
        attend_kernel,
        (total // SEG, blocks),
        [
            pl.BlockSpec(memory_space=pltpu.SMEM),
            pl.BlockSpec((HD, SPAN), lambda s, i: (0, s * blocks + i)),
            pl.BlockSpec((3 * HD, SEG), lambda s, i: (0, s)),
            pl.BlockSpec((SEG, 2 * HD), lambda s, i: (s, 0)),
            pl.BlockSpec((1, 2 * KEPT, 2 * HD), lambda s, i: (s, 0, 0)),
        ],
        [
            pl.BlockSpec((step, HD, rows_here), lambda s, i: (s * blocks + i, 0, 0)),
            pl.BlockSpec((1, 1, SPAN), lambda s, i: (s * blocks + i, 0, 0)),
        ],
        [
            shape((total // rows_here, HD, rows_here), LOW),
            shape((total // SPAN, 1, SPAN), jnp.float32),
        ],
        (flags, turned_all, turned_all, kv, prefix),
    )


def side_by_side(ref):
    return jnp.concatenate([ref[piece] for piece in range(ref.shape[0])], axis=1)


def beside(block, place):
    zero = jnp.zeros_like(block)
    return jnp.concatenate([block, zero] if place == 0 else [zero, block], axis=1)


def query_side(query_ref, rows_ref, grad_ref, out_ref, log_ref):
    query = above((query_ref[...].astype(jnp.float32) * SCALE).astype(LOW))
    grad = side_by_side(grad_ref)
    mean = jnp.sum(
        grad.astype(jnp.float32) * side_by_side(out_ref).astype(jnp.float32),
        axis=0,
        keepdims=True,
    )
    query_rows = beside((rows_ref[...].astype(jnp.float32) * SCALE).astype(LOW), 0)
    grad_rows = beside(turned(grad).astype(LOW), 1)
    return query, below(grad), mean, log_ref[0], query_rows, grad_rows


def key_side(keys, side, seen):
    query, grad, mean, log_sum, query_rows, grad_rows = side
    probs = jnp.exp(dot(keys, query) - log_sum)
    if seen is not None:
        probs = jnp.where(seen, probs, 0.0)
    d_scores = (probs * (dot(keys, grad) - mean)).astype(LOW)
    return probs.astype(LOW), d_scores


def prefix_back_kernel(
    flags_ref, query_ref, rows_ref, grad_ref, out_ref, log_ref, prefix_ref, sum_ref
):
    seg, block = pl.program_id(0), pl.program_id(1)
    side = query_side(query_ref, rows_ref, grad_ref, out_ref, log_ref)
    probs, d_scores = key_side(prefix_ref[0], side, prefix_seen(flags_ref, seg, SPAN))
    part = dot(d_scores, side[4]) + dot(probs, side[5])

    @pl.when(block == 0)
    def _():
        sum_ref[0] = part

    @pl.when(block > 0)
    def _():
        sum_ref[0] += part


def attend_back_kernel(
    flags_ref,
    query_ref,
    rows_ref,
    grad_ref,
    out_ref,
    log_ref,
    prefix_ref,
    turned_ref,
    kv_ref,
    grads_ref,
    kept_ref,
    kv_grad,
):
    seg, block = pl.program_id(0), pl.program_id(1)

    @pl.when(block == 0)
    def _():
        kv_grad[...] = jnp.zeros_like(kv_grad)

    side = query_side(query_ref, rows_ref, grad_ref, out_ref, log_ref)
    prefix = prefix_ref[0]
    _, d_scores = key_side(prefix, side, prefix_seen(flags_ref, seg, SPAN))
    query_grad = dot(turned(prefix)[:HD].astype(LOW), d_scores)

    def add(here, query_grad, seen):
        probs, d_scores = key_side(kv_ref[here, :], side, seen)
        kv_grad[here, :] += dot(d_scores, side[4]) + dot(probs, side[5])
        return query_grad + dot(turned_ref[HD : 2 * HD, here], d_scores)

    query_grad = add(at_block(block), query_grad, causal_seen())
    query_grad = lax.fori_loop(
        0, block, lambda index, grad: add(at_block(index), grad, None), query_grad
    )
    query_grad = (query_grad * SCALE).astype(LOW)
    rows = grads_ref.shape[2]
    step = SPAN // rows
    for piece in range(step):
        grads_ref[block * step + piece, :HD, :] = query_grad[:, piece * rows : (piece + 1) * rows]

    @pl.when(block == pl.num_programs(1) - 1)
    def _():
        for piece in range(SEG // rows):
            grads_ref[piece, HD:, :] = kv_grad[piece * rows : (piece + 1) * rows, :].T.astype(LOW)
        kept_ref[0] = kv_grad[SEG - KEPT :, :]


def attend_back_specs(rows_here):
    blocks = SEG // SPAN
    step = SPAN // rows_here
    return [
        pl.BlockSpec(memory_space=pltpu.SMEM),
        pl.BlockSpec((HD, SPAN), lambda s, i: (0, s * blocks + i)),
        pl.BlockSpec((SPAN, HD), lambda s, i: (s * blocks + i, 0)),
        pl.BlockSpec((step, HD, rows_here), lambda s, i: (s * blocks + i, 0, 0)),
        pl.BlockSpec((step, HD, rows_here), lambda s, i: (s * blocks + i, 0, 0)),
        pl.BlockSpec((1, 1, SPAN), lambda s, i: (s * blocks + i, 0, 0)),
        pl.BlockSpec((1, 2 * KEPT, 2 * HD), lambda s, i: (s, 0, 0)),
    ]


def prefix_back(flags, turned_all, query, grad, out, log_sums, prefix, rows_here):
    total = query.shape[0]
    return run(
        prefix_back_kernel,
        (total // SEG, SEG // SPAN),
        attend_back_specs(rows_here),
        [pl.BlockSpec((1, 2 * KEPT, 2 * HD), lambda s, i: (s, 0, 0))],
        [shape(prefix.shape, jnp.float32)],
        (flags, turned_all, query, grad, out, log_sums, prefix),
    )


def attend_back(flags, turned_all, query, grad, out, log_sums, prefix, kv, rows_here):
    total = query.shape[0]
    pieces = SEG // rows_here
    return run(
        attend_back_kernel,
        (total // SEG, SEG // SPAN),
        attend_back_specs(rows_here)
        + [
            pl.BlockSpec((3 * HD, SEG), lambda s, i: (0, s)),
            pl.BlockSpec((SEG, 2 * HD), lambda s, i: (s, 0)),
        ],
        [
            pl.BlockSpec((pieces, 3 * HD, rows_here), lambda s, i: (s, 0, 0)),
            pl.BlockSpec((1, KEPT, 2 * HD), lambda s, i: (s, 0, 0)),
        ],
        [
            shape((total // rows_here, 3 * HD, rows_here), LOW),
            shape((total // SEG, KEPT, 2 * HD), jnp.float32),
        ],
        (flags, turned_all, query, grad, out, log_sums, prefix, turned_all, kv),
        scratch=[pltpu.VMEM((SEG, 2 * HD), jnp.float32)],
    )


def returned_kernel(grads_ref, kept_ref, returned_ref, out_ref):
    rows = out_ref.shape[2]
    out_ref[0, :, : rows - KEPT] = grads_ref[0, :, : rows - KEPT]
    out_ref[0, :HD, rows - KEPT :] = grads_ref[0, :HD, rows - KEPT :]
    out_ref[0, HD:, rows - KEPT :] = (kept_ref[0] + returned_ref[0]).T.astype(LOW)


def add_returned(grads, kept, returned):
    places, feats, rows = grads.shape
    segs = kept.shape[0]
    last = places // segs
    grad_spec = pl.BlockSpec((1, feats, rows), lambda s: (s * last + last - 1, 0, 0))
    kept_spec = pl.BlockSpec((1, KEPT, 2 * HD), lambda s: (s, 0, 0))
    return run(
        returned_kernel,
        (segs,),
        [grad_spec, kept_spec, kept_spec],
        [grad_spec],
        [shape(grads.shape, LOW)],
        (grads, kept, returned),
        aliases={0: 0},
    )[0]


def out_kernel(
    part_ref, weight_ref, tokens_ref, bias_ref, gain_ref, shift_ref, resid_ref, two_ref, total
):
    step = pl.program_id(0)
    rows = part_ref.shape[2]
    part = turned(part_ref[...].reshape(-1, rows)).astype(LOW)
    added = dot(part, weight_ref[...].reshape(part.shape[1], -1))

    @pl.when(step == 0)
    def _():
        total[...] = added

    @pl.when(step > 0)
    def _():
        total[...] += added

    @pl.when(step == pl.num_programs(0) - 1)
    def _():
        resid = tokens_ref[...].astype(jnp.float32) + total[...] + bias_ref[...]
        resid_ref[...] = resid
        two_ref[...] = layer_norm(resid, gain_ref[...], shift_ref[...]).astype(LOW)


def out_project(parts, gathered, at, tokens, bias, gain, shift, step=4):
    places, feats, rows = parts.shape
    width = gathered.shape[2]
    return run(
        out_kernel,
        (places // step,),
        [
            pl.BlockSpec((step, feats, rows), lambda i: (i, 0, 0)),
            pl.BlockSpec((step, feats, width), lambda i: (i, at, 0)),
            whole(tokens),
            whole(bias),
            whole(gain),
            whole(shift),
        ],
        [pl.BlockSpec((rows, width), lambda i: (0, 0))] * 2,
        [shape((rows, width), jnp.float32), shape((rows, width), LOW)],
        (parts, gathered, tokens, bias, gain, shift),
        scratch=[pltpu.VMEM((rows, width), jnp.float32)],
    )


def owner_maps(chips, at):
    def of(core_step, y):
        return lambda i, place: at((i * chips[1] + y) * 2 + lax.rem(place[0] + core_step, 2))

    return [of(core_step, y) for core_step in (0, 1) for y in range(chips[1])]


def step_maps(chips, at):
    chips_x, chips_y = chips

    def of(y_step):
        def index(i, place):
            x = lax.rem(place[1] + i, chips_x)
            y = lax.rem(place[2] + y_step, chips_y)
            return at((x * chips_y + y) * 2 + place[0])

        return index

    return [of(y_step) for y_step in range(chips_y)]


def own_map(index):
    return lambda i, place: index(i)


def fixed(dims):
    return pl.BlockSpec(
        dims, own_map(lambda i: (0,) * len(dims)), pipeline_mode=pl.Buffered(buffer_count=1)
    )


def feed_run(body, chips, place, in_specs, out_specs, out_shape, operands, scratch, vmem):
    return pl.pallas_call(
        body,
        grid_spec=pltpu.PrefetchScalarGridSpec(
            num_scalar_prefetch=1,
            grid=(chips[0],),
            in_specs=in_specs,
            out_specs=out_specs,
            scratch_shapes=scratch,
        ),
        out_shape=out_shape,
        compiler_params=pltpu.CompilerParams(
            dimension_semantics=("arbitrary",), vmem_limit_bytes=vmem * MIB
        ),
        cost_estimate=pl.CostEstimate(flops=COST, bytes_accessed=COST, transcendentals=0),
    )(place, *operands)


def stacked(refs, axis=0):
    return jnp.concatenate([ref[0] for ref in refs], axis=axis)


def pile(refs, into):
    rows = refs[0].shape[0]
    for at, ref in enumerate(refs):
        into[at * rows : (at + 1) * rows, :] = ref[...]


def spread(source, refs):
    rows = refs[0].shape[0]
    for at, ref in enumerate(refs):
        ref[...] = source[at * rows : (at + 1) * rows, :].astype(ref.dtype)


def take(refs, *counts):
    refs = list(refs)
    return [[refs.pop(0) for _ in range(count)] for count in counts] + [refs]


def d_act_kernel(count, owners, place_ref, *refs):
    cot_refs, weight_refs, (out_ref, cots) = take(refs, count, owners)

    @pl.when(pl.program_id(0) == 0)
    def _():
        pile(cot_refs, cots)

    out_ref[...] = dot_cols(cots[...], stacked(weight_refs))


def feed_d_act(place, chips, cots, weights):
    count = len(cots)
    rows, width = cots[0].shape
    places, both, _ = weights.shape
    units = both // 2
    total = count * rows
    owners = 2 * chips[1]
    step = owners * units
    return feed_run(
        partial(d_act_kernel, count, owners),
        chips,
        place,
        [fixed((rows, width))] * count
        + [
            pl.BlockSpec((1, units, width), at)
            for at in owner_maps(chips, lambda owner: (owner, 1, 0))
        ],
        [pl.BlockSpec((total, step), own_map(lambda i: (0, i))), fixed((total, width))],
        [shape((total, places * units), jnp.float32), shape((total, width), LOW)],
        (*cots, *[weights] * owners),
        [],
        32,
    )


def feed_kernel(count, chips, place_ref, *refs):
    owners = 2 * chips[1]
    norm_refs, weight_refs, bias_refs, (d_act_ref,), back_refs, refs = take(
        refs, count, owners, owners, 1, count
    )
    norms, kept_ref, sent_ref, bias_sum_ref, back = refs
    step = pl.program_id(0)

    @pl.when(step == 0)
    def _():
        pile(norm_refs, norms)
        back[...] = jnp.zeros_like(back)

    up = stacked(weight_refs)
    pre = dot_cols(norms[...], up) + stacked(bias_refs, axis=1)
    square = pre * pre
    bent = jnp.tanh(0.7978845608 * (pre + 0.044715 * (square * pre)))
    half = 0.5 * (1.0 + bent)
    slope = half + 0.5 * pre * (1.0 - bent * bent) * (
        0.7978845608 * (1.0 + 3.0 * 0.044715 * square)
    )
    d_pre = (d_act_ref[...] * slope).astype(LOW)
    act = (pre * half).astype(LOW)
    own = act.shape[1] // 2
    kept_ref[0] = act[:, :own]
    kept_ref[1] = d_pre[:, :own]
    sent_ref[0] = act[:, own:]
    sent_ref[1] = d_pre[:, own:]
    bias_sums = jnp.sum(d_pre.astype(jnp.float32), axis=0, keepdims=True)
    units = weight_refs[0].shape[1]
    for at, index in enumerate(owner_maps(chips, lambda owner: owner)):
        bias_sum_ref[index(step, place_ref)] = bias_sums[:, at * units : (at + 1) * units]
    back[...] += dot(d_pre, up)

    @pl.when(step == pl.num_programs(0) - 1)
    def _():
        spread(back, back_refs)


def feed(place, chips, norms, weights, bias, d_act):
    count = len(norms)
    rows, width = norms[0].shape
    places, both, _ = weights.shape
    units = both // 2
    total = count * rows
    owners = 2 * chips[1]
    step = owners * units
    pair_spec = pl.BlockSpec((2, total, step // 2), own_map(lambda i: (0, 0, i)))
    results = feed_run(
        partial(feed_kernel, count, chips),
        chips,
        place,
        [fixed((rows, width))] * count
        + [
            pl.BlockSpec((1, units, width), at)
            for at in owner_maps(chips, lambda owner: (owner, 0, 0))
        ]
        + [
            pl.BlockSpec((1, 1, units), at)
            for at in owner_maps(chips, lambda owner: (owner, 0, 0))
        ]
        + [pl.BlockSpec((total, step), own_map(lambda i: (0, i)))],
        [pl.BlockSpec((rows, width), own_map(lambda i: (0, 0)))] * count
        + [fixed((total, width)), pair_spec, pair_spec, fixed((places, 1, units))],
        [shape((rows, width), LOW)] * count
        + [shape((total, width), LOW)]
        + [shape((2, total, places * units // 2), LOW)] * 2
        + [shape((places, 1, units), jnp.float32)],
        (*norms, *[weights] * owners, *[bias] * owners, d_act),
        [pltpu.VMEM((total, width), jnp.float32)],
        40,
    )
    return results[:count], results[count:]


def feed_grad_kernel(count, owners, place_ref, *refs):
    norm_refs, cot_refs, pair_refs, weight_refs, mixed_refs, (out_ref, mixed) = take(
        refs, 2, 2, 3, owners, count
    )
    kept_ref, sent_ref, other_ref = pair_refs
    step = pl.program_id(0)
    units = weight_refs[0].shape[1]

    @pl.when(step == 0)
    def _():
        mixed[...] = jnp.zeros_like(mixed)

    act = jnp.concatenate([kept_ref[0], sent_ref[0]], axis=1)
    mixed[...] += dot(act, stacked(weight_refs))

    def grad(at, rows):
        total = dot(turned(kept_ref[at]).astype(LOW), rows[0][...])
        total += dot(turned(other_ref[at]).astype(LOW), rows[1][...])
        return total.astype(LOW).reshape(out_ref.shape[0], units, -1)

    out_ref[:, :units, :] = grad(1, norm_refs)
    out_ref[:, units:, :] = grad(0, cot_refs)

    @pl.when(step == pl.num_programs(0) - 1)
    def _():
        spread(mixed, mixed_refs)


def feed_grad(place, chips, count, norms, cots, kept, sent, other, weights):
    total, width = norms[0].shape
    rows = total // count
    units = weights.shape[1] // 2
    owners = 2 * chips[1]
    pair_spec = pl.BlockSpec((2, total, owners * units // 2), own_map(lambda i: (0, 0, i)))
    results = feed_run(
        partial(feed_grad_kernel, count, owners),
        chips,
        place,
        [fixed((total, width))] * 4
        + [pair_spec] * 3
        + [
            pl.BlockSpec((1, units, width), at)
            for at in owner_maps(chips, lambda owner: (owner, 1, 0))
        ],
        [pl.BlockSpec((rows, width), own_map(lambda i: (0, 0)))] * count
        + [pl.BlockSpec((chips[1], 2 * units, width), own_map(lambda i: (i, 0, 0)))],
        [shape((rows, width), LOW)] * count
        + [shape((chips[0] * chips[1], 2 * units, width), LOW)],
        (*norms, *cots, kept, sent, other, *[weights] * owners),
        [pltpu.VMEM((total, width), jnp.float32)],
        48,
    )
    return results[:count], results[count]


def branch_kernel(
    count, resid_ref, cot_ref, gain_ref, weight_ref, *refs
):
    back_refs = refs[:count]
    d_resid_ref, d_branch_ref, sums_ref, parts_ref = refs[count:]

    @pl.when(pl.program_id(0) == 0)
    def _():
        d_two = sum(ref[...].astype(jnp.float32) for ref in back_refs)
        normed, scale = norm_parts(resid_ref[...])
        cot = cot_ref[...].astype(jnp.float32)
        d_resid = cot + norm_back(d_two, normed, scale, gain_ref[...])
        d_branch = d_resid.astype(LOW)
        d_resid_ref[...] = d_resid
        d_branch_ref[...] = d_branch
        sums_ref[0:1, :] = jnp.sum(d_two * normed, axis=0, keepdims=True)
        sums_ref[1:2, :] = jnp.sum(d_two, axis=0, keepdims=True)
        sums_ref[2:3, :] = jnp.sum(d_branch.astype(jnp.float32), axis=0, keepdims=True)
        sums_ref[3:4, :] = jnp.sum(cot, axis=0, keepdims=True)

    width = weight_ref.shape[2]
    part = dot_cols(weight_ref[...].reshape(-1, width), d_branch_ref[...])
    parts_ref[...] = part.reshape(parts_ref.shape).astype(LOW)


def branch_back(resid, cotangent, gain, gathered, at, feats, backs, step=4):
    rows, width = resid.shape
    places = gathered.shape[0]
    row_spec = pl.BlockSpec((rows, width), lambda i: (0, 0))
    return run(
        partial(branch_kernel, len(backs)),
        (places // step,),
        [
            row_spec,
            row_spec,
            whole(gain),
            pl.BlockSpec((step, feats, width), lambda i: (i, at, 0)),
        ]
        + [row_spec] * len(backs),
        [
            row_spec,
            row_spec,
            pl.BlockSpec((4, width), lambda i: (0, 0)),
            pl.BlockSpec((step, feats, rows), lambda i: (i, 0, 0)),
        ],
        [
            shape((rows, width), jnp.float32),
            shape((rows, width), LOW),
            shape((4, width), jnp.float32),
            shape((places, feats, rows), LOW),
        ],
        (resid, cotangent, gain, gathered, *backs),
    )


def branch_grad_kernel(owners, place_ref, *refs):
    own_refs, other_refs, grad_refs, out_refs = take(refs, owners, owners, 2)
    parts = jnp.concatenate([stacked(own_refs), stacked(other_refs)], axis=1)
    grads = jnp.concatenate([ref[...] for ref in grad_refs], axis=0)
    out = dot(parts, grads).astype(LOW).reshape(out_refs[0].shape)
    for at, ref in enumerate(out_refs):

        @pl.when(pl.program_id(0) == at)
        def _():
            ref[...] = out


def branch_grad(place, chips, own, other, own_grad, other_grad):
    _, feats, rows = own.shape
    width = own_grad.shape[1]
    chips_x, chips_y = chips
    part_specs = [
        pl.BlockSpec((1, feats, rows), at)
        for at in step_maps(chips, lambda owner: (owner, 0, 0))
    ]
    return feed_run(
        partial(branch_grad_kernel, chips_y),
        chips,
        place,
        part_specs * 2 + [fixed((rows, width))] * 2,
        [pl.BlockSpec((chips_y, feats, width), own_map(lambda i: (0, 0, 0)))] * chips_x,
        [shape((chips_y, feats, width), LOW)] * chips_x,
        (*[own] * chips_y, *[other] * chips_y, own_grad, other_grad),
        [],
        32,
    )


def joint_grad_kernel(
    grad_ref, rows_ref, weight_ref, gain_ref, shift_ref, out_ref, bias_ref, sums_ref, total, biases
):
    step = pl.program_id(0)
    grads = side_by_side(grad_ref)
    added = dot(grads, rows_ref[...].reshape(grads.shape[1], -1))
    summed = jnp.sum(grads.astype(jnp.float32), axis=1, keepdims=True)

    @pl.when(step == 0)
    def _():
        total[...] = added
        biases[...] = summed

    @pl.when(step > 0)
    def _():
        total[...] += added
        biases[...] += summed

    @pl.when(step == pl.num_programs(0) - 1)
    def _():
        out_ref[...] = total[...].astype(LOW)
        bias_ref[...] = biases[...]
        weight = weight_ref[...].astype(jnp.float32)
        shift_sum = jnp.sum(weight * biases[...], axis=0, keepdims=True)
        product = jnp.sum(weight * total[...], axis=0, keepdims=True)
        sums_ref[0:1, :] = (product - shift_sum * shift_ref[...]) / gain_ref[...]
        sums_ref[1:2, :] = shift_sum


def joint_grad(grads, gathered, weight, gain, shift, step=4):
    places, feats, rows = grads.shape
    width = gathered.shape[2]
    return run(
        joint_grad_kernel,
        (places // step,),
        [
            pl.BlockSpec((step, feats, rows), lambda i: (i, 0, 0)),
            pl.BlockSpec((step, rows, width), lambda i: (i, 0, 0)),
            whole(weight),
            whole(gain),
            whole(shift),
        ],
        [
            pl.BlockSpec((feats, width), lambda i: (0, 0)),
            pl.BlockSpec((feats, 1), lambda i: (0, 0)),
            pl.BlockSpec((2, width), lambda i: (0, 0)),
        ],
        [
            shape((feats, width), LOW),
            shape((feats, 1), jnp.float32),
            shape((2, width), jnp.float32),
        ],
        (grads, gathered, weight, gain, shift),
        scratch=[pltpu.VMEM((feats, width), jnp.float32), pltpu.VMEM((feats, 1), jnp.float32)],
    )


def input_kernel(part_ref, weight_ref, tokens_ref, gain_ref, d_resid_ref, out_ref, total):
    step = pl.program_id(0)
    added = dot(turned(part_ref[...]).astype(LOW), weight_ref[...])

    @pl.when(step == 0)
    def _():
        total[...] = added

    @pl.when(step > 0)
    def _():
        total[...] += added

    @pl.when(step == pl.num_programs(0) - 1)
    def _():
        normed, scale = norm_parts(tokens_ref[...].astype(jnp.float32))
        out_ref[...] = d_resid_ref[...] + norm_back(total[...], normed, scale, gain_ref[...])


def input_back(parts, weights, tokens, gain, d_resid, step=SPAN):
    feats, rows = parts.shape
    width = weights.shape[1]
    return run(
        input_kernel,
        (feats // step,),
        [
            pl.BlockSpec((step, rows), lambda i: (i, 0)),
            pl.BlockSpec((step, width), lambda i: (i, 0)),
            whole(tokens),
            whole(gain),
            whole(d_resid),
        ],
        [pl.BlockSpec((rows, width), lambda i: (0, 0))],
        [shape((rows, width), jnp.float32)],
        (parts, weights, tokens, gain, d_resid),
        scratch=[pltpu.VMEM((rows, width), jnp.float32)],
    )[0]


ITEM = "z"
HEAD = ("x", "y", "c")
CORE = "c"


def moved(value, axis, steps):
    count = lax.axis_size(axis)
    return lax.ppermute(value, axis, [(place, (place + steps) % count) for place in range(count)])


def shifted(value, axis, steps):
    count = lax.axis_size(axis)
    initial, last = (max(0, -steps), min(count, count - steps))
    return lax.ppermute(value, axis, [(source, source + steps) for source in range(initial, last)])


def all_sum(value, axes):
    for axis in axes:
        if lax.axis_size(axis) == 4:
            terms = around(value, axis)
            value = (terms[0] + terms[2]) + (terms[1] + terms[3])
            continue
        step = 1
        while step < lax.axis_size(axis):
            pairs = [(place, place ^ step) for place in range(lax.axis_size(axis))]
            value = value + lax.ppermute(value, axis, pairs)
            step *= 2
    return value


def around(value, axis):
    return [value] + [moved(value, axis, -step) for step in range(1, lax.axis_size(axis))]


def sum_back(values, axis):
    return [values[0]] + [
        moved(values[step], axis, step) for step in range(1, lax.axis_size(axis))
    ]


def item_terms(value):
    count = lax.axis_size(ITEM)
    place = lax.axis_index(ITEM)
    parts = value.reshape(count, -1, value.shape[1])
    own = [
        lax.dynamic_index_in_dim(parts, (place + step) % count, 0, keepdims=False)
        for step in range(count)
    ]
    return sum_back(own, ITEM)


def item_sum(terms):
    count = lax.axis_size(ITEM)
    place = lax.axis_index(ITEM)
    block = sum(term.astype(jnp.float32) for term in terms).astype(LOW)
    blocks = around(block, ITEM)
    rows = lax.dynamic_slice_in_dim(
        jnp.stack(blocks + blocks), (count - place) % count, count, 0
    )
    return rows.reshape(-1, block.shape[1]).astype(jnp.float32)


def head_swap(value):
    return lax.all_to_all(value, HEAD, split_axis=0, concat_axis=0, tiled=True)


def segment_flags(seg_counts):
    total_segs = seg_counts.shape[0]
    openings = jnp.cumsum(seg_counts) - seg_counts
    places = jnp.arange(total_segs, dtype=jnp.int32)
    opens_here = jnp.any((openings[:, None] == places[None, :]) & (seg_counts[:, None] > 0), axis=0)
    opens_before = jnp.concatenate([jnp.ones((1,), dtype=bool), opens_here[:-1]])
    one_back = jnp.logical_not(opens_here)
    two_back = one_back & jnp.logical_not(opens_before)
    return (one_back, two_back)


def local(
    tokens,
    cotangent,
    seg_counts,
    query_weight,
    key_weight,
    value_weight,
    query_bias,
    value_bias,
    out_weight,
    out_bias,
    first_gain,
    first_shift,
    second_gain,
    second_shift,
    up_weight,
    up_bias,
    down_weight,
    down_bias,
):
    rows, width = tokens.shape
    heads = lax.axis_size(HEAD)
    item_place = lax.axis_index(ITEM)
    group_rows = rows * heads
    seg_local = group_rows // SEG
    feats = query_weight.shape[0]
    units = up_weight.shape[0]
    hidden_here = units * heads

    def row(vector):
        return vector.reshape(1, -1)

    tokens_f = tokens.astype(jnp.float32)
    inputs_one = layer_norm(tokens_f, first_gain, first_shift).astype(LOW)
    first = jnp.concatenate([inputs_one, out_weight], axis=0)
    gathered = lax.all_gather(first, HEAD, axis=0, tiled=True).reshape(heads, -1, width)
    second = jnp.concatenate([up_weight, down_weight], axis=0)
    feed_weights = lax.all_gather(second, HEAD, axis=0, tiled=True).reshape(heads, -1, width)
    cots = around(cotangent, ITEM)
    joint_weight = jnp.concatenate([query_weight, key_weight, value_weight], axis=0)
    joint_bias = jnp.concatenate([query_bias, jnp.zeros_like(query_bias), value_bias])

    one_back, two_back = segment_flags(seg_counts)
    flags = jnp.stack([two_back, one_back], axis=1).astype(jnp.int32)
    flags = lax.dynamic_slice_in_dim(flags, item_place * seg_local, seg_local).reshape(-1)

    gathered, cots = lax.optimization_barrier((gathered, cots))
    query, kv, turned_all = project(gathered, rows, joint_weight, row(joint_bias))
    own_kept = kv.reshape(seg_local, SEG, 2 * HD)[:, SEG - KEPT :]
    table = jnp.concatenate([shifted(own_kept, ITEM, 1), own_kept], axis=0)
    prefix = jnp.concatenate(
        [table[seg_local - 2 : 2 * seg_local - 2], table[seg_local - 1 : 2 * seg_local - 1]], axis=1
    )
    attended, log_sums = attend(flags, turned_all, kv, prefix, rows)
    attended_own = head_swap(attended)
    attended_other = moved(attended_own, CORE, 1)
    resid, inputs_two = out_project(
        attended_own, gathered, rows // feats, tokens, row(out_bias), row(second_gain), row(second_shift)
    )

    joint_turn = lax.optimization_barrier((joint_weight, resid))[0]
    joint_full = lax.all_gather(joint_turn, HEAD, axis=0, tiled=True)
    norms = around(inputs_two, ITEM)
    chips = (lax.axis_size("x"), lax.axis_size("y"))
    place = jnp.stack([lax.axis_index(axis) for axis in (CORE, "x", "y")]).astype(jnp.int32)
    d_act, cots = feed_d_act(place, chips, cots, feed_weights)
    cots = [cots, moved(cots, CORE, 1)]
    bias_here = lax.dynamic_slice_in_dim(up_bias, item_place * hidden_here, hidden_here)
    backs, (norms, kept, sent, up_bias_part) = feed(
        place, chips, norms, feed_weights, bias_here.reshape(heads, 1, units), d_act
    )
    backs = sum_back(backs, ITEM)
    norms = [norms, moved(norms, CORE, 1)]
    mixeds, feed_parts = feed_grad(
        place, chips, len(backs), norms, cots, kept, sent, moved(sent, CORE, 1), feed_weights
    )
    backs, mixeds = lax.optimization_barrier((backs, mixeds))
    d_resid, d_branch, sums_two, d_parts = branch_back(
        resid, cotangent, row(second_gain), gathered, rows // feats, feats, backs
    )
    d_attended = head_swap(d_parts)
    feed_parts = lax.optimization_barrier((feed_parts, d_resid))[0]
    feed_grads = lax.psum_scatter(
        feed_parts.reshape(-1, width), ("x", "y"), scatter_dimension=0, tiled=True
    )

    outs = branch_grad(
        place, chips, attended_own, attended_other, d_branch, moved(d_branch, CORE, 1)
    )
    d_attended, outs = lax.optimization_barrier((d_attended, outs))
    outs = sum_back(outs, "x")

    d_prefix = prefix_back(
        flags, turned_all, query, d_attended, attended, log_sums, prefix, rows
    )[0]
    older, newer = d_prefix[:, :KEPT], d_prefix[:, KEPT:]
    spread = jnp.pad(older, ((seg_local - 2, 2), (0, 0), (0, 0)))
    spread = spread + jnp.pad(newer, ((seg_local - 1, 1), (0, 0), (0, 0)))
    returned = shifted(spread[:seg_local], ITEM, -1)
    joint_grads, kept_grads = attend_back(
        flags, turned_all, query, d_attended, attended, log_sums, prefix, kv, rows
    )
    returned, kept_grads, joint_full = lax.optimization_barrier((returned, kept_grads, joint_full))
    joint_grads = add_returned(joint_grads, kept_grads, spread[seg_local:] + returned)
    joint_grads, mixeds = lax.optimization_barrier((joint_grads, mixeds))
    mixeds = sum_back(mixeds, ITEM)
    grads_own = head_swap(joint_grads).reshape(-1, rows)
    joint_part, bias_part, sums_one = joint_grad(
        joint_grads, gathered, joint_weight, row(first_gain), row(first_shift)
    )
    outs, joint_part = lax.optimization_barrier((outs, joint_part))
    out_part = lax.optimization_barrier(sum(out.astype(jnp.float32) for out in outs).astype(LOW))
    out_part = sum_back([out_part[step] for step in range(lax.axis_size("y"))], "y")
    out_part = sum(out.astype(jnp.float32) for out in out_part).astype(LOW)
    small = [up_bias_part.reshape(-1), sums_two.reshape(-1), sums_one.reshape(-1)]
    small = all_sum(jnp.concatenate(small).reshape(-1, 128), (CORE, "y"))
    grads_own, out_part, small = lax.optimization_barrier((grads_own, out_part, small))
    terms = item_terms(jnp.concatenate([joint_part, out_part], axis=0))
    small = all_sum(small, ("x",))
    input_grad = input_back(grads_own, joint_full, tokens, row(first_gain), d_resid)
    input_grad, terms, small, mixeds, feed_grads = lax.optimization_barrier(
        (input_grad, terms, small, mixeds, feed_grads)
    )
    feed_grads = feed_grads.astype(jnp.float32)
    item_sums = item_sum(terms)
    mixed = sum(part.astype(jnp.float32) for part in mixeds)
    mixed_out = (resid + mixed + down_bias).astype(LOW)
    small = small.reshape(-1)
    up_bias_sums, small = small[:hidden_here], small[hidden_here:]
    up_bias_sums = lax.dynamic_update_slice_in_dim(
        jnp.zeros(up_bias.shape, jnp.float32), up_bias_sums, item_place * hidden_here, 0
    )
    small = jnp.concatenate([up_bias_sums, small, bias_part.reshape(-1)])
    small = all_sum(jnp.pad(small, (0, -small.size % 128)).reshape(-1, 128), (ITEM,)).reshape(-1)
    up_bias_grad, small = small[: up_bias.size], small[up_bias.size :]
    early_rows, late = small[: 4 * width].reshape(4, width), small[4 * width : 6 * width]
    late = late.reshape(2, width)
    bias_sums = small[6 * width : 6 * width + 3 * feats]
    return (
        mixed_out,
        input_grad,
        item_sums[:feats],
        item_sums[feats : 2 * feats],
        item_sums[2 * feats : 3 * feats],
        bias_sums[:feats],
        bias_sums[2 * feats :],
        item_sums[3 * feats :],
        early_rows[2],
        late[0],
        late[1],
        early_rows[0],
        early_rows[1],
        feed_grads[:units],
        up_bias_grad,
        feed_grads[units:],
        early_rows[3],
    )


def solution(mesh):
    sizes = (mesh.shape["item"], 4, mesh.shape["head"] // 8, 2)
    fine = Mesh(mesh.devices.reshape(sizes), (ITEM, *HEAD))
    split = P((ITEM, *HEAD), None)
    by_head = P(HEAD, None)
    return jax.shard_map(
        local,
        mesh=fine,
        in_specs=(
            split,
            split,
            P(),
            by_head,
            by_head,
            by_head,
            P(HEAD),
            P(HEAD),
            by_head,
            P(),
            P(),
            P(),
            P(),
            P(),
            split,
            P(),
            split,
            P(),
        ),
        out_specs=(
            split,
            split,
            by_head,
            by_head,
            by_head,
            P(HEAD),
            P(HEAD),
            by_head,
            P(),
            P(),
            P(),
            P(),
            P(),
            split,
            P(),
            split,
            P(),
        ),
        check_vma=False,
    )
```

```python
from functools import partial

import jax
import jax.numpy as jnp
from jax import lax
from jax.experimental import pallas as pl
from jax.experimental.pallas import tpu as pltpu
from jax.sharding import Mesh
from jax.sharding import PartitionSpec as P

HD = 64
NSUM = 50
SEG = 2048
SPAN = 512
KEPT = 64
EPSILON = 1e-05
MASKED = -1e30
SCALE = HD ** (-0.5)
MIB = 1 << 20
COST = 1 << 20
LOW = jnp.bfloat16


def dot(left, right):
    return jnp.dot(left, right, preferred_element_type=jnp.float32)


def dot_cols(left, right):
    return lax.dot_general(
        left, right, (((1,), (1,)), ((), ())), preferred_element_type=jnp.float32
    )


def turned(value):
    return value.astype(jnp.float32).T


def norm_parts(row_data):
    row_mean = jnp.mean(row_data, axis=-1, keepdims=True)
    centred = row_data - row_mean
    row_var = jnp.mean(centred * centred, axis=-1, keepdims=True)
    scale = lax.rsqrt(row_var + EPSILON)
    return centred * scale, scale


def norm_back(grad, normed, scale, gain):
    scaled = grad * gain
    return scale * (
        scaled
        - jnp.mean(scaled, axis=-1, keepdims=True)
        - normed * jnp.mean(scaled * normed, axis=-1, keepdims=True)
    )


def layer_norm(row_data, gain, shift):
    return norm_parts(row_data)[0] * gain + shift


def run(body, grid, in_specs, out_specs, out_shape, operands, scratch=(), vmem=32, aliases=None):
    return pl.pallas_call(
        body,
        grid=grid,
        in_specs=in_specs,
        out_specs=out_specs,
        out_shape=out_shape,
        scratch_shapes=scratch,
        compiler_params=pltpu.CompilerParams(
            dimension_semantics=("arbitrary",) * len(grid), vmem_limit_bytes=vmem * MIB
        ),
        input_output_aliases=aliases or {},
        cost_estimate=pl.CostEstimate(flops=COST, bytes_accessed=COST, transcendentals=0),
    )(*operands)


def shape(dims, kind):
    return jax.ShapeDtypeStruct(dims, kind)


def whole(item):
    return pl.BlockSpec(item.shape, lambda *_: (0,) * len(item.shape))


def project_kernel(rows_ref, weight_ref, bias_ref, query_ref, kv_ref, turned_ref):
    joint = dot_cols(rows_ref[...], weight_ref[...]) + bias_ref[...]
    query_ref[...] = joint[:, :HD].astype(LOW)
    kv_ref[...] = joint[:, HD:].astype(LOW)
    turned_ref[...] = joint.T.astype(LOW)


def project(rows, weight, bias):
    total, width = rows.shape
    return run(
        project_kernel,
        (total // SPAN,),
        [
            pl.BlockSpec((SPAN, width), lambda i: (i, 0)),
            whole(weight),
            whole(bias),
        ],
        [
            pl.BlockSpec((SPAN, HD), lambda i: (i, 0)),
            pl.BlockSpec((SPAN, 2 * HD), lambda i: (i, 0)),
            pl.BlockSpec((3 * HD, SPAN), lambda i: (0, i)),
        ],
        [
            shape((total, HD), LOW),
            shape((total, 2 * HD), LOW),
            shape((3 * HD, total), LOW),
        ],
        (rows, weight, bias),
    )


def prefix_seen(flags_ref, seg, columns):
    place = lax.broadcasted_iota(jnp.int32, (2 * KEPT, columns), 0)
    older = place < KEPT
    slot = jnp.where(older, place, place - KEPT) >= KEPT - NSUM
    flag = jnp.where(older, flags_ref[2 * seg], flags_ref[2 * seg + 1])
    return slot & (flag > 0)


def causal_seen():
    shape_here = (SPAN, SPAN)
    return lax.broadcasted_iota(jnp.int32, shape_here, 0) <= lax.broadcasted_iota(
        jnp.int32, shape_here, 1
    )


def above(block):
    return jnp.concatenate([block, jnp.zeros_like(block)], axis=0)


def below(block):
    return jnp.concatenate([jnp.zeros_like(block), block], axis=0)


def at_block(index):
    return pl.ds(pl.multiple_of(index * SPAN, SPAN), SPAN)


def attend_kernel(flags_ref, query_ref, turned_ref, kv_ref, prefix_ref, out_ref, log_ref):
    seg, block = pl.program_id(0), pl.program_id(1)
    query = above((query_ref[...].astype(jnp.float32) * SCALE).astype(LOW))
    own = at_block(block)
    scores = dot(kv_ref[own, :], query)
    scores = jnp.where(causal_seen(), scores, MASKED)
    top = jnp.max(scores, axis=0, keepdims=True)
    probs = jnp.exp(scores - top)
    total = jnp.sum(probs, axis=0, keepdims=True)
    mixed = dot(turned_ref[2 * HD :, own], probs.astype(LOW))

    def add(carry, scores, values):
        top, total, mixed = carry
        fresh = jnp.maximum(top, jnp.max(scores, axis=0, keepdims=True))
        fade = jnp.exp(top - fresh)
        probs = jnp.exp(scores - fresh)
        total = total * fade + jnp.sum(probs, axis=0, keepdims=True)
        return fresh, total, mixed * fade + dot(values, probs.astype(LOW))

    prefix = prefix_ref[0]
    scores = jnp.where(prefix_seen(flags_ref, seg, SPAN), dot(prefix, query), MASKED)
    carry = add((top, total, mixed), scores, turned(prefix)[HD:].astype(LOW))

    def step(index, carry):
        here = at_block(index)
        return add(carry, dot(kv_ref[here, :], query), turned_ref[2 * HD :, here])

    top, total, mixed = lax.fori_loop(0, block, step, carry)
    mixed = (mixed / total).astype(LOW)
    rows = out_ref.shape[2]
    for piece in range(SPAN // rows):
        out_ref[piece] = mixed[:, piece * rows : (piece + 1) * rows]
    log_ref[0] = top + jnp.log(total)


def attend(flags, turned_all, kv, prefix, rows_here):
    total = kv.shape[0]
    blocks = SEG // SPAN
    step = SPAN // rows_here
    return run(
        attend_kernel,
        (total // SEG, blocks),
        [
            pl.BlockSpec(memory_space=pltpu.SMEM),
            pl.BlockSpec((HD, SPAN), lambda s, i: (0, s * blocks + i)),
            pl.BlockSpec((3 * HD, SEG), lambda s, i: (0, s)),
            pl.BlockSpec((SEG, 2 * HD), lambda s, i: (s, 0)),
            pl.BlockSpec((1, 2 * KEPT, 2 * HD), lambda s, i: (s, 0, 0)),
        ],
        [
            pl.BlockSpec((step, HD, rows_here), lambda s, i: (s * blocks + i, 0, 0)),
            pl.BlockSpec((1, 1, SPAN), lambda s, i: (s * blocks + i, 0, 0)),
        ],
        [
            shape((total // rows_here, HD, rows_here), LOW),
            shape((total // SPAN, 1, SPAN), jnp.float32),
        ],
        (flags, turned_all, turned_all, kv, prefix),
    )


def side_by_side(ref):
    return jnp.concatenate([ref[piece] for piece in range(ref.shape[0])], axis=1)


def beside(block, place):
    zero = jnp.zeros_like(block)
    return jnp.concatenate([block, zero] if place == 0 else [zero, block], axis=1)


def query_side(query_ref, rows_ref, grad_ref, out_ref, log_ref):
    query = above((query_ref[...].astype(jnp.float32) * SCALE).astype(LOW))
    grad = side_by_side(grad_ref)
    mean = jnp.sum(
        grad.astype(jnp.float32) * side_by_side(out_ref).astype(jnp.float32),
        axis=0,
        keepdims=True,
    )
    query_rows = beside((rows_ref[...].astype(jnp.float32) * SCALE).astype(LOW), 0)
    grad_rows = beside(turned(grad).astype(LOW), 1)
    return query, below(grad), mean, log_ref[0], query_rows, grad_rows


def key_side(keys, side, seen):
    query, grad, mean, log_sum, query_rows, grad_rows = side
    probs = jnp.exp(dot(keys, query) - log_sum)
    if seen is not None:
        probs = jnp.where(seen, probs, 0.0)
    d_scores = (probs * (dot(keys, grad) - mean)).astype(LOW)
    return probs.astype(LOW), d_scores


def prefix_back_kernel(
    flags_ref, query_ref, rows_ref, grad_ref, out_ref, log_ref, prefix_ref, sum_ref
):
    seg, block = pl.program_id(0), pl.program_id(1)
    side = query_side(query_ref, rows_ref, grad_ref, out_ref, log_ref)
    probs, d_scores = key_side(prefix_ref[0], side, prefix_seen(flags_ref, seg, SPAN))
    part = dot(d_scores, side[4]) + dot(probs, side[5])

    @pl.when(block == 0)
    def _():
        sum_ref[0] = part

    @pl.when(block > 0)
    def _():
        sum_ref[0] += part


def attend_back_kernel(
    flags_ref,
    query_ref,
    rows_ref,
    grad_ref,
    out_ref,
    log_ref,
    prefix_ref,
    turned_ref,
    kv_ref,
    grads_ref,
    kept_ref,
    kv_grad,
):
    seg, block = pl.program_id(0), pl.program_id(1)

    @pl.when(block == 0)
    def _():
        kv_grad[...] = jnp.zeros_like(kv_grad)

    side = query_side(query_ref, rows_ref, grad_ref, out_ref, log_ref)
    prefix = prefix_ref[0]
    _, d_scores = key_side(prefix, side, prefix_seen(flags_ref, seg, SPAN))
    query_grad = dot(turned(prefix)[:HD].astype(LOW), d_scores)

    def add(here, query_grad, seen):
        probs, d_scores = key_side(kv_ref[here, :], side, seen)
        kv_grad[here, :] += dot(d_scores, side[4]) + dot(probs, side[5])
        return query_grad + dot(turned_ref[HD : 2 * HD, here], d_scores)

    query_grad = add(at_block(block), query_grad, causal_seen())
    query_grad = lax.fori_loop(
        0, block, lambda index, grad: add(at_block(index), grad, None), query_grad
    )
    query_grad = (query_grad * SCALE).astype(LOW)
    rows = grads_ref.shape[2]
    step = SPAN // rows
    for piece in range(step):
        grads_ref[block * step + piece, :HD, :] = query_grad[:, piece * rows : (piece + 1) * rows]

    @pl.when(block == pl.num_programs(1) - 1)
    def _():
        for piece in range(SEG // rows):
            grads_ref[piece, HD:, :] = kv_grad[piece * rows : (piece + 1) * rows, :].T.astype(LOW)
        kept_ref[0] = kv_grad[SEG - KEPT :, :]


def attend_back_specs(rows_here):
    blocks = SEG // SPAN
    step = SPAN // rows_here
    return [
        pl.BlockSpec(memory_space=pltpu.SMEM),
        pl.BlockSpec((HD, SPAN), lambda s, i: (0, s * blocks + i)),
        pl.BlockSpec((SPAN, HD), lambda s, i: (s * blocks + i, 0)),
        pl.BlockSpec((step, HD, rows_here), lambda s, i: (s * blocks + i, 0, 0)),
        pl.BlockSpec((step, HD, rows_here), lambda s, i: (s * blocks + i, 0, 0)),
        pl.BlockSpec((1, 1, SPAN), lambda s, i: (s * blocks + i, 0, 0)),
        pl.BlockSpec((1, 2 * KEPT, 2 * HD), lambda s, i: (s, 0, 0)),
    ]


def prefix_back(flags, turned_all, query, grad, out, log_sums, prefix, rows_here):
    total = query.shape[0]
    return run(
        prefix_back_kernel,
        (total // SEG, SEG // SPAN),
        attend_back_specs(rows_here),
        [pl.BlockSpec((1, 2 * KEPT, 2 * HD), lambda s, i: (s, 0, 0))],
        [shape(prefix.shape, jnp.float32)],
        (flags, turned_all, query, grad, out, log_sums, prefix),
    )


def attend_back(flags, turned_all, query, grad, out, log_sums, prefix, kv, rows_here):
    total = query.shape[0]
    pieces = SEG // rows_here
    return run(
        attend_back_kernel,
        (total // SEG, SEG // SPAN),
        attend_back_specs(rows_here)
        + [
            pl.BlockSpec((3 * HD, SEG), lambda s, i: (0, s)),
            pl.BlockSpec((SEG, 2 * HD), lambda s, i: (s, 0)),
        ],
        [
            pl.BlockSpec((pieces, 3 * HD, rows_here), lambda s, i: (s, 0, 0)),
            pl.BlockSpec((1, KEPT, 2 * HD), lambda s, i: (s, 0, 0)),
        ],
        [
            shape((total // rows_here, 3 * HD, rows_here), LOW),
            shape((total // SEG, KEPT, 2 * HD), jnp.float32),
        ],
        (flags, turned_all, query, grad, out, log_sums, prefix, turned_all, kv),
        scratch=[pltpu.VMEM((SEG, 2 * HD), jnp.float32)],
    )


def returned_kernel(grads_ref, kept_ref, returned_ref, out_ref):
    rows = out_ref.shape[2]
    out_ref[0, :, : rows - KEPT] = grads_ref[0, :, : rows - KEPT]
    out_ref[0, :HD, rows - KEPT :] = grads_ref[0, :HD, rows - KEPT :]
    out_ref[0, HD:, rows - KEPT :] = (kept_ref[0] + returned_ref[0]).T.astype(LOW)


def add_returned(grads, kept, returned):
    places, feats, rows = grads.shape
    segs = kept.shape[0]
    last = places // segs
    grad_spec = pl.BlockSpec((1, feats, rows), lambda s: (s * last + last - 1, 0, 0))
    kept_spec = pl.BlockSpec((1, KEPT, 2 * HD), lambda s: (s, 0, 0))
    return run(
        returned_kernel,
        (segs,),
        [grad_spec, kept_spec, kept_spec],
        [grad_spec],
        [shape(grads.shape, LOW)],
        (grads, kept, returned),
        aliases={0: 0},
    )[0]


def owner_maps(chips, at):
    def of(core_step, y):
        return lambda i, place: at((i * chips[1] + y) * 2 + lax.rem(place[0] + core_step, 2))

    return [of(core_step, y) for core_step in (0, 1) for y in range(chips[1])]


def step_maps(chips, at):
    chips_x, chips_y = chips

    def of(core_step, y_step):
        def index(i, place):
            x = lax.rem(place[1] + i, chips_x)
            y = lax.rem(place[2] + y_step, chips_y)
            return at((x * chips_y + y) * 2 + lax.rem(place[0] + core_step, 2))

        return index

    return [of(core_step, y_step) for core_step in (0, 1) for y_step in range(chips_y)]


def own_map(index):
    return lambda i, place: index(i)


def fixed(dims):
    return pl.BlockSpec(
        dims, own_map(lambda i: (0,) * len(dims)), pipeline_mode=pl.Buffered(buffer_count=1)
    )


def feed_run(body, chips, place, in_specs, out_specs, out_shape, operands, scratch, vmem):
    return pl.pallas_call(
        body,
        grid_spec=pltpu.PrefetchScalarGridSpec(
            num_scalar_prefetch=1,
            grid=(chips[0],),
            in_specs=in_specs,
            out_specs=out_specs,
            scratch_shapes=scratch,
        ),
        out_shape=out_shape,
        compiler_params=pltpu.CompilerParams(
            dimension_semantics=("arbitrary",), vmem_limit_bytes=vmem * MIB
        ),
        cost_estimate=pl.CostEstimate(flops=COST, bytes_accessed=COST, transcendentals=0),
    )(place, *operands)


def stacked(refs, axis=0):
    return jnp.concatenate([ref[0] for ref in refs], axis=axis)


def pile(refs, into):
    rows = refs[0].shape[0]
    for at, ref in enumerate(refs):
        into[at * rows : (at + 1) * rows, :] = ref[...]


def spread(source, refs):
    rows = refs[0].shape[0]
    for at, ref in enumerate(refs):
        ref[...] = source[at * rows : (at + 1) * rows, :].astype(ref.dtype)


def take(refs, *counts):
    refs = list(refs)
    return [[refs.pop(0) for _ in range(count)] for count in counts] + [refs]


def d_act_kernel(count, owners, place_ref, *refs):
    cot_refs, weight_refs, (out_ref, cots) = take(refs, count, owners)

    @pl.when(pl.program_id(0) == 0)
    def _():
        pile(cot_refs, cots)

    out_ref[...] = dot_cols(cots[...], stacked(weight_refs))


def feed_d_act(place, chips, cots, weights):
    count = len(cots)
    rows, width = cots[0].shape
    places, both, _ = weights.shape
    units = both // 2
    total = count * rows
    owners = 2 * chips[1]
    step = owners * units
    return feed_run(
        partial(d_act_kernel, count, owners),
        chips,
        place,
        [fixed((rows, width))] * count
        + [
            pl.BlockSpec((1, units, width), at)
            for at in owner_maps(chips, lambda owner: (owner, 1, 0))
        ],
        [pl.BlockSpec((total, step), own_map(lambda i: (0, i))), fixed((total, width))],
        [shape((total, places * units), jnp.float32), shape((total, width), LOW)],
        (*cots, *[weights] * owners),
        [],
        32,
    )


def feed_kernel(count, chips, place_ref, *refs):
    owners = 2 * chips[1]
    norm_refs, weight_refs, bias_refs, (d_act_ref,), back_refs, refs = take(
        refs, count, owners, owners, 1, count
    )
    norms, kept_ref, sent_ref, bias_sum_ref, back = refs
    step = pl.program_id(0)

    @pl.when(step == 0)
    def _():
        pile(norm_refs, norms)
        back[...] = jnp.zeros_like(back)

    up = stacked(weight_refs)
    pre = dot_cols(norms[...], up) + stacked(bias_refs, axis=1)
    square = pre * pre
    bent = jnp.tanh(0.7978845608 * (pre + 0.044715 * (square * pre)))
    half = 0.5 * (1.0 + bent)
    slope = half + 0.5 * pre * (1.0 - bent * bent) * (
        0.7978845608 * (1.0 + 3.0 * 0.044715 * square)
    )
    d_pre = (d_act_ref[...] * slope).astype(LOW)
    act = (pre * half).astype(LOW)
    own = act.shape[1] // 2
    kept_ref[0] = act[:, :own]
    kept_ref[1] = d_pre[:, :own]
    sent_ref[0] = act[:, own:]
    sent_ref[1] = d_pre[:, own:]
    bias_sums = jnp.sum(d_pre.astype(jnp.float32), axis=0, keepdims=True)
    units = weight_refs[0].shape[1]
    for at, index in enumerate(owner_maps(chips, lambda owner: owner)):
        bias_sum_ref[index(step, place_ref)] = bias_sums[:, at * units : (at + 1) * units]
    back[...] += dot(d_pre, up)

    @pl.when(step == pl.num_programs(0) - 1)
    def _():
        spread(back, back_refs)


def feed(place, chips, norms, weights, bias, d_act):
    count = len(norms)
    rows, width = norms[0].shape
    places, both, _ = weights.shape
    units = both // 2
    total = count * rows
    owners = 2 * chips[1]
    step = owners * units
    pair_spec = pl.BlockSpec((2, total, step // 2), own_map(lambda i: (0, 0, i)))
    results = feed_run(
        partial(feed_kernel, count, chips),
        chips,
        place,
        [fixed((rows, width))] * count
        + [
            pl.BlockSpec((1, units, width), at)
            for at in owner_maps(chips, lambda owner: (owner, 0, 0))
        ]
        + [
            pl.BlockSpec((1, 1, units), at)
            for at in owner_maps(chips, lambda owner: (owner, 0, 0))
        ]
        + [pl.BlockSpec((total, step), own_map(lambda i: (0, i)))],
        [pl.BlockSpec((rows, width), own_map(lambda i: (0, 0)))] * count
        + [fixed((total, width)), pair_spec, pair_spec, fixed((places, 1, units))],
        [shape((rows, width), LOW)] * count
        + [shape((total, width), LOW)]
        + [shape((2, total, places * units // 2), LOW)] * 2
        + [shape((places, 1, units), jnp.float32)],
        (*norms, *[weights] * owners, *[bias] * owners, d_act),
        [pltpu.VMEM((total, width), jnp.float32)],
        40,
    )
    return results[:count], results[count:]


def feed_grad_kernel(count, owners, place_ref, *refs):
    norm_refs, cot_refs, pair_refs, weight_refs, mixed_refs, (out_ref, mixed) = take(
        refs, 2, 2, 3, owners, count
    )
    kept_ref, sent_ref, other_ref = pair_refs
    step = pl.program_id(0)
    units = weight_refs[0].shape[1]

    @pl.when(step == 0)
    def _():
        mixed[...] = jnp.zeros_like(mixed)

    act = jnp.concatenate([kept_ref[0], sent_ref[0]], axis=1)
    mixed[...] += dot(act, stacked(weight_refs))

    def grad(at, rows):
        total = dot(turned(kept_ref[at]).astype(LOW), rows[0][...])
        total += dot(turned(other_ref[at]).astype(LOW), rows[1][...])
        return total.astype(LOW).reshape(out_ref.shape[0], units, -1)

    out_ref[:, :units, :] = grad(1, norm_refs)
    out_ref[:, units:, :] = grad(0, cot_refs)

    @pl.when(step == pl.num_programs(0) - 1)
    def _():
        spread(mixed, mixed_refs)


def feed_grad(place, chips, count, norms, cots, kept, sent, other, weights):
    total, width = norms[0].shape
    rows = total // count
    units = weights.shape[1] // 2
    owners = 2 * chips[1]
    pair_spec = pl.BlockSpec((2, total, owners * units // 2), own_map(lambda i: (0, 0, i)))
    results = feed_run(
        partial(feed_grad_kernel, count, owners),
        chips,
        place,
        [fixed((total, width))] * 4
        + [pair_spec] * 3
        + [
            pl.BlockSpec((1, units, width), at)
            for at in owner_maps(chips, lambda owner: (owner, 1, 0))
        ],
        [pl.BlockSpec((rows, width), own_map(lambda i: (0, 0)))] * count
        + [pl.BlockSpec((chips[1], 2 * units, width), own_map(lambda i: (i, 0, 0)))],
        [shape((rows, width), LOW)] * count
        + [shape((chips[0] * chips[1], 2 * units, width), LOW)],
        (*norms, *cots, kept, sent, other, *[weights] * owners),
        [pltpu.VMEM((total, width), jnp.float32)],
        48,
    )
    return results[:count], results[count]


def out_kernel(owners, place_ref, *refs):
    part_refs, weight_refs, refs = take(refs, owners, 2)
    tokens_ref, bias_ref, gain_ref, shift_ref, resid_ref, two_ref, total = refs
    step = pl.program_id(0)
    width = tokens_ref.shape[1]
    part = turned(stacked(part_refs)).astype(LOW)
    added = dot(part, stacked(weight_refs).reshape(-1, width))

    @pl.when(step == 0)
    def _():
        total[...] = added

    @pl.when(step > 0)
    def _():
        total[...] += added

    @pl.when(step == pl.num_programs(0) - 1)
    def _():
        resid = tokens_ref[...].astype(jnp.float32) + total[...] + bias_ref[...]
        resid_ref[...] = resid
        two_ref[...] = layer_norm(resid, gain_ref[...], shift_ref[...]).astype(LOW)


def weight_spec(weights):
    return pl.BlockSpec((1, *weights.shape[1:]), own_map(lambda i: (i, 0, 0, 0)))


def out_project(place, chips, parts, weights, tokens, bias, gain, shift):
    _, feats, rows = parts.shape
    width = tokens.shape[1]
    owners = 2 * chips[1]
    return feed_run(
        partial(out_kernel, owners),
        chips,
        place,
        [
            pl.BlockSpec((1, feats, rows), at)
            for at in step_maps(chips, lambda owner: (owner, 0, 0))
        ]
        + [weight_spec(item) for item in weights]
        + [fixed(tokens.shape), fixed(bias.shape), fixed(gain.shape), fixed(shift.shape)],
        [fixed((rows, width))] * 2,
        [shape((rows, width), jnp.float32), shape((rows, width), LOW)],
        (*[parts] * owners, *weights, tokens, bias, gain, shift),
        [pltpu.VMEM((rows, width), jnp.float32)],
        32,
    )


def branch_kernel(count, chips, place_ref, *refs):
    (resid_ref, cot_ref, gain_ref), weight_refs, back_refs, refs = take(refs, 3, 2, count)
    d_resid_ref, d_branch_ref, sums_ref, parts_ref = refs
    step = pl.program_id(0)

    @pl.when(step == 0)
    def _():
        d_two = sum(ref[...].astype(jnp.float32) for ref in back_refs)
        normed, scale = norm_parts(resid_ref[...])
        cot = cot_ref[...].astype(jnp.float32)
        d_resid = cot + norm_back(d_two, normed, scale, gain_ref[...])
        d_branch = d_resid.astype(LOW)
        d_resid_ref[...] = d_resid
        d_branch_ref[...] = d_branch
        sums_ref[0:1, :] = jnp.sum(d_two * normed, axis=0, keepdims=True)
        sums_ref[1:2, :] = jnp.sum(d_two, axis=0, keepdims=True)
        sums_ref[2:3, :] = jnp.sum(d_branch.astype(jnp.float32), axis=0, keepdims=True)
        sums_ref[3:4, :] = jnp.sum(cot, axis=0, keepdims=True)

    width = d_branch_ref.shape[1]
    part = dot_cols(stacked(weight_refs).reshape(-1, width), d_branch_ref[...]).astype(LOW)
    part = part.reshape(-1, *parts_ref.shape[1:])
    for at, index in enumerate(step_maps(chips, lambda owner: owner)):
        parts_ref[index(step, place_ref)] = part[at]


def branch_back(place, chips, resid, cotangent, gain, weights, backs):
    rows, width = resid.shape
    feats = weights[0].shape[2]
    places = 2 * chips[0] * chips[1]
    return feed_run(
        partial(branch_kernel, len(backs), chips),
        chips,
        place,
        [fixed((rows, width)), fixed((rows, width)), fixed(gain.shape)]
        + [weight_spec(item) for item in weights]
        + [fixed((rows, width))] * len(backs),
        [fixed((rows, width))] * 2 + [fixed((4, width)), fixed((places, feats, rows))],
        [
            shape((rows, width), jnp.float32),
            shape((rows, width), LOW),
            shape((4, width), jnp.float32),
            shape((places, feats, rows), LOW),
        ],
        (resid, cotangent, gain, *weights, *backs),
        [],
        32,
    )


def branch_grad_kernel(owners, place_ref, *refs):
    own_refs, other_refs, grad_refs, out_refs = take(refs, owners, owners, 2)
    parts = jnp.concatenate([stacked(own_refs), stacked(other_refs)], axis=1)
    grads = jnp.concatenate([ref[...] for ref in grad_refs], axis=0)
    out = dot(parts, grads).astype(LOW).reshape(out_refs[0].shape)
    for at, ref in enumerate(out_refs):

        @pl.when(pl.program_id(0) == at)
        def _():
            ref[...] = out


def branch_grad(place, chips, own, other, own_grad, other_grad):
    _, feats, rows = own.shape
    width = own_grad.shape[1]
    chips_x, chips_y = chips
    part_specs = [
        pl.BlockSpec((1, feats, rows), at)
        for at in step_maps(chips, lambda owner: (owner, 0, 0))[:chips_y]
    ]
    return feed_run(
        partial(branch_grad_kernel, chips_y),
        chips,
        place,
        part_specs * 2 + [fixed((rows, width))] * 2,
        [pl.BlockSpec((chips_y, feats, width), own_map(lambda i: (0, 0, 0)))] * chips_x,
        [shape((chips_y, feats, width), LOW)] * chips_x,
        (*[own] * chips_y, *[other] * chips_y, own_grad, other_grad),
        [],
        32,
    )


def joint_grad_kernel(
    grad_ref, rows_ref, weight_ref, gain_ref, shift_ref, out_ref, bias_ref, sums_ref, total, biases
):
    step = pl.program_id(0)
    grads = side_by_side(grad_ref)
    added = dot(grads, rows_ref[...])
    summed = jnp.sum(grads.astype(jnp.float32), axis=1, keepdims=True)

    @pl.when(step == 0)
    def _():
        total[...] = added
        biases[...] = summed

    @pl.when(step > 0)
    def _():
        total[...] += added
        biases[...] += summed

    @pl.when(step == pl.num_programs(0) - 1)
    def _():
        out_ref[...] = total[...].astype(LOW)
        bias_ref[...] = biases[...]
        weight = weight_ref[...].astype(jnp.float32)
        shift_sum = jnp.sum(weight * biases[...], axis=0, keepdims=True)
        product = jnp.sum(weight * total[...], axis=0, keepdims=True)
        sums_ref[0:1, :] = (product - shift_sum * shift_ref[...]) / gain_ref[...]
        sums_ref[1:2, :] = shift_sum


def joint_grad(grads, inputs, weight, gain, shift, step=4):
    places, feats, rows = grads.shape
    width = inputs.shape[1]
    return run(
        joint_grad_kernel,
        (places // step,),
        [
            pl.BlockSpec((step, feats, rows), lambda i: (i, 0, 0)),
            pl.BlockSpec((step * rows, width), lambda i: (i, 0)),
            whole(weight),
            whole(gain),
            whole(shift),
        ],
        [
            pl.BlockSpec((feats, width), lambda i: (0, 0)),
            pl.BlockSpec((feats, 1), lambda i: (0, 0)),
            pl.BlockSpec((2, width), lambda i: (0, 0)),
        ],
        [
            shape((feats, width), LOW),
            shape((feats, 1), jnp.float32),
            shape((2, width), jnp.float32),
        ],
        (grads, inputs, weight, gain, shift),
        scratch=[pltpu.VMEM((feats, width), jnp.float32), pltpu.VMEM((feats, 1), jnp.float32)],
    )


def input_kernel(part_ref, weight_ref, tokens_ref, gain_ref, d_resid_ref, out_ref, total):
    step = pl.program_id(0)
    added = dot(turned(part_ref[...]).astype(LOW), weight_ref[...])

    @pl.when(step == 0)
    def _():
        total[...] = added

    @pl.when(step > 0)
    def _():
        total[...] += added

    @pl.when(step == pl.num_programs(0) - 1)
    def _():
        normed, scale = norm_parts(tokens_ref[...].astype(jnp.float32))
        out_ref[...] = d_resid_ref[...] + norm_back(total[...], normed, scale, gain_ref[...])


def input_back(parts, weights, tokens, gain, d_resid, step=SPAN):
    feats, rows = parts.shape
    width = weights.shape[1]
    return run(
        input_kernel,
        (feats // step,),
        [
            pl.BlockSpec((step, rows), lambda i: (i, 0)),
            pl.BlockSpec((step, width), lambda i: (i, 0)),
            whole(tokens),
            whole(gain),
            whole(d_resid),
        ],
        [pl.BlockSpec((rows, width), lambda i: (0, 0))],
        [shape((rows, width), jnp.float32)],
        (parts, weights, tokens, gain, d_resid),
        scratch=[pltpu.VMEM((rows, width), jnp.float32)],
    )[0]


ITEM = "z"
HEAD = ("x", "y", "c")
CORE = "c"


def moved(value, axis, steps):
    count = lax.axis_size(axis)
    return lax.ppermute(value, axis, [(place, (place + steps) % count) for place in range(count)])


def shifted(value, axis, steps):
    count = lax.axis_size(axis)
    initial, last = (max(0, -steps), min(count, count - steps))
    return lax.ppermute(value, axis, [(source, source + steps) for source in range(initial, last)])


def all_sum(value, axes):
    for axis in axes:
        if lax.axis_size(axis) == 4:
            terms = around(value, axis)
            value = (terms[0] + terms[2]) + (terms[1] + terms[3])
            continue
        step = 1
        while step < lax.axis_size(axis):
            pairs = [(place, place ^ step) for place in range(lax.axis_size(axis))]
            value = value + lax.ppermute(value, axis, pairs)
            step *= 2
    return value


def around(value, axis):
    return [value] + [moved(value, axis, -step) for step in range(1, lax.axis_size(axis))]


def sum_back(values, axis):
    return [values[0]] + [
        moved(values[step], axis, step) for step in range(1, lax.axis_size(axis))
    ]


def item_terms(value):
    count = lax.axis_size(ITEM)
    place = lax.axis_index(ITEM)
    parts = value.reshape(count, -1, value.shape[1])
    own = [
        lax.dynamic_index_in_dim(parts, (place + step) % count, 0, keepdims=False)
        for step in range(count)
    ]
    return sum_back(own, ITEM)


def item_sum(terms):
    count = lax.axis_size(ITEM)
    place = lax.axis_index(ITEM)
    block = sum(term.astype(jnp.float32) for term in terms).astype(LOW)
    blocks = around(block, ITEM)
    rows = lax.dynamic_slice_in_dim(
        jnp.stack(blocks + blocks), (count - place) % count, count, 0
    )
    return rows.reshape(-1, block.shape[1]).astype(jnp.float32)


def head_swap(value):
    return lax.all_to_all(value, HEAD, split_axis=0, concat_axis=0, tiled=True)


def segment_flags(seg_counts):
    total_segs = seg_counts.shape[0]
    openings = jnp.cumsum(seg_counts) - seg_counts
    places = jnp.arange(total_segs, dtype=jnp.int32)
    opens_here = jnp.any((openings[:, None] == places[None, :]) & (seg_counts[:, None] > 0), axis=0)
    opens_before = jnp.concatenate([jnp.ones((1,), dtype=bool), opens_here[:-1]])
    one_back = jnp.logical_not(opens_here)
    two_back = one_back & jnp.logical_not(opens_before)
    return (one_back, two_back)


def local(
    tokens,
    cotangent,
    seg_counts,
    query_weight,
    key_weight,
    value_weight,
    query_bias,
    value_bias,
    out_weight,
    out_bias,
    first_gain,
    first_shift,
    second_gain,
    second_shift,
    up_weight,
    up_bias,
    down_weight,
    down_bias,
):
    rows, width = tokens.shape
    heads = lax.axis_size(HEAD)
    item_place = lax.axis_index(ITEM)
    group_rows = rows * heads
    seg_local = group_rows // SEG
    feats = query_weight.shape[0]
    units = up_weight.shape[0]
    hidden_here = units * heads

    def row(vector):
        return vector.reshape(1, -1)

    tokens_f = tokens.astype(jnp.float32)
    inputs_one = layer_norm(tokens_f, first_gain, first_shift).astype(LOW)
    inputs_all = lax.all_gather(inputs_one, HEAD, axis=0, tiled=True)
    out_weights = jnp.stack(around(out_weight, "y"))
    second = jnp.concatenate([up_weight, down_weight], axis=0)
    feed_weights = lax.all_gather(second, HEAD, axis=0, tiled=True).reshape(heads, -1, width)
    cots = around(cotangent, ITEM)
    joint_weight = jnp.concatenate([query_weight, key_weight, value_weight], axis=0)
    joint_bias = jnp.concatenate([query_bias, jnp.zeros_like(query_bias), value_bias])

    one_back, two_back = segment_flags(seg_counts)
    flags = jnp.stack([two_back, one_back], axis=1).astype(jnp.int32)
    flags = lax.dynamic_slice_in_dim(flags, item_place * seg_local, seg_local).reshape(-1)

    inputs_all, cots, out_weights = lax.optimization_barrier((inputs_all, cots, out_weights))
    out_weights = around(out_weights, "x")
    query, kv, turned_all = project(inputs_all, joint_weight, row(joint_bias))
    own_kept = kv.reshape(seg_local, SEG, 2 * HD)[:, SEG - KEPT :]
    table = jnp.concatenate([shifted(own_kept, ITEM, 1), own_kept], axis=0)
    prefix = jnp.concatenate(
        [table[seg_local - 2 : 2 * seg_local - 2], table[seg_local - 1 : 2 * seg_local - 1]], axis=1
    )
    attended, log_sums = attend(flags, turned_all, kv, prefix, rows)
    attended_own = head_swap(attended)
    attended_own, out_weights = lax.optimization_barrier(
        (attended_own, jnp.stack(lax.optimization_barrier((out_weights, attended))[0]))
    )
    out_weights = [out_weights, moved(out_weights, CORE, 1)]
    attended_other = moved(attended_own, CORE, 1)
    chips = (lax.axis_size("x"), lax.axis_size("y"))
    place = jnp.stack([lax.axis_index(axis) for axis in (CORE, "x", "y")]).astype(jnp.int32)
    resid, inputs_two = out_project(
        place,
        chips,
        attended_own,
        out_weights,
        tokens,
        row(out_bias),
        row(second_gain),
        row(second_shift),
    )

    joint_turn = lax.optimization_barrier((joint_weight, resid))[0]
    joint_full = lax.all_gather(joint_turn, HEAD, axis=0, tiled=True)
    norms = around(inputs_two, ITEM)
    d_act, cots = feed_d_act(place, chips, cots, feed_weights)
    cots = [cots, moved(cots, CORE, 1)]
    bias_here = lax.dynamic_slice_in_dim(up_bias, item_place * hidden_here, hidden_here)
    backs, (norms, kept, sent, up_bias_part) = feed(
        place, chips, norms, feed_weights, bias_here.reshape(heads, 1, units), d_act
    )
    backs = sum_back(backs, ITEM)
    norms = [norms, moved(norms, CORE, 1)]
    mixeds, feed_parts = feed_grad(
        place, chips, len(backs), norms, cots, kept, sent, moved(sent, CORE, 1), feed_weights
    )
    backs, mixeds = lax.optimization_barrier((backs, mixeds))
    d_resid, d_branch, sums_two, d_parts = branch_back(
        place, chips, resid, cotangent, row(second_gain), out_weights, backs
    )
    d_attended = head_swap(d_parts)
    feed_parts = lax.optimization_barrier((feed_parts, d_resid))[0]
    feed_grads = lax.psum_scatter(
        feed_parts.reshape(-1, width), ("x", "y"), scatter_dimension=0, tiled=True
    )

    outs = branch_grad(
        place, chips, attended_own, attended_other, d_branch, moved(d_branch, CORE, 1)
    )
    d_attended, outs = lax.optimization_barrier((d_attended, outs))
    outs = sum_back(outs, "x")

    d_prefix = prefix_back(
        flags, turned_all, query, d_attended, attended, log_sums, prefix, rows
    )[0]
    older, newer = d_prefix[:, :KEPT], d_prefix[:, KEPT:]
    spread = jnp.pad(older, ((seg_local - 2, 2), (0, 0), (0, 0)))
    spread = spread + jnp.pad(newer, ((seg_local - 1, 1), (0, 0), (0, 0)))
    returned = shifted(spread[:seg_local], ITEM, -1)
    joint_grads, kept_grads = attend_back(
        flags, turned_all, query, d_attended, attended, log_sums, prefix, kv, rows
    )
    returned, kept_grads, joint_full = lax.optimization_barrier((returned, kept_grads, joint_full))
    joint_grads = add_returned(joint_grads, kept_grads, spread[seg_local:] + returned)
    joint_grads, mixeds = lax.optimization_barrier((joint_grads, mixeds))
    mixeds = sum_back(mixeds, ITEM)
    grads_own = head_swap(joint_grads).reshape(-1, rows)
    joint_part, bias_part, sums_one = joint_grad(
        joint_grads, inputs_all, joint_weight, row(first_gain), row(first_shift)
    )
    outs, joint_part, sums_one = lax.optimization_barrier((outs, joint_part, sums_one))
    out_part = lax.optimization_barrier(sum(out.astype(jnp.float32) for out in outs).astype(LOW))
    terms = item_terms(joint_part)
    small = [up_bias_part.reshape(-1), sums_two.reshape(-1), sums_one.reshape(-1)]
    small = all_sum(jnp.concatenate(small).reshape(-1, 128), (CORE,))
    grads_own, out_part, small = lax.optimization_barrier((grads_own, out_part, small))
    small = all_sum(small, ("y",))
    out_part = sum_back([out_part[step] for step in range(lax.axis_size("y"))], "y")
    input_grad = input_back(grads_own, joint_full, tokens, row(first_gain), d_resid)
    input_grad, terms, small, out_part, mixeds, feed_grads = lax.optimization_barrier(
        (input_grad, terms, small, out_part, mixeds, feed_grads)
    )
    feed_grads = feed_grads.astype(jnp.float32)
    joint_sums = item_sum(terms)
    out_part = sum(out.astype(jnp.float32) for out in out_part).astype(LOW)
    outs = [out.astype(jnp.float32) for out in around(out_part, ITEM)]
    out_sum = (outs[0] + outs[2]) + (outs[1] + outs[3])
    small = all_sum(small, ("x",))
    mixed = sum(part.astype(jnp.float32) for part in mixeds)
    mixed_out = (resid + mixed + down_bias).astype(LOW)
    small = small.reshape(-1)
    up_bias_sums, small = small[:hidden_here], small[hidden_here:]
    up_bias_sums = lax.dynamic_update_slice_in_dim(
        jnp.zeros(up_bias.shape, jnp.float32), up_bias_sums, item_place * hidden_here, 0
    )
    small = jnp.concatenate([up_bias_sums, small, bias_part.reshape(-1)])
    small = all_sum(jnp.pad(small, (0, -small.size % 128)).reshape(-1, 128), (ITEM,)).reshape(-1)
    up_bias_grad, small = small[: up_bias.size], small[up_bias.size :]
    early_rows, late = small[: 4 * width].reshape(4, width), small[4 * width : 6 * width]
    late = late.reshape(2, width)
    bias_sums = small[6 * width : 6 * width + 3 * feats]
    return (
        mixed_out,
        input_grad,
        joint_sums[:feats],
        joint_sums[feats : 2 * feats],
        joint_sums[2 * feats :],
        bias_sums[:feats],
        bias_sums[2 * feats :],
        out_sum,
        early_rows[2],
        late[0],
        late[1],
        early_rows[0],
        early_rows[1],
        feed_grads[:units],
        up_bias_grad,
        feed_grads[units:],
        early_rows[3],
    )


def solution(mesh):
    sizes = (mesh.shape["item"], 4, mesh.shape["head"] // 8, 2)
    fine = Mesh(mesh.devices.reshape(sizes), (ITEM, *HEAD))
    split = P((ITEM, *HEAD), None)
    by_head = P(HEAD, None)
    return jax.shard_map(
        local,
        mesh=fine,
        in_specs=(
            split,
            split,
            P(),
            by_head,
            by_head,
            by_head,
            P(HEAD),
            P(HEAD),
            by_head,
            P(),
            P(),
            P(),
            P(),
            P(),
            split,
            P(),
            split,
            P(),
        ),
        out_specs=(
            split,
            split,
            by_head,
            by_head,
            by_head,
            P(HEAD),
            P(HEAD),
            by_head,
            P(),
            P(),
            P(),
            P(),
            P(),
            split,
            P(),
            split,
            P(),
        ),
        check_vma=False,
    )
```

```python
from functools import partial

import jax
import jax.numpy as jnp
from jax import lax
from jax.experimental import pallas as pl
from jax.experimental.pallas import tpu as pltpu
from jax.sharding import Mesh
from jax.sharding import PartitionSpec as P

HD = 64
NSUM = 50
SEG = 2048
SPAN = 512
KEPT = 64
EPSILON = 1e-05
MASKED = -1e30
SCALE = HD ** (-0.5)
MIB = 1 << 20
COST = 1 << 20
LOW = jnp.bfloat16


def dot(left, right):
    return jnp.dot(left, right, preferred_element_type=jnp.float32)


def dot_cols(left, right):
    return lax.dot_general(
        left, right, (((1,), (1,)), ((), ())), preferred_element_type=jnp.float32
    )


def turned(value):
    return value.astype(jnp.float32).T


def norm_parts(row_data):
    row_mean = jnp.mean(row_data, axis=-1, keepdims=True)
    centred = row_data - row_mean
    row_var = jnp.mean(centred * centred, axis=-1, keepdims=True)
    scale = lax.rsqrt(row_var + EPSILON)
    return centred * scale, scale


def norm_back(grad, normed, scale, gain):
    scaled = grad * gain
    return scale * (
        scaled
        - jnp.mean(scaled, axis=-1, keepdims=True)
        - normed * jnp.mean(scaled * normed, axis=-1, keepdims=True)
    )


def layer_norm(row_data, gain, shift):
    return norm_parts(row_data)[0] * gain + shift


def run(body, grid, in_specs, out_specs, out_shape, operands, scratch=(), vmem=32, aliases=None):
    return pl.pallas_call(
        body,
        grid=grid,
        in_specs=in_specs,
        out_specs=out_specs,
        out_shape=out_shape,
        scratch_shapes=scratch,
        compiler_params=pltpu.CompilerParams(
            dimension_semantics=("arbitrary",) * len(grid), vmem_limit_bytes=vmem * MIB
        ),
        input_output_aliases=aliases or {},
        cost_estimate=pl.CostEstimate(flops=COST, bytes_accessed=COST, transcendentals=0),
    )(*operands)


def shape(dims, kind):
    return jax.ShapeDtypeStruct(dims, kind)


def whole(item):
    return pl.BlockSpec(item.shape, lambda *_: (0,) * len(item.shape))


def project_kernel(rows_ref, weight_ref, bias_ref, query_ref, kv_ref, turned_ref):
    rows = rows_ref[...].reshape(SPAN, rows_ref.shape[2])
    joint = dot_cols(rows, weight_ref[...]) + bias_ref[...]
    query_ref[...] = joint[:, :HD].astype(LOW)
    kv_ref[...] = joint[:, HD:].astype(LOW)
    turned_ref[...] = joint.T.astype(LOW)


def project(gathered, rows_here, weight, bias):
    places, _, width = gathered.shape
    total = places * rows_here
    step = SPAN // rows_here
    return run(
        project_kernel,
        (total // SPAN,),
        [
            pl.BlockSpec((step, rows_here, width), lambda i: (i, 0, 0)),
            whole(weight),
            whole(bias),
        ],
        [
            pl.BlockSpec((SPAN, HD), lambda i: (i, 0)),
            pl.BlockSpec((SPAN, 2 * HD), lambda i: (i, 0)),
            pl.BlockSpec((3 * HD, SPAN), lambda i: (0, i)),
        ],
        [
            shape((total, HD), LOW),
            shape((total, 2 * HD), LOW),
            shape((3 * HD, total), LOW),
        ],
        (gathered, weight, bias),
    )


def prefix_seen(flags_ref, seg, columns):
    place = lax.broadcasted_iota(jnp.int32, (2 * KEPT, columns), 0)
    older = place < KEPT
    slot = jnp.where(older, place, place - KEPT) >= KEPT - NSUM
    flag = jnp.where(older, flags_ref[2 * seg], flags_ref[2 * seg + 1])
    return slot & (flag > 0)


def causal_seen():
    shape_here = (SPAN, SPAN)
    return lax.broadcasted_iota(jnp.int32, shape_here, 0) <= lax.broadcasted_iota(
        jnp.int32, shape_here, 1
    )


def above(block):
    return jnp.concatenate([block, jnp.zeros_like(block)], axis=0)


def below(block):
    return jnp.concatenate([jnp.zeros_like(block), block], axis=0)


def at_block(index):
    return pl.ds(pl.multiple_of(index * SPAN, SPAN), SPAN)


def attend_kernel(flags_ref, query_ref, turned_ref, kv_ref, prefix_ref, out_ref, log_ref):
    seg, block = pl.program_id(0), pl.program_id(1)
    query = above((query_ref[...].astype(jnp.float32) * SCALE).astype(LOW))
    own = at_block(block)
    scores = dot(kv_ref[own, :], query)
    scores = jnp.where(causal_seen(), scores, MASKED)
    top = jnp.max(scores, axis=0, keepdims=True)
    probs = jnp.exp(scores - top)
    total = jnp.sum(probs, axis=0, keepdims=True)
    mixed = dot(turned_ref[2 * HD :, own], probs.astype(LOW))

    def add(carry, scores, values):
        top, total, mixed = carry
        fresh = jnp.maximum(top, jnp.max(scores, axis=0, keepdims=True))
        fade = jnp.exp(top - fresh)
        probs = jnp.exp(scores - fresh)
        total = total * fade + jnp.sum(probs, axis=0, keepdims=True)
        return fresh, total, mixed * fade + dot(values, probs.astype(LOW))

    prefix = prefix_ref[0]
    scores = jnp.where(prefix_seen(flags_ref, seg, SPAN), dot(prefix, query), MASKED)
    carry = add((top, total, mixed), scores, turned(prefix)[HD:].astype(LOW))

    def step(index, carry):
        here = at_block(index)
        return add(carry, dot(kv_ref[here, :], query), turned_ref[2 * HD :, here])

    top, total, mixed = lax.fori_loop(0, block, step, carry)
    mixed = (mixed / total).astype(LOW)
    rows = out_ref.shape[2]
    for piece in range(SPAN // rows):
        out_ref[piece] = mixed[:, piece * rows : (piece + 1) * rows]
    log_ref[0] = top + jnp.log(total)


def attend(flags, turned_all, kv, prefix, rows_here):
    total = kv.shape[0]
    blocks = SEG // SPAN
    step = SPAN // rows_here
    return run(
        attend_kernel,
        (total // SEG, blocks),
        [
            pl.BlockSpec(memory_space=pltpu.SMEM),
            pl.BlockSpec((HD, SPAN), lambda s, i: (0, s * blocks + i)),
            pl.BlockSpec((3 * HD, SEG), lambda s, i: (0, s)),
            pl.BlockSpec((SEG, 2 * HD), lambda s, i: (s, 0)),
            pl.BlockSpec((1, 2 * KEPT, 2 * HD), lambda s, i: (s, 0, 0)),
        ],
        [
            pl.BlockSpec((step, HD, rows_here), lambda s, i: (s * blocks + i, 0, 0)),
            pl.BlockSpec((1, 1, SPAN), lambda s, i: (s * blocks + i, 0, 0)),
        ],
        [
            shape((total // rows_here, HD, rows_here), LOW),
            shape((total // SPAN, 1, SPAN), jnp.float32),
        ],
        (flags, turned_all, turned_all, kv, prefix),
    )


def side_by_side(ref):
    return jnp.concatenate([ref[piece] for piece in range(ref.shape[0])], axis=1)


def beside(block, place):
    zero = jnp.zeros_like(block)
    return jnp.concatenate([block, zero] if place == 0 else [zero, block], axis=1)


def query_side(query_ref, rows_ref, grad_ref, out_ref, log_ref):
    query = above((query_ref[...].astype(jnp.float32) * SCALE).astype(LOW))
    grad = side_by_side(grad_ref)
    mean = jnp.sum(
        grad.astype(jnp.float32) * side_by_side(out_ref).astype(jnp.float32),
        axis=0,
        keepdims=True,
    )
    query_rows = beside((rows_ref[...].astype(jnp.float32) * SCALE).astype(LOW), 0)
    grad_rows = beside(turned(grad).astype(LOW), 1)
    return query, below(grad), mean, log_ref[0], query_rows, grad_rows


def key_side(keys, side, seen):
    query, grad, mean, log_sum, query_rows, grad_rows = side
    probs = jnp.exp(dot(keys, query) - log_sum)
    if seen is not None:
        probs = jnp.where(seen, probs, 0.0)
    d_scores = (probs * (dot(keys, grad) - mean)).astype(LOW)
    return probs.astype(LOW), d_scores


def prefix_back_kernel(
    flags_ref, query_ref, rows_ref, grad_ref, out_ref, log_ref, prefix_ref, sum_ref
):
    seg, block = pl.program_id(0), pl.program_id(1)
    side = query_side(query_ref, rows_ref, grad_ref, out_ref, log_ref)
    probs, d_scores = key_side(prefix_ref[0], side, prefix_seen(flags_ref, seg, SPAN))
    part = dot(d_scores, side[4]) + dot(probs, side[5])

    @pl.when(block == 0)
    def _():
        sum_ref[0] = part

    @pl.when(block > 0)
    def _():
        sum_ref[0] += part


def store_shares(grads_ref, piece, part, columns):
    here = HD // grads_ref.shape[0]
    for share in range(grads_ref.shape[0]):
        for kind in (1, 2):
            first = (kind - 1) * HD + share * here
            grads_ref[share, piece, kind * here : (kind + 1) * here, columns] = part[
                first : first + here
            ]


def attend_back_kernel(
    flags_ref,
    query_ref,
    rows_ref,
    grad_ref,
    out_ref,
    log_ref,
    prefix_ref,
    turned_ref,
    kv_ref,
    grads_ref,
    kept_ref,
    kv_grad,
):
    seg, block = pl.program_id(0), pl.program_id(1)

    @pl.when(block == 0)
    def _():
        kv_grad[...] = jnp.zeros_like(kv_grad)

    side = query_side(query_ref, rows_ref, grad_ref, out_ref, log_ref)
    prefix = prefix_ref[0]
    _, d_scores = key_side(prefix, side, prefix_seen(flags_ref, seg, SPAN))
    query_grad = dot(turned(prefix)[:HD].astype(LOW), d_scores)

    def add(here, query_grad, seen):
        probs, d_scores = key_side(kv_ref[here, :], side, seen)
        kv_grad[here, :] += dot(d_scores, side[4]) + dot(probs, side[5])
        return query_grad + dot(turned_ref[HD : 2 * HD, here], d_scores)

    query_grad = add(at_block(block), query_grad, causal_seen())
    query_grad = lax.fori_loop(
        0, block, lambda index, grad: add(at_block(index), grad, None), query_grad
    )
    query_grad = (query_grad * SCALE).astype(LOW)
    rows = grads_ref.shape[3]
    step = SPAN // rows
    for piece in range(step):
        part = query_grad[:, piece * rows : (piece + 1) * rows]
        for share in range(grads_ref.shape[0]):
            here = HD // grads_ref.shape[0]
            grads_ref[share, block * step + piece, :here, :] = part[share * here : (share + 1) * here]

    @pl.when(block == pl.num_programs(1) - 1)
    def _():
        for piece in range(SEG // rows):
            part = kv_grad[piece * rows : (piece + 1) * rows, :].T.astype(LOW)
            store_shares(grads_ref, piece, part, slice(None))
        kept_ref[0] = kv_grad[SEG - KEPT :, :]


def attend_back_specs(rows_here):
    blocks = SEG // SPAN
    step = SPAN // rows_here
    return [
        pl.BlockSpec(memory_space=pltpu.SMEM),
        pl.BlockSpec((HD, SPAN), lambda s, i: (0, s * blocks + i)),
        pl.BlockSpec((SPAN, HD), lambda s, i: (s * blocks + i, 0)),
        pl.BlockSpec((step, HD, rows_here), lambda s, i: (s * blocks + i, 0, 0)),
        pl.BlockSpec((step, HD, rows_here), lambda s, i: (s * blocks + i, 0, 0)),
        pl.BlockSpec((1, 1, SPAN), lambda s, i: (s * blocks + i, 0, 0)),
        pl.BlockSpec((1, 2 * KEPT, 2 * HD), lambda s, i: (s, 0, 0)),
    ]


def prefix_back(flags, turned_all, query, grad, out, log_sums, prefix, rows_here):
    total = query.shape[0]
    return run(
        prefix_back_kernel,
        (total // SEG, SEG // SPAN),
        attend_back_specs(rows_here),
        [pl.BlockSpec((1, 2 * KEPT, 2 * HD), lambda s, i: (s, 0, 0))],
        [shape(prefix.shape, jnp.float32)],
        (flags, turned_all, query, grad, out, log_sums, prefix),
    )


def attend_back(flags, turned_all, query, grad, out, log_sums, prefix, kv, rows_here, count):
    total = query.shape[0]
    pieces = SEG // rows_here
    return run(
        attend_back_kernel,
        (total // SEG, SEG // SPAN),
        attend_back_specs(rows_here)
        + [
            pl.BlockSpec((3 * HD, SEG), lambda s, i: (0, s)),
            pl.BlockSpec((SEG, 2 * HD), lambda s, i: (s, 0)),
        ],
        [
            pl.BlockSpec(
                (count, pieces, 3 * HD // count, rows_here), lambda s, i: (0, s, 0, 0)
            ),
            pl.BlockSpec((1, KEPT, 2 * HD), lambda s, i: (s, 0, 0)),
        ],
        [
            shape((count, total // rows_here, 3 * HD // count, rows_here), LOW),
            shape((total // SEG, KEPT, 2 * HD), jnp.float32),
        ],
        (flags, turned_all, query, grad, out, log_sums, prefix, turned_all, kv),
        scratch=[pltpu.VMEM((SEG, 2 * HD), jnp.float32)],
    )


def returned_kernel(grads_ref, kept_ref, returned_ref, out_ref):
    out_ref[...] = grads_ref[...]
    part = (kept_ref[0] + returned_ref[0]).T.astype(LOW)
    store_shares(out_ref, 0, part, slice(out_ref.shape[3] - KEPT, None))


def add_returned(grads, kept, returned):
    count, places, feats, rows = grads.shape
    segs = kept.shape[0]
    last = places // segs
    grad_spec = pl.BlockSpec((count, 1, feats, rows), lambda s: (0, s * last + last - 1, 0, 0))
    kept_spec = pl.BlockSpec((1, KEPT, 2 * HD), lambda s: (s, 0, 0))
    return run(
        returned_kernel,
        (segs,),
        [grad_spec, kept_spec, kept_spec],
        [grad_spec],
        [shape(grads.shape, LOW)],
        (grads, kept, returned),
        aliases={0: 0},
    )[0]


def out_kernel(
    part_ref, weight_ref, tokens_ref, bias_ref, gain_ref, shift_ref, resid_ref, two_ref, total
):
    step = pl.program_id(0)
    rows = part_ref.shape[2]
    part = turned(part_ref[...].reshape(-1, rows)).astype(LOW)
    added = dot(part, weight_ref[...].reshape(part.shape[1], -1))

    @pl.when(step == 0)
    def _():
        total[...] = added

    @pl.when(step > 0)
    def _():
        total[...] += added

    @pl.when(step == pl.num_programs(0) - 1)
    def _():
        resid = tokens_ref[...].astype(jnp.float32) + total[...] + bias_ref[...]
        resid_ref[...] = resid
        two_ref[...] = layer_norm(resid, gain_ref[...], shift_ref[...]).astype(LOW)


def out_project(parts, gathered, at, tokens, bias, gain, shift, step=4):
    places, feats, rows = parts.shape
    width = gathered.shape[2]
    return run(
        out_kernel,
        (places // step,),
        [
            pl.BlockSpec((step, feats, rows), lambda i: (i, 0, 0)),
            pl.BlockSpec((step, feats, width), lambda i: (i, at, 0)),
            whole(tokens),
            whole(bias),
            whole(gain),
            whole(shift),
        ],
        [pl.BlockSpec((rows, width), lambda i: (0, 0))] * 2,
        [shape((rows, width), jnp.float32), shape((rows, width), LOW)],
        (parts, gathered, tokens, bias, gain, shift),
        scratch=[pltpu.VMEM((rows, width), jnp.float32)],
    )


def owner_maps(chips, at):
    def of(core_step, y):
        return lambda i, place: at((i * chips[1] + y) * 2 + lax.rem(place[0] + core_step, 2))

    return [of(core_step, y) for core_step in (0, 1) for y in range(chips[1])]


def step_maps(chips, at):
    chips_x, chips_y = chips

    def of(y_step):
        def index(i, place):
            x = lax.rem(place[1] + i, chips_x)
            y = lax.rem(place[2] + y_step, chips_y)
            return at((x * chips_y + y) * 2 + place[0])

        return index

    return [of(y_step) for y_step in range(chips_y)]


def own_map(index):
    return lambda i, place: index(i)


def fixed(dims):
    return pl.BlockSpec(
        dims, own_map(lambda i: (0,) * len(dims)), pipeline_mode=pl.Buffered(buffer_count=1)
    )


def feed_run(body, chips, place, in_specs, out_specs, out_shape, operands, scratch, vmem):
    return pl.pallas_call(
        body,
        grid_spec=pltpu.PrefetchScalarGridSpec(
            num_scalar_prefetch=1,
            grid=(chips[0],),
            in_specs=in_specs,
            out_specs=out_specs,
            scratch_shapes=scratch,
        ),
        out_shape=out_shape,
        compiler_params=pltpu.CompilerParams(
            dimension_semantics=("arbitrary",), vmem_limit_bytes=vmem * MIB
        ),
        cost_estimate=pl.CostEstimate(flops=COST, bytes_accessed=COST, transcendentals=0),
    )(place, *operands)


def stacked(refs, axis=0):
    return jnp.concatenate([ref[0] for ref in refs], axis=axis)


def pile(refs, into):
    rows = refs[0].shape[0]
    for at, ref in enumerate(refs):
        into[at * rows : (at + 1) * rows, :] = ref[...]


def spread(source, refs):
    rows = refs[0].shape[0]
    for at, ref in enumerate(refs):
        ref[...] = source[at * rows : (at + 1) * rows, :].astype(ref.dtype)


def take(refs, *counts):
    refs = list(refs)
    return [[refs.pop(0) for _ in range(count)] for count in counts] + [refs]


def d_act_kernel(count, owners, place_ref, *refs):
    cot_refs, weight_refs, (out_ref, cots) = take(refs, count, owners)

    @pl.when(pl.program_id(0) == 0)
    def _():
        pile(cot_refs, cots)

    out_ref[...] = dot_cols(cots[...], stacked(weight_refs))


def feed_d_act(place, chips, cots, weights):
    count = len(cots)
    rows, width = cots[0].shape
    places, both, _ = weights.shape
    units = both // 2
    total = count * rows
    owners = 2 * chips[1]
    step = owners * units
    return feed_run(
        partial(d_act_kernel, count, owners),
        chips,
        place,
        [fixed((rows, width))] * count
        + [
            pl.BlockSpec((1, units, width), at)
            for at in owner_maps(chips, lambda owner: (owner, 1, 0))
        ],
        [pl.BlockSpec((total, step), own_map(lambda i: (0, i))), fixed((total, width))],
        [shape((total, places * units), jnp.float32), shape((total, width), LOW)],
        (*cots, *[weights] * owners),
        [],
        32,
    )


def feed_kernel(count, chips, place_ref, *refs):
    owners = 2 * chips[1]
    norm_refs, weight_refs, bias_refs, (d_act_ref,), back_refs, refs = take(
        refs, count, owners, owners, 1, count
    )
    norms, kept_ref, sent_ref, bias_sum_ref, back = refs
    step = pl.program_id(0)

    @pl.when(step == 0)
    def _():
        pile(norm_refs, norms)
        back[...] = jnp.zeros_like(back)

    up = stacked(weight_refs)
    pre = dot_cols(norms[...], up) + stacked(bias_refs, axis=1)
    square = pre * pre
    bent = jnp.tanh(0.7978845608 * (pre + 0.044715 * (square * pre)))
    half = 0.5 * (1.0 + bent)
    slope = half + 0.5 * pre * (1.0 - bent * bent) * (
        0.7978845608 * (1.0 + 3.0 * 0.044715 * square)
    )
    d_pre = (d_act_ref[...] * slope).astype(LOW)
    act = (pre * half).astype(LOW)
    own = act.shape[1] // 2
    kept_ref[0] = act[:, :own]
    kept_ref[1] = d_pre[:, :own]
    sent_ref[0] = act[:, own:]
    sent_ref[1] = d_pre[:, own:]
    bias_sums = jnp.sum(d_pre.astype(jnp.float32), axis=0, keepdims=True)
    units = weight_refs[0].shape[1]
    for at, index in enumerate(owner_maps(chips, lambda owner: owner)):
        bias_sum_ref[index(step, place_ref)] = bias_sums[:, at * units : (at + 1) * units]
    back[...] += dot(d_pre, up)

    @pl.when(step == pl.num_programs(0) - 1)
    def _():
        spread(back, back_refs)


def feed(place, chips, norms, weights, bias, d_act):
    count = len(norms)
    rows, width = norms[0].shape
    places, both, _ = weights.shape
    units = both // 2
    total = count * rows
    owners = 2 * chips[1]
    step = owners * units
    pair_spec = pl.BlockSpec((2, total, step // 2), own_map(lambda i: (0, 0, i)))
    results = feed_run(
        partial(feed_kernel, count, chips),
        chips,
        place,
        [fixed((rows, width))] * count
        + [
            pl.BlockSpec((1, units, width), at)
            for at in owner_maps(chips, lambda owner: (owner, 0, 0))
        ]
        + [
            pl.BlockSpec((1, 1, units), at)
            for at in owner_maps(chips, lambda owner: (owner, 0, 0))
        ]
        + [pl.BlockSpec((total, step), own_map(lambda i: (0, i)))],
        [pl.BlockSpec((rows, width), own_map(lambda i: (0, 0)))] * count
        + [fixed((total, width)), pair_spec, pair_spec, fixed((places, 1, units))],
        [shape((rows, width), LOW)] * count
        + [shape((total, width), LOW)]
        + [shape((2, total, places * units // 2), LOW)] * 2
        + [shape((places, 1, units), jnp.float32)],
        (*norms, *[weights] * owners, *[bias] * owners, d_act),
        [pltpu.VMEM((total, width), jnp.float32)],
        40,
    )
    return results[:count], results[count:]


def feed_grad_kernel(count, owners, place_ref, *refs):
    norm_refs, cot_refs, pair_refs, weight_refs, mixed_refs, (out_ref, mixed) = take(
        refs, 2, 2, 3, owners, count
    )
    kept_ref, sent_ref, other_ref = pair_refs
    step = pl.program_id(0)
    units = weight_refs[0].shape[1]

    @pl.when(step == 0)
    def _():
        mixed[...] = jnp.zeros_like(mixed)

    act = jnp.concatenate([kept_ref[0], sent_ref[0]], axis=1)
    mixed[...] += dot(act, stacked(weight_refs))

    def grad(at, rows):
        total = dot(turned(kept_ref[at]).astype(LOW), rows[0][...])
        total += dot(turned(other_ref[at]).astype(LOW), rows[1][...])
        return total.astype(LOW).reshape(out_ref.shape[0], units, -1)

    out_ref[:, :units, :] = grad(1, norm_refs)
    out_ref[:, units:, :] = grad(0, cot_refs)

    @pl.when(step == pl.num_programs(0) - 1)
    def _():
        spread(mixed, mixed_refs)


def feed_grad(place, chips, count, norms, cots, kept, sent, other, weights):
    total, width = norms[0].shape
    rows = total // count
    units = weights.shape[1] // 2
    owners = 2 * chips[1]
    pair_spec = pl.BlockSpec((2, total, owners * units // 2), own_map(lambda i: (0, 0, i)))
    results = feed_run(
        partial(feed_grad_kernel, count, owners),
        chips,
        place,
        [fixed((total, width))] * 4
        + [pair_spec] * 3
        + [
            pl.BlockSpec((1, units, width), at)
            for at in owner_maps(chips, lambda owner: (owner, 1, 0))
        ],
        [pl.BlockSpec((rows, width), own_map(lambda i: (0, 0)))] * count
        + [pl.BlockSpec((chips[1], 2 * units, width), own_map(lambda i: (i, 0, 0)))],
        [shape((rows, width), LOW)] * count
        + [shape((chips[0] * chips[1], 2 * units, width), LOW)],
        (*norms, *cots, kept, sent, other, *[weights] * owners),
        [pltpu.VMEM((total, width), jnp.float32)],
        48,
    )
    return results[:count], results[count]


def branch_kernel(
    count, resid_ref, cot_ref, gain_ref, weight_ref, *refs
):
    back_refs = refs[:count]
    d_resid_ref, d_branch_ref, sums_ref, parts_ref = refs[count:]

    @pl.when(pl.program_id(0) == 0)
    def _():
        d_two = sum(ref[...].astype(jnp.float32) for ref in back_refs)
        normed, scale = norm_parts(resid_ref[...])
        cot = cot_ref[...].astype(jnp.float32)
        d_resid = cot + norm_back(d_two, normed, scale, gain_ref[...])
        d_branch = d_resid.astype(LOW)
        d_resid_ref[...] = d_resid
        d_branch_ref[...] = d_branch
        sums_ref[0:1, :] = jnp.sum(d_two * normed, axis=0, keepdims=True)
        sums_ref[1:2, :] = jnp.sum(d_two, axis=0, keepdims=True)
        sums_ref[2:3, :] = jnp.sum(d_branch.astype(jnp.float32), axis=0, keepdims=True)
        sums_ref[3:4, :] = jnp.sum(cot, axis=0, keepdims=True)

    width = weight_ref.shape[2]
    part = dot_cols(weight_ref[...].reshape(-1, width), d_branch_ref[...])
    parts_ref[...] = part.reshape(parts_ref.shape).astype(LOW)


def branch_back(resid, cotangent, gain, gathered, at, feats, backs, step=4):
    rows, width = resid.shape
    places = gathered.shape[0]
    row_spec = pl.BlockSpec((rows, width), lambda i: (0, 0))
    return run(
        partial(branch_kernel, len(backs)),
        (places // step,),
        [
            row_spec,
            row_spec,
            whole(gain),
            pl.BlockSpec((step, feats, width), lambda i: (i, at, 0)),
        ]
        + [row_spec] * len(backs),
        [
            row_spec,
            row_spec,
            pl.BlockSpec((4, width), lambda i: (0, 0)),
            pl.BlockSpec((step, feats, rows), lambda i: (i, 0, 0)),
        ],
        [
            shape((rows, width), jnp.float32),
            shape((rows, width), LOW),
            shape((4, width), jnp.float32),
            shape((places, feats, rows), LOW),
        ],
        (resid, cotangent, gain, gathered, *backs),
    )


def branch_grad_kernel(owners, place_ref, *refs):
    own_refs, other_refs, grad_refs, out_refs = take(refs, owners, owners, 2)
    parts = jnp.concatenate([stacked(own_refs), stacked(other_refs)], axis=1)
    grads = jnp.concatenate([ref[...] for ref in grad_refs], axis=0)
    out = dot(parts, grads).astype(LOW).reshape(out_refs[0].shape)
    for at, ref in enumerate(out_refs):

        @pl.when(pl.program_id(0) == at)
        def _():
            ref[...] = out


def branch_grad(place, chips, own, other, own_grad, other_grad):
    _, feats, rows = own.shape
    width = own_grad.shape[1]
    chips_x, chips_y = chips
    part_specs = [
        pl.BlockSpec((1, feats, rows), at)
        for at in step_maps(chips, lambda owner: (owner, 0, 0))
    ]
    return feed_run(
        partial(branch_grad_kernel, chips_y),
        chips,
        place,
        part_specs * 2 + [fixed((rows, width))] * 2,
        [pl.BlockSpec((chips_y, feats, width), own_map(lambda i: (0, 0, 0)))] * chips_x,
        [shape((chips_y, feats, width), LOW)] * chips_x,
        (*[own] * chips_y, *[other] * chips_y, own_grad, other_grad),
        [],
        32,
    )


def by_kind(rows, count):
    here = HD // count
    return jnp.concatenate(
        [
            rows[(share * 3 + kind) * here : (share * 3 + kind + 1) * here]
            for kind in range(3)
            for share in range(count)
        ],
        axis=0,
    )


def joint_grad_kernel(
    grad_ref, rows_ref, weight_ref, gain_ref, shift_ref, out_ref, bias_ref, sums_ref, total, biases
):
    step = pl.program_id(0)
    count, pieces = grad_ref.shape[:2]
    grads = jnp.concatenate(
        [
            jnp.concatenate([grad_ref[share, piece] for piece in range(pieces)], axis=1)
            for share in range(count)
        ],
        axis=0,
    )
    added = dot(grads, rows_ref[...].reshape(grads.shape[1], -1))
    summed = jnp.sum(grads.astype(jnp.float32), axis=1, keepdims=True)

    @pl.when(step == 0)
    def _():
        total[...] = added
        biases[...] = summed

    @pl.when(step > 0)
    def _():
        total[...] += added
        biases[...] += summed

    @pl.when(step == pl.num_programs(0) - 1)
    def _():
        out = by_kind(total[...], count)
        bias = by_kind(biases[...], count)
        out_ref[...] = out.astype(LOW)
        bias_ref[...] = bias
        weight = weight_ref[...].astype(jnp.float32)
        shift_sum = jnp.sum(weight * bias, axis=0, keepdims=True)
        product = jnp.sum(weight * out, axis=0, keepdims=True)
        sums_ref[0:1, :] = (product - shift_sum * shift_ref[...]) / gain_ref[...]
        sums_ref[1:2, :] = shift_sum


def joint_grad(grads, gathered, weight, gain, shift, step=8):
    count, places, feats, rows = grads.shape
    width = gathered.shape[2]
    total = count * feats
    return run(
        joint_grad_kernel,
        (places // step,),
        [
            pl.BlockSpec((count, step, feats, rows), lambda i: (0, i, 0, 0)),
            pl.BlockSpec((step, rows, width), lambda i: (i, 0, 0)),
            whole(weight),
            whole(gain),
            whole(shift),
        ],
        [
            pl.BlockSpec((total, width), lambda i: (0, 0)),
            pl.BlockSpec((total, 1), lambda i: (0, 0)),
            pl.BlockSpec((2, width), lambda i: (0, 0)),
        ],
        [
            shape((total, width), LOW),
            shape((total, 1), jnp.float32),
            shape((2, width), jnp.float32),
        ],
        (grads, gathered, weight, gain, shift),
        scratch=[pltpu.VMEM((total, width), jnp.float32), pltpu.VMEM((total, 1), jnp.float32)],
    )


def input_part_kernel(count, place_ref, *refs):
    part_refs, (weight_ref,), out_refs, (total,) = take(refs, count, 1, count)
    step = pl.program_id(0)
    rows = part_refs[0].shape[3]
    parts = [turned(ref[0].reshape(-1, rows)).astype(LOW) for ref in part_refs]
    added = dot(jnp.concatenate(parts, axis=0), weight_ref[...])

    @pl.when(step == 0)
    def _():
        total[...] = added

    @pl.when(step > 0)
    def _():
        total[...] += added

    @pl.when(step == pl.num_programs(0) - 1)
    def _():
        spread(total, out_refs)


def input_parts(place, chips, parts, weights, step=8):
    count, places, feats, rows = parts.shape
    width = weights.shape[1]

    def of(steps):
        return lambda i, place: (lax.rem(place[3] + steps, count), i, 0, 0)

    return feed_run(
        partial(input_part_kernel, count),
        (places // step, 1),
        place,
        [pl.BlockSpec((1, step, feats, rows), of(steps)) for steps in range(count)]
        + [pl.BlockSpec((step * feats, width), own_map(lambda i: (i, 0)))],
        [pl.BlockSpec((rows, width), own_map(lambda i: (0, 0)))] * count,
        [shape((rows, width), LOW)] * count,
        (*[parts] * count, weights),
        [pltpu.VMEM((count * rows, width), jnp.float32)],
        32,
    )


def input_kernel(count, *refs):
    part_refs, (tokens_ref, gain_ref, d_resid_ref, out_ref) = take(refs, count)
    d_one = sum(ref[...].astype(jnp.float32) for ref in part_refs)
    normed, scale = norm_parts(tokens_ref[...].astype(jnp.float32))
    out_ref[...] = d_resid_ref[...] + norm_back(d_one, normed, scale, gain_ref[...])


def input_back(parts, tokens, gain, d_resid):
    operands = (*parts, tokens, gain, d_resid)
    return run(
        partial(input_kernel, len(parts)),
        (1,),
        [whole(item) for item in operands],
        [whole(d_resid)],
        [shape(d_resid.shape, jnp.float32)],
        operands,
    )[0]


ITEM = "z"
HEAD = ("x", "y", "c")
CORE = "c"


def moved(value, axis, steps):
    count = lax.axis_size(axis)
    return lax.ppermute(value, axis, [(place, (place + steps) % count) for place in range(count)])


def shifted(value, axis, steps):
    count = lax.axis_size(axis)
    initial, last = (max(0, -steps), min(count, count - steps))
    return lax.ppermute(value, axis, [(source, source + steps) for source in range(initial, last)])


def all_sum(value, axes):
    for axis in axes:
        if lax.axis_size(axis) == 4:
            terms = around(value, axis)
            value = (terms[0] + terms[2]) + (terms[1] + terms[3])
            continue
        step = 1
        while step < lax.axis_size(axis):
            pairs = [(place, place ^ step) for place in range(lax.axis_size(axis))]
            value = value + lax.ppermute(value, axis, pairs)
            step *= 2
    return value


def around(value, axis):
    return [value] + [moved(value, axis, -step) for step in range(1, lax.axis_size(axis))]


def sum_back(values, axis):
    return [values[0]] + [
        moved(values[step], axis, step) for step in range(1, lax.axis_size(axis))
    ]


def item_terms(value):
    count = lax.axis_size(ITEM)
    place = lax.axis_index(ITEM)
    parts = value.reshape(count, -1, value.shape[1])
    own = [
        lax.dynamic_index_in_dim(parts, (place + step) % count, 0, keepdims=False)
        for step in range(count)
    ]
    return sum_back(own, ITEM)


def item_sum(terms):
    count = lax.axis_size(ITEM)
    place = lax.axis_index(ITEM)
    block = sum(term.astype(jnp.float32) for term in terms).astype(LOW)
    blocks = around(block, ITEM)
    rows = lax.dynamic_slice_in_dim(
        jnp.stack(blocks + blocks), (count - place) % count, count, 0
    )
    return rows.reshape(-1, block.shape[1]).astype(jnp.float32)


def head_swap(value):
    return lax.all_to_all(value, HEAD, split_axis=0, concat_axis=0, tiled=True)


def segment_flags(seg_counts):
    total_segs = seg_counts.shape[0]
    openings = jnp.cumsum(seg_counts) - seg_counts
    places = jnp.arange(total_segs, dtype=jnp.int32)
    opens_here = jnp.any((openings[:, None] == places[None, :]) & (seg_counts[:, None] > 0), axis=0)
    opens_before = jnp.concatenate([jnp.ones((1,), dtype=bool), opens_here[:-1]])
    one_back = jnp.logical_not(opens_here)
    two_back = one_back & jnp.logical_not(opens_before)
    return (one_back, two_back)


def local(
    tokens,
    cotangent,
    seg_counts,
    query_weight,
    key_weight,
    value_weight,
    query_bias,
    value_bias,
    out_weight,
    out_bias,
    first_gain,
    first_shift,
    second_gain,
    second_shift,
    up_weight,
    up_bias,
    down_weight,
    down_bias,
):
    rows, width = tokens.shape
    heads = lax.axis_size(HEAD)
    item_place = lax.axis_index(ITEM)
    group_rows = rows * heads
    seg_local = group_rows // SEG
    feats = query_weight.shape[0]
    units = up_weight.shape[0]
    hidden_here = units * heads

    def row(vector):
        return vector.reshape(1, -1)

    tokens_f = tokens.astype(jnp.float32)
    inputs_one = layer_norm(tokens_f, first_gain, first_shift).astype(LOW)
    first = jnp.concatenate([inputs_one, out_weight], axis=0)
    gathered = lax.all_gather(first, HEAD, axis=0, tiled=True).reshape(heads, -1, width)
    second = jnp.concatenate([up_weight, down_weight], axis=0)
    feed_weights = lax.all_gather(second, HEAD, axis=0, tiled=True).reshape(heads, -1, width)
    cots = around(cotangent, ITEM)
    joint_weight = jnp.concatenate([query_weight, key_weight, value_weight], axis=0)
    joint_bias = jnp.concatenate([query_bias, jnp.zeros_like(query_bias), value_bias])

    one_back, two_back = segment_flags(seg_counts)
    flags = jnp.stack([two_back, one_back], axis=1).astype(jnp.int32)
    flags = lax.dynamic_slice_in_dim(flags, item_place * seg_local, seg_local).reshape(-1)

    gathered, cots = lax.optimization_barrier((gathered, cots))
    query, kv, turned_all = project(gathered, rows, joint_weight, row(joint_bias))
    own_kept = kv.reshape(seg_local, SEG, 2 * HD)[:, SEG - KEPT :]
    table = jnp.concatenate([shifted(own_kept, ITEM, 1), own_kept], axis=0)
    prefix = jnp.concatenate(
        [table[seg_local - 2 : 2 * seg_local - 2], table[seg_local - 1 : 2 * seg_local - 1]], axis=1
    )
    attended, log_sums = attend(flags, turned_all, kv, prefix, rows)
    attended_own = head_swap(attended)
    attended_other = moved(attended_own, CORE, 1)
    resid, inputs_two = out_project(
        attended_own, gathered, rows // feats, tokens, row(out_bias), row(second_gain), row(second_shift)
    )

    share = feats // lax.axis_size(ITEM)
    joint_share = jnp.concatenate(
        [
            lax.dynamic_slice_in_dim(weight, item_place * share, share)
            for weight in (query_weight, key_weight, value_weight)
        ],
        axis=0,
    )
    joint_turn = lax.optimization_barrier((joint_share, resid))[0]
    joint_rows = lax.all_gather(joint_turn, HEAD, axis=0, tiled=True)
    norms = around(inputs_two, ITEM)
    chips = (lax.axis_size("x"), lax.axis_size("y"))
    place = jnp.stack([lax.axis_index(axis) for axis in (CORE, "x", "y", ITEM)]).astype(jnp.int32)
    d_act, cots = feed_d_act(place, chips, cots, feed_weights)
    cots = [cots, moved(cots, CORE, 1)]
    bias_here = lax.dynamic_slice_in_dim(up_bias, item_place * hidden_here, hidden_here)
    backs, (norms, kept, sent, up_bias_part) = feed(
        place, chips, norms, feed_weights, bias_here.reshape(heads, 1, units), d_act
    )
    backs = sum_back(backs, ITEM)
    norms = [norms, moved(norms, CORE, 1)]
    mixeds, feed_parts = feed_grad(
        place, chips, len(backs), norms, cots, kept, sent, moved(sent, CORE, 1), feed_weights
    )
    backs, mixeds = lax.optimization_barrier((backs, mixeds))
    mixeds = sum_back(mixeds, ITEM)
    d_resid, d_branch, sums_two, d_parts = branch_back(
        resid, cotangent, row(second_gain), gathered, rows // feats, feats, backs
    )
    d_attended = head_swap(d_parts)
    feed_parts = lax.optimization_barrier((feed_parts, d_resid))[0]
    feed_grads = lax.psum_scatter(
        feed_parts.reshape(-1, width), ("x", "y"), scatter_dimension=0, tiled=True
    )

    outs = branch_grad(
        place, chips, attended_own, attended_other, d_branch, moved(d_branch, CORE, 1)
    )
    d_attended, outs, mixeds = lax.optimization_barrier((d_attended, outs, mixeds))
    outs = sum_back(outs, "x")

    d_prefix = prefix_back(
        flags, turned_all, query, d_attended, attended, log_sums, prefix, rows
    )[0]
    older, newer = d_prefix[:, :KEPT], d_prefix[:, KEPT:]
    spread = jnp.pad(older, ((seg_local - 2, 2), (0, 0), (0, 0)))
    spread = spread + jnp.pad(newer, ((seg_local - 1, 1), (0, 0), (0, 0)))
    returned = shifted(spread[:seg_local], ITEM, -1)
    items = lax.axis_size(ITEM)
    joint_grads, kept_grads = attend_back(
        flags, turned_all, query, d_attended, attended, log_sums, prefix, kv, rows, items
    )
    returned, kept_grads, joint_rows = lax.optimization_barrier((returned, kept_grads, joint_rows))
    joint_grads = add_returned(joint_grads, kept_grads, spread[seg_local:] + returned)
    grads_own = lax.all_to_all(
        joint_grads.reshape(items * heads, -1, rows),
        (ITEM, *HEAD),
        split_axis=0,
        concat_axis=0,
        tiled=True,
    ).reshape(joint_grads.shape)
    joint_part, bias_part, sums_one = joint_grad(
        joint_grads, gathered, joint_weight, row(first_gain), row(first_shift)
    )
    outs, joint_part, sums_one = lax.optimization_barrier((outs, joint_part, sums_one))
    out_part = lax.optimization_barrier(sum(out.astype(jnp.float32) for out in outs).astype(LOW))
    joint_sums = item_sum(item_terms(joint_part))
    small = [up_bias_part.reshape(-1), sums_two.reshape(-1), sums_one.reshape(-1)]
    small = all_sum(jnp.concatenate(small).reshape(-1, 128), (CORE, "y", "x"))
    out_part = sum_back([out_part[step] for step in range(lax.axis_size("y"))], "y")
    out_part = sum(out.astype(jnp.float32) for out in out_part).astype(LOW)
    grads_own, out_part, small, joint_sums = lax.optimization_barrier(
        (grads_own, out_part, small, joint_sums)
    )
    parts = input_parts(place, chips, grads_own, joint_rows)
    parts, small, out_part = lax.optimization_barrier((parts, small, out_part))
    parts = sum_back(parts, ITEM)
    outs = [out.astype(jnp.float32) for out in around(out_part, ITEM)]
    out_sum = (outs[0] + outs[2]) + (outs[1] + outs[3])
    input_grad = input_back(parts, tokens, row(first_gain), d_resid)
    input_grad, feed_grads = lax.optimization_barrier((input_grad, feed_grads))
    feed_grads = feed_grads.astype(jnp.float32)
    mixed = sum(part.astype(jnp.float32) for part in mixeds)
    mixed_out = (resid + mixed + down_bias).astype(LOW)
    small = small.reshape(-1)
    up_bias_sums, small = small[:hidden_here], small[hidden_here:]
    up_bias_sums = lax.dynamic_update_slice_in_dim(
        jnp.zeros(up_bias.shape, jnp.float32), up_bias_sums, item_place * hidden_here, 0
    )
    small = jnp.concatenate([up_bias_sums, small, bias_part.reshape(-1)])
    small = all_sum(jnp.pad(small, (0, -small.size % 128)).reshape(-1, 128), (ITEM,)).reshape(-1)
    up_bias_grad, small = small[: up_bias.size], small[up_bias.size :]
    early_rows, late = small[: 4 * width].reshape(4, width), small[4 * width : 6 * width]
    late = late.reshape(2, width)
    bias_sums = small[6 * width : 6 * width + 3 * feats]
    return (
        mixed_out,
        input_grad,
        joint_sums[:feats],
        joint_sums[feats : 2 * feats],
        joint_sums[2 * feats :],
        bias_sums[:feats],
        bias_sums[2 * feats :],
        out_sum,
        early_rows[2],
        late[0],
        late[1],
        early_rows[0],
        early_rows[1],
        feed_grads[:units],
        up_bias_grad,
        feed_grads[units:],
        early_rows[3],
    )


def solution(mesh):
    sizes = (mesh.shape["item"], 4, mesh.shape["head"] // 8, 2)
    fine = Mesh(mesh.devices.reshape(sizes), (ITEM, *HEAD))
    split = P((ITEM, *HEAD), None)
    by_head = P(HEAD, None)
    return jax.shard_map(
        local,
        mesh=fine,
        in_specs=(
            split,
            split,
            P(),
            by_head,
            by_head,
            by_head,
            P(HEAD),
            P(HEAD),
            by_head,
            P(),
            P(),
            P(),
            P(),
            P(),
            split,
            P(),
            split,
            P(),
        ),
        out_specs=(
            split,
            split,
            by_head,
            by_head,
            by_head,
            P(HEAD),
            P(HEAD),
            by_head,
            P(),
            P(),
            P(),
            P(),
            P(),
            split,
            P(),
            split,
            P(),
        ),
        check_vma=False,
    )
```

```python
from functools import partial

import jax
import jax.numpy as jnp
from jax import lax
from jax.experimental import pallas as pl
from jax.experimental.pallas import tpu as pltpu
from jax.sharding import Mesh
from jax.sharding import PartitionSpec as P

HD = 64
NSUM = 50
SEG = 2048
SPAN = 512
KEPT = 64
EPSILON = 1e-05
MASKED = -1e30
SCALE = HD ** (-0.5)
MIB = 1 << 20
COST = 1 << 20
LOW = jnp.bfloat16


def dot(left, right):
    return jnp.dot(left, right, preferred_element_type=jnp.float32)


def dot_cols(left, right):
    return lax.dot_general(
        left, right, (((1,), (1,)), ((), ())), preferred_element_type=jnp.float32
    )


def turned(value):
    return value.astype(jnp.float32).T


def norm_parts(row_data):
    row_mean = jnp.mean(row_data, axis=-1, keepdims=True)
    centred = row_data - row_mean
    row_var = jnp.mean(centred * centred, axis=-1, keepdims=True)
    scale = lax.rsqrt(row_var + EPSILON)
    return centred * scale, scale


def norm_back(grad, normed, scale, gain):
    scaled = grad * gain
    return scale * (
        scaled
        - jnp.mean(scaled, axis=-1, keepdims=True)
        - normed * jnp.mean(scaled * normed, axis=-1, keepdims=True)
    )


def layer_norm(row_data, gain, shift):
    return norm_parts(row_data)[0] * gain + shift


def run(body, grid, in_specs, out_specs, out_shape, operands, scratch=(), vmem=32, aliases=None):
    return pl.pallas_call(
        body,
        grid=grid,
        in_specs=in_specs,
        out_specs=out_specs,
        out_shape=out_shape,
        scratch_shapes=scratch,
        compiler_params=pltpu.CompilerParams(
            dimension_semantics=("arbitrary",) * len(grid), vmem_limit_bytes=vmem * MIB
        ),
        input_output_aliases=aliases or {},
        cost_estimate=pl.CostEstimate(flops=COST, bytes_accessed=COST, transcendentals=0),
    )(*operands)


def shape(dims, kind):
    return jax.ShapeDtypeStruct(dims, kind)


def whole(item):
    return pl.BlockSpec(item.shape, lambda *_: (0,) * len(item.shape))


def project_kernel(rows_ref, weight_ref, bias_ref, query_ref, kv_ref, turned_ref):
    rows = rows_ref[...].reshape(SPAN, rows_ref.shape[2])
    joint = dot_cols(rows, weight_ref[...]) + bias_ref[...]
    query_ref[...] = joint[:, :HD].astype(LOW)
    kv_ref[...] = joint[:, HD:].astype(LOW)
    turned_ref[...] = joint.T.astype(LOW)


def project(gathered, rows_here, weight, bias):
    places, _, width = gathered.shape
    total = places * rows_here
    step = SPAN // rows_here
    return run(
        project_kernel,
        (total // SPAN,),
        [
            pl.BlockSpec((step, rows_here, width), lambda i: (i, 0, 0)),
            whole(weight),
            whole(bias),
        ],
        [
            pl.BlockSpec((SPAN, HD), lambda i: (i, 0)),
            pl.BlockSpec((SPAN, 2 * HD), lambda i: (i, 0)),
            pl.BlockSpec((3 * HD, SPAN), lambda i: (0, i)),
        ],
        [
            shape((total, HD), LOW),
            shape((total, 2 * HD), LOW),
            shape((3 * HD, total), LOW),
        ],
        (gathered, weight, bias),
    )


def prefix_seen(flags_ref, seg, columns):
    place = lax.broadcasted_iota(jnp.int32, (2 * KEPT, columns), 0)
    older = place < KEPT
    slot = jnp.where(older, place, place - KEPT) >= KEPT - NSUM
    flag = jnp.where(older, flags_ref[2 * seg], flags_ref[2 * seg + 1])
    return slot & (flag > 0)


def causal_seen():
    shape_here = (SPAN, SPAN)
    return lax.broadcasted_iota(jnp.int32, shape_here, 0) <= lax.broadcasted_iota(
        jnp.int32, shape_here, 1
    )


def above(block):
    return jnp.concatenate([block, jnp.zeros_like(block)], axis=0)


def below(block):
    return jnp.concatenate([jnp.zeros_like(block), block], axis=0)


def at_block(index):
    return pl.ds(pl.multiple_of(index * SPAN, SPAN), SPAN)


def attend_kernel(flags_ref, query_ref, turned_ref, kv_ref, prefix_ref, out_ref, log_ref):
    seg, block = pl.program_id(0), pl.program_id(1)
    query = above((query_ref[...].astype(jnp.float32) * SCALE).astype(LOW))
    own = at_block(block)
    scores = dot(kv_ref[own, :], query)
    scores = jnp.where(causal_seen(), scores, MASKED)
    top = jnp.max(scores, axis=0, keepdims=True)
    probs = jnp.exp(scores - top)
    total = jnp.sum(probs, axis=0, keepdims=True)
    mixed = dot(turned_ref[2 * HD :, own], probs.astype(LOW))

    def add(carry, scores, values):
        top, total, mixed = carry
        fresh = jnp.maximum(top, jnp.max(scores, axis=0, keepdims=True))
        fade = jnp.exp(top - fresh)
        probs = jnp.exp(scores - fresh)
        total = total * fade + jnp.sum(probs, axis=0, keepdims=True)
        return fresh, total, mixed * fade + dot(values, probs.astype(LOW))

    prefix = prefix_ref[0]
    scores = jnp.where(prefix_seen(flags_ref, seg, SPAN), dot(prefix, query), MASKED)
    carry = add((top, total, mixed), scores, turned(prefix)[HD:].astype(LOW))

    def step(index, carry):
        here = at_block(index)
        return add(carry, dot(kv_ref[here, :], query), turned_ref[2 * HD :, here])

    top, total, mixed = lax.fori_loop(0, block, step, carry)
    mixed = (mixed / total).astype(LOW)
    rows = out_ref.shape[2]
    for piece in range(SPAN // rows):
        out_ref[piece] = mixed[:, piece * rows : (piece + 1) * rows]
    log_ref[0] = top + jnp.log(total)


def attend(flags, turned_all, kv, prefix, rows_here):
    total = kv.shape[0]
    blocks = SEG // SPAN
    step = SPAN // rows_here
    return run(
        attend_kernel,
        (total // SEG, blocks),
        [
            pl.BlockSpec(memory_space=pltpu.SMEM),
            pl.BlockSpec((HD, SPAN), lambda s, i: (0, s * blocks + i)),
            pl.BlockSpec((3 * HD, SEG), lambda s, i: (0, s)),
            pl.BlockSpec((SEG, 2 * HD), lambda s, i: (s, 0)),
            pl.BlockSpec((1, 2 * KEPT, 2 * HD), lambda s, i: (s, 0, 0)),
        ],
        [
            pl.BlockSpec((step, HD, rows_here), lambda s, i: (s * blocks + i, 0, 0)),
            pl.BlockSpec((1, 1, SPAN), lambda s, i: (s * blocks + i, 0, 0)),
        ],
        [
            shape((total // rows_here, HD, rows_here), LOW),
            shape((total // SPAN, 1, SPAN), jnp.float32),
        ],
        (flags, turned_all, turned_all, kv, prefix),
    )


def side_by_side(ref):
    return jnp.concatenate([ref[piece] for piece in range(ref.shape[0])], axis=1)


def beside(block, place):
    zero = jnp.zeros_like(block)
    return jnp.concatenate([block, zero] if place == 0 else [zero, block], axis=1)


def query_side(query_ref, rows_ref, grad_ref, out_ref, log_ref):
    query = above((query_ref[...].astype(jnp.float32) * SCALE).astype(LOW))
    grad = side_by_side(grad_ref)
    mean = jnp.sum(
        grad.astype(jnp.float32) * side_by_side(out_ref).astype(jnp.float32),
        axis=0,
        keepdims=True,
    )
    query_rows = beside((rows_ref[...].astype(jnp.float32) * SCALE).astype(LOW), 0)
    grad_rows = beside(turned(grad).astype(LOW), 1)
    return query, below(grad), mean, log_ref[0], query_rows, grad_rows


def key_side(keys, side, seen):
    query, grad, mean, log_sum, query_rows, grad_rows = side
    probs = jnp.exp(dot(keys, query) - log_sum)
    if seen is not None:
        probs = jnp.where(seen, probs, 0.0)
    d_scores = (probs * (dot(keys, grad) - mean)).astype(LOW)
    return probs.astype(LOW), d_scores


def prefix_back_kernel(
    flags_ref, query_ref, rows_ref, grad_ref, out_ref, log_ref, prefix_ref, sum_ref
):
    seg, block = pl.program_id(0), pl.program_id(1)
    side = query_side(query_ref, rows_ref, grad_ref, out_ref, log_ref)
    probs, d_scores = key_side(prefix_ref[0], side, prefix_seen(flags_ref, seg, SPAN))
    part = dot(d_scores, side[4]) + dot(probs, side[5])

    @pl.when(block == 0)
    def _():
        sum_ref[0] = part

    @pl.when(block > 0)
    def _():
        sum_ref[0] += part


def store_shares(grads_ref, piece, part, columns):
    here = HD // grads_ref.shape[0]
    for share in range(grads_ref.shape[0]):
        for kind in (1, 2):
            first = (kind - 1) * HD + share * here
            grads_ref[share, piece, kind * here : (kind + 1) * here, columns] = part[
                first : first + here
            ]


def attend_back_kernel(
    flags_ref,
    query_ref,
    rows_ref,
    grad_ref,
    out_ref,
    log_ref,
    prefix_ref,
    turned_ref,
    kv_ref,
    grads_ref,
    kept_ref,
    kv_grad,
):
    seg, block = pl.program_id(0), pl.program_id(1)

    @pl.when(block == 0)
    def _():
        kv_grad[...] = jnp.zeros_like(kv_grad)

    side = query_side(query_ref, rows_ref, grad_ref, out_ref, log_ref)
    prefix = prefix_ref[0]
    _, d_scores = key_side(prefix, side, prefix_seen(flags_ref, seg, SPAN))
    query_grad = dot(turned(prefix)[:HD].astype(LOW), d_scores)

    def add(here, query_grad, seen):
        probs, d_scores = key_side(kv_ref[here, :], side, seen)
        kv_grad[here, :] += dot(d_scores, side[4]) + dot(probs, side[5])
        return query_grad + dot(turned_ref[HD : 2 * HD, here], d_scores)

    query_grad = add(at_block(block), query_grad, causal_seen())
    query_grad = lax.fori_loop(
        0, block, lambda index, grad: add(at_block(index), grad, None), query_grad
    )
    query_grad = (query_grad * SCALE).astype(LOW)
    rows = grads_ref.shape[3]
    step = SPAN // rows
    for piece in range(step):
        part = query_grad[:, piece * rows : (piece + 1) * rows]
        for share in range(grads_ref.shape[0]):
            here = HD // grads_ref.shape[0]
            grads_ref[share, block * step + piece, :here, :] = part[share * here : (share + 1) * here]

    @pl.when(block == pl.num_programs(1) - 1)
    def _():
        for piece in range(SEG // rows):
            part = kv_grad[piece * rows : (piece + 1) * rows, :].T.astype(LOW)
            store_shares(grads_ref, piece, part, slice(None))
        kept_ref[0] = kv_grad[SEG - KEPT :, :]


def attend_back_specs(rows_here):
    blocks = SEG // SPAN
    step = SPAN // rows_here
    return [
        pl.BlockSpec(memory_space=pltpu.SMEM),
        pl.BlockSpec((HD, SPAN), lambda s, i: (0, s * blocks + i)),
        pl.BlockSpec((SPAN, HD), lambda s, i: (s * blocks + i, 0)),
        pl.BlockSpec((step, HD, rows_here), lambda s, i: (s * blocks + i, 0, 0)),
        pl.BlockSpec((step, HD, rows_here), lambda s, i: (s * blocks + i, 0, 0)),
        pl.BlockSpec((1, 1, SPAN), lambda s, i: (s * blocks + i, 0, 0)),
        pl.BlockSpec((1, 2 * KEPT, 2 * HD), lambda s, i: (s, 0, 0)),
    ]


def prefix_back(flags, turned_all, query, grad, out, log_sums, prefix, rows_here):
    total = query.shape[0]
    return run(
        prefix_back_kernel,
        (total // SEG, SEG // SPAN),
        attend_back_specs(rows_here),
        [pl.BlockSpec((1, 2 * KEPT, 2 * HD), lambda s, i: (s, 0, 0))],
        [shape(prefix.shape, jnp.float32)],
        (flags, turned_all, query, grad, out, log_sums, prefix),
    )


def attend_back(flags, turned_all, query, grad, out, log_sums, prefix, kv, rows_here, count):
    total = query.shape[0]
    pieces = SEG // rows_here
    return run(
        attend_back_kernel,
        (total // SEG, SEG // SPAN),
        attend_back_specs(rows_here)
        + [
            pl.BlockSpec((3 * HD, SEG), lambda s, i: (0, s)),
            pl.BlockSpec((SEG, 2 * HD), lambda s, i: (s, 0)),
        ],
        [
            pl.BlockSpec(
                (count, pieces, 3 * HD // count, rows_here), lambda s, i: (0, s, 0, 0)
            ),
            pl.BlockSpec((1, KEPT, 2 * HD), lambda s, i: (s, 0, 0)),
        ],
        [
            shape((count, total // rows_here, 3 * HD // count, rows_here), LOW),
            shape((total // SEG, KEPT, 2 * HD), jnp.float32),
        ],
        (flags, turned_all, query, grad, out, log_sums, prefix, turned_all, kv),
        scratch=[pltpu.VMEM((SEG, 2 * HD), jnp.float32)],
    )


def returned_kernel(grads_ref, kept_ref, returned_ref, out_ref):
    out_ref[...] = grads_ref[...]
    part = (kept_ref[0] + returned_ref[0]).T.astype(LOW)
    store_shares(out_ref, 0, part, slice(out_ref.shape[3] - KEPT, None))


def add_returned(grads, kept, returned):
    count, places, feats, rows = grads.shape
    segs = kept.shape[0]
    last = places // segs
    grad_spec = pl.BlockSpec((count, 1, feats, rows), lambda s: (0, s * last + last - 1, 0, 0))
    kept_spec = pl.BlockSpec((1, KEPT, 2 * HD), lambda s: (s, 0, 0))
    return run(
        returned_kernel,
        (segs,),
        [grad_spec, kept_spec, kept_spec],
        [grad_spec],
        [shape(grads.shape, LOW)],
        (grads, kept, returned),
        aliases={0: 0},
    )[0]


def out_kernel(
    part_ref, weight_ref, tokens_ref, bias_ref, gain_ref, shift_ref, resid_ref, two_ref, total
):
    step = pl.program_id(0)
    rows = part_ref.shape[2]
    part = turned(part_ref[...].reshape(-1, rows)).astype(LOW)
    added = dot(part, weight_ref[...].reshape(part.shape[1], -1))

    @pl.when(step == 0)
    def _():
        total[...] = added

    @pl.when(step > 0)
    def _():
        total[...] += added

    @pl.when(step == pl.num_programs(0) - 1)
    def _():
        resid = tokens_ref[...].astype(jnp.float32) + total[...] + bias_ref[...]
        resid_ref[...] = resid
        two_ref[...] = layer_norm(resid, gain_ref[...], shift_ref[...]).astype(LOW)


def out_project(parts, gathered, at, tokens, bias, gain, shift, step=4):
    places, feats, rows = parts.shape
    width = gathered.shape[2]
    return run(
        out_kernel,
        (places // step,),
        [
            pl.BlockSpec((step, feats, rows), lambda i: (i, 0, 0)),
            pl.BlockSpec((step, feats, width), lambda i: (i, at, 0)),
            whole(tokens),
            whole(bias),
            whole(gain),
            whole(shift),
        ],
        [pl.BlockSpec((rows, width), lambda i: (0, 0))] * 2,
        [shape((rows, width), jnp.float32), shape((rows, width), LOW)],
        (parts, gathered, tokens, bias, gain, shift),
        scratch=[pltpu.VMEM((rows, width), jnp.float32)],
    )


def owner_maps(chips, at):
    def of(core_step, chip):
        return lambda i, place: at((i * chips[1] + chip) * 2 + lax.rem(place[0] + core_step, 2))

    return [of(core_step, chip) for core_step in (0, 1) for chip in range(chips[1])]


def step_maps(chips, at):
    chips_x, chips_y = chips

    def of(x_step):
        def index(i, place):
            x = lax.rem(place[1] + x_step, chips_x)
            y = lax.rem(place[2] + i, chips_y)
            return at((x * chips_y + y) * 2 + place[0])

        return index

    return [of(x_step) for x_step in range(chips_x)]


def own_map(index):
    return lambda i, place: index(i)


def fixed(dims):
    return pl.BlockSpec(
        dims, own_map(lambda i: (0,) * len(dims)), pipeline_mode=pl.Buffered(buffer_count=1)
    )


def feed_run(body, chips, place, in_specs, out_specs, out_shape, operands, scratch, vmem):
    return pl.pallas_call(
        body,
        grid_spec=pltpu.PrefetchScalarGridSpec(
            num_scalar_prefetch=1,
            grid=(chips[0],),
            in_specs=in_specs,
            out_specs=out_specs,
            scratch_shapes=scratch,
        ),
        out_shape=out_shape,
        compiler_params=pltpu.CompilerParams(
            dimension_semantics=("arbitrary",), vmem_limit_bytes=vmem * MIB
        ),
        cost_estimate=pl.CostEstimate(flops=COST, bytes_accessed=COST, transcendentals=0),
    )(place, *operands)


def stacked(refs, axis=0):
    return jnp.concatenate([ref[0] for ref in refs], axis=axis)


def pile(refs, into):
    rows = refs[0].shape[0]
    for at, ref in enumerate(refs):
        into[at * rows : (at + 1) * rows, :] = ref[...]


def spread(source, refs):
    rows = refs[0].shape[0]
    for at, ref in enumerate(refs):
        ref[...] = source[at * rows : (at + 1) * rows, :].astype(ref.dtype)


def take(refs, *counts):
    refs = list(refs)
    return [[refs.pop(0) for _ in range(count)] for count in counts] + [refs]


def d_act_kernel(count, owners, place_ref, *refs):
    cot_refs, weight_refs, (out_ref, cots) = take(refs, count, owners)

    @pl.when(pl.program_id(0) == 0)
    def _():
        pile(cot_refs, cots)

    out_ref[...] = dot_cols(cots[...], stacked(weight_refs))


def feed_d_act(place, chips, cots, weights):
    count = len(cots)
    rows, width = cots[0].shape
    places, both, _ = weights.shape
    units = both // 2
    total = count * rows
    owners = 2 * chips[1]
    step = owners * units
    return feed_run(
        partial(d_act_kernel, count, owners),
        chips,
        place,
        [fixed((rows, width))] * count
        + [
            pl.BlockSpec((1, units, width), at)
            for at in owner_maps(chips, lambda owner: (owner, 1, 0))
        ],
        [pl.BlockSpec((total, step), own_map(lambda i: (0, i))), fixed((total, width))],
        [shape((total, places * units), jnp.float32), shape((total, width), LOW)],
        (*cots, *[weights] * owners),
        [],
        32,
    )


def feed_kernel(count, chips, place_ref, *refs):
    owners = 2 * chips[1]
    norm_refs, weight_refs, bias_refs, (d_act_ref,), back_refs, refs = take(
        refs, count, owners, owners, 1, count
    )
    norms, kept_ref, sent_ref, bias_sum_ref, back = refs
    step = pl.program_id(0)

    @pl.when(step == 0)
    def _():
        pile(norm_refs, norms)
        back[...] = jnp.zeros_like(back)

    up = stacked(weight_refs)
    pre = dot_cols(norms[...], up) + stacked(bias_refs, axis=1)
    square = pre * pre
    bent = jnp.tanh(0.7978845608 * (pre + 0.044715 * (square * pre)))
    half = 0.5 * (1.0 + bent)
    slope = half + 0.5 * pre * (1.0 - bent * bent) * (
        0.7978845608 * (1.0 + 3.0 * 0.044715 * square)
    )
    d_pre = (d_act_ref[...] * slope).astype(LOW)
    act = (pre * half).astype(LOW)
    own = act.shape[1] // 2
    kept_ref[0] = act[:, :own]
    kept_ref[1] = d_pre[:, :own]
    sent_ref[0] = act[:, own:]
    sent_ref[1] = d_pre[:, own:]
    bias_sums = jnp.sum(d_pre.astype(jnp.float32), axis=0, keepdims=True)
    units = weight_refs[0].shape[1]
    for at, index in enumerate(owner_maps(chips, lambda owner: owner)):
        bias_sum_ref[index(step, place_ref)] = bias_sums[:, at * units : (at + 1) * units]
    back[...] += dot(d_pre, up)

    @pl.when(step == pl.num_programs(0) - 1)
    def _():
        spread(back, back_refs)


def feed(place, chips, norms, weights, bias, d_act):
    count = len(norms)
    rows, width = norms[0].shape
    places, both, _ = weights.shape
    units = both // 2
    total = count * rows
    owners = 2 * chips[1]
    step = owners * units
    pair_spec = pl.BlockSpec((2, total, step // 2), own_map(lambda i: (0, 0, i)))
    results = feed_run(
        partial(feed_kernel, count, chips),
        chips,
        place,
        [fixed((rows, width))] * count
        + [
            pl.BlockSpec((1, units, width), at)
            for at in owner_maps(chips, lambda owner: (owner, 0, 0))
        ]
        + [
            pl.BlockSpec((1, 1, units), at)
            for at in owner_maps(chips, lambda owner: (owner, 0, 0))
        ]
        + [pl.BlockSpec((total, step), own_map(lambda i: (0, i)))],
        [pl.BlockSpec((rows, width), own_map(lambda i: (0, 0)))] * count
        + [fixed((total, width)), pair_spec, pair_spec, fixed((places, 1, units))],
        [shape((rows, width), LOW)] * count
        + [shape((total, width), LOW)]
        + [shape((2, total, places * units // 2), LOW)] * 2
        + [shape((places, 1, units), jnp.float32)],
        (*norms, *[weights] * owners, *[bias] * owners, d_act),
        [pltpu.VMEM((total, width), jnp.float32)],
        40,
    )
    return results[:count], results[count:]


def feed_grad_kernel(count, owners, place_ref, *refs):
    norm_refs, cot_refs, pair_refs, weight_refs, mixed_refs, (out_ref, mixed) = take(
        refs, 2, 2, 3, owners, count
    )
    kept_ref, sent_ref, other_ref = pair_refs
    step = pl.program_id(0)
    units = weight_refs[0].shape[1]

    @pl.when(step == 0)
    def _():
        mixed[...] = jnp.zeros_like(mixed)

    act = jnp.concatenate([kept_ref[0], sent_ref[0]], axis=1)
    mixed[...] += dot(act, stacked(weight_refs))

    def grad(at, rows):
        total = dot(turned(kept_ref[at]).astype(LOW), rows[0][...])
        total += dot(turned(other_ref[at]).astype(LOW), rows[1][...])
        return total.astype(LOW).reshape(out_ref.shape[0], units, -1)

    out_ref[:, :units, :] = grad(1, norm_refs)
    out_ref[:, units:, :] = grad(0, cot_refs)

    @pl.when(step == pl.num_programs(0) - 1)
    def _():
        spread(mixed, mixed_refs)


def feed_grad(place, chips, count, norms, cots, kept, sent, other, weights):
    total, width = norms[0].shape
    rows = total // count
    units = weights.shape[1] // 2
    owners = 2 * chips[1]
    pair_spec = pl.BlockSpec((2, total, owners * units // 2), own_map(lambda i: (0, 0, i)))
    results = feed_run(
        partial(feed_grad_kernel, count, owners),
        chips,
        place,
        [fixed((total, width))] * 4
        + [pair_spec] * 3
        + [
            pl.BlockSpec((1, units, width), at)
            for at in owner_maps(chips, lambda owner: (owner, 1, 0))
        ],
        [pl.BlockSpec((rows, width), own_map(lambda i: (0, 0)))] * count
        + [pl.BlockSpec((chips[1], 2 * units, width), own_map(lambda i: (i, 0, 0)))],
        [shape((rows, width), LOW)] * count
        + [shape((chips[0] * chips[1], 2 * units, width), LOW)],
        (*norms, *cots, kept, sent, other, *[weights] * owners),
        [pltpu.VMEM((total, width), jnp.float32)],
        48,
    )
    return results[:count], results[count]


def branch_kernel(
    count, resid_ref, cot_ref, gain_ref, weight_ref, *refs
):
    back_refs = refs[:count]
    d_resid_ref, d_branch_ref, sums_ref, parts_ref = refs[count:]

    @pl.when(pl.program_id(0) == 0)
    def _():
        d_two = sum(ref[...].astype(jnp.float32) for ref in back_refs)
        normed, scale = norm_parts(resid_ref[...])
        cot = cot_ref[...].astype(jnp.float32)
        d_resid = cot + norm_back(d_two, normed, scale, gain_ref[...])
        d_branch = d_resid.astype(LOW)
        d_resid_ref[...] = d_resid
        d_branch_ref[...] = d_branch
        sums_ref[0:1, :] = jnp.sum(d_two * normed, axis=0, keepdims=True)
        sums_ref[1:2, :] = jnp.sum(d_two, axis=0, keepdims=True)
        sums_ref[2:3, :] = jnp.sum(d_branch.astype(jnp.float32), axis=0, keepdims=True)
        sums_ref[3:4, :] = jnp.sum(cot, axis=0, keepdims=True)

    width = weight_ref.shape[2]
    part = dot_cols(weight_ref[...].reshape(-1, width), d_branch_ref[...])
    parts_ref[...] = part.reshape(parts_ref.shape).astype(LOW)


def branch_back(resid, cotangent, gain, gathered, at, feats, backs, step=4):
    rows, width = resid.shape
    places = gathered.shape[0]
    row_spec = pl.BlockSpec((rows, width), lambda i: (0, 0))
    return run(
        partial(branch_kernel, len(backs)),
        (places // step,),
        [
            row_spec,
            row_spec,
            whole(gain),
            pl.BlockSpec((step, feats, width), lambda i: (i, at, 0)),
        ]
        + [row_spec] * len(backs),
        [
            row_spec,
            row_spec,
            pl.BlockSpec((4, width), lambda i: (0, 0)),
            pl.BlockSpec((step, feats, rows), lambda i: (i, 0, 0)),
        ],
        [
            shape((rows, width), jnp.float32),
            shape((rows, width), LOW),
            shape((4, width), jnp.float32),
            shape((places, feats, rows), LOW),
        ],
        (resid, cotangent, gain, gathered, *backs),
    )


def branch_grad_kernel(owners, place_ref, *refs):
    own_refs, other_refs, grad_refs, out_refs = take(refs, owners, owners, 2)
    parts = jnp.concatenate([stacked(own_refs), stacked(other_refs)], axis=1)
    grads = jnp.concatenate([ref[...] for ref in grad_refs], axis=0)
    out = dot(parts, grads).astype(LOW).reshape(out_refs[0].shape)
    for at, ref in enumerate(out_refs):

        @pl.when(pl.program_id(0) == at)
        def _():
            ref[...] = out


def branch_grad(place, chips, own, other, own_grad, other_grad):
    _, feats, rows = own.shape
    width = own_grad.shape[1]
    chips_x, chips_y = chips
    part_specs = [
        pl.BlockSpec((1, feats, rows), at)
        for at in step_maps(chips, lambda owner: (owner, 0, 0))
    ]
    return feed_run(
        partial(branch_grad_kernel, chips_x),
        (chips_y, chips_x),
        place,
        part_specs * 2 + [fixed((rows, width))] * 2,
        [pl.BlockSpec((chips_x, feats, width), own_map(lambda i: (0, 0, 0)))] * chips_y,
        [shape((chips_x, feats, width), LOW)] * chips_y,
        (*[own] * chips_x, *[other] * chips_x, own_grad, other_grad),
        [],
        32,
    )


def by_kind(rows, count):
    here = HD // count
    return jnp.concatenate(
        [
            rows[(share * 3 + kind) * here : (share * 3 + kind + 1) * here]
            for kind in range(3)
            for share in range(count)
        ],
        axis=0,
    )


def joint_grad_kernel(
    grad_ref, rows_ref, weight_ref, gain_ref, shift_ref, out_ref, bias_ref, sums_ref, total, biases
):
    step = pl.program_id(0)
    count, pieces = grad_ref.shape[:2]
    grads = jnp.concatenate(
        [
            jnp.concatenate([grad_ref[share, piece] for piece in range(pieces)], axis=1)
            for share in range(count)
        ],
        axis=0,
    )
    added = dot(grads, rows_ref[...].reshape(grads.shape[1], -1))
    summed = jnp.sum(grads.astype(jnp.float32), axis=1, keepdims=True)

    @pl.when(step == 0)
    def _():
        total[...] = added
        biases[...] = summed

    @pl.when(step > 0)
    def _():
        total[...] += added
        biases[...] += summed

    @pl.when(step == pl.num_programs(0) - 1)
    def _():
        out = by_kind(total[...], count)
        bias = by_kind(biases[...], count)
        out_ref[...] = out.astype(LOW)
        bias_ref[...] = bias
        weight = weight_ref[...].astype(jnp.float32)
        shift_sum = jnp.sum(weight * bias, axis=0, keepdims=True)
        product = jnp.sum(weight * out, axis=0, keepdims=True)
        sums_ref[0:1, :] = (product - shift_sum * shift_ref[...]) / gain_ref[...]
        sums_ref[1:2, :] = shift_sum


def joint_grad(grads, gathered, weight, gain, shift, step=8):
    count, places, feats, rows = grads.shape
    width = gathered.shape[2]
    total = count * feats
    return run(
        joint_grad_kernel,
        (places // step,),
        [
            pl.BlockSpec((count, step, feats, rows), lambda i: (0, i, 0, 0)),
            pl.BlockSpec((step, rows, width), lambda i: (i, 0, 0)),
            whole(weight),
            whole(gain),
            whole(shift),
        ],
        [
            pl.BlockSpec((total, width), lambda i: (0, 0)),
            pl.BlockSpec((total, 1), lambda i: (0, 0)),
            pl.BlockSpec((2, width), lambda i: (0, 0)),
        ],
        [
            shape((total, width), LOW),
            shape((total, 1), jnp.float32),
            shape((2, width), jnp.float32),
        ],
        (grads, gathered, weight, gain, shift),
        scratch=[pltpu.VMEM((total, width), jnp.float32), pltpu.VMEM((total, 1), jnp.float32)],
    )


def input_part_kernel(count, place_ref, *refs):
    part_refs, (weight_ref, small_ref), out_refs, (total,) = take(refs, count, 2, count)
    step = pl.program_id(0)
    rows = part_refs[0].shape[3]
    parts = [turned(ref[0].reshape(-1, rows)).astype(LOW) for ref in part_refs]
    added = dot(jnp.concatenate(parts, axis=0), weight_ref[...])

    @pl.when(step == 0)
    def _():
        total[...] = added

    @pl.when(step > 0)
    def _():
        total[...] += added

    @pl.when(step == pl.num_programs(0) - 1)
    def _():
        small = small_ref[...]
        rounded = small.astype(LOW)
        rest = (small - rounded.astype(jnp.float32)).astype(LOW)
        both = jnp.concatenate([rounded, rest], axis=0)
        for at, ref in enumerate(out_refs):
            ref[:rows] = total[at * rows : (at + 1) * rows, :].astype(LOW)
            ref[rows:] = both


def input_parts(place, chips, parts, weights, small, step=8):
    count, places, feats, rows = parts.shape
    width = weights.shape[1]
    total = rows + 2 * small.shape[0]

    def of(steps):
        return lambda i, place: (lax.rem(place[3] + steps, count), i, 0, 0)

    return feed_run(
        partial(input_part_kernel, count),
        (places // step, 1),
        place,
        [pl.BlockSpec((1, step, feats, rows), of(steps)) for steps in range(count)]
        + [pl.BlockSpec((step * feats, width), own_map(lambda i: (i, 0))), fixed(small.shape)],
        [pl.BlockSpec((total, width), own_map(lambda i: (0, 0)))] * count,
        [shape((total, width), LOW)] * count,
        (*[parts] * count, weights, small),
        [pltpu.VMEM((count * rows, width), jnp.float32)],
        32,
    )


def input_kernel(*refs):
    part_refs, (tokens_ref, gain_ref, d_resid_ref, out_ref, small_ref) = take(refs, 4)
    rows = tokens_ref.shape[0]
    d_one = sum(ref[:rows].astype(jnp.float32) for ref in part_refs)
    normed, scale = norm_parts(tokens_ref[...].astype(jnp.float32))
    out_ref[...] = d_resid_ref[...] + norm_back(d_one, normed, scale, gain_ref[...])
    half = small_ref.shape[0]
    small = []
    for ref in part_refs:
        both = ref[rows:].astype(jnp.float32)
        small.append(both[:half] + both[half:])
    small_ref[...] = (small[0] + small[2]) + (small[1] + small[3])


def input_back(parts, tokens, gain, d_resid):
    operands = (*parts, tokens, gain, d_resid)
    rows, width = d_resid.shape
    small = shape(((parts[0].shape[0] - rows) // 2, width), jnp.float32)
    return run(
        input_kernel,
        (1,),
        [whole(item) for item in operands],
        [whole(d_resid), whole(small)],
        [shape(d_resid.shape, jnp.float32), small],
        operands,
    )


ITEM = "z"
HEAD = ("x", "y", "c")
CORE = "c"
UNIT = "y"
OWNER = ("z", "x", "c")


def moved(value, axis, steps):
    count = lax.axis_size(axis)
    return lax.ppermute(value, axis, [(place, (place + steps) % count) for place in range(count)])


def shifted(value, axis, steps):
    count = lax.axis_size(axis)
    initial, last = (max(0, -steps), min(count, count - steps))
    return lax.ppermute(value, axis, [(source, source + steps) for source in range(initial, last)])


def swapped(value, axis, step):
    pairs = [(place, place ^ step) for place in range(lax.axis_size(axis))]
    return lax.ppermute(value, axis, pairs)


def all_sum(value, axis):
    terms = around(value, axis)
    return (terms[0] + terms[2]) + (terms[1] + terms[3])


def around(value, axis):
    return [value] + [moved(value, axis, -step) for step in range(1, lax.axis_size(axis))]


def sum_back(values, axis):
    return [values[0]] + [
        moved(values[step], axis, step) for step in range(1, lax.axis_size(axis))
    ]


def own_half(value, bit, axis, step):
    count = value.shape[0] // 2
    own = lax.dynamic_slice_in_dim(value, bit * count, count)
    other = lax.dynamic_slice_in_dim(value, (1 - bit) * count, count)
    own = own.astype(jnp.float32) + swapped(other, axis, step).astype(jnp.float32)
    return own.astype(LOW)


def both_halves(value, bit, axis, step):
    other = swapped(value, axis, step)
    first = jnp.where(bit == 0, value, other)
    return jnp.concatenate([first, jnp.where(bit == 0, other, value)], axis=0)


def pair_sum(value, axis, step):
    value = value.astype(jnp.float32) + swapped(value, axis, step).astype(jnp.float32)
    return value.astype(LOW)


def near_steps(values, axis):
    near = values[:2].astype(jnp.float32) + moved(values[2:], axis, 2).astype(jnp.float32)
    return near.astype(LOW)


def own_step(values, axis):
    own = values[0].astype(jnp.float32) + moved(values[1], axis, 1).astype(jnp.float32)
    return own.astype(LOW)


def head_swap(value):
    return lax.all_to_all(value, HEAD, split_axis=0, concat_axis=0, tiled=True)


def segment_flags(seg_counts):
    total_segs = seg_counts.shape[0]
    openings = jnp.cumsum(seg_counts) - seg_counts
    places = jnp.arange(total_segs, dtype=jnp.int32)
    opens_here = jnp.any((openings[:, None] == places[None, :]) & (seg_counts[:, None] > 0), axis=0)
    opens_before = jnp.concatenate([jnp.ones((1,), dtype=bool), opens_here[:-1]])
    one_back = jnp.logical_not(opens_here)
    two_back = one_back & jnp.logical_not(opens_before)
    return (one_back, two_back)


def local(
    tokens,
    cotangent,
    seg_counts,
    query_weight,
    key_weight,
    value_weight,
    query_bias,
    value_bias,
    out_weight,
    out_bias,
    first_gain,
    first_shift,
    second_gain,
    second_shift,
    up_weight,
    up_bias,
    down_weight,
    down_bias,
):
    rows, width = tokens.shape
    heads = lax.axis_size(HEAD)
    item_place = lax.axis_index(ITEM)
    group_rows = rows * heads
    seg_local = group_rows // SEG
    feats = query_weight.shape[0]
    units = up_weight.shape[0]
    hidden_here = units * heads

    def row(vector):
        return vector.reshape(1, -1)

    tokens_f = tokens.astype(jnp.float32)
    inputs_one = layer_norm(tokens_f, first_gain, first_shift).astype(LOW)
    first = jnp.concatenate([inputs_one, out_weight], axis=0)
    gathered = lax.all_gather(first, HEAD, axis=0, tiled=True).reshape(heads, -1, width)
    second = jnp.concatenate([up_weight, down_weight], axis=0)
    feed_weights = lax.all_gather(second, OWNER, axis=0, tiled=True).reshape(heads, -1, width)
    cots = around(cotangent, UNIT)
    joint_weight = jnp.concatenate([query_weight, key_weight, value_weight], axis=0)
    joint_bias = jnp.concatenate([query_bias, jnp.zeros_like(query_bias), value_bias])

    one_back, two_back = segment_flags(seg_counts)
    flags = jnp.stack([two_back, one_back], axis=1).astype(jnp.int32)
    flags = lax.dynamic_slice_in_dim(flags, item_place * seg_local, seg_local).reshape(-1)

    gathered, cots = lax.optimization_barrier((gathered, cots))
    query, kv, turned_all = project(gathered, rows, joint_weight, row(joint_bias))
    own_kept = kv.reshape(seg_local, SEG, 2 * HD)[:, SEG - KEPT :]
    table = jnp.concatenate([shifted(own_kept, ITEM, 1), own_kept], axis=0)
    prefix = jnp.concatenate(
        [table[seg_local - 2 : 2 * seg_local - 2], table[seg_local - 1 : 2 * seg_local - 1]], axis=1
    )
    attended, log_sums = attend(flags, turned_all, kv, prefix, rows)
    attended_own = head_swap(attended)
    attended_other = moved(attended_own, CORE, 1)
    resid, inputs_two = out_project(
        attended_own, gathered, rows // feats, tokens, row(out_bias), row(second_gain), row(second_shift)
    )

    share = feats // lax.axis_size(ITEM)
    joint_share = jnp.concatenate(
        [
            lax.dynamic_slice_in_dim(weight, item_place * share, share)
            for weight in (query_weight, key_weight, value_weight)
        ],
        axis=0,
    )
    joint_turn = lax.optimization_barrier((joint_share, resid))[0]
    joint_rows = lax.all_gather(joint_turn, HEAD, axis=0, tiled=True)
    norms = around(inputs_two, UNIT)
    sizes = [lax.axis_size(axis) for axis in ("z", "x", "y")]
    chips, owners = (sizes[1], sizes[2]), (sizes[0], sizes[1])
    place = jnp.stack([lax.axis_index(axis) for axis in (CORE, "x", "y", ITEM)]).astype(jnp.int32)
    d_act, cots = feed_d_act(place, owners, cots, feed_weights)
    cots = [cots, moved(cots, CORE, 1)]
    unit_place = lax.axis_index(UNIT)
    bias_here = lax.dynamic_index_in_dim(
        up_bias.reshape(*sizes[:2], sizes[2], -1), unit_place, 2, keepdims=False
    )
    backs, (norms, kept, sent, up_bias_part) = feed(
        place, owners, norms, feed_weights, bias_here.reshape(heads, 1, units), d_act
    )
    backs = sum_back(backs, UNIT)
    norms = [norms, moved(norms, CORE, 1)]
    mixeds, feed_parts = feed_grad(
        place, owners, len(backs), norms, cots, kept, sent, moved(sent, CORE, 1), feed_weights
    )
    backs, mixeds = lax.optimization_barrier((backs, mixeds))
    mixeds = sum_back(mixeds, UNIT)
    d_resid, d_branch, sums_two, d_parts = branch_back(
        resid, cotangent, row(second_gain), gathered, rows // feats, feats, backs
    )
    d_attended = head_swap(d_parts)
    feed_parts = lax.optimization_barrier((feed_parts, d_resid))[0]
    feed_grads = lax.psum_scatter(
        feed_parts.reshape(-1, width), OWNER[:2], scatter_dimension=0, tiled=True
    )

    outs = branch_grad(
        place, chips, attended_own, attended_other, d_branch, moved(d_branch, CORE, 1)
    )
    d_attended, outs, mixeds = lax.optimization_barrier((d_attended, outs, mixeds))
    outs = sum_back(outs, "y")

    d_prefix = prefix_back(
        flags, turned_all, query, d_attended, attended, log_sums, prefix, rows
    )[0]
    older, newer = d_prefix[:, :KEPT], d_prefix[:, KEPT:]
    spread = jnp.pad(older, ((seg_local - 2, 2), (0, 0), (0, 0)))
    spread = spread + jnp.pad(newer, ((seg_local - 1, 1), (0, 0), (0, 0)))
    returned = shifted(spread[:seg_local], ITEM, -1)
    items = lax.axis_size(ITEM)
    joint_grads, kept_grads = attend_back(
        flags, turned_all, query, d_attended, attended, log_sums, prefix, kv, rows, items
    )
    returned, kept_grads, joint_rows = lax.optimization_barrier((returned, kept_grads, joint_rows))
    joint_grads = add_returned(joint_grads, kept_grads, spread[seg_local:] + returned)
    grads_own = lax.all_to_all(
        joint_grads.reshape(items * heads, -1, rows),
        (ITEM, *HEAD),
        split_axis=0,
        concat_axis=0,
        tiled=True,
    ).reshape(joint_grads.shape)
    joint_part, bias_part, sums_one = joint_grad(
        joint_grads, gathered, joint_weight, row(first_gain), row(first_shift)
    )
    high, low = item_place // 2, item_place % 2
    outs, joint_part, sums_one = lax.optimization_barrier((outs, joint_part, sums_one))
    out_part = lax.optimization_barrier(sum(out.astype(jnp.float32) for out in outs).astype(LOW))
    out_part = near_steps(out_part, "x")
    joint_part = own_half(joint_part.reshape(4, -1, width), high, ITEM, 2)
    small = jnp.concatenate([row(up_bias_part), sums_two, sums_one], axis=0)
    small = small + swapped(small, CORE, 1)
    out_part, joint_part, small = lax.optimization_barrier((out_part, joint_part, small))
    out_part = own_step(out_part, "x")
    joint_part = own_half(joint_part, low, ITEM, 1)
    small = all_sum(small, "x")
    bias_part = jnp.pad(row(bias_part), ((0, 0), (0, width - bias_part.size)))
    small = jnp.concatenate([small, bias_part], axis=0)
    grads_own, out_part, joint_part, small = lax.optimization_barrier(
        (grads_own, out_part, joint_part, small)
    )
    parts = input_parts(place, chips, grads_own, joint_rows, small)
    parts, out_part, joint_part = lax.optimization_barrier((parts, out_part, joint_part))
    parts = sum_back(parts, ITEM)
    out_part = pair_sum(out_part, ITEM, 2)
    joint_part = both_halves(joint_part, low, ITEM, 1)
    parts, out_part, joint_part = lax.optimization_barrier((parts, out_part, joint_part))
    out_part = pair_sum(out_part, ITEM, 1)
    joint_part = both_halves(joint_part, high, ITEM, 2)
    input_grad, small = input_back(parts, tokens, row(first_gain), d_resid)
    out_sum = out_part.astype(jnp.float32)
    joint_sums = joint_part.reshape(-1, width).astype(jnp.float32)
    input_grad, feed_grads = lax.optimization_barrier((input_grad, feed_grads))
    feed_grads = feed_grads.astype(jnp.float32)
    mixed = sum(part.astype(jnp.float32) for part in mixeds)
    mixed_out = (resid + mixed + down_bias).astype(LOW)
    bias_sums = small[7, : 3 * feats]
    terms = around(small[:7], UNIT)
    small = (terms[0][1:] + terms[2][1:]) + (terms[1][1:] + terms[3][1:])
    up_bias_grad = jnp.stack([term[0] for term in terms + terms])
    up_bias_grad = lax.dynamic_slice_in_dim(
        up_bias_grad, (sizes[2] - unit_place) % sizes[2], sizes[2], 0
    )
    up_bias_grad = up_bias_grad.reshape(sizes[2], *sizes[:2], -1).transpose(1, 2, 0, 3).reshape(-1)
    early_rows, late = small[:4], small[4:]
    return (
        mixed_out,
        input_grad,
        joint_sums[:feats],
        joint_sums[feats : 2 * feats],
        joint_sums[2 * feats :],
        bias_sums[:feats],
        bias_sums[2 * feats : 3 * feats],
        out_sum,
        early_rows[2],
        late[0],
        late[1],
        early_rows[0],
        early_rows[1],
        feed_grads[:units],
        up_bias_grad,
        feed_grads[units:],
        early_rows[3],
    )


def solution(mesh):
    sizes = (mesh.shape["item"], 4, mesh.shape["head"] // 8, 2)
    fine = Mesh(mesh.devices.reshape(sizes), (ITEM, *HEAD))
    split = P((ITEM, *HEAD), None)
    by_head = P(HEAD, None)
    return jax.shard_map(
        local,
        mesh=fine,
        in_specs=(
            split,
            split,
            P(),
            by_head,
            by_head,
            by_head,
            P(HEAD),
            P(HEAD),
            by_head,
            P(),
            P(),
            P(),
            P(),
            P(),
            split,
            P(),
            split,
            P(),
        ),
        out_specs=(
            split,
            split,
            by_head,
            by_head,
            by_head,
            P(HEAD),
            P(HEAD),
            by_head,
            P(),
            P(),
            P(),
            P(),
            P(),
            split,
            P(),
            split,
            P(),
        ),
        check_vma=False,
    )
```

```python
from functools import partial

import jax
import jax.numpy as jnp
from jax import lax
from jax.experimental import pallas as pl
from jax.experimental.pallas import tpu as pltpu
from jax.sharding import Mesh
from jax.sharding import PartitionSpec as P

HD = 64
NSUM = 50
SEG = 2048
SPAN = 512
KEPT = 64
EPSILON = 1e-05
MASKED = -1e30
SCALE = HD ** (-0.5)
MIB = 1 << 20
COST = 1 << 20
LOW = jnp.bfloat16


def dot(left, right):
    return jnp.dot(left, right, preferred_element_type=jnp.float32)


def dot_cols(left, right):
    return lax.dot_general(
        left, right, (((1,), (1,)), ((), ())), preferred_element_type=jnp.float32
    )


def turned(value):
    return value.astype(jnp.float32).T


def norm_parts(row_data):
    row_mean = jnp.mean(row_data, axis=-1, keepdims=True)
    centred = row_data - row_mean
    row_var = jnp.mean(centred * centred, axis=-1, keepdims=True)
    scale = lax.rsqrt(row_var + EPSILON)
    return centred * scale, scale


def norm_back(grad, normed, scale, gain):
    scaled = grad * gain
    return scale * (
        scaled
        - jnp.mean(scaled, axis=-1, keepdims=True)
        - normed * jnp.mean(scaled * normed, axis=-1, keepdims=True)
    )


def layer_norm(row_data, gain, shift):
    return norm_parts(row_data)[0] * gain + shift


def run(body, grid, in_specs, out_specs, out_shape, operands, scratch=(), vmem=32, aliases=None):
    return pl.pallas_call(
        body,
        grid=grid,
        in_specs=in_specs,
        out_specs=out_specs,
        out_shape=out_shape,
        scratch_shapes=scratch,
        compiler_params=pltpu.CompilerParams(
            dimension_semantics=("arbitrary",) * len(grid), vmem_limit_bytes=vmem * MIB
        ),
        input_output_aliases=aliases or {},
        cost_estimate=pl.CostEstimate(flops=COST, bytes_accessed=COST, transcendentals=0),
    )(*operands)


def shape(dims, kind):
    return jax.ShapeDtypeStruct(dims, kind)


def whole(item):
    return pl.BlockSpec(item.shape, lambda *_: (0,) * len(item.shape))


def project_kernel(rows_ref, weight_ref, bias_ref, query_ref, kv_ref, turned_ref):
    rows = rows_ref[...].reshape(-1, rows_ref.shape[2])
    joint = dot_cols(rows, weight_ref[...]) + bias_ref[...]
    query_ref[...] = joint[:, :HD].astype(LOW)
    kv_ref[...] = joint[:, HD:].astype(LOW)
    turned_ref[...] = joint.T.astype(LOW)


def project(gathered, rows_here, weight, bias, span=2 * SPAN):
    places, _, width = gathered.shape
    total = places * rows_here
    step = span // rows_here
    return run(
        project_kernel,
        (total // span,),
        [
            pl.BlockSpec((step, rows_here, width), lambda i: (i, 0, 0)),
            whole(weight),
            whole(bias),
        ],
        [
            pl.BlockSpec((span, HD), lambda i: (i, 0)),
            pl.BlockSpec((span, 2 * HD), lambda i: (i, 0)),
            pl.BlockSpec((3 * HD, span), lambda i: (0, i)),
        ],
        [
            shape((total, HD), LOW),
            shape((total, 2 * HD), LOW),
            shape((3 * HD, total), LOW),
        ],
        (gathered, weight, bias),
    )


def prefix_seen(flags_ref, seg, columns):
    place = lax.broadcasted_iota(jnp.int32, (2 * KEPT, columns), 0)
    older = place < KEPT
    slot = jnp.where(older, place, place - KEPT) >= KEPT - NSUM
    flag = jnp.where(older, flags_ref[2 * seg], flags_ref[2 * seg + 1])
    return slot & (flag > 0)


def causal_seen():
    shape_here = (SPAN, SPAN)
    return lax.broadcasted_iota(jnp.int32, shape_here, 0) <= lax.broadcasted_iota(
        jnp.int32, shape_here, 1
    )


def above(block):
    return jnp.concatenate([block, jnp.zeros_like(block)], axis=0)


def below(block):
    return jnp.concatenate([jnp.zeros_like(block), block], axis=0)


def at_block(index):
    return pl.ds(pl.multiple_of(index * SPAN, SPAN), SPAN)


def attend_kernel(flags_ref, query_ref, turned_ref, kv_ref, prefix_ref, out_ref, log_ref):
    seg, block = pl.program_id(0), pl.program_id(1)
    query = above((query_ref[...].astype(jnp.float32) * SCALE).astype(LOW))
    own = at_block(block)
    scores = dot(kv_ref[own, :], query)
    scores = jnp.where(causal_seen(), scores, MASKED)
    top = jnp.max(scores, axis=0, keepdims=True)
    probs = jnp.exp(scores - top)
    total = jnp.sum(probs, axis=0, keepdims=True)
    mixed = dot(turned_ref[2 * HD :, own], probs.astype(LOW))

    def add(carry, scores, values):
        top, total, mixed = carry
        fresh = jnp.maximum(top, jnp.max(scores, axis=0, keepdims=True))
        fade = jnp.exp(top - fresh)
        probs = jnp.exp(scores - fresh)
        total = total * fade + jnp.sum(probs, axis=0, keepdims=True)
        return fresh, total, mixed * fade + dot(values, probs.astype(LOW))

    prefix = prefix_ref[0]
    scores = jnp.where(prefix_seen(flags_ref, seg, SPAN), dot(prefix, query), MASKED)
    carry = add((top, total, mixed), scores, turned(prefix)[HD:].astype(LOW))

    def step(index, carry):
        here = at_block(index)
        return add(carry, dot(kv_ref[here, :], query), turned_ref[2 * HD :, here])

    top, total, mixed = lax.fori_loop(0, block, step, carry)
    mixed = (mixed / total).astype(LOW)
    rows = out_ref.shape[2]
    for piece in range(SPAN // rows):
        out_ref[piece] = mixed[:, piece * rows : (piece + 1) * rows]
    log_ref[0] = top + jnp.log(total)


def attend(flags, turned_all, kv, prefix, rows_here):
    total = kv.shape[0]
    blocks = SEG // SPAN
    step = SPAN // rows_here
    return run(
        attend_kernel,
        (total // SEG, blocks),
        [
            pl.BlockSpec(memory_space=pltpu.SMEM),
            pl.BlockSpec((HD, SPAN), lambda s, i: (0, s * blocks + i)),
            pl.BlockSpec((3 * HD, SEG), lambda s, i: (0, s)),
            pl.BlockSpec((SEG, 2 * HD), lambda s, i: (s, 0)),
            pl.BlockSpec((1, 2 * KEPT, 2 * HD), lambda s, i: (s, 0, 0)),
        ],
        [
            pl.BlockSpec((step, HD, rows_here), lambda s, i: (s * blocks + i, 0, 0)),
            pl.BlockSpec((1, 1, SPAN), lambda s, i: (s * blocks + i, 0, 0)),
        ],
        [
            shape((total // rows_here, HD, rows_here), LOW),
            shape((total // SPAN, 1, SPAN), jnp.float32),
        ],
        (flags, turned_all, turned_all, kv, prefix),
    )


def side_by_side(ref):
    return jnp.concatenate([ref[piece] for piece in range(ref.shape[0])], axis=1)


def beside(block, place):
    zero = jnp.zeros_like(block)
    return jnp.concatenate([block, zero] if place == 0 else [zero, block], axis=1)


def query_side(query_ref, rows_ref, grad_ref, out_ref, log_ref):
    query = above((query_ref[...].astype(jnp.float32) * SCALE).astype(LOW))
    grad = side_by_side(grad_ref)
    mean = jnp.sum(
        grad.astype(jnp.float32) * side_by_side(out_ref).astype(jnp.float32),
        axis=0,
        keepdims=True,
    )
    query_rows = beside((rows_ref[...].astype(jnp.float32) * SCALE).astype(LOW), 0)
    grad_rows = beside(turned(grad).astype(LOW), 1)
    return query, below(grad), mean, log_ref[0], query_rows, grad_rows


def key_side(keys, side, seen):
    query, grad, mean, log_sum, query_rows, grad_rows = side
    probs = jnp.exp(dot(keys, query) - log_sum)
    if seen is not None:
        probs = jnp.where(seen, probs, 0.0)
    d_scores = (probs * (dot(keys, grad) - mean)).astype(LOW)
    return probs.astype(LOW), d_scores


def prefix_back_kernel(
    flags_ref, query_ref, rows_ref, grad_ref, out_ref, log_ref, prefix_ref, sum_ref
):
    seg, block = pl.program_id(0), pl.program_id(1)
    side = query_side(query_ref, rows_ref, grad_ref, out_ref, log_ref)
    probs, d_scores = key_side(prefix_ref[0], side, prefix_seen(flags_ref, seg, SPAN))
    part = dot(d_scores, side[4]) + dot(probs, side[5])

    @pl.when(block == 0)
    def _():
        sum_ref[0] = part

    @pl.when(block > 0)
    def _():
        sum_ref[0] += part


def store_shares(grads_ref, piece, part, columns):
    here = HD // grads_ref.shape[0]
    for share in range(grads_ref.shape[0]):
        for kind in (1, 2):
            first = (kind - 1) * HD + share * here
            grads_ref[share, piece, kind * here : (kind + 1) * here, columns] = part[
                first : first + here
            ]


def attend_back_kernel(
    flags_ref,
    query_ref,
    rows_ref,
    grad_ref,
    out_ref,
    log_ref,
    prefix_ref,
    turned_ref,
    kv_ref,
    grads_ref,
    kept_ref,
    kv_grad,
):
    seg, block = pl.program_id(0), pl.program_id(1)

    @pl.when(block == 0)
    def _():
        kv_grad[...] = jnp.zeros_like(kv_grad)

    side = query_side(query_ref, rows_ref, grad_ref, out_ref, log_ref)
    prefix = prefix_ref[0]
    _, d_scores = key_side(prefix, side, prefix_seen(flags_ref, seg, SPAN))
    query_grad = dot(turned(prefix)[:HD].astype(LOW), d_scores)

    def add(here, query_grad, seen):
        probs, d_scores = key_side(kv_ref[here, :], side, seen)
        kv_grad[here, :] += dot(d_scores, side[4]) + dot(probs, side[5])
        return query_grad + dot(turned_ref[HD : 2 * HD, here], d_scores)

    query_grad = add(at_block(block), query_grad, causal_seen())
    query_grad = lax.fori_loop(
        0, block, lambda index, grad: add(at_block(index), grad, None), query_grad
    )
    query_grad = (query_grad * SCALE).astype(LOW)
    rows = grads_ref.shape[3]
    step = SPAN // rows
    for piece in range(step):
        part = query_grad[:, piece * rows : (piece + 1) * rows]
        for share in range(grads_ref.shape[0]):
            here = HD // grads_ref.shape[0]
            grads_ref[share, block * step + piece, :here, :] = part[share * here : (share + 1) * here]

    @pl.when(block == pl.num_programs(1) - 1)
    def _():
        for piece in range(SEG // rows):
            part = kv_grad[piece * rows : (piece + 1) * rows, :].T.astype(LOW)
            store_shares(grads_ref, piece, part, slice(None))
        kept_ref[0] = kv_grad[SEG - KEPT :, :]


def attend_back_specs(rows_here):
    blocks = SEG // SPAN
    step = SPAN // rows_here
    return [
        pl.BlockSpec(memory_space=pltpu.SMEM),
        pl.BlockSpec((HD, SPAN), lambda s, i: (0, s * blocks + i)),
        pl.BlockSpec((SPAN, HD), lambda s, i: (s * blocks + i, 0)),
        pl.BlockSpec((step, HD, rows_here), lambda s, i: (s * blocks + i, 0, 0)),
        pl.BlockSpec((step, HD, rows_here), lambda s, i: (s * blocks + i, 0, 0)),
        pl.BlockSpec((1, 1, SPAN), lambda s, i: (s * blocks + i, 0, 0)),
        pl.BlockSpec((1, 2 * KEPT, 2 * HD), lambda s, i: (s, 0, 0)),
    ]


def prefix_back(flags, turned_all, query, grad, out, log_sums, prefix, rows_here):
    total = query.shape[0]
    return run(
        prefix_back_kernel,
        (total // SEG, SEG // SPAN),
        attend_back_specs(rows_here),
        [pl.BlockSpec((1, 2 * KEPT, 2 * HD), lambda s, i: (s, 0, 0))],
        [shape(prefix.shape, jnp.float32)],
        (flags, turned_all, query, grad, out, log_sums, prefix),
    )


def attend_back(flags, turned_all, query, grad, out, log_sums, prefix, kv, rows_here, count):
    total = query.shape[0]
    pieces = SEG // rows_here
    return run(
        attend_back_kernel,
        (total // SEG, SEG // SPAN),
        attend_back_specs(rows_here)
        + [
            pl.BlockSpec((3 * HD, SEG), lambda s, i: (0, s)),
            pl.BlockSpec((SEG, 2 * HD), lambda s, i: (s, 0)),
        ],
        [
            pl.BlockSpec(
                (count, pieces, 3 * HD // count, rows_here), lambda s, i: (0, s, 0, 0)
            ),
            pl.BlockSpec((1, KEPT, 2 * HD), lambda s, i: (s, 0, 0)),
        ],
        [
            shape((count, total // rows_here, 3 * HD // count, rows_here), LOW),
            shape((total // SEG, KEPT, 2 * HD), jnp.float32),
        ],
        (flags, turned_all, query, grad, out, log_sums, prefix, turned_all, kv),
        scratch=[pltpu.VMEM((SEG, 2 * HD), jnp.float32)],
    )


def returned_kernel(grads_ref, kept_ref, returned_ref, out_ref):
    out_ref[...] = grads_ref[...]
    part = (kept_ref[0] + returned_ref[0]).T.astype(LOW)
    store_shares(out_ref, 0, part, slice(out_ref.shape[3] - KEPT, None))


def add_returned(grads, kept, returned):
    count, places, feats, rows = grads.shape
    segs = kept.shape[0]
    last = places // segs
    grad_spec = pl.BlockSpec((count, 1, feats, rows), lambda s: (0, s * last + last - 1, 0, 0))
    kept_spec = pl.BlockSpec((1, KEPT, 2 * HD), lambda s: (s, 0, 0))
    return run(
        returned_kernel,
        (segs,),
        [grad_spec, kept_spec, kept_spec],
        [grad_spec],
        [shape(grads.shape, LOW)],
        (grads, kept, returned),
        aliases={0: 0},
    )[0]


def out_kernel(
    part_ref, weight_ref, tokens_ref, bias_ref, gain_ref, shift_ref, resid_ref, two_ref, total
):
    step = pl.program_id(0)
    rows = part_ref.shape[2]
    part = turned(part_ref[...].reshape(-1, rows)).astype(LOW)
    added = dot(part, weight_ref[...].reshape(part.shape[1], -1))

    @pl.when(step == 0)
    def _():
        total[...] = added

    @pl.when(step > 0)
    def _():
        total[...] += added

    @pl.when(step == pl.num_programs(0) - 1)
    def _():
        resid = tokens_ref[...].astype(jnp.float32) + total[...] + bias_ref[...]
        resid_ref[...] = resid
        two_ref[...] = layer_norm(resid, gain_ref[...], shift_ref[...]).astype(LOW)


def out_project(parts, gathered, at, tokens, bias, gain, shift, step=4):
    places, feats, rows = parts.shape
    width = gathered.shape[2]
    return run(
        out_kernel,
        (places // step,),
        [
            pl.BlockSpec((step, feats, rows), lambda i: (i, 0, 0)),
            pl.BlockSpec((step, feats, width), lambda i: (i, at, 0)),
            whole(tokens),
            whole(bias),
            whole(gain),
            whole(shift),
        ],
        [pl.BlockSpec((rows, width), lambda i: (0, 0))] * 2,
        [shape((rows, width), jnp.float32), shape((rows, width), LOW)],
        (parts, gathered, tokens, bias, gain, shift),
        scratch=[pltpu.VMEM((rows, width), jnp.float32)],
    )


def owner_maps(chips, at):
    def of(core_step, chip):
        return lambda i, place: at((i * chips[1] + chip) * 2 + lax.rem(place[0] + core_step, 2))

    return [of(core_step, chip) for core_step in (0, 1) for chip in range(chips[1])]


def step_maps(chips, at):
    chips_x, chips_y = chips

    def of(x_step):
        def index(i, place):
            x = lax.rem(place[1] + x_step, chips_x)
            y = lax.rem(place[2] + i, chips_y)
            return at((x * chips_y + y) * 2 + place[0])

        return index

    return [of(x_step) for x_step in range(chips_x)]


def own_map(index):
    return lambda i, place: index(i)


def fixed(dims):
    return pl.BlockSpec(
        dims, own_map(lambda i: (0,) * len(dims)), pipeline_mode=pl.Buffered(buffer_count=1)
    )


def feed_run(body, chips, place, in_specs, out_specs, out_shape, operands, scratch, vmem):
    return pl.pallas_call(
        body,
        grid_spec=pltpu.PrefetchScalarGridSpec(
            num_scalar_prefetch=1,
            grid=(chips[0],),
            in_specs=in_specs,
            out_specs=out_specs,
            scratch_shapes=scratch,
        ),
        out_shape=out_shape,
        compiler_params=pltpu.CompilerParams(
            dimension_semantics=("arbitrary",), vmem_limit_bytes=vmem * MIB
        ),
        cost_estimate=pl.CostEstimate(flops=COST, bytes_accessed=COST, transcendentals=0),
    )(place, *operands)


def stacked(refs, axis=0):
    return jnp.concatenate([ref[0] for ref in refs], axis=axis)


def pile(refs, into):
    rows = refs[0].shape[0]
    for at, ref in enumerate(refs):
        into[at * rows : (at + 1) * rows, :] = ref[...]


def spread(source, refs):
    rows = refs[0].shape[0]
    for at, ref in enumerate(refs):
        ref[...] = source[at * rows : (at + 1) * rows, :].astype(ref.dtype)


def take(refs, *counts):
    refs = list(refs)
    return [[refs.pop(0) for _ in range(count)] for count in counts] + [refs]


def d_act_kernel(count, owners, place_ref, *refs):
    cot_refs, weight_refs, (out_ref, cots) = take(refs, count, owners)

    @pl.when(pl.program_id(0) == 0)
    def _():
        pile(cot_refs, cots)

    out_ref[...] = dot_cols(cots[...], stacked(weight_refs))


def feed_d_act(place, chips, cots, weights):
    count = len(cots)
    rows, width = cots[0].shape
    places, both, _ = weights.shape
    units = both // 2
    total = count * rows
    owners = 2 * chips[1]
    step = owners * units
    return feed_run(
        partial(d_act_kernel, count, owners),
        chips,
        place,
        [fixed((rows, width))] * count
        + [
            pl.BlockSpec((1, units, width), at)
            for at in owner_maps(chips, lambda owner: (owner, 1, 0))
        ],
        [pl.BlockSpec((total, step), own_map(lambda i: (0, i))), fixed((total, width))],
        [shape((total, places * units), jnp.float32), shape((total, width), LOW)],
        (*cots, *[weights] * owners),
        [],
        32,
    )


def feed_kernel(count, chips, place_ref, *refs):
    owners = 2 * chips[1]
    norm_refs, weight_refs, bias_refs, (d_act_ref,), back_refs, refs = take(
        refs, count, owners, owners, 1, count
    )
    norms, kept_ref, sent_ref, bias_sum_ref, back = refs
    step = pl.program_id(0)

    @pl.when(step == 0)
    def _():
        pile(norm_refs, norms)
        back[...] = jnp.zeros_like(back)

    up = stacked(weight_refs)
    pre = dot_cols(norms[...], up) + stacked(bias_refs, axis=1)
    square = pre * pre
    bent = jnp.tanh(0.7978845608 * (pre + 0.044715 * (square * pre)))
    half = 0.5 * (1.0 + bent)
    slope = half + 0.5 * pre * (1.0 - bent * bent) * (
        0.7978845608 * (1.0 + 3.0 * 0.044715 * square)
    )
    d_pre = (d_act_ref[...] * slope).astype(LOW)
    act = (pre * half).astype(LOW)
    own = act.shape[1] // 2
    kept_ref[0] = act[:, :own]
    kept_ref[1] = d_pre[:, :own]
    sent_ref[0] = act[:, own:]
    sent_ref[1] = d_pre[:, own:]
    bias_sums = jnp.sum(d_pre.astype(jnp.float32), axis=0, keepdims=True)
    units = weight_refs[0].shape[1]
    for at, index in enumerate(owner_maps(chips, lambda owner: owner)):
        bias_sum_ref[index(step, place_ref)] = bias_sums[:, at * units : (at + 1) * units]
    back[...] += dot(d_pre, up)

    @pl.when(step == pl.num_programs(0) - 1)
    def _():
        spread(back, back_refs)


def feed(place, chips, norms, weights, bias, d_act):
    count = len(norms)
    rows, width = norms[0].shape
    places, both, _ = weights.shape
    units = both // 2
    total = count * rows
    owners = 2 * chips[1]
    step = owners * units
    pair_spec = pl.BlockSpec((2, total, step // 2), own_map(lambda i: (0, 0, i)))
    results = feed_run(
        partial(feed_kernel, count, chips),
        chips,
        place,
        [fixed((rows, width))] * count
        + [
            pl.BlockSpec((1, units, width), at)
            for at in owner_maps(chips, lambda owner: (owner, 0, 0))
        ]
        + [
            pl.BlockSpec((1, 1, units), at)
            for at in owner_maps(chips, lambda owner: (owner, 0, 0))
        ]
        + [pl.BlockSpec((total, step), own_map(lambda i: (0, i)))],
        [pl.BlockSpec((rows, width), own_map(lambda i: (0, 0)))] * count
        + [fixed((total, width)), pair_spec, pair_spec, fixed((places, 1, units))],
        [shape((rows, width), LOW)] * count
        + [shape((total, width), LOW)]
        + [shape((2, total, places * units // 2), LOW)] * 2
        + [shape((places, 1, units), jnp.float32)],
        (*norms, *[weights] * owners, *[bias] * owners, d_act),
        [pltpu.VMEM((total, width), jnp.float32)],
        40,
    )
    return results[:count], results[count:]


def feed_grad_kernel(count, owners, place_ref, *refs):
    norm_refs, cot_refs, pair_refs, weight_refs, mixed_refs, (out_ref, mixed) = take(
        refs, 2, 2, 3, owners, count
    )
    kept_ref, sent_ref, other_ref = pair_refs
    step = pl.program_id(0)
    units = weight_refs[0].shape[1]

    @pl.when(step == 0)
    def _():
        mixed[...] = jnp.zeros_like(mixed)

    act = jnp.concatenate([kept_ref[0], sent_ref[0]], axis=1)
    mixed[...] += dot(act, stacked(weight_refs))

    def grad(at, rows):
        total = dot(turned(kept_ref[at]).astype(LOW), rows[0][...])
        total += dot(turned(other_ref[at]).astype(LOW), rows[1][...])
        return total.astype(LOW).reshape(out_ref.shape[0], units, -1)

    out_ref[:, :units, :] = grad(1, norm_refs)
    out_ref[:, units:, :] = grad(0, cot_refs)

    @pl.when(step == pl.num_programs(0) - 1)
    def _():
        spread(mixed, mixed_refs)


def feed_grad(place, chips, count, norms, cots, kept, sent, other, weights):
    total, width = norms[0].shape
    rows = total // count
    units = weights.shape[1] // 2
    owners = 2 * chips[1]
    pair_spec = pl.BlockSpec((2, total, owners * units // 2), own_map(lambda i: (0, 0, i)))
    results = feed_run(
        partial(feed_grad_kernel, count, owners),
        chips,
        place,
        [fixed((total, width))] * 4
        + [pair_spec] * 3
        + [
            pl.BlockSpec((1, units, width), at)
            for at in owner_maps(chips, lambda owner: (owner, 1, 0))
        ],
        [pl.BlockSpec((rows, width), own_map(lambda i: (0, 0)))] * count
        + [pl.BlockSpec((chips[1], 2 * units, width), own_map(lambda i: (i, 0, 0)))],
        [shape((rows, width), LOW)] * count
        + [shape((chips[0] * chips[1], 2 * units, width), LOW)],
        (*norms, *cots, kept, sent, other, *[weights] * owners),
        [pltpu.VMEM((total, width), jnp.float32)],
        48,
    )
    return results[:count], results[count]


def branch_kernel(
    count, resid_ref, cot_ref, gain_ref, weight_ref, *refs
):
    back_refs = refs[:count]
    d_resid_ref, d_branch_ref, sums_ref, parts_ref = refs[count:]

    @pl.when(pl.program_id(0) == 0)
    def _():
        d_two = sum(ref[...].astype(jnp.float32) for ref in back_refs)
        normed, scale = norm_parts(resid_ref[...])
        cot = cot_ref[...].astype(jnp.float32)
        d_resid = cot + norm_back(d_two, normed, scale, gain_ref[...])
        d_branch = d_resid.astype(LOW)
        d_resid_ref[...] = d_resid
        d_branch_ref[...] = d_branch
        sums_ref[0:1, :] = jnp.sum(d_two * normed, axis=0, keepdims=True)
        sums_ref[1:2, :] = jnp.sum(d_two, axis=0, keepdims=True)
        sums_ref[2:3, :] = jnp.sum(d_branch.astype(jnp.float32), axis=0, keepdims=True)
        sums_ref[3:4, :] = jnp.sum(cot, axis=0, keepdims=True)

    width = weight_ref.shape[2]
    part = dot_cols(weight_ref[...].reshape(-1, width), d_branch_ref[...])
    parts_ref[...] = part.reshape(parts_ref.shape).astype(LOW)


def branch_back(resid, cotangent, gain, gathered, at, feats, backs, step=4):
    rows, width = resid.shape
    places = gathered.shape[0]
    row_spec = pl.BlockSpec((rows, width), lambda i: (0, 0))
    return run(
        partial(branch_kernel, len(backs)),
        (places // step,),
        [
            row_spec,
            row_spec,
            whole(gain),
            pl.BlockSpec((step, feats, width), lambda i: (i, at, 0)),
        ]
        + [row_spec] * len(backs),
        [
            row_spec,
            row_spec,
            pl.BlockSpec((4, width), lambda i: (0, 0)),
            pl.BlockSpec((step, feats, rows), lambda i: (i, 0, 0)),
        ],
        [
            shape((rows, width), jnp.float32),
            shape((rows, width), LOW),
            shape((4, width), jnp.float32),
            shape((places, feats, rows), LOW),
        ],
        (resid, cotangent, gain, gathered, *backs),
    )


def branch_grad_kernel(owners, place_ref, *refs):
    own_refs, other_refs, grad_refs, out_refs = take(refs, owners, owners, 2)
    parts = jnp.concatenate([stacked(own_refs), stacked(other_refs)], axis=1)
    grads = jnp.concatenate([ref[...] for ref in grad_refs], axis=0)
    out = dot(parts, grads).astype(LOW).reshape(out_refs[0].shape)
    for at, ref in enumerate(out_refs):

        @pl.when(pl.program_id(0) == at)
        def _():
            ref[...] = out


def branch_grad(place, chips, own, other, own_grad, other_grad):
    _, feats, rows = own.shape
    width = own_grad.shape[1]
    chips_x, chips_y = chips
    part_specs = [
        pl.BlockSpec((1, feats, rows), at)
        for at in step_maps(chips, lambda owner: (owner, 0, 0))
    ]
    return feed_run(
        partial(branch_grad_kernel, chips_x),
        (chips_y, chips_x),
        place,
        part_specs * 2 + [fixed((rows, width))] * 2,
        [pl.BlockSpec((chips_x, feats, width), own_map(lambda i: (0, 0, 0)))] * chips_y,
        [shape((chips_x, feats, width), LOW)] * chips_y,
        (*[own] * chips_x, *[other] * chips_x, own_grad, other_grad),
        [],
        32,
    )


def by_kind(rows, count):
    here = HD // count
    return jnp.concatenate(
        [
            rows[(share * 3 + kind) * here : (share * 3 + kind + 1) * here]
            for kind in range(3)
            for share in range(count)
        ],
        axis=0,
    )


def joint_grad_kernel(
    grad_ref, rows_ref, weight_ref, gain_ref, shift_ref, out_ref, bias_ref, sums_ref, total, biases
):
    step = pl.program_id(0)
    count, pieces = grad_ref.shape[:2]
    grads = jnp.concatenate(
        [
            jnp.concatenate([grad_ref[share, piece] for piece in range(pieces)], axis=1)
            for share in range(count)
        ],
        axis=0,
    )
    added = dot(grads, rows_ref[...].reshape(grads.shape[1], -1))
    summed = jnp.sum(grads.astype(jnp.float32), axis=1, keepdims=True)

    @pl.when(step == 0)
    def _():
        total[...] = added
        biases[...] = summed

    @pl.when(step > 0)
    def _():
        total[...] += added
        biases[...] += summed

    @pl.when(step == pl.num_programs(0) - 1)
    def _():
        out = by_kind(total[...], count)
        bias = by_kind(biases[...], count)
        out_ref[...] = out.astype(LOW)
        bias_ref[...] = bias
        weight = weight_ref[...].astype(jnp.float32)
        shift_sum = jnp.sum(weight * bias, axis=0, keepdims=True)
        product = jnp.sum(weight * out, axis=0, keepdims=True)
        sums_ref[0:1, :] = (product - shift_sum * shift_ref[...]) / gain_ref[...]
        sums_ref[1:2, :] = shift_sum


def joint_grad(grads, gathered, weight, gain, shift, step=8):
    count, places, feats, rows = grads.shape
    width = gathered.shape[2]
    total = count * feats
    return run(
        joint_grad_kernel,
        (places // step,),
        [
            pl.BlockSpec((count, step, feats, rows), lambda i: (0, i, 0, 0)),
            pl.BlockSpec((step, rows, width), lambda i: (i, 0, 0)),
            whole(weight),
            whole(gain),
            whole(shift),
        ],
        [
            pl.BlockSpec((total, width), lambda i: (0, 0)),
            pl.BlockSpec((total, 1), lambda i: (0, 0)),
            pl.BlockSpec((2, width), lambda i: (0, 0)),
        ],
        [
            shape((total, width), LOW),
            shape((total, 1), jnp.float32),
            shape((2, width), jnp.float32),
        ],
        (grads, gathered, weight, gain, shift),
        scratch=[pltpu.VMEM((total, width), jnp.float32), pltpu.VMEM((total, 1), jnp.float32)],
    )


def input_kernel(part_ref, weight_ref, tokens_ref, gain_ref, d_resid_ref, out_ref, total):
    step = pl.program_id(0)
    added = dot(turned(part_ref[...]).astype(LOW), weight_ref[...])

    @pl.when(step == 0)
    def _():
        total[...] = added

    @pl.when(step > 0)
    def _():
        total[...] += added

    @pl.when(step == pl.num_programs(0) - 1)
    def _():
        normed, scale = norm_parts(tokens_ref[...].astype(jnp.float32))
        out_ref[...] = d_resid_ref[...] + norm_back(total[...], normed, scale, gain_ref[...])


def input_back(parts, weights, tokens, gain, d_resid, steps=6):
    feats, rows = parts.shape
    width = weights.shape[1]
    step = feats // steps
    return run(
        input_kernel,
        (steps,),
        [
            pl.BlockSpec((step, rows), lambda i: (i, 0)),
            pl.BlockSpec((step, width), lambda i: (i, 0)),
            whole(tokens),
            whole(gain),
            whole(d_resid),
        ],
        [pl.BlockSpec((rows, width), lambda i: (0, 0))],
        [shape((rows, width), jnp.float32)],
        (parts, weights, tokens, gain, d_resid),
        scratch=[pltpu.VMEM((rows, width), jnp.float32)],
    )[0]


ITEM = "z"
HEAD = ("x", "y", "c")
CORE = "c"
UNIT = "y"
OWNER = ("z", "x", "c")


def moved(value, axis, steps):
    count = lax.axis_size(axis)
    return lax.ppermute(value, axis, [(place, (place + steps) % count) for place in range(count)])


def shifted(value, axis, steps):
    count = lax.axis_size(axis)
    initial, last = (max(0, -steps), min(count, count - steps))
    return lax.ppermute(value, axis, [(source, source + steps) for source in range(initial, last)])


def swapped(value, axis, step):
    pairs = [(place, place ^ step) for place in range(lax.axis_size(axis))]
    return lax.ppermute(value, axis, pairs)


def all_sum(value, axis):
    terms = around(value, axis)
    return (terms[0] + terms[2]) + (terms[1] + terms[3])


def around(value, axis):
    return [value] + [moved(value, axis, -step) for step in range(1, lax.axis_size(axis))]


def sum_back(values, axis):
    return [values[0]] + [
        moved(values[step], axis, step) for step in range(1, lax.axis_size(axis))
    ]


def own_half(value, bit, axis, step):
    count = value.shape[0] // 2
    own = lax.dynamic_slice_in_dim(value, bit * count, count)
    other = lax.dynamic_slice_in_dim(value, (1 - bit) * count, count)
    own = own.astype(jnp.float32) + swapped(other, axis, step).astype(jnp.float32)
    return own.astype(LOW)


def both_halves(value, bit, axis, step):
    other = swapped(value, axis, step)
    first = jnp.where(bit == 0, value, other)
    return jnp.concatenate([first, jnp.where(bit == 0, other, value)], axis=0)


def pair_sum(value, axis, step):
    value = value.astype(jnp.float32) + swapped(value, axis, step).astype(jnp.float32)
    return value.astype(LOW)


def near_steps(values, axis):
    near = values[:2].astype(jnp.float32) + moved(values[2:], axis, 2).astype(jnp.float32)
    return near.astype(LOW)


def own_step(values, axis):
    own = values[0].astype(jnp.float32) + moved(values[1], axis, 1).astype(jnp.float32)
    return own.astype(LOW)


def head_swap(value):
    return lax.all_to_all(value, HEAD, split_axis=0, concat_axis=0, tiled=True)


def segment_flags(seg_counts):
    total_segs = seg_counts.shape[0]
    openings = jnp.cumsum(seg_counts) - seg_counts
    places = jnp.arange(total_segs, dtype=jnp.int32)
    opens_here = jnp.any((openings[:, None] == places[None, :]) & (seg_counts[:, None] > 0), axis=0)
    opens_before = jnp.concatenate([jnp.ones((1,), dtype=bool), opens_here[:-1]])
    one_back = jnp.logical_not(opens_here)
    two_back = one_back & jnp.logical_not(opens_before)
    return (one_back, two_back)


def local(
    tokens,
    cotangent,
    seg_counts,
    query_weight,
    key_weight,
    value_weight,
    query_bias,
    value_bias,
    out_weight,
    out_bias,
    first_gain,
    first_shift,
    second_gain,
    second_shift,
    up_weight,
    up_bias,
    down_weight,
    down_bias,
):
    rows, width = tokens.shape
    heads = lax.axis_size(HEAD)
    item_place = lax.axis_index(ITEM)
    group_rows = rows * heads
    seg_local = group_rows // SEG
    feats = query_weight.shape[0]
    units = up_weight.shape[0]
    hidden_here = units * heads

    def row(vector):
        return vector.reshape(1, -1)

    tokens_f = tokens.astype(jnp.float32)
    inputs_one = layer_norm(tokens_f, first_gain, first_shift).astype(LOW)
    first = jnp.concatenate([inputs_one, out_weight], axis=0)
    gathered = lax.all_gather(first, HEAD, axis=0, tiled=True).reshape(heads, -1, width)
    second = jnp.concatenate([up_weight, down_weight], axis=0)
    feed_weights = lax.all_gather(second, OWNER, axis=0, tiled=True).reshape(heads, -1, width)
    joint_weight = jnp.concatenate([query_weight, key_weight, value_weight], axis=0)
    joint_bias = jnp.concatenate([query_bias, jnp.zeros_like(query_bias), value_bias])

    one_back, two_back = segment_flags(seg_counts)
    flags = jnp.stack([two_back, one_back], axis=1).astype(jnp.int32)
    flags = lax.dynamic_slice_in_dim(flags, item_place * seg_local, seg_local).reshape(-1)

    gathered, cot_turn = lax.optimization_barrier((gathered, cotangent))
    cots = around(cot_turn, UNIT)
    query, kv, turned_all = project(gathered, rows, joint_weight, row(joint_bias))
    own_kept = kv.reshape(seg_local, SEG, 2 * HD)[:, SEG - KEPT :]
    table = jnp.concatenate([shifted(own_kept, ITEM, 1), own_kept], axis=0)
    prefix = jnp.concatenate(
        [table[seg_local - 2 : 2 * seg_local - 2], table[seg_local - 1 : 2 * seg_local - 1]], axis=1
    )
    attended, log_sums = attend(flags, turned_all, kv, prefix, rows)
    attended, cots = lax.optimization_barrier((attended, cots))
    attended_own = head_swap(attended)
    attended_other = moved(attended_own, CORE, 1)
    resid, inputs_two = out_project(
        attended_own, gathered, rows // feats, tokens, row(out_bias), row(second_gain), row(second_shift)
    )

    joint_turn = lax.optimization_barrier((joint_weight, resid))[0]
    joint_full = lax.all_gather(joint_turn, HEAD, axis=0, tiled=True)
    norms = around(inputs_two, UNIT)
    sizes = [lax.axis_size(axis) for axis in ("z", "x", "y")]
    chips, owners = (sizes[1], sizes[2]), (sizes[0], sizes[1])
    place = jnp.stack([lax.axis_index(axis) for axis in (CORE, "x", "y", ITEM)]).astype(jnp.int32)
    d_act, cots = feed_d_act(place, owners, cots, feed_weights)
    cots = [cots, moved(cots, CORE, 1)]
    unit_place = lax.axis_index(UNIT)
    bias_here = lax.dynamic_index_in_dim(
        up_bias.reshape(*sizes[:2], sizes[2], -1), unit_place, 2, keepdims=False
    )
    backs, (norms, kept, sent, up_bias_part) = feed(
        place, owners, norms, feed_weights, bias_here.reshape(heads, 1, units), d_act
    )
    backs = sum_back(backs, UNIT)
    norms = [norms, moved(norms, CORE, 1)]
    mixeds, feed_parts = feed_grad(
        place, owners, len(backs), norms, cots, kept, sent, moved(sent, CORE, 1), feed_weights
    )
    backs, mixeds = lax.optimization_barrier((backs, mixeds))
    d_resid, d_branch, sums_two, d_parts = branch_back(
        resid, cotangent, row(second_gain), gathered, rows // feats, feats, backs
    )
    d_attended = head_swap(d_parts)
    feed_parts = lax.optimization_barrier((feed_parts, d_resid))[0]
    feed_grads = lax.psum_scatter(
        feed_parts.reshape(-1, width), OWNER[:2], scatter_dimension=0, tiled=True
    )

    outs = branch_grad(
        place, chips, attended_own, attended_other, d_branch, moved(d_branch, CORE, 1)
    )
    d_attended, outs, mixeds = lax.optimization_barrier((d_attended, outs, mixeds))
    near, far = jnp.stack(mixeds[:2]), moved(jnp.stack(mixeds[2:]), UNIT, 2)
    outs = sum_back(outs, "y")

    d_prefix = prefix_back(
        flags, turned_all, query, d_attended, attended, log_sums, prefix, rows
    )[0]
    older, newer = d_prefix[:, :KEPT], d_prefix[:, KEPT:]
    spread = jnp.pad(older, ((seg_local - 2, 2), (0, 0), (0, 0)))
    spread = spread + jnp.pad(newer, ((seg_local - 1, 1), (0, 0), (0, 0)))
    returned = shifted(spread[:seg_local], ITEM, -1)
    joint_grads, kept_grads = attend_back(
        flags, turned_all, query, d_attended, attended, log_sums, prefix, kv, rows, 1
    )
    returned, kept_grads, joint_full = lax.optimization_barrier((returned, kept_grads, joint_full))
    joint_grads = add_returned(joint_grads, kept_grads, spread[seg_local:] + returned)
    grads_own = head_swap(joint_grads[0]).reshape(-1, rows)
    joint_part, bias_part, sums_one = joint_grad(
        joint_grads, gathered, joint_weight, row(first_gain), row(first_shift)
    )
    high, low = item_place // 2, item_place % 2
    outs, near, far, joint_part, sums_one = lax.optimization_barrier(
        (outs, near, far, joint_part, sums_one)
    )
    out_part = lax.optimization_barrier(sum(out.astype(jnp.float32) for out in outs).astype(LOW))
    out_part = near_steps(out_part, "x")
    near = (near.astype(jnp.float32) + far.astype(jnp.float32)).astype(LOW)
    mixed = own_step(near, UNIT)
    joint_part = own_half(joint_part.reshape(4, -1, width), high, ITEM, 2)
    small = jnp.concatenate([row(up_bias_part), sums_two, sums_one], axis=0)
    small = small + swapped(small, CORE, 1)
    out_part, joint_part, small = lax.optimization_barrier((out_part, joint_part, small))
    out_part = own_step(out_part, "x")
    joint_part = own_half(joint_part, low, ITEM, 1)
    small = all_sum(small, "x")
    bias_part = jnp.pad(row(bias_part), ((0, 0), (0, width - bias_part.size)))
    small = jnp.concatenate([small, bias_part], axis=0)
    grads_own, out_part, joint_part, small, mixed = lax.optimization_barrier(
        (grads_own, out_part, joint_part, small, mixed)
    )
    input_grad = input_back(grads_own, joint_full, tokens, row(first_gain), d_resid)
    out_part = pair_sum(out_part, ITEM, 2)
    joint_part = both_halves(joint_part, low, ITEM, 1)
    small = all_sum(small, ITEM)
    input_grad, out_part, joint_part, small, feed_grads = lax.optimization_barrier(
        (input_grad, out_part, joint_part, small, feed_grads)
    )
    out_sum = pair_sum(out_part, ITEM, 1).astype(jnp.float32)
    joint_sums = both_halves(joint_part, high, ITEM, 2).reshape(-1, width).astype(jnp.float32)
    feed_grads = feed_grads.astype(jnp.float32)
    mixed_out = (resid + mixed.astype(jnp.float32) + down_bias).astype(LOW)
    bias_sums = small[7, : 3 * feats]
    terms = around(small[:7], UNIT)
    small = (terms[0][1:] + terms[2][1:]) + (terms[1][1:] + terms[3][1:])
    up_bias_grad = jnp.stack([term[0] for term in terms + terms])
    up_bias_grad = lax.dynamic_slice_in_dim(
        up_bias_grad, (sizes[2] - unit_place) % sizes[2], sizes[2], 0
    )
    up_bias_grad = up_bias_grad.reshape(sizes[2], *sizes[:2], -1).transpose(1, 2, 0, 3).reshape(-1)
    early_rows, late = small[:4], small[4:]
    return (
        mixed_out,
        input_grad,
        joint_sums[:feats],
        joint_sums[feats : 2 * feats],
        joint_sums[2 * feats :],
        bias_sums[:feats],
        bias_sums[2 * feats : 3 * feats],
        out_sum,
        early_rows[2],
        late[0],
        late[1],
        early_rows[0],
        early_rows[1],
        feed_grads[:units],
        up_bias_grad,
        feed_grads[units:],
        early_rows[3],
    )


def solution(mesh):
    sizes = (mesh.shape["item"], 4, mesh.shape["head"] // 8, 2)
    fine = Mesh(mesh.devices.reshape(sizes), (ITEM, *HEAD))
    split = P((ITEM, *HEAD), None)
    by_head = P(HEAD, None)
    return jax.shard_map(
        local,
        mesh=fine,
        in_specs=(
            split,
            split,
            P(),
            by_head,
            by_head,
            by_head,
            P(HEAD),
            P(HEAD),
            by_head,
            P(),
            P(),
            P(),
            P(),
            P(),
            split,
            P(),
            split,
            P(),
        ),
        out_specs=(
            split,
            split,
            by_head,
            by_head,
            by_head,
            P(HEAD),
            P(HEAD),
            by_head,
            P(),
            P(),
            P(),
            P(),
            P(),
            split,
            P(),
            split,
            P(),
        ),
        check_vma=False,
    )
```

```python
from functools import partial

import jax
import jax.numpy as jnp
from jax import lax
from jax.experimental import pallas as pl
from jax.experimental.pallas import tpu as pltpu
from jax.sharding import Mesh
from jax.sharding import PartitionSpec as P

HD = 64
NSUM = 50
SEG = 2048
SPAN = 512
KEPT = 64
EPSILON = 1e-05
MASKED = -1e30
SCALE = HD ** (-0.5)
MIB = 1 << 20
COST = 1 << 20
LOW = jnp.bfloat16


def dot(left, right):
    return jnp.dot(left, right, preferred_element_type=jnp.float32)


def dot_cols(left, right):
    return lax.dot_general(
        left, right, (((1,), (1,)), ((), ())), preferred_element_type=jnp.float32
    )


def turned(value):
    return value.astype(jnp.float32).T


def norm_parts(row_data):
    row_mean = jnp.mean(row_data, axis=-1, keepdims=True)
    centred = row_data - row_mean
    row_var = jnp.mean(centred * centred, axis=-1, keepdims=True)
    scale = lax.rsqrt(row_var + EPSILON)
    return centred * scale, scale


def norm_back(grad, normed, scale, gain):
    scaled = grad * gain
    return scale * (
        scaled
        - jnp.mean(scaled, axis=-1, keepdims=True)
        - normed * jnp.mean(scaled * normed, axis=-1, keepdims=True)
    )


def layer_norm(row_data, gain, shift):
    return norm_parts(row_data)[0] * gain + shift


def run(body, grid, in_specs, out_specs, out_shape, operands, scratch=(), vmem=32, aliases=None):
    return pl.pallas_call(
        body,
        grid=grid,
        in_specs=in_specs,
        out_specs=out_specs,
        out_shape=out_shape,
        scratch_shapes=scratch,
        compiler_params=pltpu.CompilerParams(
            dimension_semantics=("arbitrary",) * len(grid), vmem_limit_bytes=vmem * MIB
        ),
        input_output_aliases=aliases or {},
        cost_estimate=pl.CostEstimate(flops=COST, bytes_accessed=COST, transcendentals=0),
    )(*operands)


def shape(dims, kind):
    return jax.ShapeDtypeStruct(dims, kind)


def whole(item):
    return pl.BlockSpec(item.shape, lambda *_: (0,) * len(item.shape))


def project_kernel(rows_ref, weight_ref, bias_ref, query_ref, kv_ref, turned_ref):
    rows = rows_ref[...].reshape(-1, rows_ref.shape[2])
    joint = dot_cols(rows, weight_ref[...]) + bias_ref[...]
    query_ref[...] = joint[:, :HD].astype(LOW)
    kv_ref[...] = joint[:, HD:].astype(LOW)
    turned_ref[...] = joint.T.astype(LOW)


def project(gathered, rows_here, weight, bias, span=2 * SPAN):
    places, _, width = gathered.shape
    total = places * rows_here
    step = span // rows_here
    return run(
        project_kernel,
        (total // span,),
        [
            pl.BlockSpec((step, rows_here, width), lambda i: (i, 0, 0)),
            whole(weight),
            whole(bias),
        ],
        [
            pl.BlockSpec((span, HD), lambda i: (i, 0)),
            pl.BlockSpec((span, 2 * HD), lambda i: (i, 0)),
            pl.BlockSpec((3 * HD, span), lambda i: (0, i)),
        ],
        [
            shape((total, HD), LOW),
            shape((total, 2 * HD), LOW),
            shape((3 * HD, total), LOW),
        ],
        (gathered, weight, bias),
    )


def prefix_seen(flags_ref, seg, columns):
    place = lax.broadcasted_iota(jnp.int32, (2 * KEPT, columns), 0)
    older = place < KEPT
    slot = jnp.where(older, place, place - KEPT) >= KEPT - NSUM
    flag = jnp.where(older, flags_ref[2 * seg], flags_ref[2 * seg + 1])
    return slot & (flag > 0)


def causal_seen():
    shape_here = (SPAN, SPAN)
    return lax.broadcasted_iota(jnp.int32, shape_here, 0) <= lax.broadcasted_iota(
        jnp.int32, shape_here, 1
    )


def above(block):
    return jnp.concatenate([block, jnp.zeros_like(block)], axis=0)


def below(block):
    return jnp.concatenate([jnp.zeros_like(block), block], axis=0)


def at_block(index):
    return pl.ds(pl.multiple_of(index * SPAN, SPAN), SPAN)


def attend_kernel(flags_ref, query_ref, turned_ref, kv_ref, prefix_ref, out_ref, log_ref):
    seg, block = pl.program_id(0), pl.program_id(1)
    query = above((query_ref[...].astype(jnp.float32) * SCALE).astype(LOW))
    own = at_block(block)
    scores = dot(kv_ref[own, :], query)
    scores = jnp.where(causal_seen(), scores, MASKED)
    top = jnp.max(scores, axis=0, keepdims=True)
    probs = jnp.exp(scores - top)
    total = jnp.sum(probs, axis=0, keepdims=True)
    mixed = dot(turned_ref[2 * HD :, own], probs.astype(LOW))

    def add(carry, scores, values):
        top, total, mixed = carry
        fresh = jnp.maximum(top, jnp.max(scores, axis=0, keepdims=True))
        fade = jnp.exp(top - fresh)
        probs = jnp.exp(scores - fresh)
        total = total * fade + jnp.sum(probs, axis=0, keepdims=True)
        return fresh, total, mixed * fade + dot(values, probs.astype(LOW))

    prefix = prefix_ref[0]
    scores = jnp.where(prefix_seen(flags_ref, seg, SPAN), dot(prefix, query), MASKED)
    carry = add((top, total, mixed), scores, turned(prefix)[HD:].astype(LOW))

    def step(index, carry):
        here = at_block(index)
        return add(carry, dot(kv_ref[here, :], query), turned_ref[2 * HD :, here])

    top, total, mixed = lax.fori_loop(0, block, step, carry)
    mixed = (mixed / total).astype(LOW)
    rows = out_ref.shape[2]
    for piece in range(SPAN // rows):
        out_ref[piece] = mixed[:, piece * rows : (piece + 1) * rows]
    log_ref[0] = top + jnp.log(total)


def attend(flags, turned_all, kv, prefix, rows_here):
    total = kv.shape[0]
    blocks = SEG // SPAN
    step = SPAN // rows_here
    return run(
        attend_kernel,
        (total // SEG, blocks),
        [
            pl.BlockSpec(memory_space=pltpu.SMEM),
            pl.BlockSpec((HD, SPAN), lambda s, i: (0, s * blocks + i)),
            pl.BlockSpec((3 * HD, SEG), lambda s, i: (0, s)),
            pl.BlockSpec((SEG, 2 * HD), lambda s, i: (s, 0)),
            pl.BlockSpec((1, 2 * KEPT, 2 * HD), lambda s, i: (s, 0, 0)),
        ],
        [
            pl.BlockSpec((step, HD, rows_here), lambda s, i: (s * blocks + i, 0, 0)),
            pl.BlockSpec((1, 1, SPAN), lambda s, i: (s * blocks + i, 0, 0)),
        ],
        [
            shape((total // rows_here, HD, rows_here), LOW),
            shape((total // SPAN, 1, SPAN), jnp.float32),
        ],
        (flags, turned_all, turned_all, kv, prefix),
    )


def side_by_side(ref):
    return jnp.concatenate([ref[piece] for piece in range(ref.shape[0])], axis=1)


def beside(block, place):
    zero = jnp.zeros_like(block)
    return jnp.concatenate([block, zero] if place == 0 else [zero, block], axis=1)


def query_side(query_ref, rows_ref, grad_ref, out_ref, log_ref):
    query = above((query_ref[...].astype(jnp.float32) * SCALE).astype(LOW))
    grad = side_by_side(grad_ref)
    mean = jnp.sum(
        grad.astype(jnp.float32) * side_by_side(out_ref).astype(jnp.float32),
        axis=0,
        keepdims=True,
    )
    query_rows = beside((rows_ref[...].astype(jnp.float32) * SCALE).astype(LOW), 0)
    grad_rows = beside(turned(grad).astype(LOW), 1)
    return query, below(grad), mean, log_ref[0], query_rows, grad_rows


def key_side(keys, side, seen):
    query, grad, mean, log_sum, query_rows, grad_rows = side
    probs = jnp.exp(dot(keys, query) - log_sum)
    if seen is not None:
        probs = jnp.where(seen, probs, 0.0)
    d_scores = (probs * (dot(keys, grad) - mean)).astype(LOW)
    return probs.astype(LOW), d_scores


def prefix_back_kernel(
    flags_ref, query_ref, rows_ref, grad_ref, out_ref, log_ref, prefix_ref, sum_ref
):
    seg, block = pl.program_id(0), pl.program_id(1)
    side = query_side(query_ref, rows_ref, grad_ref, out_ref, log_ref)
    probs, d_scores = key_side(prefix_ref[0], side, prefix_seen(flags_ref, seg, SPAN))
    part = dot(d_scores, side[4]) + dot(probs, side[5])

    @pl.when(block == 0)
    def _():
        sum_ref[0] = part

    @pl.when(block > 0)
    def _():
        sum_ref[0] += part


def store_shares(grads_ref, piece, part, columns):
    here = HD // grads_ref.shape[0]
    for share in range(grads_ref.shape[0]):
        for kind in (1, 2):
            first = (kind - 1) * HD + share * here
            grads_ref[share, piece, kind * here : (kind + 1) * here, columns] = part[
                first : first + here
            ]


def attend_back_kernel(
    flags_ref,
    query_ref,
    rows_ref,
    grad_ref,
    out_ref,
    log_ref,
    prefix_ref,
    turned_ref,
    kv_ref,
    grads_ref,
    kept_ref,
    kv_grad,
):
    seg, block = pl.program_id(0), pl.program_id(1)

    @pl.when(block == 0)
    def _():
        kv_grad[...] = jnp.zeros_like(kv_grad)

    side = query_side(query_ref, rows_ref, grad_ref, out_ref, log_ref)
    prefix = prefix_ref[0]
    _, d_scores = key_side(prefix, side, prefix_seen(flags_ref, seg, SPAN))
    query_grad = dot(turned(prefix)[:HD].astype(LOW), d_scores)

    def add(here, query_grad, seen):
        probs, d_scores = key_side(kv_ref[here, :], side, seen)
        kv_grad[here, :] += dot(d_scores, side[4]) + dot(probs, side[5])
        return query_grad + dot(turned_ref[HD : 2 * HD, here], d_scores)

    query_grad = add(at_block(block), query_grad, causal_seen())
    query_grad = lax.fori_loop(
        0, block, lambda index, grad: add(at_block(index), grad, None), query_grad
    )
    query_grad = (query_grad * SCALE).astype(LOW)
    rows = grads_ref.shape[3]
    step = SPAN // rows
    for piece in range(step):
        part = query_grad[:, piece * rows : (piece + 1) * rows]
        for share in range(grads_ref.shape[0]):
            here = HD // grads_ref.shape[0]
            grads_ref[share, block * step + piece, :here, :] = part[share * here : (share + 1) * here]

    @pl.when(block == pl.num_programs(1) - 1)
    def _():
        for piece in range(SEG // rows):
            part = kv_grad[piece * rows : (piece + 1) * rows, :].T.astype(LOW)
            store_shares(grads_ref, piece, part, slice(None))
        kept_ref[0] = kv_grad[SEG - KEPT :, :]


def attend_back_specs(rows_here):
    blocks = SEG // SPAN
    step = SPAN // rows_here
    return [
        pl.BlockSpec(memory_space=pltpu.SMEM),
        pl.BlockSpec((HD, SPAN), lambda s, i: (0, s * blocks + i)),
        pl.BlockSpec((SPAN, HD), lambda s, i: (s * blocks + i, 0)),
        pl.BlockSpec((step, HD, rows_here), lambda s, i: (s * blocks + i, 0, 0)),
        pl.BlockSpec((step, HD, rows_here), lambda s, i: (s * blocks + i, 0, 0)),
        pl.BlockSpec((1, 1, SPAN), lambda s, i: (s * blocks + i, 0, 0)),
        pl.BlockSpec((1, 2 * KEPT, 2 * HD), lambda s, i: (s, 0, 0)),
    ]


def prefix_back(flags, turned_all, query, grad, out, log_sums, prefix, rows_here):
    total = query.shape[0]
    return run(
        prefix_back_kernel,
        (total // SEG, SEG // SPAN),
        attend_back_specs(rows_here),
        [pl.BlockSpec((1, 2 * KEPT, 2 * HD), lambda s, i: (s, 0, 0))],
        [shape(prefix.shape, jnp.float32)],
        (flags, turned_all, query, grad, out, log_sums, prefix),
    )


def attend_back(flags, turned_all, query, grad, out, log_sums, prefix, kv, rows_here, count):
    total = query.shape[0]
    pieces = SEG // rows_here
    return run(
        attend_back_kernel,
        (total // SEG, SEG // SPAN),
        attend_back_specs(rows_here)
        + [
            pl.BlockSpec((3 * HD, SEG), lambda s, i: (0, s)),
            pl.BlockSpec((SEG, 2 * HD), lambda s, i: (s, 0)),
        ],
        [
            pl.BlockSpec(
                (count, pieces, 3 * HD // count, rows_here), lambda s, i: (0, s, 0, 0)
            ),
            pl.BlockSpec((1, KEPT, 2 * HD), lambda s, i: (s, 0, 0)),
        ],
        [
            shape((count, total // rows_here, 3 * HD // count, rows_here), LOW),
            shape((total // SEG, KEPT, 2 * HD), jnp.float32),
        ],
        (flags, turned_all, query, grad, out, log_sums, prefix, turned_all, kv),
        scratch=[pltpu.VMEM((SEG, 2 * HD), jnp.float32)],
    )


def returned_kernel(grads_ref, kept_ref, returned_ref, out_ref):
    out_ref[...] = grads_ref[...]
    part = (kept_ref[0] + returned_ref[0]).T.astype(LOW)
    store_shares(out_ref, 0, part, slice(out_ref.shape[3] - KEPT, None))


def add_returned(grads, kept, returned):
    count, places, feats, rows = grads.shape
    segs = kept.shape[0]
    last = places // segs
    grad_spec = pl.BlockSpec((count, 1, feats, rows), lambda s: (0, s * last + last - 1, 0, 0))
    kept_spec = pl.BlockSpec((1, KEPT, 2 * HD), lambda s: (s, 0, 0))
    return run(
        returned_kernel,
        (segs,),
        [grad_spec, kept_spec, kept_spec],
        [grad_spec],
        [shape(grads.shape, LOW)],
        (grads, kept, returned),
        aliases={0: 0},
    )[0]


def out_kernel(
    part_ref, weight_ref, tokens_ref, bias_ref, gain_ref, shift_ref, resid_ref, two_ref, total
):
    step = pl.program_id(0)
    rows = part_ref.shape[2]
    part = turned(part_ref[...].reshape(-1, rows)).astype(LOW)
    added = dot(part, weight_ref[...].reshape(part.shape[1], -1))

    @pl.when(step == 0)
    def _():
        total[...] = added

    @pl.when(step > 0)
    def _():
        total[...] += added

    @pl.when(step == pl.num_programs(0) - 1)
    def _():
        resid = tokens_ref[...].astype(jnp.float32) + total[...] + bias_ref[...]
        resid_ref[...] = resid
        two_ref[...] = layer_norm(resid, gain_ref[...], shift_ref[...]).astype(LOW)


def out_project(parts, gathered, at, tokens, bias, gain, shift, step=4):
    places, feats, rows = parts.shape
    width = gathered.shape[2]
    return run(
        out_kernel,
        (places // step,),
        [
            pl.BlockSpec((step, feats, rows), lambda i: (i, 0, 0)),
            pl.BlockSpec((step, feats, width), lambda i: (i, at, 0)),
            whole(tokens),
            whole(bias),
            whole(gain),
            whole(shift),
        ],
        [pl.BlockSpec((rows, width), lambda i: (0, 0))] * 2,
        [shape((rows, width), jnp.float32), shape((rows, width), LOW)],
        (parts, gathered, tokens, bias, gain, shift),
        scratch=[pltpu.VMEM((rows, width), jnp.float32)],
    )


def owner_maps(chips, at):
    def of(core_step, chip):
        return lambda i, place: at((i * chips[1] + chip) * 2 + lax.rem(place[0] + core_step, 2))

    return [of(core_step, chip) for core_step in (0, 1) for chip in range(chips[1])]


def own_map(index):
    return lambda i, place: index(i)


def fixed(dims):
    return pl.BlockSpec(
        dims, own_map(lambda i: (0,) * len(dims)), pipeline_mode=pl.Buffered(buffer_count=1)
    )


def feed_run(body, chips, place, in_specs, out_specs, out_shape, operands, scratch, vmem):
    return pl.pallas_call(
        body,
        grid_spec=pltpu.PrefetchScalarGridSpec(
            num_scalar_prefetch=1,
            grid=(chips[0],),
            in_specs=in_specs,
            out_specs=out_specs,
            scratch_shapes=scratch,
        ),
        out_shape=out_shape,
        compiler_params=pltpu.CompilerParams(
            dimension_semantics=("arbitrary",), vmem_limit_bytes=vmem * MIB
        ),
        cost_estimate=pl.CostEstimate(flops=COST, bytes_accessed=COST, transcendentals=0),
    )(place, *operands)


def stacked(refs, axis=0):
    return jnp.concatenate([ref[0] for ref in refs], axis=axis)


def pile(refs, into):
    rows = refs[0].shape[0]
    for at, ref in enumerate(refs):
        into[at * rows : (at + 1) * rows, :] = ref[...]


def spread(source, refs):
    rows = refs[0].shape[0]
    for at, ref in enumerate(refs):
        ref[...] = source[at * rows : (at + 1) * rows, :].astype(ref.dtype)


def take(refs, *counts):
    refs = list(refs)
    return [[refs.pop(0) for _ in range(count)] for count in counts] + [refs]


def d_act_kernel(count, owners, place_ref, *refs):
    cot_refs, weight_refs, (out_ref, cots) = take(refs, count, owners)

    @pl.when(pl.program_id(0) == 0)
    def _():
        pile(cot_refs, cots)

    out_ref[...] = dot_cols(cots[...], stacked(weight_refs))


def feed_d_act(place, chips, cots, weights):
    count = len(cots)
    rows, width = cots[0].shape
    places, both, _ = weights.shape
    units = both // 2
    total = count * rows
    owners = 2 * chips[1]
    step = owners * units
    return feed_run(
        partial(d_act_kernel, count, owners),
        chips,
        place,
        [fixed((rows, width))] * count
        + [
            pl.BlockSpec((1, units, width), at)
            for at in owner_maps(chips, lambda owner: (owner, 1, 0))
        ],
        [pl.BlockSpec((total, step), own_map(lambda i: (0, i))), fixed((total, width))],
        [shape((total, places * units), jnp.float32), shape((total, width), LOW)],
        (*cots, *[weights] * owners),
        [],
        32,
    )


def feed_kernel(count, chips, place_ref, *refs):
    owners = 2 * chips[1]
    norm_refs, weight_refs, bias_refs, (d_act_ref,), back_refs, refs = take(
        refs, count, owners, owners, 1, count
    )
    norms, kept_ref, sent_ref, bias_sum_ref, back = refs
    step = pl.program_id(0)

    @pl.when(step == 0)
    def _():
        pile(norm_refs, norms)
        back[...] = jnp.zeros_like(back)

    up = stacked(weight_refs)
    pre = dot_cols(norms[...], up) + stacked(bias_refs, axis=1)
    square = pre * pre
    bent = jnp.tanh(0.7978845608 * (pre + 0.044715 * (square * pre)))
    half = 0.5 * (1.0 + bent)
    slope = half + 0.5 * pre * (1.0 - bent * bent) * (
        0.7978845608 * (1.0 + 3.0 * 0.044715 * square)
    )
    d_pre = (d_act_ref[...] * slope).astype(LOW)
    act = (pre * half).astype(LOW)
    own = act.shape[1] // 2
    kept_ref[0] = act[:, :own]
    kept_ref[1] = d_pre[:, :own]
    sent_ref[0] = act[:, own:]
    sent_ref[1] = d_pre[:, own:]
    bias_sums = jnp.sum(d_pre.astype(jnp.float32), axis=0, keepdims=True)
    units = weight_refs[0].shape[1]
    for at, index in enumerate(owner_maps(chips, lambda owner: owner)):
        bias_sum_ref[index(step, place_ref)] = bias_sums[:, at * units : (at + 1) * units]
    back[...] += dot(d_pre, up)

    @pl.when(step == pl.num_programs(0) - 1)
    def _():
        spread(back, back_refs)


def feed(place, chips, norms, weights, bias, d_act):
    count = len(norms)
    rows, width = norms[0].shape
    places, both, _ = weights.shape
    units = both // 2
    total = count * rows
    owners = 2 * chips[1]
    step = owners * units
    pair_spec = pl.BlockSpec((2, total, step // 2), own_map(lambda i: (0, 0, i)))
    results = feed_run(
        partial(feed_kernel, count, chips),
        chips,
        place,
        [fixed((rows, width))] * count
        + [
            pl.BlockSpec((1, units, width), at)
            for at in owner_maps(chips, lambda owner: (owner, 0, 0))
        ]
        + [
            pl.BlockSpec((1, 1, units), at)
            for at in owner_maps(chips, lambda owner: (owner, 0, 0))
        ]
        + [pl.BlockSpec((total, step), own_map(lambda i: (0, i)))],
        [pl.BlockSpec((rows, width), own_map(lambda i: (0, 0)))] * count
        + [fixed((total, width)), pair_spec, pair_spec, fixed((places, 1, units))],
        [shape((rows, width), LOW)] * count
        + [shape((total, width), LOW)]
        + [shape((2, total, places * units // 2), LOW)] * 2
        + [shape((places, 1, units), jnp.float32)],
        (*norms, *[weights] * owners, *[bias] * owners, d_act),
        [pltpu.VMEM((total, width), jnp.float32)],
        40,
    )
    return results[:count], results[count:]


def feed_grad_kernel(count, owners, place_ref, *refs):
    norm_refs, cot_refs, pair_refs, weight_refs, mixed_refs, (out_ref, mixed) = take(
        refs, 2, 2, 3, owners, count
    )
    kept_ref, sent_ref, other_ref = pair_refs
    step = pl.program_id(0)
    units = weight_refs[0].shape[1]

    @pl.when(step == 0)
    def _():
        mixed[...] = jnp.zeros_like(mixed)

    act = jnp.concatenate([kept_ref[0], sent_ref[0]], axis=1)
    mixed[...] += dot(act, stacked(weight_refs))

    def grad(at, rows):
        total = dot(turned(kept_ref[at]).astype(LOW), rows[0][...])
        total += dot(turned(other_ref[at]).astype(LOW), rows[1][...])
        return total.astype(LOW).reshape(out_ref.shape[0], units, -1)

    out_ref[:, :units, :] = grad(1, norm_refs)
    out_ref[:, units:, :] = grad(0, cot_refs)

    @pl.when(step == pl.num_programs(0) - 1)
    def _():
        spread(mixed, mixed_refs)


def feed_grad(place, chips, count, norms, cots, kept, sent, other, weights):
    total, width = norms[0].shape
    rows = total // count
    units = weights.shape[1] // 2
    owners = 2 * chips[1]
    pair_spec = pl.BlockSpec((2, total, owners * units // 2), own_map(lambda i: (0, 0, i)))
    results = feed_run(
        partial(feed_grad_kernel, count, owners),
        chips,
        place,
        [fixed((total, width))] * 4
        + [pair_spec] * 3
        + [
            pl.BlockSpec((1, units, width), at)
            for at in owner_maps(chips, lambda owner: (owner, 1, 0))
        ],
        [pl.BlockSpec((rows, width), own_map(lambda i: (0, 0)))] * count
        + [pl.BlockSpec((chips[1], 2 * units, width), own_map(lambda i: (i, 0, 0)))],
        [shape((rows, width), LOW)] * count
        + [shape((chips[0] * chips[1], 2 * units, width), LOW)],
        (*norms, *cots, kept, sent, other, *[weights] * owners),
        [pltpu.VMEM((total, width), jnp.float32)],
        48,
    )
    return results[:count], results[count]


def branch_kernel(count, place_ref, *refs):
    (resid_ref, cot_ref, gain_ref, weight_ref, part_ref), back_refs, refs = take(refs, 5, count)
    (d_resid_ref, sums_ref, parts_ref), sent_refs, (d_branch_ref,) = take(refs, 3, count)
    step = pl.program_id(0)

    @pl.when(step == 0)
    def _():
        d_two = sum(ref[...].astype(jnp.float32) for ref in back_refs)
        normed, scale = norm_parts(resid_ref[...])
        cot = cot_ref[...].astype(jnp.float32)
        d_resid = cot + norm_back(d_two, normed, scale, gain_ref[...])
        d_branch = d_resid.astype(LOW)
        d_resid_ref[...] = d_resid
        d_branch_ref[...] = d_branch
        sums_ref[0:1, :] = jnp.sum(d_two * normed, axis=0, keepdims=True)
        sums_ref[1:2, :] = jnp.sum(d_two, axis=0, keepdims=True)
        sums_ref[2:3, :] = jnp.sum(d_branch.astype(jnp.float32), axis=0, keepdims=True)
        sums_ref[3:4, :] = jnp.sum(cot, axis=0, keepdims=True)

    width = weight_ref.shape[2]
    part = dot_cols(weight_ref[...].reshape(-1, width), d_branch_ref[...])
    parts_ref[...] = part.reshape(parts_ref.shape).astype(LOW)

    @pl.when(step == pl.num_programs(0) - 1)
    def _():
        places, feats, rows = part_ref.shape
        share = feats // count
        more = places * share * rows // width
        for at, ref in enumerate(sent_refs):
            first = lax.rem(place_ref[3] + at, count) * share
            taken = part_ref[:, pl.ds(pl.multiple_of(first, share), share), :]
            taken = taken.reshape(places * share, rows)
            ref[:rows, :] = d_branch_ref[...]
            ref[rows:, :] = jnp.concatenate(
                [taken[more * at : more * (at + 1)] for at in range(width // rows)], axis=1
            )


def branch_back(place, resid, cotangent, gain, gathered, at, attended, backs, step=4):
    rows, width = resid.shape
    places, feats, _ = attended.shape
    count = len(backs)
    row_spec = pl.BlockSpec((rows, width), lambda i: (0, 0))
    sent = shape((rows + places * feats // count * rows // width, width), LOW)
    results = run(
        partial(branch_kernel, count),
        (places // step,),
        [
            pl.BlockSpec(memory_space=pltpu.SMEM),
            row_spec,
            row_spec,
            whole(gain),
            pl.BlockSpec((step, feats, width), lambda i: (i, at, 0)),
            whole(attended),
        ]
        + [row_spec] * count,
        [
            row_spec,
            pl.BlockSpec((4, width), lambda i: (0, 0)),
            pl.BlockSpec((step, feats, rows), lambda i: (i, 0, 0)),
        ]
        + [whole(sent)] * count,
        [
            shape((rows, width), jnp.float32),
            shape((4, width), jnp.float32),
            shape((places, feats, rows), LOW),
        ]
        + [sent] * count,
        (place, resid, cotangent, gain, gathered, attended, *backs),
        scratch=[pltpu.VMEM((rows, width), LOW)],
    )
    return (*results[:3], results[3:])


def branch_grad_kernel(count, chips, rows, place_ref, *refs):
    sent_refs, (own_ref, other_ref, parts) = take(refs, count)
    chips_x, chips_y = chips
    places, feats = parts.shape[1:3]
    for at, ref in enumerate(sent_refs):
        taken = ref[rows:, :]
        taken = [taken[:, rows * at : rows * (at + 1)] for at in range(taken.shape[1] // rows)]
        parts[at] = jnp.concatenate(taken, axis=0).reshape(places, feats, rows)
    grads = jnp.concatenate([ref[:rows, :] for ref in sent_refs], axis=0)

    def owner(at, core):
        x = lax.rem(place_ref[1] + at // chips_y, chips_x)
        y = lax.rem(place_ref[2] + at % chips_y, chips_y)
        return (x * chips_y + y) * 2 + core

    for ref, core in ((own_ref, place_ref[0]), (other_ref, 1 - place_ref[0])):
        left = [
            jnp.concatenate([parts[step, owner(at, core)] for step in range(count)], axis=1)
            for at in range(chips_x * chips_y)
        ]
        out = dot(jnp.concatenate(left, axis=0), grads)
        ref[...] = out.astype(LOW).reshape(chips_x * chips_y, feats, -1)


def branch_grad(place, chips, rows, sent):
    count = len(sent)
    places = 2 * chips[0] * chips[1]
    more, width = sent[0].shape
    feats = (more - rows) * width // rows // places
    out = shape((places // 2, feats, width), LOW)
    return feed_run(
        partial(branch_grad_kernel, count, chips, rows),
        (1,),
        place,
        [fixed(sent[0].shape)] * count,
        [fixed(out.shape)] * 2,
        [out] * 2,
        sent,
        [pltpu.VMEM((count, places, feats, rows), LOW)],
        32,
    )


def by_kind(rows, count):
    here = HD // count
    return jnp.concatenate(
        [
            rows[(share * 3 + kind) * here : (share * 3 + kind + 1) * here]
            for kind in range(3)
            for share in range(count)
        ],
        axis=0,
    )


def joint_grad_kernel(
    grad_ref, rows_ref, weight_ref, gain_ref, shift_ref, out_ref, bias_ref, sums_ref, total, biases
):
    step = pl.program_id(0)
    count, pieces = grad_ref.shape[:2]
    grads = jnp.concatenate(
        [
            jnp.concatenate([grad_ref[share, piece] for piece in range(pieces)], axis=1)
            for share in range(count)
        ],
        axis=0,
    )
    added = dot(grads, rows_ref[...].reshape(grads.shape[1], -1))
    summed = jnp.sum(grads.astype(jnp.float32), axis=1, keepdims=True)

    @pl.when(step == 0)
    def _():
        total[...] = added
        biases[...] = summed

    @pl.when(step > 0)
    def _():
        total[...] += added
        biases[...] += summed

    @pl.when(step == pl.num_programs(0) - 1)
    def _():
        out = by_kind(total[...], count)
        bias = by_kind(biases[...], count)
        out_ref[...] = out.astype(LOW)
        bias_ref[...] = bias
        weight = weight_ref[...].astype(jnp.float32)
        shift_sum = jnp.sum(weight * bias, axis=0, keepdims=True)
        product = jnp.sum(weight * out, axis=0, keepdims=True)
        sums_ref[0:1, :] = (product - shift_sum * shift_ref[...]) / gain_ref[...]
        sums_ref[1:2, :] = shift_sum


def joint_grad(grads, gathered, weight, gain, shift, step=8):
    count, places, feats, rows = grads.shape
    width = gathered.shape[2]
    total = count * feats
    return run(
        joint_grad_kernel,
        (places // step,),
        [
            pl.BlockSpec((count, step, feats, rows), lambda i: (0, i, 0, 0)),
            pl.BlockSpec((step, rows, width), lambda i: (i, 0, 0)),
            whole(weight),
            whole(gain),
            whole(shift),
        ],
        [
            pl.BlockSpec((total, width), lambda i: (0, 0)),
            pl.BlockSpec((total, 1), lambda i: (0, 0)),
            pl.BlockSpec((2, width), lambda i: (0, 0)),
        ],
        [
            shape((total, width), LOW),
            shape((total, 1), jnp.float32),
            shape((2, width), jnp.float32),
        ],
        (grads, gathered, weight, gain, shift),
        scratch=[pltpu.VMEM((total, width), jnp.float32), pltpu.VMEM((total, 1), jnp.float32)],
    )


def input_kernel(part_ref, weight_ref, tokens_ref, gain_ref, d_resid_ref, out_ref, total):
    step = pl.program_id(0)
    added = dot(turned(part_ref[...]).astype(LOW), weight_ref[...])

    @pl.when(step == 0)
    def _():
        total[...] = added

    @pl.when(step > 0)
    def _():
        total[...] += added

    @pl.when(step == pl.num_programs(0) - 1)
    def _():
        normed, scale = norm_parts(tokens_ref[...].astype(jnp.float32))
        out_ref[...] = d_resid_ref[...] + norm_back(total[...], normed, scale, gain_ref[...])


def input_back(parts, weights, tokens, gain, d_resid, steps=6):
    feats, rows = parts.shape
    width = weights.shape[1]
    step = feats // steps
    return run(
        input_kernel,
        (steps,),
        [
            pl.BlockSpec((step, rows), lambda i: (i, 0)),
            pl.BlockSpec((step, width), lambda i: (i, 0)),
            whole(tokens),
            whole(gain),
            whole(d_resid),
        ],
        [pl.BlockSpec((rows, width), lambda i: (0, 0))],
        [shape((rows, width), jnp.float32)],
        (parts, weights, tokens, gain, d_resid),
        scratch=[pltpu.VMEM((rows, width), jnp.float32)],
    )[0]


ITEM = "z"
HEAD = ("x", "y", "c")
CORE = "c"


def moved(value, axis, steps):
    count = lax.axis_size(axis)
    return lax.ppermute(value, axis, [(place, (place + steps) % count) for place in range(count)])


def shifted(value, axis, steps):
    count = lax.axis_size(axis)
    initial, last = (max(0, -steps), min(count, count - steps))
    return lax.ppermute(value, axis, [(source, source + steps) for source in range(initial, last)])


def swapped(value, axis, step):
    pairs = [(place, place ^ step) for place in range(lax.axis_size(axis))]
    return lax.ppermute(value, axis, pairs)


def all_sum(value, axis):
    terms = around(value, axis)
    return (terms[0] + terms[2]) + (terms[1] + terms[3])


def around(value, axis):
    return [value] + [moved(value, axis, -step) for step in range(1, lax.axis_size(axis))]


def sum_back(values, axis):
    return [values[0]] + [
        moved(values[step], axis, step) for step in range(1, lax.axis_size(axis))
    ]


def own_half(value, bit, axis, step):
    count = value.shape[0] // 2
    own = lax.dynamic_slice_in_dim(value, bit * count, count)
    other = lax.dynamic_slice_in_dim(value, (1 - bit) * count, count)
    own = own.astype(jnp.float32) + swapped(other, axis, step).astype(jnp.float32)
    return own.astype(LOW)


def both_halves(value, bit, axis, step):
    other = swapped(value, axis, step)
    first = jnp.where(bit == 0, value, other)
    return jnp.concatenate([first, jnp.where(bit == 0, other, value)], axis=0)


def pair_sum(value, axis, step):
    value = value.astype(jnp.float32) + swapped(value, axis, step).astype(jnp.float32)
    return value.astype(LOW)


def step_sum(values, axis):
    terms = sum_back([values[step] for step in range(values.shape[0])], axis)
    return sum(term.astype(jnp.float32) for term in terms).astype(LOW)


def own_step(values, axis):
    own = values[0].astype(jnp.float32) + moved(values[1], axis, 1).astype(jnp.float32)
    return own.astype(LOW)


def head_swap(value):
    return lax.all_to_all(value, HEAD, split_axis=0, concat_axis=0, tiled=True)


def segment_flags(seg_counts):
    total_segs = seg_counts.shape[0]
    openings = jnp.cumsum(seg_counts) - seg_counts
    places = jnp.arange(total_segs, dtype=jnp.int32)
    opens_here = jnp.any((openings[:, None] == places[None, :]) & (seg_counts[:, None] > 0), axis=0)
    opens_before = jnp.concatenate([jnp.ones((1,), dtype=bool), opens_here[:-1]])
    one_back = jnp.logical_not(opens_here)
    two_back = one_back & jnp.logical_not(opens_before)
    return (one_back, two_back)


def local(
    tokens,
    cotangent,
    seg_counts,
    query_weight,
    key_weight,
    value_weight,
    query_bias,
    value_bias,
    out_weight,
    out_bias,
    first_gain,
    first_shift,
    second_gain,
    second_shift,
    up_weight,
    up_bias,
    down_weight,
    down_bias,
):
    rows, width = tokens.shape
    heads = lax.axis_size(HEAD)
    item_place = lax.axis_index(ITEM)
    group_rows = rows * heads
    seg_local = group_rows // SEG
    feats = query_weight.shape[0]
    units = up_weight.shape[0]
    hidden_here = units * heads

    def row(vector):
        return vector.reshape(1, -1)

    tokens_f = tokens.astype(jnp.float32)
    inputs_one = layer_norm(tokens_f, first_gain, first_shift).astype(LOW)
    first = jnp.concatenate([inputs_one, out_weight], axis=0)
    gathered = lax.all_gather(first, HEAD, axis=0, tiled=True).reshape(heads, -1, width)
    second = jnp.concatenate([up_weight, down_weight], axis=0)
    feed_weights = lax.all_gather(second, HEAD, axis=0, tiled=True).reshape(heads, -1, width)
    cots = around(cotangent, ITEM)
    joint_weight = jnp.concatenate([query_weight, key_weight, value_weight], axis=0)
    joint_bias = jnp.concatenate([query_bias, jnp.zeros_like(query_bias), value_bias])

    one_back, two_back = segment_flags(seg_counts)
    flags = jnp.stack([two_back, one_back], axis=1).astype(jnp.int32)
    flags = lax.dynamic_slice_in_dim(flags, item_place * seg_local, seg_local).reshape(-1)

    gathered, cots = lax.optimization_barrier((gathered, cots))
    query, kv, turned_all = project(gathered, rows, joint_weight, row(joint_bias))
    own_kept = kv.reshape(seg_local, SEG, 2 * HD)[:, SEG - KEPT :]
    table = jnp.concatenate([shifted(own_kept, ITEM, 1), own_kept], axis=0)
    prefix = jnp.concatenate(
        [table[seg_local - 2 : 2 * seg_local - 2], table[seg_local - 1 : 2 * seg_local - 1]], axis=1
    )
    attended, log_sums = attend(flags, turned_all, kv, prefix, rows)
    attended_own = head_swap(attended)
    resid, inputs_two = out_project(
        attended_own, gathered, rows // feats, tokens, row(out_bias), row(second_gain), row(second_shift)
    )

    joint_turn = lax.optimization_barrier((joint_weight, resid))[0]
    joint_full = lax.all_gather(joint_turn, HEAD, axis=0, tiled=True)
    norms = around(inputs_two, ITEM)
    chips = (lax.axis_size("x"), lax.axis_size("y"))
    place = jnp.stack([lax.axis_index(axis) for axis in (CORE, "x", "y", ITEM)]).astype(jnp.int32)
    d_act, cots = feed_d_act(place, chips, cots, feed_weights)
    cots = [cots, moved(cots, CORE, 1)]
    bias_here = lax.dynamic_slice_in_dim(up_bias, item_place * hidden_here, hidden_here)
    backs, (norms, kept, sent, up_bias_part) = feed(
        place, chips, norms, feed_weights, bias_here.reshape(heads, 1, units), d_act
    )
    backs = sum_back(backs, ITEM)
    norms = [norms, moved(norms, CORE, 1)]
    mixeds, feed_parts = feed_grad(
        place, chips, len(backs), norms, cots, kept, sent, moved(sent, CORE, 1), feed_weights
    )
    backs, mixeds = lax.optimization_barrier((backs, mixeds))
    d_resid, sums_two, d_parts, sent = branch_back(
        place, resid, cotangent, row(second_gain), gathered, rows // feats, attended_own, backs
    )
    sent = sum_back(sent, ITEM)
    d_attended = head_swap(d_parts)
    feed_parts = lax.optimization_barrier((feed_parts, d_resid))[0]
    feed_grads = lax.psum_scatter(
        feed_parts.reshape(-1, width), ("x", "y"), scatter_dimension=0, tiled=True
    )
    d_attended, mixeds = lax.optimization_barrier((d_attended, mixeds))
    d_prefix = prefix_back(
        flags, turned_all, query, d_attended, attended, log_sums, prefix, rows
    )[0]
    older, newer = d_prefix[:, :KEPT], d_prefix[:, KEPT:]
    spread = jnp.pad(older, ((seg_local - 2, 2), (0, 0), (0, 0)))
    spread = spread + jnp.pad(newer, ((seg_local - 1, 1), (0, 0), (0, 0)))
    returned = shifted(spread[:seg_local], ITEM, -1)
    joint_grads, kept_grads = attend_back(
        flags, turned_all, query, d_attended, attended, log_sums, prefix, kv, rows, 1
    )
    mixeds, kept_grads = lax.optimization_barrier((mixeds, kept_grads))
    near, far = jnp.stack(mixeds[:2]), moved(jnp.stack(mixeds[2:]), ITEM, 2)
    returned, kept_grads, joint_full = lax.optimization_barrier((returned, kept_grads, joint_full))
    joint_grads = add_returned(joint_grads, kept_grads, spread[seg_local:] + returned)
    grads_own = head_swap(joint_grads[0]).reshape(-1, rows)
    joint_part, bias_part, sums_one = joint_grad(
        joint_grads, gathered, joint_weight, row(first_gain), row(first_shift)
    )
    high, low = item_place // 2, item_place % 2
    joint_part, sums_one, sent = lax.optimization_barrier((joint_part, sums_one, sent))
    out_part, out_other = branch_grad(place, chips, rows, sent)
    out_part = out_part.astype(jnp.float32) + moved(out_other, CORE, 1).astype(jnp.float32)
    joint_part = own_half(joint_part.reshape(4, -1, width), high, ITEM, 2)
    small = jnp.concatenate([row(up_bias_part), sums_two, sums_one], axis=0)
    small = small + swapped(small, CORE, 1)
    grads_own, out_part, joint_part, small = lax.optimization_barrier(
        (grads_own, out_part.astype(LOW), joint_part, small)
    )
    input_grad = input_back(grads_own, joint_full, tokens, row(first_gain), d_resid)
    near, far, small = lax.optimization_barrier((near, far, small))
    mixed = (near.astype(jnp.float32) + far.astype(jnp.float32)).astype(LOW)
    mixed = own_step(mixed, ITEM)
    out_part = step_sum(out_part.reshape(chips[0], -1, width), "x")
    joint_part = own_half(joint_part, low, ITEM, 1)
    small = small + swapped(small, "x", 2)
    input_grad, out_part, joint_part, small = lax.optimization_barrier(
        (input_grad, out_part, joint_part, small)
    )
    out_part = step_sum(out_part.reshape(chips[1], -1, width), "y")
    joint_part = both_halves(joint_part, low, ITEM, 1)
    small = small + swapped(small, "x", 1)
    out_part, joint_part, small, mixed = lax.optimization_barrier(
        (out_part, joint_part, small, mixed)
    )
    out_part = both_halves(out_part, low, ITEM, 1)
    joint_sums = both_halves(joint_part, high, ITEM, 2).reshape(-1, width).astype(jnp.float32)
    small = all_sum(small, "y")
    out_part, joint_sums, small, feed_grads = lax.optimization_barrier(
        (out_part, joint_sums, small, feed_grads)
    )
    out_sum = both_halves(out_part, high, ITEM, 2).astype(jnp.float32)
    bias_part = jnp.pad(row(bias_part), ((0, 0), (0, width - bias_part.size)))
    terms = around(jnp.concatenate([small, bias_part], axis=0), ITEM)
    feed_grads = feed_grads.astype(jnp.float32)
    mixed_out = (resid + mixed.astype(jnp.float32) + down_bias).astype(LOW)
    small = (terms[0][1:] + terms[2][1:]) + (terms[1][1:] + terms[3][1:])
    bias_sums = small[6, : 3 * feats]
    up_bias_grad = jnp.stack([term[0] for term in terms + terms])
    up_bias_grad = lax.dynamic_slice_in_dim(
        up_bias_grad, lax.axis_size(ITEM) - item_place, lax.axis_size(ITEM), 0
    ).reshape(-1)
    early_rows, late = small[:4], small[4:6]
    return (
        mixed_out,
        input_grad,
        joint_sums[:feats],
        joint_sums[feats : 2 * feats],
        joint_sums[2 * feats :],
        bias_sums[:feats],
        bias_sums[2 * feats : 3 * feats],
        out_sum,
        early_rows[2],
        late[0],
        late[1],
        early_rows[0],
        early_rows[1],
        feed_grads[:units],
        up_bias_grad,
        feed_grads[units:],
        early_rows[3],
    )


def solution(mesh):
    sizes = (mesh.shape["item"], 4, mesh.shape["head"] // 8, 2)
    fine = Mesh(mesh.devices.reshape(sizes), (ITEM, *HEAD))
    split = P((ITEM, *HEAD), None)
    by_head = P(HEAD, None)
    return jax.shard_map(
        local,
        mesh=fine,
        in_specs=(
            split,
            split,
            P(),
            by_head,
            by_head,
            by_head,
            P(HEAD),
            P(HEAD),
            by_head,
            P(),
            P(),
            P(),
            P(),
            P(),
            split,
            P(),
            split,
            P(),
        ),
        out_specs=(
            split,
            split,
            by_head,
            by_head,
            by_head,
            P(HEAD),
            P(HEAD),
            by_head,
            P(),
            P(),
            P(),
            P(),
            P(),
            split,
            P(),
            split,
            P(),
        ),
        check_vma=False,
    )
```

```python
from functools import partial

import jax
import jax.numpy as jnp
from jax import lax
from jax.experimental import pallas as pl
from jax.experimental.pallas import tpu as pltpu
from jax.sharding import Mesh
from jax.sharding import PartitionSpec as P

HD = 64
NSUM = 50
SEG = 2048
SPAN = 512
KEPT = 64
EPSILON = 1e-05
MASKED = -1e30
SCALE = HD ** (-0.5)
MIB = 1 << 20
COST = 1 << 20
LOW = jnp.bfloat16


def dot(left, right):
    return jnp.dot(left, right, preferred_element_type=jnp.float32)


def dot_cols(left, right):
    return lax.dot_general(
        left, right, (((1,), (1,)), ((), ())), preferred_element_type=jnp.float32
    )


def turned(value):
    return value.astype(jnp.float32).T


def norm_parts(row_data):
    row_mean = jnp.mean(row_data, axis=-1, keepdims=True)
    centred = row_data - row_mean
    row_var = jnp.mean(centred * centred, axis=-1, keepdims=True)
    scale = lax.rsqrt(row_var + EPSILON)
    return centred * scale, scale


def norm_back(grad, normed, scale, gain):
    scaled = grad * gain
    return scale * (
        scaled
        - jnp.mean(scaled, axis=-1, keepdims=True)
        - normed * jnp.mean(scaled * normed, axis=-1, keepdims=True)
    )


def layer_norm(row_data, gain, shift):
    return norm_parts(row_data)[0] * gain + shift


def run(body, grid, in_specs, out_specs, out_shape, operands, scratch=(), vmem=32, aliases=None):
    return pl.pallas_call(
        body,
        grid=grid,
        in_specs=in_specs,
        out_specs=out_specs,
        out_shape=out_shape,
        scratch_shapes=scratch,
        compiler_params=pltpu.CompilerParams(
            dimension_semantics=("arbitrary",) * len(grid), vmem_limit_bytes=vmem * MIB
        ),
        input_output_aliases=aliases or {},
        cost_estimate=pl.CostEstimate(flops=COST, bytes_accessed=COST, transcendentals=0),
    )(*operands)


def shape(dims, kind):
    return jax.ShapeDtypeStruct(dims, kind)


def whole(item):
    return pl.BlockSpec(item.shape, lambda *_: (0,) * len(item.shape))


def project_kernel(rows_ref, weight_ref, bias_ref, query_ref, kv_ref, turned_ref):
    rows = rows_ref[...].reshape(-1, rows_ref.shape[2])
    joint = dot_cols(rows, weight_ref[...]) + bias_ref[...]
    query_ref[...] = joint[:, :HD].astype(LOW)
    kv_ref[...] = joint[:, HD:].astype(LOW)
    turned_ref[...] = joint.T.astype(LOW)


def project(gathered, rows_here, weight, bias, span=2 * SPAN):
    places, _, width = gathered.shape
    total = places * rows_here
    step = span // rows_here
    return run(
        project_kernel,
        (total // span,),
        [
            pl.BlockSpec((step, rows_here, width), lambda i: (i, 0, 0)),
            whole(weight),
            whole(bias),
        ],
        [
            pl.BlockSpec((span, HD), lambda i: (i, 0)),
            pl.BlockSpec((span, 2 * HD), lambda i: (i, 0)),
            pl.BlockSpec((3 * HD, span), lambda i: (0, i)),
        ],
        [
            shape((total, HD), LOW),
            shape((total, 2 * HD), LOW),
            shape((3 * HD, total), LOW),
        ],
        (gathered, weight, bias),
    )


def prefix_seen(flags_ref, seg, columns):
    place = lax.broadcasted_iota(jnp.int32, (2 * KEPT, columns), 0)
    older = place < KEPT
    slot = jnp.where(older, place, place - KEPT) >= KEPT - NSUM
    flag = jnp.where(older, flags_ref[2 * seg], flags_ref[2 * seg + 1])
    return slot & (flag > 0)


def causal_seen():
    shape_here = (SPAN, SPAN)
    return lax.broadcasted_iota(jnp.int32, shape_here, 0) <= lax.broadcasted_iota(
        jnp.int32, shape_here, 1
    )


def above(block):
    return jnp.concatenate([block, jnp.zeros_like(block)], axis=0)


def below(block):
    return jnp.concatenate([jnp.zeros_like(block), block], axis=0)


def at_block(index):
    return pl.ds(pl.multiple_of(index * SPAN, SPAN), SPAN)


def attend_kernel(flags_ref, query_ref, turned_ref, kv_ref, prefix_ref, out_ref, log_ref):
    seg, block = pl.program_id(0), pl.program_id(1)
    query = above((query_ref[...].astype(jnp.float32) * SCALE).astype(LOW))
    own = at_block(block)
    scores = dot(kv_ref[own, :], query)
    scores = jnp.where(causal_seen(), scores, MASKED)
    top = jnp.max(scores, axis=0, keepdims=True)
    probs = jnp.exp(scores - top)
    total = jnp.sum(probs, axis=0, keepdims=True)
    mixed = dot(turned_ref[2 * HD :, own], probs.astype(LOW))

    def add(carry, scores, values):
        top, total, mixed = carry
        fresh = jnp.maximum(top, jnp.max(scores, axis=0, keepdims=True))
        fade = jnp.exp(top - fresh)
        probs = jnp.exp(scores - fresh)
        total = total * fade + jnp.sum(probs, axis=0, keepdims=True)
        return fresh, total, mixed * fade + dot(values, probs.astype(LOW))

    prefix = prefix_ref[0]
    scores = jnp.where(prefix_seen(flags_ref, seg, SPAN), dot(prefix, query), MASKED)
    carry = add((top, total, mixed), scores, turned(prefix)[HD:].astype(LOW))

    def step(index, carry):
        here = at_block(index)
        return add(carry, dot(kv_ref[here, :], query), turned_ref[2 * HD :, here])

    top, total, mixed = lax.fori_loop(0, block, step, carry)
    mixed = (mixed / total).astype(LOW)
    rows = out_ref.shape[2]
    for piece in range(SPAN // rows):
        out_ref[piece] = mixed[:, piece * rows : (piece + 1) * rows]
    log_ref[0] = top + jnp.log(total)


def attend(flags, turned_all, kv, prefix, rows_here):
    total = kv.shape[0]
    blocks = SEG // SPAN
    step = SPAN // rows_here
    return run(
        attend_kernel,
        (total // SEG, blocks),
        [
            pl.BlockSpec(memory_space=pltpu.SMEM),
            pl.BlockSpec((HD, SPAN), lambda s, i: (0, s * blocks + i)),
            pl.BlockSpec((3 * HD, SEG), lambda s, i: (0, s)),
            pl.BlockSpec((SEG, 2 * HD), lambda s, i: (s, 0)),
            pl.BlockSpec((1, 2 * KEPT, 2 * HD), lambda s, i: (s, 0, 0)),
        ],
        [
            pl.BlockSpec((step, HD, rows_here), lambda s, i: (s * blocks + i, 0, 0)),
            pl.BlockSpec((1, 1, SPAN), lambda s, i: (s * blocks + i, 0, 0)),
        ],
        [
            shape((total // rows_here, HD, rows_here), LOW),
            shape((total // SPAN, 1, SPAN), jnp.float32),
        ],
        (flags, turned_all, turned_all, kv, prefix),
    )


def side_by_side(ref):
    return jnp.concatenate([ref[piece] for piece in range(ref.shape[0])], axis=1)


def beside(block, place):
    zero = jnp.zeros_like(block)
    return jnp.concatenate([block, zero] if place == 0 else [zero, block], axis=1)


def query_side(query_ref, rows_ref, grad_ref, out_ref, log_ref):
    query = above((query_ref[...].astype(jnp.float32) * SCALE).astype(LOW))
    grad = side_by_side(grad_ref)
    mean = jnp.sum(
        grad.astype(jnp.float32) * side_by_side(out_ref).astype(jnp.float32),
        axis=0,
        keepdims=True,
    )
    query_rows = beside((rows_ref[...].astype(jnp.float32) * SCALE).astype(LOW), 0)
    grad_rows = beside(turned(grad).astype(LOW), 1)
    return query, below(grad), mean, log_ref[0], query_rows, grad_rows


def key_side(keys, side, seen):
    query, grad, mean, log_sum, query_rows, grad_rows = side
    probs = jnp.exp(dot(keys, query) - log_sum)
    if seen is not None:
        probs = jnp.where(seen, probs, 0.0)
    d_scores = (probs * (dot(keys, grad) - mean)).astype(LOW)
    return probs.astype(LOW), d_scores


def prefix_back_kernel(
    flags_ref, query_ref, rows_ref, grad_ref, out_ref, log_ref, prefix_ref, sum_ref
):
    seg, block = pl.program_id(0), pl.program_id(1)
    side = query_side(query_ref, rows_ref, grad_ref, out_ref, log_ref)
    probs, d_scores = key_side(prefix_ref[0], side, prefix_seen(flags_ref, seg, SPAN))
    part = dot(d_scores, side[4]) + dot(probs, side[5])

    @pl.when(block == 0)
    def _():
        sum_ref[0] = part

    @pl.when(block > 0)
    def _():
        sum_ref[0] += part


def store_shares(grads_ref, piece, part, columns):
    here = HD // grads_ref.shape[0]
    for share in range(grads_ref.shape[0]):
        for kind in (1, 2):
            first = (kind - 1) * HD + share * here
            grads_ref[share, piece, kind * here : (kind + 1) * here, columns] = part[
                first : first + here
            ]


def attend_back_kernel(
    flags_ref,
    query_ref,
    rows_ref,
    grad_ref,
    out_ref,
    log_ref,
    prefix_ref,
    turned_ref,
    kv_ref,
    grads_ref,
    kept_ref,
    kv_grad,
):
    seg, block = pl.program_id(0), pl.program_id(1)

    @pl.when(block == 0)
    def _():
        kv_grad[...] = jnp.zeros_like(kv_grad)

    side = query_side(query_ref, rows_ref, grad_ref, out_ref, log_ref)
    prefix = prefix_ref[0]
    _, d_scores = key_side(prefix, side, prefix_seen(flags_ref, seg, SPAN))
    query_grad = dot(turned(prefix)[:HD].astype(LOW), d_scores)

    def add(here, query_grad, seen):
        probs, d_scores = key_side(kv_ref[here, :], side, seen)
        kv_grad[here, :] += dot(d_scores, side[4]) + dot(probs, side[5])
        return query_grad + dot(turned_ref[HD : 2 * HD, here], d_scores)

    query_grad = add(at_block(block), query_grad, causal_seen())
    query_grad = lax.fori_loop(
        0, block, lambda index, grad: add(at_block(index), grad, None), query_grad
    )
    query_grad = (query_grad * SCALE).astype(LOW)
    rows = grads_ref.shape[3]
    step = SPAN // rows
    for piece in range(step):
        part = query_grad[:, piece * rows : (piece + 1) * rows]
        for share in range(grads_ref.shape[0]):
            here = HD // grads_ref.shape[0]
            grads_ref[share, block * step + piece, :here, :] = part[share * here : (share + 1) * here]

    @pl.when(block == pl.num_programs(1) - 1)
    def _():
        for piece in range(SEG // rows):
            part = kv_grad[piece * rows : (piece + 1) * rows, :].T.astype(LOW)
            store_shares(grads_ref, piece, part, slice(None))
        kept_ref[0] = kv_grad[SEG - KEPT :, :]


def attend_back_specs(rows_here):
    blocks = SEG // SPAN
    step = SPAN // rows_here
    return [
        pl.BlockSpec(memory_space=pltpu.SMEM),
        pl.BlockSpec((HD, SPAN), lambda s, i: (0, s * blocks + i)),
        pl.BlockSpec((SPAN, HD), lambda s, i: (s * blocks + i, 0)),
        pl.BlockSpec((step, HD, rows_here), lambda s, i: (s * blocks + i, 0, 0)),
        pl.BlockSpec((step, HD, rows_here), lambda s, i: (s * blocks + i, 0, 0)),
        pl.BlockSpec((1, 1, SPAN), lambda s, i: (s * blocks + i, 0, 0)),
        pl.BlockSpec((1, 2 * KEPT, 2 * HD), lambda s, i: (s, 0, 0)),
    ]


def prefix_back(flags, turned_all, query, grad, out, log_sums, prefix, rows_here):
    total = query.shape[0]
    return run(
        prefix_back_kernel,
        (total // SEG, SEG // SPAN),
        attend_back_specs(rows_here),
        [pl.BlockSpec((1, 2 * KEPT, 2 * HD), lambda s, i: (s, 0, 0))],
        [shape(prefix.shape, jnp.float32)],
        (flags, turned_all, query, grad, out, log_sums, prefix),
    )


def attend_back(flags, turned_all, query, grad, out, log_sums, prefix, kv, rows_here, count):
    total = query.shape[0]
    pieces = SEG // rows_here
    return run(
        attend_back_kernel,
        (total // SEG, SEG // SPAN),
        attend_back_specs(rows_here)
        + [
            pl.BlockSpec((3 * HD, SEG), lambda s, i: (0, s)),
            pl.BlockSpec((SEG, 2 * HD), lambda s, i: (s, 0)),
        ],
        [
            pl.BlockSpec(
                (count, pieces, 3 * HD // count, rows_here), lambda s, i: (0, s, 0, 0)
            ),
            pl.BlockSpec((1, KEPT, 2 * HD), lambda s, i: (s, 0, 0)),
        ],
        [
            shape((count, total // rows_here, 3 * HD // count, rows_here), LOW),
            shape((total // SEG, KEPT, 2 * HD), jnp.float32),
        ],
        (flags, turned_all, query, grad, out, log_sums, prefix, turned_all, kv),
        scratch=[pltpu.VMEM((SEG, 2 * HD), jnp.float32)],
    )


def returned_kernel(grads_ref, kept_ref, returned_ref, out_ref):
    out_ref[...] = grads_ref[...]
    part = (kept_ref[0] + returned_ref[0]).T.astype(LOW)
    store_shares(out_ref, 0, part, slice(out_ref.shape[3] - KEPT, None))


def add_returned(grads, kept, returned):
    count, places, feats, rows = grads.shape
    segs = kept.shape[0]
    last = places // segs
    grad_spec = pl.BlockSpec((count, 1, feats, rows), lambda s: (0, s * last + last - 1, 0, 0))
    kept_spec = pl.BlockSpec((1, KEPT, 2 * HD), lambda s: (s, 0, 0))
    return run(
        returned_kernel,
        (segs,),
        [grad_spec, kept_spec, kept_spec],
        [grad_spec],
        [shape(grads.shape, LOW)],
        (grads, kept, returned),
        aliases={0: 0},
    )[0]


def out_kernel(
    part_ref, weight_ref, tokens_ref, bias_ref, gain_ref, shift_ref, resid_ref, two_ref, total
):
    step = pl.program_id(0)
    rows = part_ref.shape[2]
    part = turned(part_ref[...].reshape(-1, rows)).astype(LOW)
    added = dot(part, weight_ref[...].reshape(part.shape[1], -1))

    @pl.when(step == 0)
    def _():
        total[...] = added

    @pl.when(step > 0)
    def _():
        total[...] += added

    @pl.when(step == pl.num_programs(0) - 1)
    def _():
        resid = tokens_ref[...].astype(jnp.float32) + total[...] + bias_ref[...]
        resid_ref[...] = resid
        two_ref[...] = layer_norm(resid, gain_ref[...], shift_ref[...]).astype(LOW)


def out_project(parts, gathered, at, tokens, bias, gain, shift, step=4):
    places, feats, rows = parts.shape
    width = gathered.shape[2]
    return run(
        out_kernel,
        (places // step,),
        [
            pl.BlockSpec((step, feats, rows), lambda i: (i, 0, 0)),
            pl.BlockSpec((step, feats, width), lambda i: (i, at, 0)),
            whole(tokens),
            whole(bias),
            whole(gain),
            whole(shift),
        ],
        [pl.BlockSpec((rows, width), lambda i: (0, 0))] * 2,
        [shape((rows, width), jnp.float32), shape((rows, width), LOW)],
        (parts, gathered, tokens, bias, gain, shift),
        scratch=[pltpu.VMEM((rows, width), jnp.float32)],
    )


def owner_maps(chips, at):
    def of(core_step, chip):
        return lambda i, place: at((i * chips[1] + chip) * 2 + lax.rem(place[0] + core_step, 2))

    return [of(core_step, chip) for core_step in (0, 1) for chip in range(chips[1])]


def own_map(index):
    return lambda i, place: index(i)


def fixed(dims):
    return pl.BlockSpec(
        dims, own_map(lambda i: (0,) * len(dims)), pipeline_mode=pl.Buffered(buffer_count=1)
    )


def feed_run(body, chips, place, in_specs, out_specs, out_shape, operands, scratch, vmem):
    return pl.pallas_call(
        body,
        grid_spec=pltpu.PrefetchScalarGridSpec(
            num_scalar_prefetch=1,
            grid=(chips[0],),
            in_specs=in_specs,
            out_specs=out_specs,
            scratch_shapes=scratch,
        ),
        out_shape=out_shape,
        compiler_params=pltpu.CompilerParams(
            dimension_semantics=("arbitrary",), vmem_limit_bytes=vmem * MIB
        ),
        cost_estimate=pl.CostEstimate(flops=COST, bytes_accessed=COST, transcendentals=0),
    )(place, *operands)


def stacked(refs, axis=0):
    return jnp.concatenate([ref[0] for ref in refs], axis=axis)


def pile(refs, into):
    rows = refs[0].shape[0]
    for at, ref in enumerate(refs):
        into[at * rows : (at + 1) * rows, :] = ref[...]


def spread(source, refs):
    rows = refs[0].shape[0]
    for at, ref in enumerate(refs):
        ref[...] = source[at * rows : (at + 1) * rows, :].astype(ref.dtype)


def take(refs, *counts):
    refs = list(refs)
    return [[refs.pop(0) for _ in range(count)] for count in counts] + [refs]


def d_act_kernel(count, owners, place_ref, *refs):
    cot_refs, weight_refs, (out_ref, cots) = take(refs, count, owners)

    @pl.when(pl.program_id(0) == 0)
    def _():
        pile(cot_refs, cots)

    out_ref[...] = dot_cols(cots[...], stacked(weight_refs))


def feed_d_act(place, chips, cots, weights):
    count = len(cots)
    rows, width = cots[0].shape
    places, both, _ = weights.shape
    units = both // 2
    total = count * rows
    owners = 2 * chips[1]
    step = owners * units
    return feed_run(
        partial(d_act_kernel, count, owners),
        chips,
        place,
        [fixed((rows, width))] * count
        + [
            pl.BlockSpec((1, units, width), at)
            for at in owner_maps(chips, lambda owner: (owner, 1, 0))
        ],
        [pl.BlockSpec((total, step), own_map(lambda i: (0, i))), fixed((total, width))],
        [shape((total, places * units), jnp.float32), shape((total, width), LOW)],
        (*cots, *[weights] * owners),
        [],
        32,
    )


def feed_kernel(count, chips, place_ref, *refs):
    owners = 2 * chips[1]
    norm_refs, weight_refs, bias_refs, (d_act_ref,), back_refs, refs = take(
        refs, count, owners, owners, 1, count
    )
    norms, kept_ref, sent_ref, bias_sum_ref, back = refs
    step = pl.program_id(0)

    @pl.when(step == 0)
    def _():
        pile(norm_refs, norms)
        back[...] = jnp.zeros_like(back)

    up = stacked(weight_refs)
    pre = dot_cols(norms[...], up) + stacked(bias_refs, axis=1)
    square = pre * pre
    bent = jnp.tanh(0.7978845608 * (pre + 0.044715 * (square * pre)))
    half = 0.5 * (1.0 + bent)
    slope = half + 0.5 * pre * (1.0 - bent * bent) * (
        0.7978845608 * (1.0 + 3.0 * 0.044715 * square)
    )
    d_pre = (d_act_ref[...] * slope).astype(LOW)
    act = (pre * half).astype(LOW)
    own = act.shape[1] // 2
    kept_ref[0] = act[:, :own]
    kept_ref[1] = d_pre[:, :own]
    sent_ref[0] = act[:, own:]
    sent_ref[1] = d_pre[:, own:]
    bias_sums = jnp.sum(d_pre.astype(jnp.float32), axis=0, keepdims=True)
    units = weight_refs[0].shape[1]
    for at, index in enumerate(owner_maps(chips, lambda owner: owner)):
        bias_sum_ref[index(step, place_ref)] = bias_sums[:, at * units : (at + 1) * units]
    back[...] += dot(d_pre, up)

    @pl.when(step == pl.num_programs(0) - 1)
    def _():
        spread(back, back_refs)


def feed(place, chips, norms, weights, bias, d_act):
    count = len(norms)
    rows, width = norms[0].shape
    places, both, _ = weights.shape
    units = both // 2
    total = count * rows
    owners = 2 * chips[1]
    step = owners * units
    pair_spec = pl.BlockSpec((2, total, step // 2), own_map(lambda i: (0, 0, i)))
    results = feed_run(
        partial(feed_kernel, count, chips),
        chips,
        place,
        [fixed((rows, width))] * count
        + [
            pl.BlockSpec((1, units, width), at)
            for at in owner_maps(chips, lambda owner: (owner, 0, 0))
        ]
        + [
            pl.BlockSpec((1, 1, units), at)
            for at in owner_maps(chips, lambda owner: (owner, 0, 0))
        ]
        + [pl.BlockSpec((total, step), own_map(lambda i: (0, i)))],
        [pl.BlockSpec((rows, width), own_map(lambda i: (0, 0)))] * count
        + [fixed((total, width)), pair_spec, pair_spec, fixed((places, 1, units))],
        [shape((rows, width), LOW)] * count
        + [shape((total, width), LOW)]
        + [shape((2, total, places * units // 2), LOW)] * 2
        + [shape((places, 1, units), jnp.float32)],
        (*norms, *[weights] * owners, *[bias] * owners, d_act),
        [pltpu.VMEM((total, width), jnp.float32)],
        40,
    )
    return results[:count], results[count:]


def feed_grad_kernel(count, owners, place_ref, *refs):
    norm_refs, cot_refs, pair_refs, weight_refs, mixed_refs, (out_ref, mixed) = take(
        refs, 2, 2, 3, owners, count
    )
    kept_ref, sent_ref, other_ref = pair_refs
    step = pl.program_id(0)
    units = weight_refs[0].shape[1]

    @pl.when(step == 0)
    def _():
        mixed[...] = jnp.zeros_like(mixed)

    act = jnp.concatenate([kept_ref[0], sent_ref[0]], axis=1)
    mixed[...] += dot(act, stacked(weight_refs))

    def grad(at, rows):
        total = dot(turned(kept_ref[at]).astype(LOW), rows[0][...])
        total += dot(turned(other_ref[at]).astype(LOW), rows[1][...])
        return total.astype(LOW).reshape(out_ref.shape[0], units, -1)

    out_ref[:, :units, :] = grad(1, norm_refs)
    out_ref[:, units:, :] = grad(0, cot_refs)

    @pl.when(step == pl.num_programs(0) - 1)
    def _():
        spread(mixed, mixed_refs)


def feed_grad(place, chips, count, norms, cots, kept, sent, other, weights):
    total, width = norms[0].shape
    rows = total // count
    units = weights.shape[1] // 2
    owners = 2 * chips[1]
    pair_spec = pl.BlockSpec((2, total, owners * units // 2), own_map(lambda i: (0, 0, i)))
    results = feed_run(
        partial(feed_grad_kernel, count, owners),
        chips,
        place,
        [fixed((total, width))] * 4
        + [pair_spec] * 3
        + [
            pl.BlockSpec((1, units, width), at)
            for at in owner_maps(chips, lambda owner: (owner, 1, 0))
        ],
        [pl.BlockSpec((rows, width), own_map(lambda i: (0, 0)))] * count
        + [pl.BlockSpec((chips[1], 2 * units, width), own_map(lambda i: (i, 0, 0)))],
        [shape((rows, width), LOW)] * count
        + [shape((chips[0] * chips[1], 2 * units, width), LOW)],
        (*norms, *cots, kept, sent, other, *[weights] * owners),
        [pltpu.VMEM((total, width), jnp.float32)],
        48,
    )
    return results[:count], results[count]


def branch_kernel(count, place_ref, *refs):
    (resid_ref, cot_ref, gain_ref, weight_ref, part_ref), back_refs, refs = take(refs, 5, count)
    (d_resid_ref, sums_ref, parts_ref), sent_refs, (d_branch_ref,) = take(refs, 3, count)
    step = pl.program_id(0)

    @pl.when(step == 0)
    def _():
        d_two = sum(ref[...].astype(jnp.float32) for ref in back_refs)
        normed, scale = norm_parts(resid_ref[...])
        cot = cot_ref[...].astype(jnp.float32)
        d_resid = cot + norm_back(d_two, normed, scale, gain_ref[...])
        d_branch = d_resid.astype(LOW)
        d_resid_ref[...] = d_resid
        d_branch_ref[...] = d_branch
        sums_ref[0:1, :] = jnp.sum(d_two * normed, axis=0, keepdims=True)
        sums_ref[1:2, :] = jnp.sum(d_two, axis=0, keepdims=True)
        sums_ref[2:3, :] = jnp.sum(d_branch.astype(jnp.float32), axis=0, keepdims=True)
        sums_ref[3:4, :] = jnp.sum(cot, axis=0, keepdims=True)

    width = weight_ref.shape[2]
    part = dot_cols(weight_ref[...].reshape(-1, width), d_branch_ref[...])
    parts_ref[...] = part.reshape(parts_ref.shape).astype(LOW)

    @pl.when(step == pl.num_programs(0) - 1)
    def _():
        places, feats, rows = part_ref.shape
        share = feats // count
        more = places * share * rows // width
        for at, ref in enumerate(sent_refs):
            first = lax.rem(place_ref[3] + at, count) * share
            taken = part_ref[:, pl.ds(pl.multiple_of(first, share), share), :]
            taken = taken.reshape(places * share, rows)
            ref[:rows, :] = d_branch_ref[...]
            ref[rows:, :] = jnp.concatenate(
                [taken[more * at : more * (at + 1)] for at in range(width // rows)], axis=1
            )


def branch_back(place, resid, cotangent, gain, gathered, at, attended, backs, step=4):
    rows, width = resid.shape
    places, feats, _ = attended.shape
    count = len(backs)
    row_spec = pl.BlockSpec((rows, width), lambda i: (0, 0))
    sent = shape((rows + places * feats // count * rows // width, width), LOW)
    results = run(
        partial(branch_kernel, count),
        (places // step,),
        [
            pl.BlockSpec(memory_space=pltpu.SMEM),
            row_spec,
            row_spec,
            whole(gain),
            pl.BlockSpec((step, feats, width), lambda i: (i, at, 0)),
            whole(attended),
        ]
        + [row_spec] * count,
        [
            row_spec,
            pl.BlockSpec((4, width), lambda i: (0, 0)),
            pl.BlockSpec((step, feats, rows), lambda i: (i, 0, 0)),
        ]
        + [whole(sent)] * count,
        [
            shape((rows, width), jnp.float32),
            shape((4, width), jnp.float32),
            shape((places, feats, rows), LOW),
        ]
        + [sent] * count,
        (place, resid, cotangent, gain, gathered, attended, *backs),
        scratch=[pltpu.VMEM((rows, width), LOW)],
    )
    return (*results[:3], results[3:])


SMALL = 8


def packed(small):
    rounded = small.astype(LOW)
    return jnp.concatenate([rounded, (small - rounded.astype(jnp.float32)).astype(LOW)], axis=0)


def unpacked(rows):
    rows = rows.astype(jnp.float32)
    return rows[:SMALL] + rows[SMALL:]


def even_sum(terms):
    return (terms[0] + terms[2]) + (terms[1] + terms[3])


def branch_grad_kernel(count, chips, rows, place_ref, *refs):
    sent_refs, small_refs, (own_ref, other_ref, small_ref, parts) = take(refs, count, 3)
    chips_x, chips_y = chips
    places, feats = parts.shape[1:3]
    for at, ref in enumerate(sent_refs):
        taken = ref[rows:, :]
        taken = [taken[:, rows * at : rows * (at + 1)] for at in range(taken.shape[1] // rows)]
        parts[at] = jnp.concatenate(taken, axis=0).reshape(places, feats, rows)
    grads = jnp.concatenate([ref[:rows, :] for ref in sent_refs], axis=0)

    def owner(at, core):
        x = lax.rem(place_ref[1] + at // chips_y, chips_x)
        y = lax.rem(place_ref[2] + at % chips_y, chips_y)
        return (x * chips_y + y) * 2 + core

    def grad(core):
        left = [
            jnp.concatenate([parts[step, owner(at, core)] for step in range(count)], axis=1)
            for at in range(chips_x * chips_y)
        ]
        return dot(jnp.concatenate(left, axis=0), grads).astype(LOW)

    total = own_ref.shape[0]
    small_ref[...] = jnp.zeros_like(small_ref)
    first = 0
    for ref in small_refs:
        small_ref[first : first + ref.shape[0], :] = ref[...]
        first += ref.shape[0]
    other_ref[:total, :] = grad(1 - place_ref[0])
    other_ref[total:, :] = packed(small_ref[...])
    own_ref[...] = grad(place_ref[0])


def branch_grad(place, chips, rows, sent, small):
    count = len(sent)
    places = 2 * chips[0] * chips[1]
    more, width = sent[0].shape
    feats = (more - rows) * width // rows // places
    total = places // 2 * feats
    out_shape = [
        shape((total, width), LOW),
        shape((total + 2 * SMALL, width), LOW),
        shape((SMALL, width), jnp.float32),
    ]
    return feed_run(
        partial(branch_grad_kernel, count, chips, rows),
        (1,),
        place,
        [fixed(sent[0].shape)] * count + [fixed(item.shape) for item in small],
        [fixed(item.shape) for item in out_shape],
        out_shape,
        (*sent, *small),
        [pltpu.VMEM((count, places, feats, rows), LOW)],
        32,
    )


def step_run(body, operands, out_shape):
    return run(
        body,
        (1,),
        [whole(item) for item in operands],
        [whole(item) for item in out_shape],
        out_shape,
        operands,
    )


def core_step_kernel(own_ref, other_ref, small_ref, *out_refs):
    total = own_ref.shape[0]
    rows = total // len(out_refs)
    out = own_ref[...].astype(jnp.float32) + other_ref[:total, :].astype(jnp.float32)
    out = out.astype(LOW)
    small = packed(small_ref[...] + unpacked(other_ref[total:, :]))
    for at, ref in enumerate(out_refs):
        ref[:rows, :] = out[at * rows : (at + 1) * rows]
        ref[rows:, :] = small


def core_step(own, other, small, count):
    rows, width = own.shape
    out = shape((rows // count + 2 * SMALL, width), LOW)
    return step_run(core_step_kernel, (own, other, small), [out] * count)


def chip_step_kernel(count, *refs):
    term_refs, out_refs = take(refs, count)
    total = term_refs[0].shape[0] - 2 * SMALL
    rows = total // len(out_refs)
    out = sum(ref[:total, :].astype(jnp.float32) for ref in term_refs).astype(LOW)
    small = packed(even_sum([unpacked(ref[total:, :]) for ref in term_refs]))
    for at, ref in enumerate(out_refs):
        ref[:rows, :] = out[at * rows : (at + 1) * rows]
        ref[rows:, :] = small


def chip_step(terms, count):
    rows, width = terms[0].shape
    out = shape(((rows - 2 * SMALL) // count + 2 * SMALL, width), LOW)
    return step_run(partial(chip_step_kernel, len(terms)), tuple(terms), [out] * count)


def item_step_kernel(count, *refs):
    term_refs, joint_refs, (bias_ref, out_ref) = take(refs, count, count)
    rows = term_refs[0].shape[0] - 2 * SMALL
    out = sum(ref[:rows, :].astype(jnp.float32) for ref in term_refs)
    small = even_sum([unpacked(ref[rows:, :]) for ref in term_refs])
    place = lax.broadcasted_iota(jnp.int32, small.shape, 0)
    small = jnp.where(place == SMALL - 1, bias_ref[...], small)
    joint = sum(ref[...].astype(jnp.float32) for ref in joint_refs)
    out_ref[:rows, :] = out.astype(LOW)
    out_ref[rows : rows + 2 * SMALL, :] = packed(small)
    out_ref[rows + 2 * SMALL :, :] = joint.astype(LOW)


def item_step(terms, joint, bias):
    rows, width = terms[0].shape
    out = shape((rows + joint[0].shape[0], width), LOW)
    return step_run(partial(item_step_kernel, len(terms)), (*terms, *joint, bias), [out])[0]


def last_kernel(count, rows, place_ref, *refs):
    term_refs, (out_ref, joint_ref, small_ref, units_ref) = take(refs, count)
    small = []
    for at, ref in enumerate(term_refs):
        item = lax.rem(place_ref[3] + at, count)
        out_ref[pl.ds(pl.multiple_of(item * rows, rows), rows), :] = ref[:rows, :].astype(
            jnp.float32
        )
        joint = ref[rows + 2 * SMALL :, :].astype(jnp.float32)
        here = joint.shape[0]
        joint_ref[pl.ds(pl.multiple_of(item * here, here), here), :] = joint
        small.append(unpacked(ref[rows : rows + 2 * SMALL, :]))
        units_ref[item] = small[-1][0:1]
    small_ref[...] = even_sum(small)


def last_step(place, terms, rows):
    count = len(terms)
    total, width = terms[0].shape
    joint = total - rows - 2 * SMALL
    out_shape = [
        shape((count * rows, width), jnp.float32),
        shape((count * joint, width), jnp.float32),
        shape((SMALL, width), jnp.float32),
        shape((count, 1, width), jnp.float32),
    ]
    return run(
        partial(last_kernel, count, rows),
        (1,),
        [pl.BlockSpec(memory_space=pltpu.SMEM)] + [whole(item) for item in terms],
        [whole(item) for item in out_shape],
        out_shape,
        (place, *terms),
    )


def joint_grad_kernel(count, place_ref, *refs):
    (grad_ref, rows_ref, weight_ref, gain_ref, shift_ref), out_refs, refs = take(refs, 5, count)
    bias_ref, sums_ref, total, biases, bias_row = refs
    step = pl.program_id(0)
    grads = side_by_side(grad_ref)
    added = dot(grads, rows_ref[...].reshape(grads.shape[1], -1))
    summed = jnp.sum(grads.astype(jnp.float32), axis=1, keepdims=True)
    summed_row = dot_cols(jnp.ones((8, grads.shape[1]), LOW), grads)

    @pl.when(step == 0)
    def _():
        total[...] = added
        biases[...] = summed
        bias_row[...] = summed_row

    @pl.when(step > 0)
    def _():
        total[...] += added
        biases[...] += summed
        bias_row[...] += summed_row

    @pl.when(step == pl.num_programs(0) - 1)
    def _():
        rows = out_refs[0].shape[0]
        for at, ref in enumerate(out_refs):
            first = lax.rem(place_ref[3] + at, count) * rows
            ref[...] = total[pl.ds(pl.multiple_of(first, rows), rows), :].astype(LOW)
        bias_ref[...] = jnp.zeros_like(bias_ref)
        bias_ref[:, : bias_row.shape[1]] = bias_row[0:1, :]
        weight = weight_ref[...].astype(jnp.float32)
        shift_sum = jnp.sum(weight * biases[...], axis=0, keepdims=True)
        product = jnp.sum(weight * total[...], axis=0, keepdims=True)
        sums_ref[0:1, :] = (product - shift_sum * shift_ref[...]) / gain_ref[...]
        sums_ref[1:2, :] = shift_sum


def joint_grad(place, count, grads, gathered, weight, gain, shift, step=8):
    places, feats, rows = grads.shape
    width = gathered.shape[2]
    results = run(
        partial(joint_grad_kernel, count),
        (places // step,),
        [
            pl.BlockSpec(memory_space=pltpu.SMEM),
            pl.BlockSpec((step, feats, rows), lambda i: (i, 0, 0)),
            pl.BlockSpec((step, rows, width), lambda i: (i, 0, 0)),
            whole(weight),
            whole(gain),
            whole(shift),
        ],
        [pl.BlockSpec((feats // count, width), lambda i: (0, 0))] * count
        + [
            pl.BlockSpec((1, width), lambda i: (0, 0)),
            pl.BlockSpec((2, width), lambda i: (0, 0)),
        ],
        [shape((feats // count, width), LOW)] * count
        + [shape((1, width), jnp.float32), shape((2, width), jnp.float32)],
        (place, grads, gathered, weight, gain, shift),
        scratch=[
            pltpu.VMEM((feats, width), jnp.float32),
            pltpu.VMEM((feats, 1), jnp.float32),
            pltpu.VMEM((8, feats), jnp.float32),
        ],
    )
    return results[:count], *results[count:]


def input_kernel(part_ref, weight_ref, tokens_ref, gain_ref, d_resid_ref, out_ref, total):
    step = pl.program_id(0)
    added = dot(turned(part_ref[...]).astype(LOW), weight_ref[...])

    @pl.when(step == 0)
    def _():
        total[...] = added

    @pl.when(step > 0)
    def _():
        total[...] += added

    @pl.when(step == pl.num_programs(0) - 1)
    def _():
        normed, scale = norm_parts(tokens_ref[...].astype(jnp.float32))
        out_ref[...] = d_resid_ref[...] + norm_back(total[...], normed, scale, gain_ref[...])


def input_back(parts, weights, tokens, gain, d_resid, steps=6):
    feats, rows = parts.shape
    width = weights.shape[1]
    step = feats // steps
    return run(
        input_kernel,
        (steps,),
        [
            pl.BlockSpec((step, rows), lambda i: (i, 0)),
            pl.BlockSpec((step, width), lambda i: (i, 0)),
            whole(tokens),
            whole(gain),
            whole(d_resid),
        ],
        [pl.BlockSpec((rows, width), lambda i: (0, 0))],
        [shape((rows, width), jnp.float32)],
        (parts, weights, tokens, gain, d_resid),
        scratch=[pltpu.VMEM((rows, width), jnp.float32)],
    )[0]


ITEM = "z"
HEAD = ("x", "y", "c")
CORE = "c"


def moved(value, axis, steps):
    count = lax.axis_size(axis)
    return lax.ppermute(value, axis, [(place, (place + steps) % count) for place in range(count)])


def shifted(value, axis, steps):
    count = lax.axis_size(axis)
    initial, last = (max(0, -steps), min(count, count - steps))
    return lax.ppermute(value, axis, [(source, source + steps) for source in range(initial, last)])


def around(value, axis):
    return [value] + [moved(value, axis, -step) for step in range(1, lax.axis_size(axis))]


def sum_back(values, axis):
    return [values[0]] + [
        moved(values[step], axis, step) for step in range(1, lax.axis_size(axis))
    ]


def own_step(values, axis):
    own = values[0].astype(jnp.float32) + moved(values[1], axis, 1).astype(jnp.float32)
    return own.astype(LOW)


def head_swap(value):
    return lax.all_to_all(value, HEAD, split_axis=0, concat_axis=0, tiled=True)


def segment_flags(seg_counts):
    total_segs = seg_counts.shape[0]
    openings = jnp.cumsum(seg_counts) - seg_counts
    places = jnp.arange(total_segs, dtype=jnp.int32)
    opens_here = jnp.any((openings[:, None] == places[None, :]) & (seg_counts[:, None] > 0), axis=0)
    opens_before = jnp.concatenate([jnp.ones((1,), dtype=bool), opens_here[:-1]])
    one_back = jnp.logical_not(opens_here)
    two_back = one_back & jnp.logical_not(opens_before)
    return (one_back, two_back)


def local(
    tokens,
    cotangent,
    seg_counts,
    query_weight,
    key_weight,
    value_weight,
    query_bias,
    value_bias,
    out_weight,
    out_bias,
    first_gain,
    first_shift,
    second_gain,
    second_shift,
    up_weight,
    up_bias,
    down_weight,
    down_bias,
):
    rows, width = tokens.shape
    heads = lax.axis_size(HEAD)
    item_place = lax.axis_index(ITEM)
    group_rows = rows * heads
    seg_local = group_rows // SEG
    feats = query_weight.shape[0]
    units = up_weight.shape[0]
    hidden_here = units * heads

    def row(vector):
        return vector.reshape(1, -1)

    tokens_f = tokens.astype(jnp.float32)
    inputs_one = layer_norm(tokens_f, first_gain, first_shift).astype(LOW)
    first = jnp.concatenate([inputs_one, out_weight], axis=0)
    gathered = lax.all_gather(first, HEAD, axis=0, tiled=True).reshape(heads, -1, width)
    second = jnp.concatenate([up_weight, down_weight], axis=0)
    feed_weights = lax.all_gather(second, HEAD, axis=0, tiled=True).reshape(heads, -1, width)
    cots = around(cotangent, ITEM)
    joint_weight = jnp.concatenate([query_weight, key_weight, value_weight], axis=0)
    joint_bias = jnp.concatenate([query_bias, jnp.zeros_like(query_bias), value_bias])

    one_back, two_back = segment_flags(seg_counts)
    flags = jnp.stack([two_back, one_back], axis=1).astype(jnp.int32)
    flags = lax.dynamic_slice_in_dim(flags, item_place * seg_local, seg_local).reshape(-1)

    gathered, cots = lax.optimization_barrier((gathered, cots))
    query, kv, turned_all = project(gathered, rows, joint_weight, row(joint_bias))
    own_kept = kv.reshape(seg_local, SEG, 2 * HD)[:, SEG - KEPT :]
    table = jnp.concatenate([shifted(own_kept, ITEM, 1), own_kept], axis=0)
    prefix = jnp.concatenate(
        [table[seg_local - 2 : 2 * seg_local - 2], table[seg_local - 1 : 2 * seg_local - 1]], axis=1
    )
    attended, log_sums = attend(flags, turned_all, kv, prefix, rows)
    attended_own = head_swap(attended)
    resid, inputs_two = out_project(
        attended_own, gathered, rows // feats, tokens, row(out_bias), row(second_gain), row(second_shift)
    )

    joint_turn = lax.optimization_barrier((joint_weight, resid))[0]
    joint_full = lax.all_gather(joint_turn, HEAD, axis=0, tiled=True)
    norms = around(inputs_two, ITEM)
    chips = (lax.axis_size("x"), lax.axis_size("y"))
    place = jnp.stack([lax.axis_index(axis) for axis in (CORE, "x", "y", ITEM)]).astype(jnp.int32)
    d_act, cots = feed_d_act(place, chips, cots, feed_weights)
    cots = [cots, moved(cots, CORE, 1)]
    bias_here = lax.dynamic_slice_in_dim(up_bias, item_place * hidden_here, hidden_here)
    backs, (norms, kept, sent, up_bias_part) = feed(
        place, chips, norms, feed_weights, bias_here.reshape(heads, 1, units), d_act
    )
    backs = sum_back(backs, ITEM)
    norms = [norms, moved(norms, CORE, 1)]
    mixeds, feed_parts = feed_grad(
        place, chips, len(backs), norms, cots, kept, sent, moved(sent, CORE, 1), feed_weights
    )
    backs, mixeds = lax.optimization_barrier((backs, mixeds))
    d_resid, sums_two, d_parts, sent = branch_back(
        place, resid, cotangent, row(second_gain), gathered, rows // feats, attended_own, backs
    )
    sent = sum_back(sent, ITEM)
    d_attended = head_swap(d_parts)
    feed_parts = lax.optimization_barrier((feed_parts, d_resid))[0]
    feed_grads = lax.psum_scatter(
        feed_parts.reshape(-1, width), ("x", "y"), scatter_dimension=0, tiled=True
    )
    d_attended, mixeds = lax.optimization_barrier((d_attended, mixeds))
    d_prefix = prefix_back(
        flags, turned_all, query, d_attended, attended, log_sums, prefix, rows
    )[0]
    older, newer = d_prefix[:, :KEPT], d_prefix[:, KEPT:]
    spread = jnp.pad(older, ((seg_local - 2, 2), (0, 0), (0, 0)))
    spread = spread + jnp.pad(newer, ((seg_local - 1, 1), (0, 0), (0, 0)))
    returned = shifted(spread[:seg_local], ITEM, -1)
    joint_grads, kept_grads = attend_back(
        flags, turned_all, query, d_attended, attended, log_sums, prefix, kv, rows, 1
    )
    returned, kept_grads, joint_full = lax.optimization_barrier((returned, kept_grads, joint_full))
    joint_grads = add_returned(joint_grads, kept_grads, spread[seg_local:] + returned)
    grads_own = head_swap(joint_grads[0]).reshape(-1, rows)
    joint_parts, bias_part, sums_one = joint_grad(
        place,
        lax.axis_size(ITEM),
        joint_grads[0],
        gathered,
        joint_weight,
        row(first_gain),
        row(first_shift),
    )
    joint_parts, sums_one, sent = lax.optimization_barrier((joint_parts, sums_one, sent))
    out_own, out_other, small = branch_grad(
        place, chips, rows, sent, (row(up_bias_part), sums_two, sums_one)
    )
    joint_parts = sum_back(joint_parts, ITEM)
    terms = core_step(out_own, moved(out_other, CORE, 1), small, chips[0])
    grads_own, terms, joint_parts, mixeds = lax.optimization_barrier(
        (grads_own, terms, joint_parts, mixeds)
    )
    near, far = jnp.stack(mixeds[:2]), moved(jnp.stack(mixeds[2:]), ITEM, 2)
    terms = sum_back(terms, "x")
    input_grad = input_back(grads_own, joint_full, tokens, row(first_gain), d_resid)
    input_grad, terms = lax.optimization_barrier((input_grad, terms))
    terms = sum_back(chip_step(terms, chips[1]), "y")
    terms, near, far = lax.optimization_barrier((terms, near, far))
    near = (near.astype(jnp.float32) + far.astype(jnp.float32)).astype(LOW)
    mixed = own_step(near, ITEM)
    terms = around(item_step(terms, joint_parts, bias_part), ITEM)
    terms, feed_grads = lax.optimization_barrier((terms, feed_grads))
    share = feats // lax.axis_size(ITEM)
    out_sum, joint_sums, small, up_bias_grad = last_step(place, terms, share)
    up_bias_grad = up_bias_grad.reshape(-1)
    bias_sums, early_rows, late = small[SMALL - 1, : 3 * feats], small[1:5], small[5:7]
    feed_grads = feed_grads.astype(jnp.float32)
    mixed_out = (resid + mixed.astype(jnp.float32) + down_bias).astype(LOW)
    return (
        mixed_out,
        input_grad,
        joint_sums[:feats],
        joint_sums[feats : 2 * feats],
        joint_sums[2 * feats :],
        bias_sums[:feats],
        bias_sums[2 * feats : 3 * feats],
        out_sum,
        early_rows[2],
        late[0],
        late[1],
        early_rows[0],
        early_rows[1],
        feed_grads[:units],
        up_bias_grad,
        feed_grads[units:],
        early_rows[3],
    )


def solution(mesh):
    sizes = (mesh.shape["item"], 4, mesh.shape["head"] // 8, 2)
    fine = Mesh(mesh.devices.reshape(sizes), (ITEM, *HEAD))
    split = P((ITEM, *HEAD), None)
    by_head = P(HEAD, None)
    return jax.shard_map(
        local,
        mesh=fine,
        in_specs=(
            split,
            split,
            P(),
            by_head,
            by_head,
            by_head,
            P(HEAD),
            P(HEAD),
            by_head,
            P(),
            P(),
            P(),
            P(),
            P(),
            split,
            P(),
            split,
            P(),
        ),
        out_specs=(
            split,
            split,
            by_head,
            by_head,
            by_head,
            P(HEAD),
            P(HEAD),
            by_head,
            P(),
            P(),
            P(),
            P(),
            P(),
            split,
            P(),
            split,
            P(),
        ),
        check_vma=False,
    )
```

```python
import math
from functools import partial

import jax
import jax.numpy as jnp
from jax import lax
from jax.experimental import pallas as pl
from jax.experimental.pallas import tpu as pltpu
from jax.sharding import Mesh
from jax.sharding import PartitionSpec as P

HD = 64
NSUM = 50
SEG = 2048
SPAN = 512
KEPT = 64
EPSILON = 1e-05
MASKED = -1e30
SCALE = HD ** (-0.5)
MIB = 1 << 20
COST = 1 << 20
BIG = 1 << 17
LOW = jnp.bfloat16


def dot(left, right):
    return jnp.dot(left, right, preferred_element_type=jnp.float32)


def dot_cols(left, right):
    return lax.dot_general(
        left, right, (((1,), (1,)), ((), ())), preferred_element_type=jnp.float32
    )


def turned(value):
    return value.astype(jnp.float32).T


def norm_parts(row_data):
    row_mean = jnp.mean(row_data, axis=-1, keepdims=True)
    centred = row_data - row_mean
    row_var = jnp.mean(centred * centred, axis=-1, keepdims=True)
    scale = lax.rsqrt(row_var + EPSILON)
    return centred * scale, scale


def norm_back(grad, normed, scale, gain):
    scaled = grad * gain
    return scale * (
        scaled
        - jnp.mean(scaled, axis=-1, keepdims=True)
        - normed * jnp.mean(scaled * normed, axis=-1, keepdims=True)
    )


def layer_norm(row_data, gain, shift):
    return norm_parts(row_data)[0] * gain + shift


def in_hbm(operands, received):
    kept = [id(item) for item in received]
    return [
        pltpu.with_memory_space_constraint(item, pltpu.HBM)
        if item.size >= BIG and id(item) not in kept
        else item
        for item in operands
    ]


def out_hbm(shapes):
    return [
        pltpu.HBM(item.shape, item.dtype) if math.prod(item.shape) >= BIG else item
        for item in shapes
    ]


def run(body, grid, in_specs, out_specs, out_shape, operands, scratch=(), vmem=32, aliases=None, received=()):
    return pl.pallas_call(
        body,
        grid=grid,
        in_specs=in_specs,
        out_specs=out_specs,
        out_shape=out_hbm(out_shape),
        scratch_shapes=scratch,
        compiler_params=pltpu.CompilerParams(
            dimension_semantics=("arbitrary",) * len(grid), vmem_limit_bytes=vmem * MIB
        ),
        input_output_aliases=aliases or {},
        cost_estimate=pl.CostEstimate(flops=COST, bytes_accessed=COST, transcendentals=0),
    )(*in_hbm(operands, received))


def shape(dims, kind):
    return jax.ShapeDtypeStruct(dims, kind)


def whole(item):
    return pl.BlockSpec(item.shape, lambda *_: (0,) * len(item.shape))


def project_kernel(rows_ref, weight_ref, bias_ref, query_ref, kv_ref, turned_ref):
    rows = rows_ref[...].reshape(-1, rows_ref.shape[2])
    joint = dot_cols(rows, weight_ref[...]) + bias_ref[...]
    query_ref[...] = joint[:, :HD].astype(LOW)
    kv_ref[...] = joint[:, HD:].astype(LOW)
    turned_ref[...] = joint.T.astype(LOW)


def project(gathered, rows_here, weight, bias, span=2 * SPAN):
    places, _, width = gathered.shape
    total = places * rows_here
    step = span // rows_here
    return run(
        project_kernel,
        (total // span,),
        [
            pl.BlockSpec((step, rows_here, width), lambda i: (i, 0, 0)),
            whole(weight),
            whole(bias),
        ],
        [
            pl.BlockSpec((span, HD), lambda i: (i, 0)),
            pl.BlockSpec((span, 2 * HD), lambda i: (i, 0)),
            pl.BlockSpec((3 * HD, span), lambda i: (0, i)),
        ],
        [
            shape((total, HD), LOW),
            shape((total, 2 * HD), LOW),
            shape((3 * HD, total), LOW),
        ],
        (gathered, weight, bias),
    )


def prefix_seen(flags_ref, seg, columns):
    place = lax.broadcasted_iota(jnp.int32, (2 * KEPT, columns), 0)
    older = place < KEPT
    slot = jnp.where(older, place, place - KEPT) >= KEPT - NSUM
    flag = jnp.where(older, flags_ref[2 * seg], flags_ref[2 * seg + 1])
    return slot & (flag > 0)


def causal_seen():
    shape_here = (SPAN, SPAN)
    return lax.broadcasted_iota(jnp.int32, shape_here, 0) <= lax.broadcasted_iota(
        jnp.int32, shape_here, 1
    )


def above(block):
    return jnp.concatenate([block, jnp.zeros_like(block)], axis=0)


def below(block):
    return jnp.concatenate([jnp.zeros_like(block), block], axis=0)


def at_block(index):
    return pl.ds(pl.multiple_of(index * SPAN, SPAN), SPAN)


def attend_kernel(flags_ref, query_ref, turned_ref, kv_ref, prefix_ref, out_ref, log_ref):
    seg, block = pl.program_id(0), pl.program_id(1)
    query = above((query_ref[...].astype(jnp.float32) * SCALE).astype(LOW))
    own = at_block(block)
    scores = dot(kv_ref[own, :], query)
    scores = jnp.where(causal_seen(), scores, MASKED)
    top = jnp.max(scores, axis=0, keepdims=True)
    probs = jnp.exp(scores - top)
    total = jnp.sum(probs, axis=0, keepdims=True)
    mixed = dot(turned_ref[2 * HD :, own], probs.astype(LOW))

    def add(carry, scores, values):
        top, total, mixed = carry
        fresh = jnp.maximum(top, jnp.max(scores, axis=0, keepdims=True))
        fade = jnp.exp(top - fresh)
        probs = jnp.exp(scores - fresh)
        total = total * fade + jnp.sum(probs, axis=0, keepdims=True)
        return fresh, total, mixed * fade + dot(values, probs.astype(LOW))

    prefix = prefix_ref[0]
    scores = jnp.where(prefix_seen(flags_ref, seg, SPAN), dot(prefix, query), MASKED)
    carry = add((top, total, mixed), scores, turned(prefix)[HD:].astype(LOW))

    def step(index, carry):
        here = at_block(index)
        return add(carry, dot(kv_ref[here, :], query), turned_ref[2 * HD :, here])

    top, total, mixed = lax.fori_loop(0, block, step, carry)
    mixed = (mixed / total).astype(LOW)
    rows = out_ref.shape[2]
    for piece in range(SPAN // rows):
        out_ref[piece] = mixed[:, piece * rows : (piece + 1) * rows]
    log_ref[0] = top + jnp.log(total)


def attend(flags, turned_all, kv, prefix, rows_here):
    total = kv.shape[0]
    blocks = SEG // SPAN
    step = SPAN // rows_here
    return run(
        attend_kernel,
        (total // SEG, blocks),
        [
            pl.BlockSpec(memory_space=pltpu.SMEM),
            pl.BlockSpec((HD, SPAN), lambda s, i: (0, s * blocks + i)),
            pl.BlockSpec((3 * HD, SEG), lambda s, i: (0, s)),
            pl.BlockSpec((SEG, 2 * HD), lambda s, i: (s, 0)),
            pl.BlockSpec((1, 2 * KEPT, 2 * HD), lambda s, i: (s, 0, 0)),
        ],
        [
            pl.BlockSpec((step, HD, rows_here), lambda s, i: (s * blocks + i, 0, 0)),
            pl.BlockSpec((1, 1, SPAN), lambda s, i: (s * blocks + i, 0, 0)),
        ],
        [
            shape((total // rows_here, HD, rows_here), LOW),
            shape((total // SPAN, 1, SPAN), jnp.float32),
        ],
        (flags, turned_all, turned_all, kv, prefix),
    )


def side_by_side(ref):
    return jnp.concatenate([ref[piece] for piece in range(ref.shape[0])], axis=1)


def beside(block, place):
    zero = jnp.zeros_like(block)
    return jnp.concatenate([block, zero] if place == 0 else [zero, block], axis=1)


def query_side(query_ref, rows_ref, grad_ref, out_ref, log_ref):
    query = above((query_ref[...].astype(jnp.float32) * SCALE).astype(LOW))
    grad = side_by_side(grad_ref)
    mean = jnp.sum(
        grad.astype(jnp.float32) * side_by_side(out_ref).astype(jnp.float32),
        axis=0,
        keepdims=True,
    )
    query_rows = beside((rows_ref[...].astype(jnp.float32) * SCALE).astype(LOW), 0)
    grad_rows = beside(turned(grad).astype(LOW), 1)
    return query, below(grad), mean, log_ref[0], query_rows, grad_rows


def key_side(keys, side, seen):
    query, grad, mean, log_sum, query_rows, grad_rows = side
    probs = jnp.exp(dot(keys, query) - log_sum)
    if seen is not None:
        probs = jnp.where(seen, probs, 0.0)
    d_scores = (probs * (dot(keys, grad) - mean)).astype(LOW)
    return probs.astype(LOW), d_scores


def prefix_back_kernel(
    flags_ref, query_ref, rows_ref, grad_ref, out_ref, log_ref, prefix_ref, sum_ref
):
    seg, block = pl.program_id(0), pl.program_id(1)
    side = query_side(query_ref, rows_ref, grad_ref, out_ref, log_ref)
    probs, d_scores = key_side(prefix_ref[0], side, prefix_seen(flags_ref, seg, SPAN))
    part = dot(d_scores, side[4]) + dot(probs, side[5])

    @pl.when(block == 0)
    def _():
        sum_ref[0] = part

    @pl.when(block > 0)
    def _():
        sum_ref[0] += part


def store_shares(grads_ref, piece, part, columns):
    here = HD // grads_ref.shape[0]
    for share in range(grads_ref.shape[0]):
        for kind in (1, 2):
            first = (kind - 1) * HD + share * here
            grads_ref[share, piece, kind * here : (kind + 1) * here, columns] = part[
                first : first + here
            ]


def attend_back_kernel(
    flags_ref,
    query_ref,
    rows_ref,
    grad_ref,
    out_ref,
    log_ref,
    prefix_ref,
    turned_ref,
    kv_ref,
    grads_ref,
    kept_ref,
    kv_grad,
):
    seg, block = pl.program_id(0), pl.program_id(1)

    @pl.when(block == 0)
    def _():
        kv_grad[...] = jnp.zeros_like(kv_grad)

    side = query_side(query_ref, rows_ref, grad_ref, out_ref, log_ref)
    prefix = prefix_ref[0]
    _, d_scores = key_side(prefix, side, prefix_seen(flags_ref, seg, SPAN))
    query_grad = dot(turned(prefix)[:HD].astype(LOW), d_scores)

    def add(here, query_grad, seen):
        probs, d_scores = key_side(kv_ref[here, :], side, seen)
        kv_grad[here, :] += dot(d_scores, side[4]) + dot(probs, side[5])
        return query_grad + dot(turned_ref[HD : 2 * HD, here], d_scores)

    query_grad = add(at_block(block), query_grad, causal_seen())
    query_grad = lax.fori_loop(
        0, block, lambda index, grad: add(at_block(index), grad, None), query_grad
    )
    query_grad = (query_grad * SCALE).astype(LOW)
    rows = grads_ref.shape[3]
    step = SPAN // rows
    for piece in range(step):
        part = query_grad[:, piece * rows : (piece + 1) * rows]
        for share in range(grads_ref.shape[0]):
            here = HD // grads_ref.shape[0]
            grads_ref[share, block * step + piece, :here, :] = part[share * here : (share + 1) * here]

    @pl.when(block == pl.num_programs(1) - 1)
    def _():
        for piece in range(SEG // rows):
            part = kv_grad[piece * rows : (piece + 1) * rows, :].T.astype(LOW)
            store_shares(grads_ref, piece, part, slice(None))
        kept_ref[0] = kv_grad[SEG - KEPT :, :]


def attend_back_specs(rows_here):
    blocks = SEG // SPAN
    step = SPAN // rows_here
    return [
        pl.BlockSpec(memory_space=pltpu.SMEM),
        pl.BlockSpec((HD, SPAN), lambda s, i: (0, s * blocks + i)),
        pl.BlockSpec((SPAN, HD), lambda s, i: (s * blocks + i, 0)),
        pl.BlockSpec((step, HD, rows_here), lambda s, i: (s * blocks + i, 0, 0)),
        pl.BlockSpec((step, HD, rows_here), lambda s, i: (s * blocks + i, 0, 0)),
        pl.BlockSpec((1, 1, SPAN), lambda s, i: (s * blocks + i, 0, 0)),
        pl.BlockSpec((1, 2 * KEPT, 2 * HD), lambda s, i: (s, 0, 0)),
    ]


def prefix_back(flags, turned_all, query, grad, out, log_sums, prefix, rows_here):
    total = query.shape[0]
    return run(
        prefix_back_kernel,
        (total // SEG, SEG // SPAN),
        attend_back_specs(rows_here),
        [pl.BlockSpec((1, 2 * KEPT, 2 * HD), lambda s, i: (s, 0, 0))],
        [shape(prefix.shape, jnp.float32)],
        (flags, turned_all, query, grad, out, log_sums, prefix),
        received=(grad,),
    )


def attend_back(flags, turned_all, query, grad, out, log_sums, prefix, kv, rows_here, count):
    total = query.shape[0]
    pieces = SEG // rows_here
    return run(
        attend_back_kernel,
        (total // SEG, SEG // SPAN),
        attend_back_specs(rows_here)
        + [
            pl.BlockSpec((3 * HD, SEG), lambda s, i: (0, s)),
            pl.BlockSpec((SEG, 2 * HD), lambda s, i: (s, 0)),
        ],
        [
            pl.BlockSpec(
                (count, pieces, 3 * HD // count, rows_here), lambda s, i: (0, s, 0, 0)
            ),
            pl.BlockSpec((1, KEPT, 2 * HD), lambda s, i: (s, 0, 0)),
        ],
        [
            shape((count, total // rows_here, 3 * HD // count, rows_here), LOW),
            shape((total // SEG, KEPT, 2 * HD), jnp.float32),
        ],
        (flags, turned_all, query, grad, out, log_sums, prefix, turned_all, kv),
        received=(grad,),
        scratch=[pltpu.VMEM((SEG, 2 * HD), jnp.float32)],
    )


def returned_kernel(grads_ref, kept_ref, returned_ref, out_ref):
    out_ref[...] = grads_ref[...]
    part = (kept_ref[0] + returned_ref[0]).T.astype(LOW)
    store_shares(out_ref, 0, part, slice(out_ref.shape[3] - KEPT, None))


def add_returned(grads, kept, returned):
    count, places, feats, rows = grads.shape
    segs = kept.shape[0]
    last = places // segs
    grad_spec = pl.BlockSpec((count, 1, feats, rows), lambda s: (0, s * last + last - 1, 0, 0))
    kept_spec = pl.BlockSpec((1, KEPT, 2 * HD), lambda s: (s, 0, 0))
    return run(
        returned_kernel,
        (segs,),
        [grad_spec, kept_spec, kept_spec],
        [grad_spec],
        [shape(grads.shape, LOW)],
        (grads, kept, returned),
        aliases={0: 0},
    )[0]


def out_kernel(
    part_ref, weight_ref, tokens_ref, bias_ref, gain_ref, shift_ref, resid_ref, two_ref, total
):
    step = pl.program_id(0)
    rows = part_ref.shape[2]
    part = turned(part_ref[...].reshape(-1, rows)).astype(LOW)
    added = dot(part, weight_ref[...].reshape(part.shape[1], -1))

    @pl.when(step == 0)
    def _():
        total[...] = added

    @pl.when(step > 0)
    def _():
        total[...] += added

    @pl.when(step == pl.num_programs(0) - 1)
    def _():
        resid = tokens_ref[...].astype(jnp.float32) + total[...] + bias_ref[...]
        resid_ref[...] = resid
        two_ref[...] = layer_norm(resid, gain_ref[...], shift_ref[...]).astype(LOW)


def out_project(parts, gathered, at, tokens, bias, gain, shift, step=4):
    places, feats, rows = parts.shape
    width = gathered.shape[2]
    return run(
        out_kernel,
        (places // step,),
        [
            pl.BlockSpec((step, feats, rows), lambda i: (i, 0, 0)),
            pl.BlockSpec((step, feats, width), lambda i: (i, at, 0)),
            whole(tokens),
            whole(bias),
            whole(gain),
            whole(shift),
        ],
        [pl.BlockSpec((rows, width), lambda i: (0, 0))] * 2,
        [shape((rows, width), jnp.float32), shape((rows, width), LOW)],
        (parts, gathered, tokens, bias, gain, shift),
        received=(parts,),
        scratch=[pltpu.VMEM((rows, width), jnp.float32)],
    )


def owner_maps(chips, at):
    def of(core_step, chip):
        return lambda i, place: at((i * chips[1] + chip) * 2 + lax.rem(place[0] + core_step, 2))

    return [of(core_step, chip) for core_step in (0, 1) for chip in range(chips[1])]


def own_map(index):
    return lambda i, place: index(i)


def fixed(dims):
    return pl.BlockSpec(
        dims, own_map(lambda i: (0,) * len(dims)), pipeline_mode=pl.Buffered(buffer_count=1)
    )


def feed_run(
    body, chips, place, in_specs, out_specs, out_shape, operands, scratch, vmem, received=()
):
    return pl.pallas_call(
        body,
        grid_spec=pltpu.PrefetchScalarGridSpec(
            num_scalar_prefetch=1,
            grid=(chips[0],),
            in_specs=in_specs,
            out_specs=out_specs,
            scratch_shapes=scratch,
        ),
        out_shape=out_hbm(out_shape),
        compiler_params=pltpu.CompilerParams(
            dimension_semantics=("arbitrary",), vmem_limit_bytes=vmem * MIB
        ),
        cost_estimate=pl.CostEstimate(flops=COST, bytes_accessed=COST, transcendentals=0),
    )(place, *in_hbm(operands, received))


def stacked(refs, axis=0):
    return jnp.concatenate([ref[0] for ref in refs], axis=axis)


def pile(refs, into):
    rows = refs[0].shape[0]
    for at, ref in enumerate(refs):
        into[at * rows : (at + 1) * rows, :] = ref[...]


def spread(source, refs):
    rows = refs[0].shape[0]
    for at, ref in enumerate(refs):
        ref[...] = source[at * rows : (at + 1) * rows, :].astype(ref.dtype)


def take(refs, *counts):
    refs = list(refs)
    return [[refs.pop(0) for _ in range(count)] for count in counts] + [refs]


def d_act_kernel(count, owners, place_ref, *refs):
    cot_refs, weight_refs, (out_ref, cots) = take(refs, count, owners)

    @pl.when(pl.program_id(0) == 0)
    def _():
        pile(cot_refs, cots)

    out_ref[...] = dot_cols(cots[...], stacked(weight_refs))


def feed_d_act(place, chips, cots, weights):
    count = len(cots)
    rows, width = cots[0].shape
    places, both, _ = weights.shape
    units = both // 2
    total = count * rows
    owners = 2 * chips[1]
    step = owners * units
    return feed_run(
        partial(d_act_kernel, count, owners),
        chips,
        place,
        [fixed((rows, width))] * count
        + [
            pl.BlockSpec((1, units, width), at)
            for at in owner_maps(chips, lambda owner: (owner, 1, 0))
        ],
        [pl.BlockSpec((total, step), own_map(lambda i: (0, i))), fixed((total, width))],
        [shape((total, places * units), jnp.float32), shape((total, width), LOW)],
        (*cots, *[weights] * owners),
        [],
        32,
        received=cots[1:],
    )


def feed_kernel(count, chips, place_ref, *refs):
    owners = 2 * chips[1]
    norm_refs, weight_refs, bias_refs, (d_act_ref,), back_refs, refs = take(
        refs, count, owners, owners, 1, count
    )
    norms, kept_ref, sent_ref, bias_sum_ref, back = refs
    step = pl.program_id(0)

    @pl.when(step == 0)
    def _():
        pile(norm_refs, norms)
        back[...] = jnp.zeros_like(back)

    up = stacked(weight_refs)
    pre = dot_cols(norms[...], up) + stacked(bias_refs, axis=1)
    square = pre * pre
    bent = jnp.tanh(0.7978845608 * (pre + 0.044715 * (square * pre)))
    half = 0.5 * (1.0 + bent)
    slope = half + 0.5 * pre * (1.0 - bent * bent) * (
        0.7978845608 * (1.0 + 3.0 * 0.044715 * square)
    )
    d_pre = (d_act_ref[...] * slope).astype(LOW)
    act = (pre * half).astype(LOW)
    own = act.shape[1] // 2
    kept_ref[0] = act[:, :own]
    kept_ref[1] = d_pre[:, :own]
    sent_ref[0] = act[:, own:]
    sent_ref[1] = d_pre[:, own:]
    bias_sums = jnp.sum(d_pre.astype(jnp.float32), axis=0, keepdims=True)
    units = weight_refs[0].shape[1]
    for at, index in enumerate(owner_maps(chips, lambda owner: owner)):
        bias_sum_ref[index(step, place_ref)] = bias_sums[:, at * units : (at + 1) * units]
    back[...] += dot(d_pre, up)

    @pl.when(step == pl.num_programs(0) - 1)
    def _():
        spread(back, back_refs)


def feed(place, chips, norms, weights, bias, d_act):
    count = len(norms)
    rows, width = norms[0].shape
    places, both, _ = weights.shape
    units = both // 2
    total = count * rows
    owners = 2 * chips[1]
    step = owners * units
    pair_spec = pl.BlockSpec((2, total, step // 2), own_map(lambda i: (0, 0, i)))
    results = feed_run(
        partial(feed_kernel, count, chips),
        chips,
        place,
        [fixed((rows, width))] * count
        + [
            pl.BlockSpec((1, units, width), at)
            for at in owner_maps(chips, lambda owner: (owner, 0, 0))
        ]
        + [
            pl.BlockSpec((1, 1, units), at)
            for at in owner_maps(chips, lambda owner: (owner, 0, 0))
        ]
        + [pl.BlockSpec((total, step), own_map(lambda i: (0, i)))],
        [pl.BlockSpec((rows, width), own_map(lambda i: (0, 0)))] * count
        + [fixed((total, width)), pair_spec, pair_spec, fixed((places, 1, units))],
        [shape((rows, width), LOW)] * count
        + [shape((total, width), LOW)]
        + [shape((2, total, places * units // 2), LOW)] * 2
        + [shape((places, 1, units), jnp.float32)],
        (*norms, *[weights] * owners, *[bias] * owners, d_act),
        [pltpu.VMEM((total, width), jnp.float32)],
        40,
        received=norms[1:],
    )
    return results[:count], results[count:]


def feed_grad_kernel(count, owners, place_ref, *refs):
    norm_refs, cot_refs, pair_refs, weight_refs, mixed_refs, (out_ref, mixed) = take(
        refs, 2, 2, 3, owners, count
    )
    kept_ref, sent_ref, other_ref = pair_refs
    step = pl.program_id(0)
    units = weight_refs[0].shape[1]

    @pl.when(step == 0)
    def _():
        mixed[...] = jnp.zeros_like(mixed)

    act = jnp.concatenate([kept_ref[0], sent_ref[0]], axis=1)
    mixed[...] += dot(act, stacked(weight_refs))

    def grad(at, rows):
        total = dot(turned(kept_ref[at]).astype(LOW), rows[0][...])
        total += dot(turned(other_ref[at]).astype(LOW), rows[1][...])
        return total.astype(LOW).reshape(out_ref.shape[0], units, -1)

    out_ref[:, :units, :] = grad(1, norm_refs)
    out_ref[:, units:, :] = grad(0, cot_refs)

    @pl.when(step == pl.num_programs(0) - 1)
    def _():
        spread(mixed, mixed_refs)


def feed_grad(place, chips, count, norms, cots, kept, sent, other, weights):
    total, width = norms[0].shape
    rows = total // count
    units = weights.shape[1] // 2
    owners = 2 * chips[1]
    pair_spec = pl.BlockSpec((2, total, owners * units // 2), own_map(lambda i: (0, 0, i)))
    results = feed_run(
        partial(feed_grad_kernel, count, owners),
        chips,
        place,
        [fixed((total, width))] * 4
        + [pair_spec] * 3
        + [
            pl.BlockSpec((1, units, width), at)
            for at in owner_maps(chips, lambda owner: (owner, 1, 0))
        ],
        [pl.BlockSpec((rows, width), own_map(lambda i: (0, 0)))] * count
        + [pl.BlockSpec((chips[1], 2 * units, width), own_map(lambda i: (i, 0, 0)))],
        [shape((rows, width), LOW)] * count
        + [shape((chips[0] * chips[1], 2 * units, width), LOW)],
        (*norms, *cots, kept, sent, other, *[weights] * owners),
        [pltpu.VMEM((total, width), jnp.float32)],
        48,
        received=(norms[1], cots[1], other),
    )
    return results[:count], results[count]


def branch_kernel(count, place_ref, *refs):
    (resid_ref, cot_ref, gain_ref, weight_ref, part_ref), refs = take(refs, 5)
    back_refs, mixed_refs, refs = take(refs, count, count)
    (d_resid_ref, sums_ref, parts_ref), sent_refs, (d_branch_ref,) = take(refs, 3, count)
    step = pl.program_id(0)

    @pl.when(step == 0)
    def _():
        d_two = sum(ref[...].astype(jnp.float32) for ref in back_refs)
        normed, scale = norm_parts(resid_ref[...])
        cot = cot_ref[...].astype(jnp.float32)
        d_resid = cot + norm_back(d_two, normed, scale, gain_ref[...])
        d_branch = d_resid.astype(LOW)
        d_resid_ref[...] = d_resid
        d_branch_ref[...] = d_branch
        sums_ref[0:1, :] = jnp.sum(d_two * normed, axis=0, keepdims=True)
        sums_ref[1:2, :] = jnp.sum(d_two, axis=0, keepdims=True)
        sums_ref[2:3, :] = jnp.sum(d_branch.astype(jnp.float32), axis=0, keepdims=True)
        sums_ref[3:4, :] = jnp.sum(cot, axis=0, keepdims=True)

    width = weight_ref.shape[2]
    part = dot_cols(weight_ref[...].reshape(-1, width), d_branch_ref[...])
    parts_ref[...] = part.reshape(parts_ref.shape).astype(LOW)

    @pl.when(step == pl.num_programs(0) - 1)
    def _():
        places, feats, rows = part_ref.shape
        share = feats // count
        more = places * share * rows // width
        for at, ref in enumerate(sent_refs):
            first = lax.rem(place_ref[3] + at, count) * share
            taken = part_ref[:, pl.ds(pl.multiple_of(first, share), share), :]
            taken = taken.reshape(places * share, rows)
            ref[:rows, :] = d_branch_ref[...]
            ref[rows : 2 * rows, :] = mixed_refs[at][...]
            ref[2 * rows :, :] = jnp.concatenate(
                [taken[more * at : more * (at + 1)] for at in range(width // rows)], axis=1
            )


def branch_back(place, resid, cotangent, gain, gathered, at, attended, backs, mixeds, step=4):
    rows, width = resid.shape
    places, feats, _ = attended.shape
    count = len(backs)
    row_spec = pl.BlockSpec((rows, width), lambda i: (0, 0))
    sent = shape((2 * rows + places * feats // count * rows // width, width), LOW)
    results = run(
        partial(branch_kernel, count),
        (places // step,),
        [
            pl.BlockSpec(memory_space=pltpu.SMEM),
            row_spec,
            row_spec,
            whole(gain),
            pl.BlockSpec((step, feats, width), lambda i: (i, at, 0)),
            whole(attended),
        ]
        + [row_spec] * (2 * count),
        [
            row_spec,
            pl.BlockSpec((4, width), lambda i: (0, 0)),
            pl.BlockSpec((step, feats, rows), lambda i: (i, 0, 0)),
        ]
        + [whole(sent)] * count,
        [
            shape((rows, width), jnp.float32),
            shape((4, width), jnp.float32),
            shape((places, feats, rows), LOW),
        ]
        + [sent] * count,
        (place, resid, cotangent, gain, gathered, attended, *backs, *mixeds),
        received=backs[1:],
        scratch=[pltpu.VMEM((rows, width), LOW)],
    )
    return (*results[:3], results[3:])


SMALL = 8


def packed(small):
    rounded = small.astype(LOW)
    return jnp.concatenate([rounded, (small - rounded.astype(jnp.float32)).astype(LOW)], axis=0)


def unpacked(rows):
    rows = rows.astype(jnp.float32)
    return rows[:SMALL] + rows[SMALL:]


def even_sum(terms):
    return (terms[0] + terms[2]) + (terms[1] + terms[3])


def branch_grad_kernel(count, chips, rows, place_ref, *refs):
    sent_refs, small_refs, (own_ref, other_ref, small_ref, parts) = take(refs, count, 3)
    chips_x, chips_y = chips
    places, feats = parts.shape[1:3]
    for at, ref in enumerate(sent_refs):
        taken = ref[2 * rows :, :]
        taken = [taken[:, rows * at : rows * (at + 1)] for at in range(taken.shape[1] // rows)]
        parts[at] = jnp.concatenate(taken, axis=0).reshape(places, feats, rows)
    grads = jnp.concatenate([ref[:rows, :] for ref in sent_refs], axis=0)

    def owner(at, core):
        x = lax.rem(place_ref[1] + at // chips_y, chips_x)
        y = lax.rem(place_ref[2] + at % chips_y, chips_y)
        return (x * chips_y + y) * 2 + core

    def grad(core):
        left = [
            jnp.concatenate([parts[step, owner(at, core)] for step in range(count)], axis=1)
            for at in range(chips_x * chips_y)
        ]
        return dot(jnp.concatenate(left, axis=0), grads).astype(LOW)

    total = own_ref.shape[0]
    small_ref[...] = jnp.zeros_like(small_ref)
    first = 0
    for ref in small_refs:
        small_ref[first : first + ref.shape[0], :] = ref[...]
        first += ref.shape[0]
    other_ref[:total, :] = grad(1 - place_ref[0])
    other_ref[total:, :] = packed(small_ref[...])
    own_ref[...] = grad(place_ref[0])


def branch_grad(place, chips, rows, sent, small):
    count = len(sent)
    places = 2 * chips[0] * chips[1]
    more, width = sent[0].shape
    feats = (more - 2 * rows) * width // rows // places
    total = places // 2 * feats
    out_shape = [
        shape((total, width), LOW),
        shape((total + 2 * SMALL, width), LOW),
        shape((SMALL, width), jnp.float32),
    ]
    return feed_run(
        partial(branch_grad_kernel, count, chips, rows),
        (1,),
        place,
        [fixed(sent[0].shape)] * count + [fixed(item.shape) for item in small],
        [fixed(item.shape) for item in out_shape],
        out_shape,
        (*sent, *small),
        [pltpu.VMEM((count, places, feats, rows), LOW)],
        32,
        received=sent[1:],
    )


def step_run(body, operands, out_shape, received):
    return run(
        body,
        (1,),
        [whole(item) for item in operands],
        [whole(item) for item in out_shape],
        out_shape,
        operands,
        received=received,
    )


def core_step_kernel(own_ref, other_ref, small_ref, *out_refs):
    total = own_ref.shape[0]
    rows = total // len(out_refs)
    out = own_ref[...].astype(jnp.float32) + other_ref[:total, :].astype(jnp.float32)
    out = out.astype(LOW)
    small = packed(small_ref[...] + unpacked(other_ref[total:, :]))
    for at, ref in enumerate(out_refs):
        ref[:rows, :] = out[at * rows : (at + 1) * rows]
        ref[rows:, :] = small


def core_step(own, other, small, count):
    rows, width = own.shape
    out = shape((rows // count + 2 * SMALL, width), LOW)
    return step_run(core_step_kernel, (own, other, small), [out] * count, (other,))


def chip_step_kernel(count, *refs):
    term_refs, out_refs = take(refs, count)
    total = term_refs[0].shape[0] - 2 * SMALL
    rows = total // len(out_refs)
    out = sum(ref[:total, :].astype(jnp.float32) for ref in term_refs).astype(LOW)
    small = packed(even_sum([unpacked(ref[total:, :]) for ref in term_refs]))
    for at, ref in enumerate(out_refs):
        ref[:rows, :] = out[at * rows : (at + 1) * rows]
        ref[rows:, :] = small


def chip_step(terms, count):
    rows, width = terms[0].shape
    out = shape(((rows - 2 * SMALL) // count + 2 * SMALL, width), LOW)
    return step_run(partial(chip_step_kernel, len(terms)), tuple(terms), [out] * count, terms[1:])


def item_step_kernel(count, *refs):
    term_refs, joint_refs, (bias_ref, out_ref) = take(refs, count, count)
    rows = term_refs[0].shape[0] - 2 * SMALL
    out = sum(ref[:rows, :].astype(jnp.float32) for ref in term_refs)
    small = even_sum([unpacked(ref[rows:, :]) for ref in term_refs])
    place = lax.broadcasted_iota(jnp.int32, small.shape, 0)
    small = jnp.where(place == SMALL - 1, bias_ref[...], small)
    joint = sum(ref[...].astype(jnp.float32) for ref in joint_refs)
    out_ref[:rows, :] = out.astype(LOW)
    out_ref[rows : rows + 2 * SMALL, :] = packed(small)
    out_ref[rows + 2 * SMALL :, :] = joint.astype(LOW)


def item_step(terms, joint, bias):
    rows, width = terms[0].shape
    out = shape((rows + joint[0].shape[0], width), LOW)
    return step_run(partial(item_step_kernel, len(terms)), (*terms, *joint, bias), [out], terms[1:] + joint[1:])[0]


def last_kernel(count, rows, place_ref, *refs):
    term_refs, (out_ref, joint_ref, small_ref, units_ref) = take(refs, count)
    small = []
    for at, ref in enumerate(term_refs):
        item = lax.rem(place_ref[3] + at, count)
        out_ref[pl.ds(pl.multiple_of(item * rows, rows), rows), :] = ref[:rows, :].astype(
            jnp.float32
        )
        joint = ref[rows + 2 * SMALL :, :].astype(jnp.float32)
        here = joint.shape[0]
        joint_ref[pl.ds(pl.multiple_of(item * here, here), here), :] = joint
        small.append(unpacked(ref[rows : rows + 2 * SMALL, :]))
        units_ref[item] = small[-1][0:1]
    small_ref[...] = even_sum(small)


def last_step(place, terms, rows):
    count = len(terms)
    total, width = terms[0].shape
    joint = total - rows - 2 * SMALL
    out_shape = [
        shape((count * rows, width), jnp.float32),
        shape((count * joint, width), jnp.float32),
        shape((SMALL, width), jnp.float32),
        shape((count, 1, width), jnp.float32),
    ]
    return run(
        partial(last_kernel, count, rows),
        (1,),
        [pl.BlockSpec(memory_space=pltpu.SMEM)] + [whole(item) for item in terms],
        [whole(item) for item in out_shape],
        out_shape,
        (place, *terms),
        received=terms[1:],
    )


def joint_grad_kernel(count, place_ref, *refs):
    (grad_ref, rows_ref, weight_ref, gain_ref, shift_ref), out_refs, refs = take(refs, 5, count)
    bias_ref, sums_ref, total, biases, bias_row = refs
    step = pl.program_id(0)
    grads = side_by_side(grad_ref)
    added = dot(grads, rows_ref[...].reshape(grads.shape[1], -1))
    summed = jnp.sum(grads.astype(jnp.float32), axis=1, keepdims=True)
    summed_row = dot_cols(jnp.ones((8, grads.shape[1]), LOW), grads)

    @pl.when(step == 0)
    def _():
        total[...] = added
        biases[...] = summed
        bias_row[...] = summed_row

    @pl.when(step > 0)
    def _():
        total[...] += added
        biases[...] += summed
        bias_row[...] += summed_row

    @pl.when(step == pl.num_programs(0) - 1)
    def _():
        rows = out_refs[0].shape[0]
        for at, ref in enumerate(out_refs):
            first = lax.rem(place_ref[3] + at, count) * rows
            ref[...] = total[pl.ds(pl.multiple_of(first, rows), rows), :].astype(LOW)
        bias_ref[...] = jnp.zeros_like(bias_ref)
        bias_ref[:, : bias_row.shape[1]] = bias_row[0:1, :]
        weight = weight_ref[...].astype(jnp.float32)
        shift_sum = jnp.sum(weight * biases[...], axis=0, keepdims=True)
        product = jnp.sum(weight * total[...], axis=0, keepdims=True)
        sums_ref[0:1, :] = (product - shift_sum * shift_ref[...]) / gain_ref[...]
        sums_ref[1:2, :] = shift_sum


def joint_grad(place, count, grads, gathered, weight, gain, shift, step=8):
    places, feats, rows = grads.shape
    width = gathered.shape[2]
    results = run(
        partial(joint_grad_kernel, count),
        (places // step,),
        [
            pl.BlockSpec(memory_space=pltpu.SMEM),
            pl.BlockSpec((step, feats, rows), lambda i: (i, 0, 0)),
            pl.BlockSpec((step, rows, width), lambda i: (i, 0, 0)),
            whole(weight),
            whole(gain),
            whole(shift),
        ],
        [pl.BlockSpec((feats // count, width), lambda i: (0, 0))] * count
        + [
            pl.BlockSpec((1, width), lambda i: (0, 0)),
            pl.BlockSpec((2, width), lambda i: (0, 0)),
        ],
        [shape((feats // count, width), LOW)] * count
        + [shape((1, width), jnp.float32), shape((2, width), jnp.float32)],
        (place, grads, gathered, weight, gain, shift),
        scratch=[
            pltpu.VMEM((feats, width), jnp.float32),
            pltpu.VMEM((feats, 1), jnp.float32),
            pltpu.VMEM((8, feats), jnp.float32),
        ],
    )
    return results[:count], *results[count:]


def input_kernel(part_ref, weight_ref, tokens_ref, gain_ref, d_resid_ref, out_ref, total):
    step = pl.program_id(0)
    added = dot(turned(part_ref[...]).astype(LOW), weight_ref[...])

    @pl.when(step == 0)
    def _():
        total[...] = added

    @pl.when(step > 0)
    def _():
        total[...] += added

    @pl.when(step == pl.num_programs(0) - 1)
    def _():
        normed, scale = norm_parts(tokens_ref[...].astype(jnp.float32))
        out_ref[...] = d_resid_ref[...] + norm_back(total[...], normed, scale, gain_ref[...])


def input_back(parts, weights, tokens, gain, d_resid, steps=6):
    feats, rows = parts.shape
    width = weights.shape[1]
    step = feats // steps
    return run(
        input_kernel,
        (steps,),
        [
            pl.BlockSpec((step, rows), lambda i: (i, 0)),
            pl.BlockSpec((step, width), lambda i: (i, 0)),
            whole(tokens),
            whole(gain),
            whole(d_resid),
        ],
        [pl.BlockSpec((rows, width), lambda i: (0, 0))],
        [shape((rows, width), jnp.float32)],
        (parts, weights, tokens, gain, d_resid),
        received=(parts,),
        scratch=[pltpu.VMEM((rows, width), jnp.float32)],
    )[0]


ITEM = "z"
HEAD = ("x", "y", "c")
CORE = "c"


def moved(value, axis, steps):
    count = lax.axis_size(axis)
    return lax.ppermute(value, axis, [(place, (place + steps) % count) for place in range(count)])


def shifted(value, axis, steps):
    count = lax.axis_size(axis)
    initial, last = (max(0, -steps), min(count, count - steps))
    return lax.ppermute(value, axis, [(source, source + steps) for source in range(initial, last)])


def around(value, axis):
    return [value] + [moved(value, axis, -step) for step in range(1, lax.axis_size(axis))]


def sum_back(values, axis):
    return [values[0]] + [
        moved(values[step], axis, step) for step in range(1, lax.axis_size(axis))
    ]


def head_swap(value):
    return lax.all_to_all(value, HEAD, split_axis=0, concat_axis=0, tiled=True)


def segment_flags(seg_counts):
    total_segs = seg_counts.shape[0]
    openings = jnp.cumsum(seg_counts) - seg_counts
    places = jnp.arange(total_segs, dtype=jnp.int32)
    opens_here = jnp.any((openings[:, None] == places[None, :]) & (seg_counts[:, None] > 0), axis=0)
    opens_before = jnp.concatenate([jnp.ones((1,), dtype=bool), opens_here[:-1]])
    one_back = jnp.logical_not(opens_here)
    two_back = one_back & jnp.logical_not(opens_before)
    return (one_back, two_back)


def local(
    tokens,
    cotangent,
    seg_counts,
    query_weight,
    key_weight,
    value_weight,
    query_bias,
    value_bias,
    out_weight,
    out_bias,
    first_gain,
    first_shift,
    second_gain,
    second_shift,
    up_weight,
    up_bias,
    down_weight,
    down_bias,
):
    rows, width = tokens.shape
    heads = lax.axis_size(HEAD)
    item_place = lax.axis_index(ITEM)
    group_rows = rows * heads
    seg_local = group_rows // SEG
    feats = query_weight.shape[0]
    units = up_weight.shape[0]
    hidden_here = units * heads

    def row(vector):
        return vector.reshape(1, -1)

    tokens_f = tokens.astype(jnp.float32)
    inputs_one = layer_norm(tokens_f, first_gain, first_shift).astype(LOW)
    first = jnp.concatenate([inputs_one, out_weight], axis=0)
    gathered = lax.all_gather(first, HEAD, axis=0, tiled=True).reshape(heads, -1, width)
    second = jnp.concatenate([up_weight, down_weight], axis=0)
    feed_weights = lax.all_gather(second, HEAD, axis=0, tiled=True).reshape(heads, -1, width)
    cots = around(cotangent, ITEM)
    joint_weight = jnp.concatenate([query_weight, key_weight, value_weight], axis=0)
    joint_bias = jnp.concatenate([query_bias, jnp.zeros_like(query_bias), value_bias])

    one_back, two_back = segment_flags(seg_counts)
    flags = jnp.stack([two_back, one_back], axis=1).astype(jnp.int32)
    flags = lax.dynamic_slice_in_dim(flags, item_place * seg_local, seg_local).reshape(-1)

    gathered, cots = lax.optimization_barrier((gathered, cots))
    query, kv, turned_all = project(gathered, rows, joint_weight, row(joint_bias))
    own_kept = kv.reshape(seg_local, SEG, 2 * HD)[:, SEG - KEPT :]
    table = jnp.concatenate([shifted(own_kept, ITEM, 1), own_kept], axis=0)
    prefix = jnp.concatenate(
        [table[seg_local - 2 : 2 * seg_local - 2], table[seg_local - 1 : 2 * seg_local - 1]], axis=1
    )
    attended, log_sums = attend(flags, turned_all, kv, prefix, rows)
    attended_own = head_swap(attended)
    resid, inputs_two = out_project(
        attended_own, gathered, rows // feats, tokens, row(out_bias), row(second_gain), row(second_shift)
    )

    joint_turn = lax.optimization_barrier((joint_weight, resid))[0]
    joint_full = lax.all_gather(joint_turn, HEAD, axis=0, tiled=True)
    norms = around(inputs_two, ITEM)
    chips = (lax.axis_size("x"), lax.axis_size("y"))
    place = jnp.stack([lax.axis_index(axis) for axis in (CORE, "x", "y", ITEM)]).astype(jnp.int32)
    d_act, cots = feed_d_act(place, chips, cots, feed_weights)
    cots = [cots, moved(cots, CORE, 1)]
    bias_here = lax.dynamic_slice_in_dim(up_bias, item_place * hidden_here, hidden_here)
    backs, (norms, kept, sent, up_bias_part) = feed(
        place, chips, norms, feed_weights, bias_here.reshape(heads, 1, units), d_act
    )
    backs = sum_back(backs, ITEM)
    norms = [norms, moved(norms, CORE, 1)]
    mixeds, feed_parts = feed_grad(
        place, chips, len(backs), norms, cots, kept, sent, moved(sent, CORE, 1), feed_weights
    )
    backs, mixeds = lax.optimization_barrier((backs, mixeds))
    d_resid, sums_two, d_parts, sent = branch_back(
        place,
        resid,
        cotangent,
        row(second_gain),
        gathered,
        rows // feats,
        attended_own,
        backs,
        mixeds,
    )
    sent = sum_back(sent, ITEM)
    d_attended = head_swap(d_parts)
    feed_parts = lax.optimization_barrier((feed_parts, d_resid))[0]
    feed_grads = lax.psum_scatter(
        feed_parts.reshape(-1, width), ("x", "y"), scatter_dimension=0, tiled=True
    )
    d_prefix = prefix_back(
        flags, turned_all, query, d_attended, attended, log_sums, prefix, rows
    )[0]
    older, newer = d_prefix[:, :KEPT], d_prefix[:, KEPT:]
    spread = jnp.pad(older, ((seg_local - 2, 2), (0, 0), (0, 0)))
    spread = spread + jnp.pad(newer, ((seg_local - 1, 1), (0, 0), (0, 0)))
    returned = shifted(spread[:seg_local], ITEM, -1)
    joint_grads, kept_grads = attend_back(
        flags, turned_all, query, d_attended, attended, log_sums, prefix, kv, rows, 1
    )
    returned, kept_grads, joint_full = lax.optimization_barrier((returned, kept_grads, joint_full))
    joint_grads = add_returned(joint_grads, kept_grads, spread[seg_local:] + returned)
    grads_own = head_swap(joint_grads[0]).reshape(-1, rows)
    joint_parts, bias_part, sums_one = joint_grad(
        place,
        lax.axis_size(ITEM),
        joint_grads[0],
        gathered,
        joint_weight,
        row(first_gain),
        row(first_shift),
    )
    joint_parts, sums_one, sent = lax.optimization_barrier((joint_parts, sums_one, sent))
    out_own, out_other, small = branch_grad(
        place, chips, rows, sent, (row(up_bias_part), sums_two, sums_one)
    )
    joint_parts = sum_back(joint_parts, ITEM)
    terms = core_step(out_own, moved(out_other, CORE, 1), small, chips[0])
    grads_own, terms, joint_parts = lax.optimization_barrier((grads_own, terms, joint_parts))
    terms = sum_back(terms, "x")
    input_grad = input_back(grads_own, joint_full, tokens, row(first_gain), d_resid)
    input_grad, terms, sent = lax.optimization_barrier((input_grad, terms, sent))
    mixed = sum(part[rows : 2 * rows].astype(jnp.float32) for part in sent)
    terms = sum_back(chip_step(terms, chips[1]), "y")
    terms = around(item_step(terms, joint_parts, bias_part), ITEM)
    terms, feed_grads = lax.optimization_barrier((terms, feed_grads))
    share = feats // lax.axis_size(ITEM)
    out_sum, joint_sums, small, up_bias_grad = last_step(place, terms, share)
    up_bias_grad = up_bias_grad.reshape(-1)
    bias_sums, early_rows, late = small[SMALL - 1, : 3 * feats], small[1:5], small[5:7]
    feed_grads = feed_grads.astype(jnp.float32)
    mixed_out = (resid + mixed + down_bias).astype(LOW)
    return (
        mixed_out,
        input_grad,
        joint_sums[:feats],
        joint_sums[feats : 2 * feats],
        joint_sums[2 * feats :],
        bias_sums[:feats],
        bias_sums[2 * feats : 3 * feats],
        out_sum,
        early_rows[2],
        late[0],
        late[1],
        early_rows[0],
        early_rows[1],
        feed_grads[:units],
        up_bias_grad,
        feed_grads[units:],
        early_rows[3],
    )


def solution(mesh):
    sizes = (mesh.shape["item"], 4, mesh.shape["head"] // 8, 2)
    fine = Mesh(mesh.devices.reshape(sizes), (ITEM, *HEAD))
    split = P((ITEM, *HEAD), None)
    by_head = P(HEAD, None)
    return jax.shard_map(
        local,
        mesh=fine,
        in_specs=(
            split,
            split,
            P(),
            by_head,
            by_head,
            by_head,
            P(HEAD),
            P(HEAD),
            by_head,
            P(),
            P(),
            P(),
            P(),
            P(),
            split,
            P(),
            split,
            P(),
        ),
        out_specs=(
            split,
            split,
            by_head,
            by_head,
            by_head,
            P(HEAD),
            P(HEAD),
            by_head,
            P(),
            P(),
            P(),
            P(),
            P(),
            split,
            P(),
            split,
            P(),
        ),
        check_vma=False,
    )
```

```python
import math
from functools import partial

import jax
import jax.numpy as jnp
from jax import lax
from jax.experimental import pallas as pl
from jax.experimental.pallas import tpu as pltpu
from jax.sharding import Mesh
from jax.sharding import PartitionSpec as P

HD = 64
NSUM = 50
SEG = 2048
SPAN = 512
KEPT = 64
EPSILON = 1e-05
MASKED = -1e30
SCALE = HD ** (-0.5)
MIB = 1 << 20
COST = 1 << 20
BIG = 1 << 17
LOW = jnp.bfloat16


def dot(left, right):
    return jnp.dot(left, right, preferred_element_type=jnp.float32)


def dot_cols(left, right):
    return lax.dot_general(
        left, right, (((1,), (1,)), ((), ())), preferred_element_type=jnp.float32
    )


def turned(value):
    return value.astype(jnp.float32).T


def norm_parts(row_data):
    row_mean = jnp.mean(row_data, axis=-1, keepdims=True)
    centred = row_data - row_mean
    row_var = jnp.mean(centred * centred, axis=-1, keepdims=True)
    scale = lax.rsqrt(row_var + EPSILON)
    return centred * scale, scale


def norm_back(grad, normed, scale, gain):
    scaled = grad * gain
    return scale * (
        scaled
        - jnp.mean(scaled, axis=-1, keepdims=True)
        - normed * jnp.mean(scaled * normed, axis=-1, keepdims=True)
    )


def layer_norm(row_data, gain, shift):
    return norm_parts(row_data)[0] * gain + shift


def in_hbm(operands, received):
    kept = [id(item) for item in received]
    return [
        pltpu.with_memory_space_constraint(item, pltpu.HBM)
        if item.size >= BIG and id(item) not in kept
        else item
        for item in operands
    ]


def out_hbm(shapes):
    return [
        pltpu.HBM(item.shape, item.dtype) if math.prod(item.shape) >= BIG else item
        for item in shapes
    ]


def run(body, grid, in_specs, out_specs, out_shape, operands, scratch=(), vmem=32, aliases=None, received=()):
    return pl.pallas_call(
        body,
        grid=grid,
        in_specs=in_specs,
        out_specs=out_specs,
        out_shape=out_hbm(out_shape),
        scratch_shapes=scratch,
        compiler_params=pltpu.CompilerParams(
            dimension_semantics=("arbitrary",) * len(grid), vmem_limit_bytes=vmem * MIB
        ),
        input_output_aliases=aliases or {},
        cost_estimate=pl.CostEstimate(flops=COST, bytes_accessed=COST, transcendentals=0),
    )(*in_hbm(operands, received))


def shape(dims, kind):
    return jax.ShapeDtypeStruct(dims, kind)


def whole(item):
    return pl.BlockSpec(item.shape, lambda *_: (0,) * len(item.shape))


def project_kernel(rows_ref, weight_ref, bias_ref, query_ref, kv_ref, turned_ref):
    rows = rows_ref[...].reshape(-1, rows_ref.shape[2])
    joint = dot_cols(rows, weight_ref[...]) + bias_ref[...]
    query_ref[...] = joint[:, :HD].astype(LOW)
    kv_ref[...] = joint[:, HD:].astype(LOW)
    turned_ref[...] = joint.T.astype(LOW)


def project(gathered, rows_here, weight, bias, span=2 * SPAN):
    places, _, width = gathered.shape
    total = places * rows_here
    step = span // rows_here
    return run(
        project_kernel,
        (total // span,),
        [
            pl.BlockSpec((step, rows_here, width), lambda i: (i, 0, 0)),
            whole(weight),
            whole(bias),
        ],
        [
            pl.BlockSpec((span, HD), lambda i: (i, 0)),
            pl.BlockSpec((span, 2 * HD), lambda i: (i, 0)),
            pl.BlockSpec((3 * HD, span), lambda i: (0, i)),
        ],
        [
            shape((total, HD), LOW),
            shape((total, 2 * HD), LOW),
            shape((3 * HD, total), LOW),
        ],
        (gathered, weight, bias),
    )


def prefix_seen(flags_ref, seg, columns):
    place = lax.broadcasted_iota(jnp.int32, (2 * KEPT, columns), 0)
    older = place < KEPT
    slot = jnp.where(older, place, place - KEPT) >= KEPT - NSUM
    flag = jnp.where(older, flags_ref[2 * seg], flags_ref[2 * seg + 1])
    return slot & (flag > 0)


def causal_seen():
    shape_here = (SPAN, SPAN)
    return lax.broadcasted_iota(jnp.int32, shape_here, 0) <= lax.broadcasted_iota(
        jnp.int32, shape_here, 1
    )


def above(block):
    return jnp.concatenate([block, jnp.zeros_like(block)], axis=0)


def below(block):
    return jnp.concatenate([jnp.zeros_like(block), block], axis=0)


def at_block(index):
    return pl.ds(pl.multiple_of(index * SPAN, SPAN), SPAN)


def attend_kernel(flags_ref, query_ref, turned_ref, kv_ref, prefix_ref, out_ref, log_ref):
    seg, block = pl.program_id(0), pl.program_id(1)
    query = above((query_ref[...].astype(jnp.float32) * SCALE).astype(LOW))
    own = at_block(block)
    scores = dot(kv_ref[own, :], query)
    scores = jnp.where(causal_seen(), scores, MASKED)
    top = jnp.max(scores, axis=0, keepdims=True)
    probs = jnp.exp(scores - top)
    total = jnp.sum(probs, axis=0, keepdims=True)
    mixed = dot(turned_ref[2 * HD :, own], probs.astype(LOW))

    def add(carry, scores, values):
        top, total, mixed = carry
        fresh = jnp.maximum(top, jnp.max(scores, axis=0, keepdims=True))
        fade = jnp.exp(top - fresh)
        probs = jnp.exp(scores - fresh)
        total = total * fade + jnp.sum(probs, axis=0, keepdims=True)
        return fresh, total, mixed * fade + dot(values, probs.astype(LOW))

    prefix = prefix_ref[0]
    scores = jnp.where(prefix_seen(flags_ref, seg, SPAN), dot(prefix, query), MASKED)
    carry = add((top, total, mixed), scores, turned(prefix)[HD:].astype(LOW))

    def step(index, carry):
        here = at_block(index)
        return add(carry, dot(kv_ref[here, :], query), turned_ref[2 * HD :, here])

    top, total, mixed = lax.fori_loop(0, block, step, carry)
    mixed = (mixed / total).astype(LOW)
    rows = out_ref.shape[2]
    for piece in range(SPAN // rows):
        out_ref[piece] = mixed[:, piece * rows : (piece + 1) * rows]
    log_ref[0] = top + jnp.log(total)


def attend(flags, turned_all, kv, prefix, rows_here):
    total = kv.shape[0]
    blocks = SEG // SPAN
    step = SPAN // rows_here
    return run(
        attend_kernel,
        (total // SEG, blocks),
        [
            pl.BlockSpec(memory_space=pltpu.SMEM),
            pl.BlockSpec((HD, SPAN), lambda s, i: (0, s * blocks + i)),
            pl.BlockSpec((3 * HD, SEG), lambda s, i: (0, s)),
            pl.BlockSpec((SEG, 2 * HD), lambda s, i: (s, 0)),
            pl.BlockSpec((1, 2 * KEPT, 2 * HD), lambda s, i: (s, 0, 0)),
        ],
        [
            pl.BlockSpec((step, HD, rows_here), lambda s, i: (s * blocks + i, 0, 0)),
            pl.BlockSpec((1, 1, SPAN), lambda s, i: (s * blocks + i, 0, 0)),
        ],
        [
            shape((total // rows_here, HD, rows_here), LOW),
            shape((total // SPAN, 1, SPAN), jnp.float32),
        ],
        (flags, turned_all, turned_all, kv, prefix),
    )


def side_by_side(ref):
    return jnp.concatenate([ref[piece] for piece in range(ref.shape[0])], axis=1)


def beside(block, place):
    zero = jnp.zeros_like(block)
    return jnp.concatenate([block, zero] if place == 0 else [zero, block], axis=1)


def query_side(query_ref, rows_ref, grad_ref, out_ref, log_ref):
    query = above((query_ref[...].astype(jnp.float32) * SCALE).astype(LOW))
    grad = side_by_side(grad_ref)
    mean = jnp.sum(
        grad.astype(jnp.float32) * side_by_side(out_ref).astype(jnp.float32),
        axis=0,
        keepdims=True,
    )
    query_rows = beside((rows_ref[...].astype(jnp.float32) * SCALE).astype(LOW), 0)
    grad_rows = beside(turned(grad).astype(LOW), 1)
    return query, below(grad), mean, log_ref[0], query_rows, grad_rows


def key_side(keys, side, seen):
    query, grad, mean, log_sum, query_rows, grad_rows = side
    probs = jnp.exp(dot(keys, query) - log_sum)
    if seen is not None:
        probs = jnp.where(seen, probs, 0.0)
    d_scores = (probs * (dot(keys, grad) - mean)).astype(LOW)
    return probs.astype(LOW), d_scores


def prefix_back_kernel(
    flags_ref, query_ref, rows_ref, grad_ref, out_ref, log_ref, prefix_ref, sum_ref
):
    seg, block = pl.program_id(0), pl.program_id(1)
    side = query_side(query_ref, rows_ref, grad_ref, out_ref, log_ref)
    probs, d_scores = key_side(prefix_ref[0], side, prefix_seen(flags_ref, seg, SPAN))
    part = dot(d_scores, side[4]) + dot(probs, side[5])

    @pl.when(block == 0)
    def _():
        sum_ref[0] = part

    @pl.when(block > 0)
    def _():
        sum_ref[0] += part


def store_shares(grads_ref, piece, part, columns):
    here = HD // grads_ref.shape[0]
    for share in range(grads_ref.shape[0]):
        for kind in (1, 2):
            first = (kind - 1) * HD + share * here
            grads_ref[share, piece, kind * here : (kind + 1) * here, columns] = part[
                first : first + here
            ]


def attend_back_kernel(
    flags_ref,
    query_ref,
    rows_ref,
    grad_ref,
    out_ref,
    log_ref,
    prefix_ref,
    turned_ref,
    kv_ref,
    grads_ref,
    kept_ref,
    kv_grad,
):
    seg, block = pl.program_id(0), pl.program_id(1)

    @pl.when(block == 0)
    def _():
        kv_grad[...] = jnp.zeros_like(kv_grad)

    side = query_side(query_ref, rows_ref, grad_ref, out_ref, log_ref)
    prefix = prefix_ref[0]
    _, d_scores = key_side(prefix, side, prefix_seen(flags_ref, seg, SPAN))
    query_grad = dot(turned(prefix)[:HD].astype(LOW), d_scores)

    def add(here, query_grad, seen):
        probs, d_scores = key_side(kv_ref[here, :], side, seen)
        kv_grad[here, :] += dot(d_scores, side[4]) + dot(probs, side[5])
        return query_grad + dot(turned_ref[HD : 2 * HD, here], d_scores)

    query_grad = add(at_block(block), query_grad, causal_seen())
    query_grad = lax.fori_loop(
        0, block, lambda index, grad: add(at_block(index), grad, None), query_grad
    )
    query_grad = (query_grad * SCALE).astype(LOW)
    rows = grads_ref.shape[3]
    step = SPAN // rows
    for piece in range(step):
        part = query_grad[:, piece * rows : (piece + 1) * rows]
        for share in range(grads_ref.shape[0]):
            here = HD // grads_ref.shape[0]
            grads_ref[share, block * step + piece, :here, :] = part[share * here : (share + 1) * here]

    @pl.when(block == pl.num_programs(1) - 1)
    def _():
        for piece in range(SEG // rows):
            part = kv_grad[piece * rows : (piece + 1) * rows, :].T.astype(LOW)
            store_shares(grads_ref, piece, part, slice(None))
        kept_ref[0] = kv_grad[SEG - KEPT :, :]


def attend_back_specs(rows_here):
    blocks = SEG // SPAN
    step = SPAN // rows_here
    return [
        pl.BlockSpec(memory_space=pltpu.SMEM),
        pl.BlockSpec((HD, SPAN), lambda s, i: (0, s * blocks + i)),
        pl.BlockSpec((SPAN, HD), lambda s, i: (s * blocks + i, 0)),
        pl.BlockSpec((step, HD, rows_here), lambda s, i: (s * blocks + i, 0, 0)),
        pl.BlockSpec((step, HD, rows_here), lambda s, i: (s * blocks + i, 0, 0)),
        pl.BlockSpec((1, 1, SPAN), lambda s, i: (s * blocks + i, 0, 0)),
        pl.BlockSpec((1, 2 * KEPT, 2 * HD), lambda s, i: (s, 0, 0)),
    ]


def prefix_back(flags, turned_all, query, grad, out, log_sums, prefix, rows_here):
    total = query.shape[0]
    return run(
        prefix_back_kernel,
        (total // SEG, SEG // SPAN),
        attend_back_specs(rows_here),
        [pl.BlockSpec((1, 2 * KEPT, 2 * HD), lambda s, i: (s, 0, 0))],
        [shape(prefix.shape, jnp.float32)],
        (flags, turned_all, query, grad, out, log_sums, prefix),
        received=(grad,),
    )


def attend_back(flags, turned_all, query, grad, out, log_sums, prefix, kv, rows_here, count):
    total = query.shape[0]
    pieces = SEG // rows_here
    return run(
        attend_back_kernel,
        (total // SEG, SEG // SPAN),
        attend_back_specs(rows_here)
        + [
            pl.BlockSpec((3 * HD, SEG), lambda s, i: (0, s)),
            pl.BlockSpec((SEG, 2 * HD), lambda s, i: (s, 0)),
        ],
        [
            pl.BlockSpec(
                (count, pieces, 3 * HD // count, rows_here), lambda s, i: (0, s, 0, 0)
            ),
            pl.BlockSpec((1, KEPT, 2 * HD), lambda s, i: (s, 0, 0)),
        ],
        [
            shape((count, total // rows_here, 3 * HD // count, rows_here), LOW),
            shape((total // SEG, KEPT, 2 * HD), jnp.float32),
        ],
        (flags, turned_all, query, grad, out, log_sums, prefix, turned_all, kv),
        received=(grad,),
        scratch=[pltpu.VMEM((SEG, 2 * HD), jnp.float32)],
    )


def returned_kernel(grads_ref, kept_ref, returned_ref, out_ref):
    out_ref[...] = grads_ref[...]
    part = (kept_ref[0] + returned_ref[0]).T.astype(LOW)
    store_shares(out_ref, 0, part, slice(out_ref.shape[3] - KEPT, None))


def add_returned(grads, kept, returned):
    count, places, feats, rows = grads.shape
    segs = kept.shape[0]
    last = places // segs
    grad_spec = pl.BlockSpec((count, 1, feats, rows), lambda s: (0, s * last + last - 1, 0, 0))
    kept_spec = pl.BlockSpec((1, KEPT, 2 * HD), lambda s: (s, 0, 0))
    return run(
        returned_kernel,
        (segs,),
        [grad_spec, kept_spec, kept_spec],
        [grad_spec],
        [shape(grads.shape, LOW)],
        (grads, kept, returned),
        aliases={0: 0},
    )[0]


def out_kernel(
    part_ref, weight_ref, tokens_ref, bias_ref, gain_ref, shift_ref, resid_ref, two_ref, total
):
    step = pl.program_id(0)
    rows = part_ref.shape[2]
    part = turned(part_ref[...].reshape(-1, rows)).astype(LOW)
    added = dot(part, weight_ref[...].reshape(part.shape[1], -1))

    @pl.when(step == 0)
    def _():
        total[...] = added

    @pl.when(step > 0)
    def _():
        total[...] += added

    @pl.when(step == pl.num_programs(0) - 1)
    def _():
        resid = tokens_ref[...].astype(jnp.float32) + total[...] + bias_ref[...]
        resid_ref[...] = resid
        two_ref[...] = layer_norm(resid, gain_ref[...], shift_ref[...]).astype(LOW)


def out_project(parts, gathered, at, tokens, bias, gain, shift, step=8):
    places, feats, rows = parts.shape
    width = gathered.shape[2]
    return run(
        out_kernel,
        (places // step,),
        [
            pl.BlockSpec((step, feats, rows), lambda i: (i, 0, 0)),
            pl.BlockSpec((step, feats, width), lambda i: (i, at, 0)),
            whole(tokens),
            whole(bias),
            whole(gain),
            whole(shift),
        ],
        [pl.BlockSpec((rows, width), lambda i: (0, 0))] * 2,
        [shape((rows, width), jnp.float32), shape((rows, width), LOW)],
        (parts, gathered, tokens, bias, gain, shift),
        received=(parts,),
        scratch=[pltpu.VMEM((rows, width), jnp.float32)],
    )


def owner_maps(chips, at):
    def of(core_step, chip):
        return lambda i, place: at((i * chips[1] + chip) * 2 + lax.rem(place[0] + core_step, 2))

    return [of(core_step, chip) for core_step in (0, 1) for chip in range(chips[1])]


def own_map(index):
    return lambda i, place: index(i)


def fixed(dims):
    return pl.BlockSpec(
        dims, own_map(lambda i: (0,) * len(dims)), pipeline_mode=pl.Buffered(buffer_count=1)
    )


def feed_run(
    body, chips, place, in_specs, out_specs, out_shape, operands, scratch, vmem, received=()
):
    return pl.pallas_call(
        body,
        grid_spec=pltpu.PrefetchScalarGridSpec(
            num_scalar_prefetch=1,
            grid=(chips[0],),
            in_specs=in_specs,
            out_specs=out_specs,
            scratch_shapes=scratch,
        ),
        out_shape=out_hbm(out_shape),
        compiler_params=pltpu.CompilerParams(
            dimension_semantics=("arbitrary",), vmem_limit_bytes=vmem * MIB
        ),
        cost_estimate=pl.CostEstimate(flops=COST, bytes_accessed=COST, transcendentals=0),
    )(place, *in_hbm(operands, received))


def stacked(refs, axis=0):
    return jnp.concatenate([ref[0] for ref in refs], axis=axis)


def pile(refs, into):
    rows = refs[0].shape[0]
    for at, ref in enumerate(refs):
        into[at * rows : (at + 1) * rows, :] = ref[...]


def spread(source, refs):
    rows = refs[0].shape[0]
    for at, ref in enumerate(refs):
        ref[...] = source[at * rows : (at + 1) * rows, :].astype(ref.dtype)


def take(refs, *counts):
    refs = list(refs)
    return [[refs.pop(0) for _ in range(count)] for count in counts] + [refs]


def d_act_kernel(count, owners, place_ref, *refs):
    cot_refs, weight_refs, (out_ref, cots) = take(refs, count, owners)

    @pl.when(pl.program_id(0) == 0)
    def _():
        pile(cot_refs, cots)

    out_ref[...] = dot_cols(cots[...], stacked(weight_refs))


def feed_d_act(place, chips, cots, weights):
    count = len(cots)
    rows, width = cots[0].shape
    places, both, _ = weights.shape
    units = both // 2
    total = count * rows
    owners = 2 * chips[1]
    step = owners * units
    return feed_run(
        partial(d_act_kernel, count, owners),
        chips,
        place,
        [fixed((rows, width))] * count
        + [
            pl.BlockSpec((1, units, width), at)
            for at in owner_maps(chips, lambda owner: (owner, 1, 0))
        ],
        [pl.BlockSpec((total, step), own_map(lambda i: (0, i))), fixed((total, width))],
        [shape((total, places * units), jnp.float32), shape((total, width), LOW)],
        (*cots, *[weights] * owners),
        [],
        32,
        received=cots[1:],
    )


def feed_kernel(count, chips, place_ref, *refs):
    owners = 2 * chips[1]
    norm_refs, weight_refs, bias_refs, (d_act_ref,), back_refs, refs = take(
        refs, count, owners, owners, 1, count
    )
    norms, kept_ref, sent_ref, bias_sum_ref, back = refs
    step = pl.program_id(0)

    @pl.when(step == 0)
    def _():
        pile(norm_refs, norms)
        back[...] = jnp.zeros_like(back)

    units = weight_refs[0].shape[1]
    half = owners // 2
    added = []
    for ref, first in ((kept_ref, 0), (sent_ref, half)):
        up = stacked(weight_refs[first : first + half])
        bias = stacked(bias_refs[first : first + half], axis=1)
        here = slice(first * units, (first + half) * units)
        pre = dot_cols(norms[...], up) + bias
        square = pre * pre
        bent = jnp.tanh(0.7978845608 * (pre + 0.044715 * (square * pre)))
        up_half = 0.5 * (1.0 + bent)
        slope = up_half + 0.5 * pre * (1.0 - bent * bent) * (
            0.7978845608 * (1.0 + 3.0 * 0.044715 * square)
        )
        d_pre = (d_act_ref[:, here] * slope).astype(LOW)
        ref[0] = (pre * up_half).astype(LOW)
        ref[1] = d_pre
        bias_sums = jnp.sum(d_pre.astype(jnp.float32), axis=0, keepdims=True)
        for at, index in enumerate(owner_maps(chips, lambda owner: owner)[first : first + half]):
            bias_sum_ref[index(step, place_ref)] = bias_sums[:, at * units : (at + 1) * units]
        added.append(dot(d_pre, up))
    back[...] += added[0] + added[1]

    @pl.when(step == pl.num_programs(0) - 1)
    def _():
        spread(back, back_refs)


def feed(place, chips, norms, weights, bias, d_act):
    count = len(norms)
    rows, width = norms[0].shape
    places, both, _ = weights.shape
    units = both // 2
    total = count * rows
    owners = 2 * chips[1]
    step = owners * units
    pair_spec = pl.BlockSpec((2, total, step // 2), own_map(lambda i: (0, 0, i)))
    results = feed_run(
        partial(feed_kernel, count, chips),
        chips,
        place,
        [fixed((rows, width))] * count
        + [
            pl.BlockSpec((1, units, width), at)
            for at in owner_maps(chips, lambda owner: (owner, 0, 0))
        ]
        + [
            pl.BlockSpec((1, 1, units), at)
            for at in owner_maps(chips, lambda owner: (owner, 0, 0))
        ]
        + [pl.BlockSpec((total, step), own_map(lambda i: (0, i)))],
        [pl.BlockSpec((rows, width), own_map(lambda i: (0, 0)))] * count
        + [fixed((total, width)), pair_spec, pair_spec, fixed((places, 1, units))],
        [shape((rows, width), LOW)] * count
        + [shape((total, width), LOW)]
        + [shape((2, total, places * units // 2), LOW)] * 2
        + [shape((places, 1, units), jnp.float32)],
        (*norms, *[weights] * owners, *[bias] * owners, d_act),
        [pltpu.VMEM((total, width), jnp.float32)],
        40,
        received=norms[1:],
    )
    return results[:count], results[count:]


def feed_grad_kernel(count, owners, place_ref, *refs):
    norm_refs, cot_refs, pair_refs, weight_refs, mixed_refs, (out_ref, mixed) = take(
        refs, 2, 2, 3, owners, count
    )
    kept_ref, sent_ref, other_ref = pair_refs
    step = pl.program_id(0)
    units = weight_refs[0].shape[1]

    @pl.when(step == 0)
    def _():
        mixed[...] = jnp.zeros_like(mixed)

    act = jnp.concatenate([kept_ref[0], sent_ref[0]], axis=1)
    mixed[...] += dot(act, stacked(weight_refs))

    def grad(at, rows):
        total = dot(turned(kept_ref[at]).astype(LOW), rows[0][...])
        total += dot(turned(other_ref[at]).astype(LOW), rows[1][...])
        return total.astype(LOW).reshape(out_ref.shape[0], units, -1)

    out_ref[:, :units, :] = grad(1, norm_refs)
    out_ref[:, units:, :] = grad(0, cot_refs)

    @pl.when(step == pl.num_programs(0) - 1)
    def _():
        spread(mixed, mixed_refs)


def feed_grad(place, chips, count, norms, cots, kept, sent, other, weights):
    total, width = norms[0].shape
    rows = total // count
    units = weights.shape[1] // 2
    owners = 2 * chips[1]
    pair_spec = pl.BlockSpec((2, total, owners * units // 2), own_map(lambda i: (0, 0, i)))
    results = feed_run(
        partial(feed_grad_kernel, count, owners),
        chips,
        place,
        [fixed((total, width))] * 4
        + [pair_spec] * 3
        + [
            pl.BlockSpec((1, units, width), at)
            for at in owner_maps(chips, lambda owner: (owner, 1, 0))
        ],
        [pl.BlockSpec((rows, width), own_map(lambda i: (0, 0)))] * count
        + [pl.BlockSpec((chips[1], 2 * units, width), own_map(lambda i: (i, 0, 0)))],
        [shape((rows, width), LOW)] * count
        + [shape((chips[0] * chips[1], 2 * units, width), LOW)],
        (*norms, *cots, kept, sent, other, *[weights] * owners),
        [pltpu.VMEM((total, width), jnp.float32)],
        48,
        received=(norms[1], cots[1], other),
    )
    return results[:count], results[count]


def branch_kernel(count, place_ref, *refs):
    (resid_ref, cot_ref, gain_ref, weight_ref, part_ref), back_refs, refs = take(refs, 5, count)
    (d_resid_ref, sums_ref, parts_ref), sent_refs, (d_branch_ref,) = take(refs, 3, count)
    step = pl.program_id(0)

    @pl.when(step == 0)
    def _():
        d_two = sum(ref[...].astype(jnp.float32) for ref in back_refs)
        normed, scale = norm_parts(resid_ref[...])
        cot = cot_ref[...].astype(jnp.float32)
        d_resid = cot + norm_back(d_two, normed, scale, gain_ref[...])
        d_branch = d_resid.astype(LOW)
        d_resid_ref[...] = d_resid
        d_branch_ref[...] = d_branch
        sums_ref[0:1, :] = jnp.sum(d_two * normed, axis=0, keepdims=True)
        sums_ref[1:2, :] = jnp.sum(d_two, axis=0, keepdims=True)
        sums_ref[2:3, :] = jnp.sum(d_branch.astype(jnp.float32), axis=0, keepdims=True)
        sums_ref[3:4, :] = jnp.sum(cot, axis=0, keepdims=True)

    width = weight_ref.shape[2]
    part = dot_cols(weight_ref[...].reshape(-1, width), d_branch_ref[...])
    parts_ref[...] = part.reshape(parts_ref.shape).astype(LOW)

    @pl.when(step == pl.num_programs(0) - 1)
    def _():
        places, feats, rows = part_ref.shape
        share = feats // count
        more = places * share * rows // width
        for at, ref in enumerate(sent_refs):
            first = lax.rem(place_ref[3] + at, count) * share
            taken = part_ref[:, pl.ds(pl.multiple_of(first, share), share), :]
            taken = taken.reshape(places * share, rows)
            ref[:rows, :] = d_branch_ref[...]
            ref[rows:, :] = jnp.concatenate(
                [taken[more * at : more * (at + 1)] for at in range(width // rows)], axis=1
            )


def branch_back(place, resid, cotangent, gain, gathered, at, attended, backs, step=8):
    rows, width = resid.shape
    places, feats, _ = attended.shape
    count = len(backs)
    row_spec = pl.BlockSpec((rows, width), lambda i: (0, 0))
    sent = shape((rows + places * feats // count * rows // width, width), LOW)
    results = run(
        partial(branch_kernel, count),
        (places // step,),
        [
            pl.BlockSpec(memory_space=pltpu.SMEM),
            row_spec,
            row_spec,
            whole(gain),
            pl.BlockSpec((step, feats, width), lambda i: (i, at, 0)),
            whole(attended),
        ]
        + [row_spec] * count,
        [
            row_spec,
            pl.BlockSpec((4, width), lambda i: (0, 0)),
            pl.BlockSpec((step, feats, rows), lambda i: (i, 0, 0)),
        ]
        + [whole(sent)] * count,
        [
            shape((rows, width), jnp.float32),
            shape((4, width), jnp.float32),
            shape((places, feats, rows), LOW),
        ]
        + [sent] * count,
        (place, resid, cotangent, gain, gathered, attended, *backs),
        received=backs[1:],
        scratch=[pltpu.VMEM((rows, width), LOW)],
    )
    return (*results[:3], results[3:])


SMALL = 8


def packed(small):
    rounded = small.astype(LOW)
    return jnp.concatenate([rounded, (small - rounded.astype(jnp.float32)).astype(LOW)], axis=0)


def unpacked(rows):
    rows = rows.astype(jnp.float32)
    return rows[:SMALL] + rows[SMALL:]


def even_sum(terms):
    return (terms[0] + terms[2]) + (terms[1] + terms[3])


def branch_grad_kernel(count, chips, rows, place_ref, *refs):
    sent_refs, small_refs, (own_ref, other_ref, small_ref, parts) = take(refs, count, 3)
    chips_x, chips_y = chips
    places, feats = parts.shape[1:3]
    for at, ref in enumerate(sent_refs):
        taken = ref[rows:, :]
        taken = [taken[:, rows * at : rows * (at + 1)] for at in range(taken.shape[1] // rows)]
        parts[at] = jnp.concatenate(taken, axis=0).reshape(places, feats, rows)
    grads = jnp.concatenate([ref[:rows, :] for ref in sent_refs], axis=0)

    def owner(at, core):
        x = lax.rem(place_ref[1] + at // chips_y, chips_x)
        y = lax.rem(place_ref[2] + at % chips_y, chips_y)
        return (x * chips_y + y) * 2 + core

    def grad(core):
        left = [
            jnp.concatenate([parts[step, owner(at, core)] for step in range(count)], axis=1)
            for at in range(chips_x * chips_y)
        ]
        return dot(jnp.concatenate(left, axis=0), grads).astype(LOW)

    total = own_ref.shape[0]
    small_ref[...] = jnp.zeros_like(small_ref)
    first = 0
    for ref in small_refs:
        small_ref[first : first + ref.shape[0], :] = ref[...]
        first += ref.shape[0]
    other_ref[:total, :] = grad(1 - place_ref[0])
    other_ref[total:, :] = packed(small_ref[...])
    own_ref[...] = grad(place_ref[0])


def branch_grad(place, chips, rows, sent, small):
    count = len(sent)
    places = 2 * chips[0] * chips[1]
    more, width = sent[0].shape
    feats = (more - rows) * width // rows // places
    total = places // 2 * feats
    out_shape = [
        shape((total, width), LOW),
        shape((total + 2 * SMALL, width), LOW),
        shape((SMALL, width), jnp.float32),
    ]
    return feed_run(
        partial(branch_grad_kernel, count, chips, rows),
        (1,),
        place,
        [fixed(sent[0].shape)] * count + [fixed(item.shape) for item in small],
        [fixed(item.shape) for item in out_shape],
        out_shape,
        (*sent, *small),
        [pltpu.VMEM((count, places, feats, rows), LOW)],
        32,
        received=sent[1:],
    )


def step_run(body, place, operands, out_shape, received):
    return run(
        body,
        (1,),
        [pl.BlockSpec(memory_space=pltpu.SMEM)] + [whole(item) for item in operands],
        [whole(item) for item in out_shape],
        out_shape,
        (place, *operands),
        received=received,
    )


def lay_out(out, small, first, ref):
    count = ref.shape[0]
    rows = out.shape[0] // count
    for step in range(count):
        to = lax.rem(first + step, count)
        ref[to, :rows, :] = out[step * rows : (step + 1) * rows]
        ref[to, rows:, :] = small


def core_step_kernel(place_ref, own_ref, other_ref, small_ref, out_ref):
    total = own_ref.shape[0]
    out = own_ref[...].astype(jnp.float32) + other_ref[:total, :].astype(jnp.float32)
    small = packed(small_ref[...] + unpacked(other_ref[total:, :]))
    lay_out(out.astype(LOW), small, place_ref[1], out_ref)


def core_step(place, own, other, small, count):
    rows, width = own.shape
    out = shape((count, rows // count + 2 * SMALL, width), LOW)
    return step_run(core_step_kernel, place, (own, other, small), [out], (other,))[0]


def summed(ref):
    total = ref.shape[1] - 2 * SMALL
    out = sum(ref[at, :total, :].astype(jnp.float32) for at in range(ref.shape[0]))
    return out, sum(unpacked(ref[at, total:, :]) for at in range(ref.shape[0]))


def chip_step_kernel(place_ref, term_ref, out_ref):
    out, small = summed(term_ref)
    lay_out(out.astype(LOW), packed(small), place_ref[2], out_ref)


def chip_step(place, terms, count):
    _, rows, width = terms.shape
    out = shape((count, (rows - 2 * SMALL) // count + 2 * SMALL, width), LOW)
    return step_run(chip_step_kernel, place, (terms,), [out], (terms,))[0]


def item_step_kernel(count, place_ref, *refs):
    (term_ref,), joint_refs, mixed_refs, refs = take(refs, 1, count, count)
    bias_ref, resid_ref, down_bias_ref, out_ref, mixed_ref = refs
    out, small = summed(term_ref)
    place = lax.broadcasted_iota(jnp.int32, small.shape, 0)
    small = jnp.where(place == SMALL - 1, bias_ref[...], small)
    rows = out.shape[0]
    joint = sum(ref[...].astype(jnp.float32) for ref in joint_refs)
    mixed = sum(ref[...].astype(jnp.float32) for ref in mixed_refs)
    out_ref[:rows, :] = out.astype(LOW)
    out_ref[rows : rows + 2 * SMALL, :] = packed(small)
    out_ref[rows + 2 * SMALL :, :] = joint.astype(LOW)
    mixed_ref[...] = (resid_ref[...] + mixed + down_bias_ref[...]).astype(LOW)


def item_step(place, terms, joint, mixeds, bias, resid, down_bias):
    _, rows, width = terms.shape
    return step_run(
        partial(item_step_kernel, len(joint)),
        place,
        (terms, *joint, *mixeds, bias, resid, down_bias),
        [shape((rows + joint[0].shape[0], width), LOW), shape(resid.shape, LOW)],
        [terms, *joint[1:], *mixeds[1:]],
    )


def last_kernel(count, rows, place_ref, *refs):
    term_refs, (out_ref, joint_ref, small_ref, units_ref) = take(refs, count)
    small = []
    for at, ref in enumerate(term_refs):
        item = lax.rem(place_ref[3] + at, count)
        out_ref[pl.ds(pl.multiple_of(item * rows, rows), rows), :] = ref[:rows, :].astype(
            jnp.float32
        )
        joint = ref[rows + 2 * SMALL :, :].astype(jnp.float32)
        here = joint.shape[0]
        joint_ref[pl.ds(pl.multiple_of(item * here, here), here), :] = joint
        small.append(unpacked(ref[rows : rows + 2 * SMALL, :]))
        units_ref[item] = small[-1][0:1]
    small_ref[...] = even_sum(small)


def last_step(place, terms, rows):
    count = len(terms)
    total, width = terms[0].shape
    joint = total - rows - 2 * SMALL
    out_shape = [
        shape((count * rows, width), jnp.float32),
        shape((count * joint, width), jnp.float32),
        shape((SMALL, width), jnp.float32),
        shape((count, 1, width), jnp.float32),
    ]
    return run(
        partial(last_kernel, count, rows),
        (1,),
        [pl.BlockSpec(memory_space=pltpu.SMEM)] + [whole(item) for item in terms],
        [whole(item) for item in out_shape],
        out_shape,
        (place, *terms),
        received=terms[1:],
    )


def joint_grad_kernel(count, place_ref, *refs):
    (grad_ref, rows_ref, weight_ref, gain_ref, shift_ref), out_refs, refs = take(refs, 5, count)
    bias_ref, sums_ref, total, biases, bias_row = refs
    step = pl.program_id(0)
    grads = side_by_side(grad_ref)
    added = dot(grads, rows_ref[...].reshape(grads.shape[1], -1))
    summed = jnp.sum(grads.astype(jnp.float32), axis=1, keepdims=True)
    summed_row = dot_cols(jnp.ones((8, grads.shape[1]), LOW), grads)

    @pl.when(step == 0)
    def _():
        total[...] = added
        biases[...] = summed
        bias_row[...] = summed_row

    @pl.when(step > 0)
    def _():
        total[...] += added
        biases[...] += summed
        bias_row[...] += summed_row

    @pl.when(step == pl.num_programs(0) - 1)
    def _():
        rows = out_refs[0].shape[0]
        for at, ref in enumerate(out_refs):
            first = lax.rem(place_ref[3] + at, count) * rows
            ref[...] = total[pl.ds(pl.multiple_of(first, rows), rows), :].astype(LOW)
        bias_ref[...] = jnp.zeros_like(bias_ref)
        bias_ref[:, : bias_row.shape[1]] = bias_row[0:1, :]
        weight = weight_ref[...].astype(jnp.float32)
        shift_sum = jnp.sum(weight * biases[...], axis=0, keepdims=True)
        product = jnp.sum(weight * total[...], axis=0, keepdims=True)
        sums_ref[0:1, :] = (product - shift_sum * shift_ref[...]) / gain_ref[...]
        sums_ref[1:2, :] = shift_sum


def joint_grad(place, count, grads, gathered, weight, gain, shift, step=8):
    places, feats, rows = grads.shape
    width = gathered.shape[2]
    results = run(
        partial(joint_grad_kernel, count),
        (places // step,),
        [
            pl.BlockSpec(memory_space=pltpu.SMEM),
            pl.BlockSpec((step, feats, rows), lambda i: (i, 0, 0)),
            pl.BlockSpec((step, rows, width), lambda i: (i, 0, 0)),
            whole(weight),
            whole(gain),
            whole(shift),
        ],
        [pl.BlockSpec((feats // count, width), lambda i: (0, 0))] * count
        + [
            pl.BlockSpec((1, width), lambda i: (0, 0)),
            pl.BlockSpec((2, width), lambda i: (0, 0)),
        ],
        [shape((feats // count, width), LOW)] * count
        + [shape((1, width), jnp.float32), shape((2, width), jnp.float32)],
        (place, grads, gathered, weight, gain, shift),
        scratch=[
            pltpu.VMEM((feats, width), jnp.float32),
            pltpu.VMEM((feats, 1), jnp.float32),
            pltpu.VMEM((8, feats), jnp.float32),
        ],
    )
    return results[:count], *results[count:]


def input_kernel(part_ref, weight_ref, tokens_ref, gain_ref, d_resid_ref, out_ref, total):
    step = pl.program_id(0)
    added = dot(turned(part_ref[...]).astype(LOW), weight_ref[...])

    @pl.when(step == 0)
    def _():
        total[...] = added

    @pl.when(step > 0)
    def _():
        total[...] += added

    @pl.when(step == pl.num_programs(0) - 1)
    def _():
        normed, scale = norm_parts(tokens_ref[...].astype(jnp.float32))
        out_ref[...] = d_resid_ref[...] + norm_back(total[...], normed, scale, gain_ref[...])


def input_back(parts, weights, tokens, gain, d_resid, steps=6):
    feats, rows = parts.shape
    width = weights.shape[1]
    step = feats // steps
    return run(
        input_kernel,
        (steps,),
        [
            pl.BlockSpec((step, rows), lambda i: (i, 0)),
            pl.BlockSpec((step, width), lambda i: (i, 0)),
            whole(tokens),
            whole(gain),
            whole(d_resid),
        ],
        [pl.BlockSpec((rows, width), lambda i: (0, 0))],
        [shape((rows, width), jnp.float32)],
        (parts, weights, tokens, gain, d_resid),
        received=(parts,),
        scratch=[pltpu.VMEM((rows, width), jnp.float32)],
    )[0]


ITEM = "z"
HEAD = ("x", "y", "c")
CORE = "c"


def moved(value, axis, steps):
    count = lax.axis_size(axis)
    return lax.ppermute(value, axis, [(place, (place + steps) % count) for place in range(count)])


def shifted(value, axis, steps):
    count = lax.axis_size(axis)
    initial, last = (max(0, -steps), min(count, count - steps))
    return lax.ppermute(value, axis, [(source, source + steps) for source in range(initial, last)])


def around(value, axis):
    return [value] + [moved(value, axis, -step) for step in range(1, lax.axis_size(axis))]


def sum_back(values, axis):
    return [values[0]] + [
        moved(values[step], axis, step) for step in range(1, lax.axis_size(axis))
    ]


def exchanged(value, axis):
    return lax.all_to_all(value, axis, split_axis=0, concat_axis=0, tiled=True)


def head_swap(value):
    return lax.all_to_all(value, HEAD, split_axis=0, concat_axis=0, tiled=True)


def segment_flags(seg_counts):
    total_segs = seg_counts.shape[0]
    openings = jnp.cumsum(seg_counts) - seg_counts
    places = jnp.arange(total_segs, dtype=jnp.int32)
    opens_here = jnp.any((openings[:, None] == places[None, :]) & (seg_counts[:, None] > 0), axis=0)
    opens_before = jnp.concatenate([jnp.ones((1,), dtype=bool), opens_here[:-1]])
    one_back = jnp.logical_not(opens_here)
    two_back = one_back & jnp.logical_not(opens_before)
    return (one_back, two_back)


def local(
    tokens,
    cotangent,
    seg_counts,
    query_weight,
    key_weight,
    value_weight,
    query_bias,
    value_bias,
    out_weight,
    out_bias,
    first_gain,
    first_shift,
    second_gain,
    second_shift,
    up_weight,
    up_bias,
    down_weight,
    down_bias,
):
    rows, width = tokens.shape
    heads = lax.axis_size(HEAD)
    item_place = lax.axis_index(ITEM)
    group_rows = rows * heads
    seg_local = group_rows // SEG
    feats = query_weight.shape[0]
    units = up_weight.shape[0]
    hidden_here = units * heads

    def row(vector):
        return vector.reshape(1, -1)

    tokens_f = tokens.astype(jnp.float32)
    inputs_one = layer_norm(tokens_f, first_gain, first_shift).astype(LOW)
    first = jnp.concatenate([inputs_one, out_weight], axis=0)
    gathered = lax.all_gather(first, HEAD, axis=0, tiled=True).reshape(heads, -1, width)
    second = jnp.concatenate([up_weight, down_weight], axis=0)
    feed_weights = lax.all_gather(second, HEAD, axis=0, tiled=True).reshape(heads, -1, width)
    cots = around(cotangent, ITEM)
    joint_weight = jnp.concatenate([query_weight, key_weight, value_weight], axis=0)
    joint_bias = jnp.concatenate([query_bias, jnp.zeros_like(query_bias), value_bias])

    one_back, two_back = segment_flags(seg_counts)
    flags = jnp.stack([two_back, one_back], axis=1).astype(jnp.int32)
    flags = lax.dynamic_slice_in_dim(flags, item_place * seg_local, seg_local).reshape(-1)

    gathered, cots = lax.optimization_barrier((gathered, cots))
    query, kv, turned_all = project(gathered, rows, joint_weight, row(joint_bias))
    own_kept = kv.reshape(seg_local, SEG, 2 * HD)[:, SEG - KEPT :]
    table = jnp.concatenate([shifted(own_kept, ITEM, 1), own_kept], axis=0)
    prefix = jnp.concatenate(
        [table[seg_local - 2 : 2 * seg_local - 2], table[seg_local - 1 : 2 * seg_local - 1]], axis=1
    )
    attended, log_sums = attend(flags, turned_all, kv, prefix, rows)
    attended_own = head_swap(attended)
    resid, inputs_two = out_project(
        attended_own, gathered, rows // feats, tokens, row(out_bias), row(second_gain), row(second_shift)
    )

    joint_turn = lax.optimization_barrier((joint_weight, resid))[0]
    joint_full = lax.all_gather(joint_turn, HEAD, axis=0, tiled=True)
    norms = around(inputs_two, ITEM)
    chips = (lax.axis_size("x"), lax.axis_size("y"))
    place = jnp.stack([lax.axis_index(axis) for axis in (CORE, "x", "y", ITEM)]).astype(jnp.int32)
    d_act, cots = feed_d_act(place, chips, cots, feed_weights)
    cots = [cots, moved(cots, CORE, 1)]
    bias_here = lax.dynamic_slice_in_dim(up_bias, item_place * hidden_here, hidden_here)
    backs, (norms, kept, sent, up_bias_part) = feed(
        place, chips, norms, feed_weights, bias_here.reshape(heads, 1, units), d_act
    )
    backs = sum_back(backs, ITEM)
    norms = [norms, moved(norms, CORE, 1)]
    mixeds, feed_parts = feed_grad(
        place, chips, len(backs), norms, cots, kept, sent, moved(sent, CORE, 1), feed_weights
    )
    backs, mixeds = lax.optimization_barrier((backs, mixeds))
    d_resid, sums_two, d_parts, sent = branch_back(
        place,
        resid,
        cotangent,
        row(second_gain),
        gathered,
        rows // feats,
        attended_own,
        backs,
    )
    sent = sum_back(sent, ITEM)
    d_attended = head_swap(d_parts)
    feed_parts = lax.optimization_barrier((feed_parts, d_resid))[0]
    feed_grads = lax.psum_scatter(
        feed_parts.reshape(-1, width), ("x", "y"), scatter_dimension=0, tiled=True
    )
    d_prefix = prefix_back(
        flags, turned_all, query, d_attended, attended, log_sums, prefix, rows
    )[0]
    older, newer = d_prefix[:, :KEPT], d_prefix[:, KEPT:]
    spread = jnp.pad(older, ((seg_local - 2, 2), (0, 0), (0, 0)))
    spread = spread + jnp.pad(newer, ((seg_local - 1, 1), (0, 0), (0, 0)))
    returned = shifted(spread[:seg_local], ITEM, -1)
    joint_grads, kept_grads = attend_back(
        flags, turned_all, query, d_attended, attended, log_sums, prefix, kv, rows, 1
    )
    returned, kept_grads, joint_full = lax.optimization_barrier((returned, kept_grads, joint_full))
    joint_grads = add_returned(joint_grads, kept_grads, spread[seg_local:] + returned)
    grads_own = head_swap(joint_grads[0]).reshape(-1, rows)
    joint_parts, bias_part, sums_one = joint_grad(
        place,
        lax.axis_size(ITEM),
        joint_grads[0],
        gathered,
        joint_weight,
        row(first_gain),
        row(first_shift),
    )
    joint_parts, sums_one, sent = lax.optimization_barrier((joint_parts, sums_one, sent))
    joint_parts = sum_back(joint_parts, ITEM)
    out_own, out_other, small = branch_grad(
        place, chips, rows, sent, (row(up_bias_part), sums_two, sums_one)
    )
    terms = core_step(place, out_own, moved(out_other, CORE, 1), small, chips[0])
    grads_own, terms, joint_parts, mixeds = lax.optimization_barrier(
        (grads_own, terms, joint_parts, mixeds)
    )
    mixeds = sum_back(mixeds, ITEM)
    terms = exchanged(terms, "x")
    input_grad = input_back(grads_own, joint_full, tokens, row(first_gain), d_resid)
    input_grad, terms, mixeds = lax.optimization_barrier((input_grad, terms, mixeds))
    terms = exchanged(chip_step(place, terms, chips[1]), "y")
    terms, mixed_out = item_step(
        place, terms, joint_parts, mixeds, bias_part, resid, row(down_bias)
    )
    terms = around(terms, ITEM)
    terms, feed_grads = lax.optimization_barrier((terms, feed_grads))
    share = feats // lax.axis_size(ITEM)
    out_sum, joint_sums, small, up_bias_grad = last_step(place, terms, share)
    up_bias_grad = up_bias_grad.reshape(-1)
    bias_sums, early_rows, late = small[SMALL - 1, : 3 * feats], small[1:5], small[5:7]
    feed_grads = feed_grads.astype(jnp.float32)
    return (
        mixed_out,
        input_grad,
        joint_sums[:feats],
        joint_sums[feats : 2 * feats],
        joint_sums[2 * feats :],
        bias_sums[:feats],
        bias_sums[2 * feats : 3 * feats],
        out_sum,
        early_rows[2],
        late[0],
        late[1],
        early_rows[0],
        early_rows[1],
        feed_grads[:units],
        up_bias_grad,
        feed_grads[units:],
        early_rows[3],
    )


def solution(mesh):
    sizes = (mesh.shape["item"], 4, mesh.shape["head"] // 8, 2)
    fine = Mesh(mesh.devices.reshape(sizes), (ITEM, *HEAD))
    split = P((ITEM, *HEAD), None)
    by_head = P(HEAD, None)
    return jax.shard_map(
        local,
        mesh=fine,
        in_specs=(
            split,
            split,
            P(),
            by_head,
            by_head,
            by_head,
            P(HEAD),
            P(HEAD),
            by_head,
            P(),
            P(),
            P(),
            P(),
            P(),
            split,
            P(),
            split,
            P(),
        ),
        out_specs=(
            split,
            split,
            by_head,
            by_head,
            by_head,
            P(HEAD),
            P(HEAD),
            by_head,
            P(),
            P(),
            P(),
            P(),
            P(),
            split,
            P(),
            split,
            P(),
        ),
        check_vma=False,
    )
```

```python
import math
from functools import partial

import jax
import jax.numpy as jnp
from jax import lax
from jax.experimental import pallas as pl
from jax.experimental.pallas import tpu as pltpu
from jax.sharding import Mesh
from jax.sharding import PartitionSpec as P

HD = 64
NSUM = 50
SEG = 2048
SPAN = 512
KEPT = 64
EPSILON = 1e-05
MASKED = -1e30
SCALE = HD ** (-0.5)
MIB = 1 << 20
COST = 1 << 20
BIG = 1 << 17
LOW = jnp.bfloat16


def dot(left, right):
    return jnp.dot(left, right, preferred_element_type=jnp.float32)


def dot_cols(left, right):
    return lax.dot_general(
        left, right, (((1,), (1,)), ((), ())), preferred_element_type=jnp.float32
    )


def turned(value):
    return value.astype(jnp.float32).T


def norm_parts(row_data):
    row_mean = jnp.mean(row_data, axis=-1, keepdims=True)
    centred = row_data - row_mean
    row_var = jnp.mean(centred * centred, axis=-1, keepdims=True)
    scale = lax.rsqrt(row_var + EPSILON)
    return centred * scale, scale


def norm_back(grad, normed, scale, gain):
    scaled = grad * gain
    return scale * (
        scaled
        - jnp.mean(scaled, axis=-1, keepdims=True)
        - normed * jnp.mean(scaled * normed, axis=-1, keepdims=True)
    )


def layer_norm(row_data, gain, shift):
    return norm_parts(row_data)[0] * gain + shift


def in_hbm(operands, received):
    kept = [id(item) for item in received]
    return [
        pltpu.with_memory_space_constraint(item, pltpu.HBM)
        if item.size >= BIG and id(item) not in kept
        else item
        for item in operands
    ]


def out_hbm(shapes):
    return [
        pltpu.HBM(item.shape, item.dtype) if math.prod(item.shape) >= BIG else item
        for item in shapes
    ]


def run(body, grid, in_specs, out_specs, out_shape, operands, scratch=(), vmem=32, aliases=None, received=()):
    return pl.pallas_call(
        body,
        grid=grid,
        in_specs=in_specs,
        out_specs=out_specs,
        out_shape=out_hbm(out_shape),
        scratch_shapes=scratch,
        compiler_params=pltpu.CompilerParams(
            dimension_semantics=("arbitrary",) * len(grid), vmem_limit_bytes=vmem * MIB
        ),
        input_output_aliases=aliases or {},
        cost_estimate=pl.CostEstimate(flops=COST, bytes_accessed=COST, transcendentals=0),
    )(*in_hbm(operands, received))


def shape(dims, kind):
    return jax.ShapeDtypeStruct(dims, kind)


def whole(item):
    return pl.BlockSpec(item.shape, lambda *_: (0,) * len(item.shape))


def project_kernel(rows_ref, weight_ref, bias_ref, query_ref, kv_ref, turned_ref):
    rows = rows_ref[...].reshape(-1, rows_ref.shape[2])
    joint = dot_cols(rows, weight_ref[...]) + bias_ref[...]
    query_ref[...] = joint[:, :HD].astype(LOW)
    kv_ref[...] = joint[:, HD:].astype(LOW)
    turned_ref[...] = joint.T.astype(LOW)


def project(gathered, rows_here, weight, bias, span=2 * SPAN):
    places, _, width = gathered.shape
    total = places * rows_here
    step = span // rows_here
    return run(
        project_kernel,
        (total // span,),
        [
            pl.BlockSpec((step, rows_here, width), lambda i: (i, 0, 0)),
            whole(weight),
            whole(bias),
        ],
        [
            pl.BlockSpec((span, HD), lambda i: (i, 0)),
            pl.BlockSpec((span, 2 * HD), lambda i: (i, 0)),
            pl.BlockSpec((3 * HD, span), lambda i: (0, i)),
        ],
        [
            shape((total, HD), LOW),
            shape((total, 2 * HD), LOW),
            shape((3 * HD, total), LOW),
        ],
        (gathered, weight, bias),
    )


def prefix_seen(flags_ref, seg, columns):
    place = lax.broadcasted_iota(jnp.int32, (2 * KEPT, columns), 0)
    older = place < KEPT
    slot = jnp.where(older, place, place - KEPT) >= KEPT - NSUM
    flag = jnp.where(older, flags_ref[2 * seg], flags_ref[2 * seg + 1])
    return slot & (flag > 0)


def causal_seen():
    shape_here = (SPAN, SPAN)
    return lax.broadcasted_iota(jnp.int32, shape_here, 0) <= lax.broadcasted_iota(
        jnp.int32, shape_here, 1
    )


def above(block):
    return jnp.concatenate([block, jnp.zeros_like(block)], axis=0)


def below(block):
    return jnp.concatenate([jnp.zeros_like(block), block], axis=0)


def at_block(index):
    return pl.ds(pl.multiple_of(index * SPAN, SPAN), SPAN)


def attend_kernel(flags_ref, query_ref, turned_ref, kv_ref, prefix_ref, out_ref, log_ref):
    seg, block = pl.program_id(0), pl.program_id(1)
    query = above((query_ref[...].astype(jnp.float32) * SCALE).astype(LOW))
    own = at_block(block)
    scores = dot(kv_ref[own, :], query)
    scores = jnp.where(causal_seen(), scores, MASKED)
    top = jnp.max(scores, axis=0, keepdims=True)
    probs = jnp.exp(scores - top)
    total = jnp.sum(probs, axis=0, keepdims=True)
    mixed = dot(turned_ref[2 * HD :, own], probs.astype(LOW))

    def add(carry, scores, values):
        top, total, mixed = carry
        fresh = jnp.maximum(top, jnp.max(scores, axis=0, keepdims=True))
        fade = jnp.exp(top - fresh)
        probs = jnp.exp(scores - fresh)
        total = total * fade + jnp.sum(probs, axis=0, keepdims=True)
        return fresh, total, mixed * fade + dot(values, probs.astype(LOW))

    prefix = prefix_ref[0]
    scores = jnp.where(prefix_seen(flags_ref, seg, SPAN), dot(prefix, query), MASKED)
    carry = add((top, total, mixed), scores, turned(prefix)[HD:].astype(LOW))

    def step(index, carry):
        here = at_block(index)
        return add(carry, dot(kv_ref[here, :], query), turned_ref[2 * HD :, here])

    top, total, mixed = lax.fori_loop(0, block, step, carry)
    mixed = (mixed / total).astype(LOW)
    rows = out_ref.shape[2]
    for piece in range(SPAN // rows):
        out_ref[piece] = mixed[:, piece * rows : (piece + 1) * rows]
    log_ref[0] = top + jnp.log(total)


def attend(flags, turned_all, kv, prefix, rows_here):
    total = kv.shape[0]
    blocks = SEG // SPAN
    step = SPAN // rows_here
    return run(
        attend_kernel,
        (total // SEG, blocks),
        [
            pl.BlockSpec(memory_space=pltpu.SMEM),
            pl.BlockSpec((HD, SPAN), lambda s, i: (0, s * blocks + i)),
            pl.BlockSpec((3 * HD, SEG), lambda s, i: (0, s)),
            pl.BlockSpec((SEG, 2 * HD), lambda s, i: (s, 0)),
            pl.BlockSpec((1, 2 * KEPT, 2 * HD), lambda s, i: (s, 0, 0)),
        ],
        [
            pl.BlockSpec((step, HD, rows_here), lambda s, i: (s * blocks + i, 0, 0)),
            pl.BlockSpec((1, 1, SPAN), lambda s, i: (s * blocks + i, 0, 0)),
        ],
        [
            shape((total // rows_here, HD, rows_here), LOW),
            shape((total // SPAN, 1, SPAN), jnp.float32),
        ],
        (flags, turned_all, turned_all, kv, prefix),
    )


def side_by_side(ref):
    return jnp.concatenate([ref[piece] for piece in range(ref.shape[0])], axis=1)


def beside(block, place):
    zero = jnp.zeros_like(block)
    return jnp.concatenate([block, zero] if place == 0 else [zero, block], axis=1)


def query_side(query_ref, rows_ref, grad_ref, out_ref, log_ref):
    query = above((query_ref[...].astype(jnp.float32) * SCALE).astype(LOW))
    grad = side_by_side(grad_ref)
    mean = jnp.sum(
        grad.astype(jnp.float32) * side_by_side(out_ref).astype(jnp.float32),
        axis=0,
        keepdims=True,
    )
    query_rows = beside((rows_ref[...].astype(jnp.float32) * SCALE).astype(LOW), 0)
    grad_rows = beside(turned(grad).astype(LOW), 1)
    return query, below(grad), mean, log_ref[0], query_rows, grad_rows


def key_side(keys, side, seen):
    query, grad, mean, log_sum, query_rows, grad_rows = side
    probs = jnp.exp(dot(keys, query) - log_sum)
    if seen is not None:
        probs = jnp.where(seen, probs, 0.0)
    d_scores = (probs * (dot(keys, grad) - mean)).astype(LOW)
    return probs.astype(LOW), d_scores


def prefix_back_kernel(
    flags_ref, query_ref, rows_ref, grad_ref, out_ref, log_ref, prefix_ref, sum_ref
):
    seg, block = pl.program_id(0), pl.program_id(1)
    side = query_side(query_ref, rows_ref, grad_ref, out_ref, log_ref)
    probs, d_scores = key_side(prefix_ref[0], side, prefix_seen(flags_ref, seg, SPAN))
    part = dot(d_scores, side[4]) + dot(probs, side[5])

    @pl.when(block == 0)
    def _():
        sum_ref[0] = part

    @pl.when(block > 0)
    def _():
        sum_ref[0] += part


def store_shares(grads_ref, piece, part, columns):
    here = HD // grads_ref.shape[0]
    for share in range(grads_ref.shape[0]):
        for kind in (1, 2):
            first = (kind - 1) * HD + share * here
            grads_ref[share, piece, kind * here : (kind + 1) * here, columns] = part[
                first : first + here
            ]


def attend_back_kernel(
    flags_ref,
    query_ref,
    rows_ref,
    grad_ref,
    out_ref,
    log_ref,
    prefix_ref,
    turned_ref,
    kv_ref,
    grads_ref,
    kept_ref,
    kv_grad,
):
    seg, block = pl.program_id(0), pl.program_id(1)

    @pl.when(block == 0)
    def _():
        kv_grad[...] = jnp.zeros_like(kv_grad)

    side = query_side(query_ref, rows_ref, grad_ref, out_ref, log_ref)
    prefix = prefix_ref[0]
    _, d_scores = key_side(prefix, side, prefix_seen(flags_ref, seg, SPAN))
    query_grad = dot(turned(prefix)[:HD].astype(LOW), d_scores)

    def add(here, query_grad, seen):
        probs, d_scores = key_side(kv_ref[here, :], side, seen)
        kv_grad[here, :] += dot(d_scores, side[4]) + dot(probs, side[5])
        return query_grad + dot(turned_ref[HD : 2 * HD, here], d_scores)

    query_grad = add(at_block(block), query_grad, causal_seen())
    query_grad = lax.fori_loop(
        0, block, lambda index, grad: add(at_block(index), grad, None), query_grad
    )
    query_grad = (query_grad * SCALE).astype(LOW)
    rows = grads_ref.shape[3]
    step = SPAN // rows
    for piece in range(step):
        part = query_grad[:, piece * rows : (piece + 1) * rows]
        for share in range(grads_ref.shape[0]):
            here = HD // grads_ref.shape[0]
            grads_ref[share, block * step + piece, :here, :] = part[share * here : (share + 1) * here]

    @pl.when(block == pl.num_programs(1) - 1)
    def _():
        for piece in range(SEG // rows):
            part = kv_grad[piece * rows : (piece + 1) * rows, :].T.astype(LOW)
            store_shares(grads_ref, piece, part, slice(None))
        kept_ref[0] = kv_grad[SEG - KEPT :, :]


def attend_back_specs(rows_here):
    blocks = SEG // SPAN
    step = SPAN // rows_here
    return [
        pl.BlockSpec(memory_space=pltpu.SMEM),
        pl.BlockSpec((HD, SPAN), lambda s, i: (0, s * blocks + i)),
        pl.BlockSpec((SPAN, HD), lambda s, i: (s * blocks + i, 0)),
        pl.BlockSpec((step, HD, rows_here), lambda s, i: (s * blocks + i, 0, 0)),
        pl.BlockSpec((step, HD, rows_here), lambda s, i: (s * blocks + i, 0, 0)),
        pl.BlockSpec((1, 1, SPAN), lambda s, i: (s * blocks + i, 0, 0)),
        pl.BlockSpec((1, 2 * KEPT, 2 * HD), lambda s, i: (s, 0, 0)),
    ]


def prefix_back(flags, turned_all, query, grad, out, log_sums, prefix, rows_here):
    total = query.shape[0]
    return run(
        prefix_back_kernel,
        (total // SEG, SEG // SPAN),
        attend_back_specs(rows_here),
        [pl.BlockSpec((1, 2 * KEPT, 2 * HD), lambda s, i: (s, 0, 0))],
        [shape(prefix.shape, jnp.float32)],
        (flags, turned_all, query, grad, out, log_sums, prefix),
        received=(grad,),
    )


def attend_back(flags, turned_all, query, grad, out, log_sums, prefix, kv, rows_here, count):
    total = query.shape[0]
    pieces = SEG // rows_here
    return run(
        attend_back_kernel,
        (total // SEG, SEG // SPAN),
        attend_back_specs(rows_here)
        + [
            pl.BlockSpec((3 * HD, SEG), lambda s, i: (0, s)),
            pl.BlockSpec((SEG, 2 * HD), lambda s, i: (s, 0)),
        ],
        [
            pl.BlockSpec(
                (count, pieces, 3 * HD // count, rows_here), lambda s, i: (0, s, 0, 0)
            ),
            pl.BlockSpec((1, KEPT, 2 * HD), lambda s, i: (s, 0, 0)),
        ],
        [
            shape((count, total // rows_here, 3 * HD // count, rows_here), LOW),
            shape((total // SEG, KEPT, 2 * HD), jnp.float32),
        ],
        (flags, turned_all, query, grad, out, log_sums, prefix, turned_all, kv),
        received=(grad,),
        scratch=[pltpu.VMEM((SEG, 2 * HD), jnp.float32)],
    )


def returned_kernel(grads_ref, kept_ref, returned_ref, out_ref):
    out_ref[...] = grads_ref[...]
    part = (kept_ref[0] + returned_ref[0]).T.astype(LOW)
    store_shares(out_ref, 0, part, slice(out_ref.shape[3] - KEPT, None))


def add_returned(grads, kept, returned):
    count, places, feats, rows = grads.shape
    segs = kept.shape[0]
    last = places // segs
    grad_spec = pl.BlockSpec((count, 1, feats, rows), lambda s: (0, s * last + last - 1, 0, 0))
    kept_spec = pl.BlockSpec((1, KEPT, 2 * HD), lambda s: (s, 0, 0))
    return run(
        returned_kernel,
        (segs,),
        [grad_spec, kept_spec, kept_spec],
        [grad_spec],
        [shape(grads.shape, LOW)],
        (grads, kept, returned),
        aliases={0: 0},
    )[0]


def out_kernel(
    part_ref, weight_ref, tokens_ref, bias_ref, gain_ref, shift_ref, resid_ref, two_ref, total
):
    step = pl.program_id(0)
    rows = part_ref.shape[2]
    part = turned(part_ref[...].reshape(-1, rows)).astype(LOW)
    added = dot(part, weight_ref[...].reshape(part.shape[1], -1))

    @pl.when(step == 0)
    def _():
        total[...] = added

    @pl.when(step > 0)
    def _():
        total[...] += added

    @pl.when(step == pl.num_programs(0) - 1)
    def _():
        resid = tokens_ref[...].astype(jnp.float32) + total[...] + bias_ref[...]
        resid_ref[...] = resid
        two_ref[...] = layer_norm(resid, gain_ref[...], shift_ref[...]).astype(LOW)


def out_project(parts, gathered, at, tokens, bias, gain, shift, step=8):
    places, feats, rows = parts.shape
    width = gathered.shape[2]
    return run(
        out_kernel,
        (places // step,),
        [
            pl.BlockSpec((step, feats, rows), lambda i: (i, 0, 0)),
            pl.BlockSpec((step, feats, width), lambda i: (i, at, 0)),
            whole(tokens),
            whole(bias),
            whole(gain),
            whole(shift),
        ],
        [pl.BlockSpec((rows, width), lambda i: (0, 0))] * 2,
        [shape((rows, width), jnp.float32), shape((rows, width), LOW)],
        (parts, gathered, tokens, bias, gain, shift),
        received=(parts,),
        scratch=[pltpu.VMEM((rows, width), jnp.float32)],
    )


def owner_maps(chips, at):
    def of(core_step, chip):
        return lambda i, place: at((i * chips[1] + chip) * 2 + lax.rem(place[0] + core_step, 2))

    return [of(core_step, chip) for core_step in (0, 1) for chip in range(chips[1])]


def own_map(index):
    return lambda i, place: index(i)


def fixed(dims):
    return pl.BlockSpec(
        dims, own_map(lambda i: (0,) * len(dims)), pipeline_mode=pl.Buffered(buffer_count=1)
    )


def feed_run(
    body, chips, place, in_specs, out_specs, out_shape, operands, scratch, vmem, received=()
):
    return pl.pallas_call(
        body,
        grid_spec=pltpu.PrefetchScalarGridSpec(
            num_scalar_prefetch=1,
            grid=(chips[0],),
            in_specs=in_specs,
            out_specs=out_specs,
            scratch_shapes=scratch,
        ),
        out_shape=out_hbm(out_shape),
        compiler_params=pltpu.CompilerParams(
            dimension_semantics=("arbitrary",), vmem_limit_bytes=vmem * MIB
        ),
        cost_estimate=pl.CostEstimate(flops=COST, bytes_accessed=COST, transcendentals=0),
    )(place, *in_hbm(operands, received))


def stacked(refs, axis=0):
    return jnp.concatenate([ref[0] for ref in refs], axis=axis)


def pile(refs, into):
    rows = refs[0].shape[0]
    for at, ref in enumerate(refs):
        into[at * rows : (at + 1) * rows, :] = ref[...]


def spread(source, refs):
    rows = refs[0].shape[0]
    for at, ref in enumerate(refs):
        ref[...] = source[at * rows : (at + 1) * rows, :].astype(ref.dtype)


def take(refs, *counts):
    refs = list(refs)
    return [[refs.pop(0) for _ in range(count)] for count in counts] + [refs]


def d_act_kernel(count, owners, place_ref, *refs):
    cot_refs, weight_refs, (out_ref, cots) = take(refs, count, owners)

    @pl.when(pl.program_id(0) == 0)
    def _():
        pile(cot_refs, cots)

    out_ref[...] = dot_cols(cots[...], stacked(weight_refs))


def feed_d_act(place, chips, cots, weights):
    count = len(cots)
    rows, width = cots[0].shape
    places, both, _ = weights.shape
    units = both // 2
    total = count * rows
    owners = 2 * chips[1]
    step = owners * units
    return feed_run(
        partial(d_act_kernel, count, owners),
        chips,
        place,
        [fixed((rows, width))] * count
        + [
            pl.BlockSpec((1, units, width), at)
            for at in owner_maps(chips, lambda owner: (owner, 1, 0))
        ],
        [pl.BlockSpec((total, step), own_map(lambda i: (0, i))), fixed((total, width))],
        [shape((total, places * units), jnp.float32), shape((total, width), LOW)],
        (*cots, *[weights] * owners),
        [],
        32,
        received=cots[1:],
    )


def feed_kernel(count, chips, place_ref, *refs):
    owners = 2 * chips[1]
    norm_refs, weight_refs, bias_refs, (d_act_ref,), back_refs, refs = take(
        refs, count, owners, owners, 1, count
    )
    norms, kept_ref, sent_ref, bias_sum_ref, back = refs
    step = pl.program_id(0)

    @pl.when(step == 0)
    def _():
        pile(norm_refs, norms)
        back[...] = jnp.zeros_like(back)

    units = weight_refs[0].shape[1]
    half = owners // 2
    added = []
    for ref, first in ((kept_ref, 0), (sent_ref, half)):
        up = stacked(weight_refs[first : first + half])
        bias = stacked(bias_refs[first : first + half], axis=1)
        here = slice(first * units, (first + half) * units)
        pre = dot_cols(norms[...], up) + bias
        square = pre * pre
        bent = jnp.tanh(0.7978845608 * (pre + 0.044715 * (square * pre)))
        up_half = 0.5 * (1.0 + bent)
        slope = up_half + 0.5 * pre * (1.0 - bent * bent) * (
            0.7978845608 * (1.0 + 3.0 * 0.044715 * square)
        )
        d_pre = (d_act_ref[:, here] * slope).astype(LOW)
        ref[0] = (pre * up_half).astype(LOW)
        ref[1] = d_pre
        bias_sums = jnp.sum(d_pre.astype(jnp.float32), axis=0, keepdims=True)
        for at, index in enumerate(owner_maps(chips, lambda owner: owner)[first : first + half]):
            bias_sum_ref[index(step, place_ref)] = bias_sums[:, at * units : (at + 1) * units]
        added.append(dot(d_pre, up))
    back[...] += added[0] + added[1]

    @pl.when(step == pl.num_programs(0) - 1)
    def _():
        spread(back, back_refs)


def feed(place, chips, norms, weights, bias, d_act):
    count = len(norms)
    rows, width = norms[0].shape
    places, both, _ = weights.shape
    units = both // 2
    total = count * rows
    owners = 2 * chips[1]
    step = owners * units
    pair_spec = pl.BlockSpec((2, total, step // 2), own_map(lambda i: (0, 0, i)))
    results = feed_run(
        partial(feed_kernel, count, chips),
        chips,
        place,
        [fixed((rows, width))] * count
        + [
            pl.BlockSpec((1, units, width), at)
            for at in owner_maps(chips, lambda owner: (owner, 0, 0))
        ]
        + [
            pl.BlockSpec((1, 1, units), at)
            for at in owner_maps(chips, lambda owner: (owner, 0, 0))
        ]
        + [pl.BlockSpec((total, step), own_map(lambda i: (0, i)))],
        [pl.BlockSpec((rows, width), own_map(lambda i: (0, 0)))] * count
        + [fixed((total, width)), pair_spec, pair_spec, fixed((places, 1, units))],
        [shape((rows, width), LOW)] * count
        + [shape((total, width), LOW)]
        + [shape((2, total, places * units // 2), LOW)] * 2
        + [shape((places, 1, units), jnp.float32)],
        (*norms, *[weights] * owners, *[bias] * owners, d_act),
        [pltpu.VMEM((total, width), jnp.float32)],
        40,
        received=norms[1:],
    )
    return results[:count], results[count:]


def feed_grad_kernel(owners, place_ref, *refs):
    norm_refs, cot_refs, pair_refs, weight_refs, mixed_refs, (out_ref, mixed) = take(
        refs, 2, 2, 3, owners, 2
    )
    kept_ref, sent_ref, other_ref = pair_refs
    step = pl.program_id(0)
    units = weight_refs[0].shape[1]

    @pl.when(step == 0)
    def _():
        mixed[...] = jnp.zeros_like(mixed)

    act = jnp.concatenate([kept_ref[0], sent_ref[0]], axis=1)
    mixed[...] += dot(act, stacked(weight_refs))

    def grad(at, rows):
        total = dot(turned(kept_ref[at]).astype(LOW), rows[0][...])
        total += dot(turned(other_ref[at]).astype(LOW), rows[1][...])
        return total.astype(LOW).reshape(out_ref.shape[0], units, -1)

    out_ref[:, :units, :] = grad(1, norm_refs)
    out_ref[:, units:, :] = grad(0, cot_refs)

    @pl.when(step == pl.num_programs(0) - 1)
    def _():
        spread(mixed, mixed_refs)


def feed_grad(place, chips, norms, cots, kept, sent, other, weights):
    total, width = norms[0].shape
    rows = total // 2
    units = weights.shape[1] // 2
    owners = 2 * chips[1]
    pair_spec = pl.BlockSpec((2, total, owners * units // 2), own_map(lambda i: (0, 0, i)))
    results = feed_run(
        partial(feed_grad_kernel, owners),
        chips,
        place,
        [fixed((total, width))] * 4
        + [pair_spec] * 3
        + [
            pl.BlockSpec((1, units, width), at)
            for at in owner_maps(chips, lambda owner: (owner, 1, 0))
        ],
        [pl.BlockSpec((rows, width), own_map(lambda i: (0, 0)))] * 2
        + [pl.BlockSpec((chips[1], 2 * units, width), own_map(lambda i: (i, 0, 0)))],
        [shape((rows, width), LOW)] * 2
        + [shape((chips[0] * chips[1], 2 * units, width), LOW)],
        (*norms, *cots, kept, sent, other, *[weights] * owners),
        [pltpu.VMEM((total, width), jnp.float32)],
        48,
        received=(norms[1], cots[1], other),
    )
    return results


def branch_kernel(count, place_ref, *refs):
    (resid_ref, cot_ref, gain_ref, weight_ref, part_ref), back_refs, refs = take(refs, 5, count)
    (d_resid_ref, sums_ref, parts_ref), sent_refs, (d_branch_ref,) = take(refs, 3, count)
    step = pl.program_id(0)

    @pl.when(step == 0)
    def _():
        d_two = sum(ref[...].astype(jnp.float32) for ref in back_refs)
        normed, scale = norm_parts(resid_ref[...])
        cot = cot_ref[...].astype(jnp.float32)
        d_resid = cot + norm_back(d_two, normed, scale, gain_ref[...])
        d_branch = d_resid.astype(LOW)
        d_resid_ref[...] = d_resid
        d_branch_ref[...] = d_branch
        sums_ref[0:1, :] = jnp.sum(d_two * normed, axis=0, keepdims=True)
        sums_ref[1:2, :] = jnp.sum(d_two, axis=0, keepdims=True)
        sums_ref[2:3, :] = jnp.sum(d_branch.astype(jnp.float32), axis=0, keepdims=True)
        sums_ref[3:4, :] = jnp.sum(cot, axis=0, keepdims=True)

    width = weight_ref.shape[2]
    part = dot_cols(weight_ref[...].reshape(-1, width), d_branch_ref[...])
    parts_ref[...] = part.reshape(parts_ref.shape).astype(LOW)

    @pl.when(step == pl.num_programs(0) - 1)
    def _():
        places, feats, rows = part_ref.shape
        share = feats // count
        more = places * share * rows // width
        for at, ref in enumerate(sent_refs):
            first = lax.rem(place_ref[3] + at, count) * share
            taken = part_ref[:, pl.ds(pl.multiple_of(first, share), share), :]
            taken = taken.reshape(places * share, rows)
            ref[:rows, :] = d_branch_ref[...]
            ref[rows:, :] = jnp.concatenate(
                [taken[more * at : more * (at + 1)] for at in range(width // rows)], axis=1
            )


def branch_back(place, resid, cotangent, gain, gathered, at, attended, backs, step=8):
    rows, width = resid.shape
    places, feats, _ = attended.shape
    count = len(backs)
    row_spec = pl.BlockSpec((rows, width), lambda i: (0, 0))
    sent = shape((rows + places * feats // count * rows // width, width), LOW)
    results = run(
        partial(branch_kernel, count),
        (places // step,),
        [
            pl.BlockSpec(memory_space=pltpu.SMEM),
            row_spec,
            row_spec,
            whole(gain),
            pl.BlockSpec((step, feats, width), lambda i: (i, at, 0)),
            whole(attended),
        ]
        + [row_spec] * count,
        [
            row_spec,
            pl.BlockSpec((4, width), lambda i: (0, 0)),
            pl.BlockSpec((step, feats, rows), lambda i: (i, 0, 0)),
        ]
        + [whole(sent)] * count,
        [
            shape((rows, width), jnp.float32),
            shape((4, width), jnp.float32),
            shape((places, feats, rows), LOW),
        ]
        + [sent] * count,
        (place, resid, cotangent, gain, gathered, attended, *backs),
        received=backs[1:],
        scratch=[pltpu.VMEM((rows, width), LOW)],
    )
    return (*results[:3], results[3:])


SMALL = 8


def packed(small):
    rounded = small.astype(LOW)
    return jnp.concatenate([rounded, (small - rounded.astype(jnp.float32)).astype(LOW)], axis=0)


def unpacked(rows):
    rows = rows.astype(jnp.float32)
    return rows[:SMALL] + rows[SMALL:]


def even_sum(terms):
    return (terms[0] + terms[2]) + (terms[1] + terms[3])


def branch_grad_kernel(count, chips, rows, place_ref, *refs):
    sent_refs, small_refs, (own_ref, other_ref, small_ref, parts) = take(refs, count, 3)
    chips_x, chips_y = chips
    places, feats = parts.shape[1:3]
    for at, ref in enumerate(sent_refs):
        taken = ref[rows:, :]
        taken = [taken[:, rows * at : rows * (at + 1)] for at in range(taken.shape[1] // rows)]
        parts[at] = jnp.concatenate(taken, axis=0).reshape(places, feats, rows)
    grads = jnp.concatenate([ref[:rows, :] for ref in sent_refs], axis=0)

    def owner(at, core):
        x = lax.rem(place_ref[1] + at // chips_y, chips_x)
        y = lax.rem(place_ref[2] + at % chips_y, chips_y)
        return (x * chips_y + y) * 2 + core

    def grad(core):
        left = [
            jnp.concatenate([parts[step, owner(at, core)] for step in range(count)], axis=1)
            for at in range(chips_x * chips_y)
        ]
        return dot(jnp.concatenate(left, axis=0), grads).astype(LOW)

    total = own_ref.shape[0]
    small_ref[...] = jnp.zeros_like(small_ref)
    first = 0
    for ref in small_refs:
        small_ref[first : first + ref.shape[0], :] = ref[...]
        first += ref.shape[0]
    other_ref[:total, :] = grad(1 - place_ref[0])
    other_ref[total:, :] = packed(small_ref[...])
    own_ref[...] = grad(place_ref[0])


def branch_grad(place, chips, rows, sent, small):
    count = len(sent)
    places = 2 * chips[0] * chips[1]
    more, width = sent[0].shape
    feats = (more - rows) * width // rows // places
    total = places // 2 * feats
    out_shape = [
        shape((total, width), LOW),
        shape((total + 2 * SMALL, width), LOW),
        shape((SMALL, width), jnp.float32),
    ]
    return feed_run(
        partial(branch_grad_kernel, count, chips, rows),
        (1,),
        place,
        [fixed(sent[0].shape)] * count + [fixed(item.shape) for item in small],
        [fixed(item.shape) for item in out_shape],
        out_shape,
        (*sent, *small),
        [pltpu.VMEM((count, places, feats, rows), LOW)],
        32,
        received=sent[1:],
    )


def step_run(body, operands, out_shape, received):
    return run(
        body,
        (1,),
        [whole(item) for item in operands],
        [whole(item) for item in out_shape],
        out_shape,
        operands,
        received=received,
    )


def core_step_kernel(own_ref, other_ref, small_ref, *out_refs):
    total = own_ref.shape[0]
    rows = total // len(out_refs)
    out = own_ref[...].astype(jnp.float32) + other_ref[:total, :].astype(jnp.float32)
    out = out.astype(LOW)
    small = packed(small_ref[...] + unpacked(other_ref[total:, :]))
    for at, ref in enumerate(out_refs):
        ref[:rows, :] = out[at * rows : (at + 1) * rows]
        ref[rows:, :] = small


def core_step(own, other, small, count):
    rows, width = own.shape
    out = shape((rows // count + 2 * SMALL, width), LOW)
    return step_run(core_step_kernel, (own, other, small), [out] * count, (other,))


def chip_step_kernel(count, *refs):
    term_refs, out_refs = take(refs, count)
    total = term_refs[0].shape[0] - 2 * SMALL
    rows = total // len(out_refs)
    out = sum(ref[:total, :].astype(jnp.float32) for ref in term_refs).astype(LOW)
    small = packed(even_sum([unpacked(ref[total:, :]) for ref in term_refs]))
    for at, ref in enumerate(out_refs):
        ref[:rows, :] = out[at * rows : (at + 1) * rows]
        ref[rows:, :] = small


def chip_step(terms, count):
    rows, width = terms[0].shape
    out = shape(((rows - 2 * SMALL) // count + 2 * SMALL, width), LOW)
    return step_run(partial(chip_step_kernel, len(terms)), tuple(terms), [out] * count, terms[1:])


def item_step_kernel(count, *refs):
    term_refs, (bias_ref, out_ref) = take(refs, count)
    rows = term_refs[0].shape[0] - 2 * SMALL
    out = sum(ref[:rows, :].astype(jnp.float32) for ref in term_refs)
    small = even_sum([unpacked(ref[rows:, :]) for ref in term_refs])
    place = lax.broadcasted_iota(jnp.int32, small.shape, 0)
    small = jnp.where(place == SMALL - 1, bias_ref[...], small)
    out_ref[:rows, :] = out.astype(LOW)
    out_ref[rows:, :] = packed(small)


def item_step(terms, bias):
    out = shape(terms[0].shape, LOW)
    return step_run(partial(item_step_kernel, len(terms)), (*terms, bias), [out], terms[1:])[0]


def last_kernel(count, rows, place_ref, *refs):
    term_refs, (out_ref, small_ref, units_ref) = take(refs, count)
    small = []
    for at, ref in enumerate(term_refs):
        item = lax.rem(place_ref[3] + at, count)
        out_ref[pl.ds(pl.multiple_of(item * rows, rows), rows), :] = ref[:rows, :].astype(
            jnp.float32
        )
        small.append(unpacked(ref[rows:, :]))
        units_ref[item] = small[-1][0:1]
    small_ref[...] = even_sum(small)


def last_step(place, terms, rows):
    count = len(terms)
    width = terms[0].shape[1]
    out_shape = [
        shape((count * rows, width), jnp.float32),
        shape((SMALL, width), jnp.float32),
        shape((count, 1, width), jnp.float32),
    ]
    return run(
        partial(last_kernel, count, rows),
        (1,),
        [pl.BlockSpec(memory_space=pltpu.SMEM)] + [whole(item) for item in terms],
        [whole(item) for item in out_shape],
        out_shape,
        (place, *terms),
        received=terms[1:],
    )


def joint_grad_kernel(count, place_ref, *refs):
    (grad_ref, rows_ref, weight_ref, gain_ref, shift_ref), out_refs, refs = take(refs, 5, count)
    bias_ref, sums_ref, total, biases, bias_row = refs
    step = pl.program_id(0)
    grads = side_by_side(grad_ref)
    added = dot(grads, rows_ref[...].reshape(grads.shape[1], -1))
    summed = jnp.sum(grads.astype(jnp.float32), axis=1, keepdims=True)
    summed_row = dot_cols(jnp.ones((8, grads.shape[1]), LOW), grads)

    @pl.when(step == 0)
    def _():
        total[...] = added
        biases[...] = summed
        bias_row[...] = summed_row

    @pl.when(step > 0)
    def _():
        total[...] += added
        biases[...] += summed
        bias_row[...] += summed_row

    @pl.when(step == pl.num_programs(0) - 1)
    def _():
        rows = out_refs[0].shape[0]
        for at, ref in enumerate(out_refs):
            first = lax.rem(place_ref[3] + at, count) * rows
            ref[...] = total[pl.ds(pl.multiple_of(first, rows), rows), :].astype(LOW)
        bias_ref[...] = jnp.zeros_like(bias_ref)
        bias_ref[:, : bias_row.shape[1]] = bias_row[0:1, :]
        weight = weight_ref[...].astype(jnp.float32)
        shift_sum = jnp.sum(weight * biases[...], axis=0, keepdims=True)
        product = jnp.sum(weight * total[...], axis=0, keepdims=True)
        sums_ref[0:1, :] = (product - shift_sum * shift_ref[...]) / gain_ref[...]
        sums_ref[1:2, :] = shift_sum


def joint_grad(place, count, grads, gathered, weight, gain, shift, step=8):
    places, feats, rows = grads.shape
    width = gathered.shape[2]
    results = run(
        partial(joint_grad_kernel, count),
        (places // step,),
        [
            pl.BlockSpec(memory_space=pltpu.SMEM),
            pl.BlockSpec((step, feats, rows), lambda i: (i, 0, 0)),
            pl.BlockSpec((step, rows, width), lambda i: (i, 0, 0)),
            whole(weight),
            whole(gain),
            whole(shift),
        ],
        [pl.BlockSpec((feats // count, width), lambda i: (0, 0))] * count
        + [
            pl.BlockSpec((1, width), lambda i: (0, 0)),
            pl.BlockSpec((2, width), lambda i: (0, 0)),
        ],
        [shape((feats // count, width), LOW)] * count
        + [shape((1, width), jnp.float32), shape((2, width), jnp.float32)],
        (place, grads, gathered, weight, gain, shift),
        scratch=[
            pltpu.VMEM((feats, width), jnp.float32),
            pltpu.VMEM((feats, 1), jnp.float32),
            pltpu.VMEM((8, feats), jnp.float32),
        ],
    )
    return results[:count], *results[count:]


def input_kernel(part_ref, weight_ref, tokens_ref, gain_ref, d_resid_ref, out_ref, total):
    step = pl.program_id(0)
    added = dot(turned(part_ref[...]).astype(LOW), weight_ref[...])

    @pl.when(step == 0)
    def _():
        total[...] = added

    @pl.when(step > 0)
    def _():
        total[...] += added

    @pl.when(step == pl.num_programs(0) - 1)
    def _():
        normed, scale = norm_parts(tokens_ref[...].astype(jnp.float32))
        out_ref[...] = d_resid_ref[...] + norm_back(total[...], normed, scale, gain_ref[...])


def input_back(parts, weights, tokens, gain, d_resid, steps=6):
    feats, rows = parts.shape
    width = weights.shape[1]
    step = feats // steps
    return run(
        input_kernel,
        (steps,),
        [
            pl.BlockSpec((step, rows), lambda i: (i, 0)),
            pl.BlockSpec((step, width), lambda i: (i, 0)),
            whole(tokens),
            whole(gain),
            whole(d_resid),
        ],
        [pl.BlockSpec((rows, width), lambda i: (0, 0))],
        [shape((rows, width), jnp.float32)],
        (parts, weights, tokens, gain, d_resid),
        received=(parts,),
        scratch=[pltpu.VMEM((rows, width), jnp.float32)],
    )[0]


ITEM = "z"
HEAD = ("x", "y", "c")
CORE = "c"


def moved(value, axis, steps):
    count = lax.axis_size(axis)
    return lax.ppermute(value, axis, [(place, (place + steps) % count) for place in range(count)])


def shifted(value, axis, steps):
    count = lax.axis_size(axis)
    initial, last = (max(0, -steps), min(count, count - steps))
    return lax.ppermute(value, axis, [(source, source + steps) for source in range(initial, last)])


def around(value, axis):
    return [value] + [moved(value, axis, -step) for step in range(1, lax.axis_size(axis))]


def sum_back(values, axis):
    return [values[0]] + [
        moved(values[step], axis, step) for step in range(1, lax.axis_size(axis))
    ]


def both_halves(value, bit, axis, step):
    pairs = [(place, place ^ step) for place in range(lax.axis_size(axis))]
    other = lax.ppermute(value, axis, pairs)
    first = jnp.where(bit == 0, value, other)
    return jnp.concatenate([first, jnp.where(bit == 0, other, value)], axis=0)


def head_swap(value):
    return lax.all_to_all(value, HEAD, split_axis=0, concat_axis=0, tiled=True)


def segment_flags(seg_counts):
    total_segs = seg_counts.shape[0]
    openings = jnp.cumsum(seg_counts) - seg_counts
    places = jnp.arange(total_segs, dtype=jnp.int32)
    opens_here = jnp.any((openings[:, None] == places[None, :]) & (seg_counts[:, None] > 0), axis=0)
    opens_before = jnp.concatenate([jnp.ones((1,), dtype=bool), opens_here[:-1]])
    one_back = jnp.logical_not(opens_here)
    two_back = one_back & jnp.logical_not(opens_before)
    return (one_back, two_back)


def local(
    tokens,
    cotangent,
    seg_counts,
    query_weight,
    key_weight,
    value_weight,
    query_bias,
    value_bias,
    out_weight,
    out_bias,
    first_gain,
    first_shift,
    second_gain,
    second_shift,
    up_weight,
    up_bias,
    down_weight,
    down_bias,
):
    rows, width = tokens.shape
    heads = lax.axis_size(HEAD)
    item_place = lax.axis_index(ITEM)
    group_rows = rows * heads
    seg_local = group_rows // SEG
    feats = query_weight.shape[0]
    units = up_weight.shape[0]
    hidden_here = units * heads

    def row(vector):
        return vector.reshape(1, -1)

    tokens_f = tokens.astype(jnp.float32)
    inputs_one = layer_norm(tokens_f, first_gain, first_shift).astype(LOW)
    first = jnp.concatenate([inputs_one, out_weight], axis=0)
    gathered = lax.all_gather(first, HEAD, axis=0, tiled=True).reshape(heads, -1, width)
    second = jnp.concatenate([up_weight, down_weight], axis=0)
    feed_weights = lax.all_gather(second, HEAD, axis=0, tiled=True).reshape(heads, -1, width)
    cots = around(cotangent, ITEM)
    joint_weight = jnp.concatenate([query_weight, key_weight, value_weight], axis=0)
    joint_bias = jnp.concatenate([query_bias, jnp.zeros_like(query_bias), value_bias])

    one_back, two_back = segment_flags(seg_counts)
    flags = jnp.stack([two_back, one_back], axis=1).astype(jnp.int32)
    flags = lax.dynamic_slice_in_dim(flags, item_place * seg_local, seg_local).reshape(-1)

    gathered, cots = lax.optimization_barrier((gathered, cots))
    query, kv, turned_all = project(gathered, rows, joint_weight, row(joint_bias))
    own_kept = kv.reshape(seg_local, SEG, 2 * HD)[:, SEG - KEPT :]
    table = jnp.concatenate([shifted(own_kept, ITEM, 1), own_kept], axis=0)
    prefix = jnp.concatenate(
        [table[seg_local - 2 : 2 * seg_local - 2], table[seg_local - 1 : 2 * seg_local - 1]], axis=1
    )
    attended, log_sums = attend(flags, turned_all, kv, prefix, rows)
    attended_own = head_swap(attended)
    resid, inputs_two = out_project(
        attended_own, gathered, rows // feats, tokens, row(out_bias), row(second_gain), row(second_shift)
    )

    joint_turn = lax.optimization_barrier((joint_weight, resid))[0]
    joint_full = lax.all_gather(joint_turn, HEAD, axis=0, tiled=True)
    norms = around(inputs_two, ITEM)
    chips = (lax.axis_size("x"), lax.axis_size("y"))
    place = jnp.stack([lax.axis_index(axis) for axis in (CORE, "x", "y", ITEM)]).astype(jnp.int32)
    d_act, cots = feed_d_act(place, chips, cots, feed_weights)
    cots = [cots, moved(cots, CORE, 1)]
    bias_here = lax.dynamic_slice_in_dim(up_bias, item_place * hidden_here, hidden_here)
    backs, (norms, kept, sent, up_bias_part) = feed(
        place, chips, norms, feed_weights, bias_here.reshape(heads, 1, units), d_act
    )
    backs = sum_back(backs, ITEM)
    norms = [norms, moved(norms, CORE, 1)]
    near, far, feed_parts = feed_grad(
        place, chips, norms, cots, kept, sent, moved(sent, CORE, 1), feed_weights
    )
    backs, near, far = lax.optimization_barrier((backs, near, far))
    d_resid, sums_two, d_parts, sent = branch_back(
        place,
        resid,
        cotangent,
        row(second_gain),
        gathered,
        rows // feats,
        attended_own,
        backs,
    )
    sent = sum_back(sent, ITEM)
    d_attended = head_swap(d_parts)
    d_attended, far = lax.optimization_barrier((d_attended, moved(far, ITEM, 2)))
    feed_parts = lax.optimization_barrier((feed_parts, d_resid))[0]
    feed_grads = lax.psum_scatter(
        feed_parts.reshape(-1, width), ("x", "y"), scatter_dimension=0, tiled=True
    )
    d_prefix = prefix_back(
        flags, turned_all, query, d_attended, attended, log_sums, prefix, rows
    )[0]
    older, newer = d_prefix[:, :KEPT], d_prefix[:, KEPT:]
    spread = jnp.pad(older, ((seg_local - 2, 2), (0, 0), (0, 0)))
    spread = spread + jnp.pad(newer, ((seg_local - 1, 1), (0, 0), (0, 0)))
    returned = shifted(spread[:seg_local], ITEM, -1)
    joint_grads, kept_grads = attend_back(
        flags, turned_all, query, d_attended, attended, log_sums, prefix, kv, rows, 1
    )
    returned, kept_grads, joint_full = lax.optimization_barrier((returned, kept_grads, joint_full))
    joint_grads = add_returned(joint_grads, kept_grads, spread[seg_local:] + returned)
    grads_own = head_swap(joint_grads[0]).reshape(-1, rows)
    joint_parts, bias_part, sums_one = joint_grad(
        place,
        lax.axis_size(ITEM),
        joint_grads[0],
        gathered,
        joint_weight,
        row(first_gain),
        row(first_shift),
    )
    joint_parts, sums_one, sent, near, far = lax.optimization_barrier(
        (joint_parts, sums_one, sent, near, far)
    )
    out_own, out_other, small = branch_grad(
        place, chips, rows, sent, (row(up_bias_part), sums_two, sums_one)
    )
    joint_parts = sum_back(joint_parts, ITEM)
    near = (near.astype(jnp.float32) + far.astype(jnp.float32)).astype(LOW)
    terms = core_step(out_own, moved(out_other, CORE, 1), small, chips[0])
    grads_own, terms, joint_parts, near = lax.optimization_barrier(
        (grads_own, terms, joint_parts, near)
    )
    high, low = item_place // 2, item_place % 2
    terms = sum_back(terms, "x")
    mixed = moved(near[rows:], ITEM, 1)
    joint_sums = sum(part.astype(jnp.float32) for part in joint_parts).astype(LOW)
    joint_sums = both_halves(joint_sums, low, ITEM, 1)
    input_grad = input_back(grads_own, joint_full, tokens, row(first_gain), d_resid)
    input_grad, terms, mixed, joint_sums = lax.optimization_barrier(
        (input_grad, terms, mixed, joint_sums)
    )
    mixed = near[:rows].astype(jnp.float32) + mixed.astype(jnp.float32)
    terms = sum_back(chip_step(terms, chips[1]), "y")
    joint_sums = both_halves(joint_sums, high, ITEM, 2)
    terms, joint_sums = lax.optimization_barrier((terms, joint_sums))
    terms = around(item_step(terms, bias_part), ITEM)
    joint_sums = joint_sums.astype(jnp.float32)
    mixed_out = (resid + mixed + down_bias).astype(LOW)
    terms, feed_grads = lax.optimization_barrier((terms, feed_grads))
    share = feats // lax.axis_size(ITEM)
    out_sum, small, up_bias_grad = last_step(place, terms, share)
    up_bias_grad = up_bias_grad.reshape(-1)
    bias_sums, early_rows, late = small[SMALL - 1, : 3 * feats], small[1:5], small[5:7]
    feed_grads = feed_grads.astype(jnp.float32)
    return (
        mixed_out,
        input_grad,
        joint_sums[:feats],
        joint_sums[feats : 2 * feats],
        joint_sums[2 * feats :],
        bias_sums[:feats],
        bias_sums[2 * feats : 3 * feats],
        out_sum,
        early_rows[2],
        late[0],
        late[1],
        early_rows[0],
        early_rows[1],
        feed_grads[:units],
        up_bias_grad,
        feed_grads[units:],
        early_rows[3],
    )


def solution(mesh):
    sizes = (mesh.shape["item"], 4, mesh.shape["head"] // 8, 2)
    fine = Mesh(mesh.devices.reshape(sizes), (ITEM, *HEAD))
    split = P((ITEM, *HEAD), None)
    by_head = P(HEAD, None)
    return jax.shard_map(
        local,
        mesh=fine,
        in_specs=(
            split,
            split,
            P(),
            by_head,
            by_head,
            by_head,
            P(HEAD),
            P(HEAD),
            by_head,
            P(),
            P(),
            P(),
            P(),
            P(),
            split,
            P(),
            split,
            P(),
        ),
        out_specs=(
            split,
            split,
            by_head,
            by_head,
            by_head,
            P(HEAD),
            P(HEAD),
            by_head,
            P(),
            P(),
            P(),
            P(),
            P(),
            split,
            P(),
            split,
            P(),
        ),
        check_vma=False,
    )
```

```python
import math
from functools import partial

import jax
import jax.numpy as jnp
from jax import lax
from jax.experimental import pallas as pl
from jax.experimental.pallas import tpu as pltpu
from jax.sharding import Mesh
from jax.sharding import PartitionSpec as P

HD = 64
NSUM = 50
SEG = 2048
SPAN = 512
KEPT = 64
EPSILON = 1e-05
MASKED = -1e30
SCALE = HD ** (-0.5)
MIB = 1 << 20
COST = 1 << 20
BIG = 1 << 17
LOW = jnp.bfloat16


def dot(left, right):
    return jnp.dot(left, right, preferred_element_type=jnp.float32)


def dot_cols(left, right):
    return lax.dot_general(
        left, right, (((1,), (1,)), ((), ())), preferred_element_type=jnp.float32
    )


def turned(value):
    return value.astype(jnp.float32).T


def norm_parts(row_data):
    row_mean = jnp.mean(row_data, axis=-1, keepdims=True)
    centred = row_data - row_mean
    row_var = jnp.mean(centred * centred, axis=-1, keepdims=True)
    scale = lax.rsqrt(row_var + EPSILON)
    return centred * scale, scale


def norm_back(grad, normed, scale, gain):
    scaled = grad * gain
    return scale * (
        scaled
        - jnp.mean(scaled, axis=-1, keepdims=True)
        - normed * jnp.mean(scaled * normed, axis=-1, keepdims=True)
    )


def layer_norm(row_data, gain, shift):
    return norm_parts(row_data)[0] * gain + shift


def in_hbm(operands, received):
    kept = [id(item) for item in received]
    return [
        pltpu.with_memory_space_constraint(item, pltpu.HBM)
        if item.size >= BIG and id(item) not in kept
        else item
        for item in operands
    ]


def out_hbm(shapes):
    return [
        pltpu.HBM(item.shape, item.dtype) if math.prod(item.shape) >= BIG else item
        for item in shapes
    ]


def run(body, grid, in_specs, out_specs, out_shape, operands, scratch=(), vmem=32, aliases=None, received=()):
    return pl.pallas_call(
        body,
        grid=grid,
        in_specs=in_specs,
        out_specs=out_specs,
        out_shape=out_hbm(out_shape),
        scratch_shapes=scratch,
        compiler_params=pltpu.CompilerParams(
            dimension_semantics=("arbitrary",) * len(grid), vmem_limit_bytes=vmem * MIB
        ),
        input_output_aliases=aliases or {},
        cost_estimate=pl.CostEstimate(flops=COST, bytes_accessed=COST, transcendentals=0),
    )(*in_hbm(operands, received))


def shape(dims, kind):
    return jax.ShapeDtypeStruct(dims, kind)


def whole(item):
    return pl.BlockSpec(item.shape, lambda *_: (0,) * len(item.shape))


def first_kernel(tokens_ref, gain_ref, shift_ref, weight_ref, out_ref):
    rows = tokens_ref.shape[0]
    normed = layer_norm(tokens_ref[...].astype(jnp.float32), gain_ref[...], shift_ref[...])
    out_ref[:rows, :] = normed.astype(LOW)
    out_ref[rows:, :] = weight_ref[...]


def first_norm(tokens, gain, shift, weight):
    operands = (tokens, gain, shift, weight)
    out = shape((tokens.shape[0] + weight.shape[0], tokens.shape[1]), LOW)
    return run(
        first_kernel, (1,), [whole(item) for item in operands], [whole(out)], [out], operands
    )[0]


def project_kernel(rows_ref, weight_ref, bias_ref, query_ref, kv_ref, turned_ref):
    rows = rows_ref[...].reshape(-1, rows_ref.shape[2])
    joint = dot_cols(rows, weight_ref[...]) + bias_ref[...]
    query_ref[...] = joint[:, :HD].astype(LOW)
    kv_ref[...] = joint[:, HD:].astype(LOW)
    turned_ref[...] = joint.T.astype(LOW)


def project(gathered, rows_here, weight, bias, span=2 * SPAN):
    places, _, width = gathered.shape
    total = places * rows_here
    step = span // rows_here
    return run(
        project_kernel,
        (total // span,),
        [
            pl.BlockSpec((step, rows_here, width), lambda i: (i, 0, 0)),
            whole(weight),
            whole(bias),
        ],
        [
            pl.BlockSpec((span, HD), lambda i: (i, 0)),
            pl.BlockSpec((span, 2 * HD), lambda i: (i, 0)),
            pl.BlockSpec((3 * HD, span), lambda i: (0, i)),
        ],
        [
            shape((total, HD), LOW),
            shape((total, 2 * HD), LOW),
            shape((3 * HD, total), LOW),
        ],
        (gathered, weight, bias),
    )


def prefix_seen(flags_ref, seg, columns):
    place = lax.broadcasted_iota(jnp.int32, (2 * KEPT, columns), 0)
    older = place < KEPT
    slot = jnp.where(older, place, place - KEPT) >= KEPT - NSUM
    flag = jnp.where(older, flags_ref[2 * seg], flags_ref[2 * seg + 1])
    return slot & (flag > 0)


def causal_seen():
    shape_here = (SPAN, SPAN)
    return lax.broadcasted_iota(jnp.int32, shape_here, 0) <= lax.broadcasted_iota(
        jnp.int32, shape_here, 1
    )


def above(block):
    return jnp.concatenate([block, jnp.zeros_like(block)], axis=0)


def below(block):
    return jnp.concatenate([jnp.zeros_like(block), block], axis=0)


def at_block(index):
    return pl.ds(pl.multiple_of(index * SPAN, SPAN), SPAN)


def attend_kernel(flags_ref, query_ref, turned_ref, kv_ref, prefix_ref, out_ref, log_ref):
    seg, block = pl.program_id(0), pl.program_id(1)
    query = above((query_ref[...].astype(jnp.float32) * SCALE).astype(LOW))
    own = at_block(block)
    scores = dot(kv_ref[own, :], query)
    scores = jnp.where(causal_seen(), scores, MASKED)
    top = jnp.max(scores, axis=0, keepdims=True)
    probs = jnp.exp(scores - top)
    total = jnp.sum(probs, axis=0, keepdims=True)
    mixed = dot(turned_ref[2 * HD :, own], probs.astype(LOW))

    def add(carry, scores, values):
        top, total, mixed = carry
        fresh = jnp.maximum(top, jnp.max(scores, axis=0, keepdims=True))
        fade = jnp.exp(top - fresh)
        probs = jnp.exp(scores - fresh)
        total = total * fade + jnp.sum(probs, axis=0, keepdims=True)
        return fresh, total, mixed * fade + dot(values, probs.astype(LOW))

    prefix = prefix_ref[0]
    scores = jnp.where(prefix_seen(flags_ref, seg, SPAN), dot(prefix, query), MASKED)
    carry = add((top, total, mixed), scores, turned(prefix)[HD:].astype(LOW))

    def step(index, carry):
        here = at_block(index)
        return add(carry, dot(kv_ref[here, :], query), turned_ref[2 * HD :, here])

    top, total, mixed = lax.fori_loop(0, block, step, carry)
    mixed = (mixed / total).astype(LOW)
    rows = out_ref.shape[2]
    for piece in range(SPAN // rows):
        out_ref[piece] = mixed[:, piece * rows : (piece + 1) * rows]
    log_ref[0] = top + jnp.log(total)


def attend(flags, turned_all, kv, prefix, rows_here):
    total = kv.shape[0]
    blocks = SEG // SPAN
    step = SPAN // rows_here
    return run(
        attend_kernel,
        (total // SEG, blocks),
        [
            pl.BlockSpec(memory_space=pltpu.SMEM),
            pl.BlockSpec((HD, SPAN), lambda s, i: (0, s * blocks + i)),
            pl.BlockSpec((3 * HD, SEG), lambda s, i: (0, s)),
            pl.BlockSpec((SEG, 2 * HD), lambda s, i: (s, 0)),
            pl.BlockSpec((1, 2 * KEPT, 2 * HD), lambda s, i: (s, 0, 0)),
        ],
        [
            pl.BlockSpec((step, HD, rows_here), lambda s, i: (s * blocks + i, 0, 0)),
            pl.BlockSpec((1, 1, SPAN), lambda s, i: (s * blocks + i, 0, 0)),
        ],
        [
            shape((total // rows_here, HD, rows_here), LOW),
            shape((total // SPAN, 1, SPAN), jnp.float32),
        ],
        (flags, turned_all, turned_all, kv, prefix),
    )


def side_by_side(ref):
    return jnp.concatenate([ref[piece] for piece in range(ref.shape[0])], axis=1)


def beside(block, place):
    zero = jnp.zeros_like(block)
    return jnp.concatenate([block, zero] if place == 0 else [zero, block], axis=1)


def query_side(query_ref, rows_ref, grad_ref, out_ref, log_ref):
    query = above((query_ref[...].astype(jnp.float32) * SCALE).astype(LOW))
    grad = side_by_side(grad_ref)
    mean = jnp.sum(
        grad.astype(jnp.float32) * side_by_side(out_ref).astype(jnp.float32),
        axis=0,
        keepdims=True,
    )
    query_rows = beside((rows_ref[...].astype(jnp.float32) * SCALE).astype(LOW), 0)
    grad_rows = beside(turned(grad).astype(LOW), 1)
    return query, below(grad), mean, log_ref[0], query_rows, grad_rows


def key_side(keys, side, seen):
    query, grad, mean, log_sum, query_rows, grad_rows = side
    probs = jnp.exp(dot(keys, query) - log_sum)
    if seen is not None:
        probs = jnp.where(seen, probs, 0.0)
    d_scores = (probs * (dot(keys, grad) - mean)).astype(LOW)
    return probs.astype(LOW), d_scores


def prefix_back_kernel(
    flags_ref, query_ref, rows_ref, grad_ref, out_ref, log_ref, prefix_ref, sum_ref
):
    seg, block = pl.program_id(0), pl.program_id(1)
    side = query_side(query_ref, rows_ref, grad_ref, out_ref, log_ref)
    probs, d_scores = key_side(prefix_ref[0], side, prefix_seen(flags_ref, seg, SPAN))
    part = dot(d_scores, side[4]) + dot(probs, side[5])

    @pl.when(block == 0)
    def _():
        sum_ref[0] = part

    @pl.when(block > 0)
    def _():
        sum_ref[0] += part


def store_shares(grads_ref, piece, part, columns):
    here = HD // grads_ref.shape[0]
    for share in range(grads_ref.shape[0]):
        for kind in (1, 2):
            first = (kind - 1) * HD + share * here
            grads_ref[share, piece, kind * here : (kind + 1) * here, columns] = part[
                first : first + here
            ]


def attend_back_kernel(
    flags_ref,
    query_ref,
    rows_ref,
    grad_ref,
    out_ref,
    log_ref,
    prefix_ref,
    turned_ref,
    kv_ref,
    grads_ref,
    kept_ref,
    kv_grad,
):
    seg, block = pl.program_id(0), pl.program_id(1)

    @pl.when(block == 0)
    def _():
        kv_grad[...] = jnp.zeros_like(kv_grad)

    side = query_side(query_ref, rows_ref, grad_ref, out_ref, log_ref)
    prefix = prefix_ref[0]
    _, d_scores = key_side(prefix, side, prefix_seen(flags_ref, seg, SPAN))
    query_grad = dot(turned(prefix)[:HD].astype(LOW), d_scores)

    def add(here, query_grad, seen):
        probs, d_scores = key_side(kv_ref[here, :], side, seen)
        kv_grad[here, :] += dot(d_scores, side[4]) + dot(probs, side[5])
        return query_grad + dot(turned_ref[HD : 2 * HD, here], d_scores)

    query_grad = add(at_block(block), query_grad, causal_seen())
    query_grad = lax.fori_loop(
        0, block, lambda index, grad: add(at_block(index), grad, None), query_grad
    )
    query_grad = (query_grad * SCALE).astype(LOW)
    rows = grads_ref.shape[3]
    step = SPAN // rows
    for piece in range(step):
        part = query_grad[:, piece * rows : (piece + 1) * rows]
        for share in range(grads_ref.shape[0]):
            here = HD // grads_ref.shape[0]
            grads_ref[share, block * step + piece, :here, :] = part[share * here : (share + 1) * here]

    @pl.when(block == pl.num_programs(1) - 1)
    def _():
        for piece in range(SEG // rows):
            part = kv_grad[piece * rows : (piece + 1) * rows, :].T.astype(LOW)
            store_shares(grads_ref, piece, part, slice(None))
        kept_ref[0] = kv_grad[SEG - KEPT :, :]


def attend_back_specs(rows_here):
    blocks = SEG // SPAN
    step = SPAN // rows_here
    return [
        pl.BlockSpec(memory_space=pltpu.SMEM),
        pl.BlockSpec((HD, SPAN), lambda s, i: (0, s * blocks + i)),
        pl.BlockSpec((SPAN, HD), lambda s, i: (s * blocks + i, 0)),
        pl.BlockSpec((step, HD, rows_here), lambda s, i: (s * blocks + i, 0, 0)),
        pl.BlockSpec((step, HD, rows_here), lambda s, i: (s * blocks + i, 0, 0)),
        pl.BlockSpec((1, 1, SPAN), lambda s, i: (s * blocks + i, 0, 0)),
        pl.BlockSpec((1, 2 * KEPT, 2 * HD), lambda s, i: (s, 0, 0)),
    ]


def prefix_back(flags, turned_all, query, grad, out, log_sums, prefix, rows_here):
    total = query.shape[0]
    return run(
        prefix_back_kernel,
        (total // SEG, SEG // SPAN),
        attend_back_specs(rows_here),
        [pl.BlockSpec((1, 2 * KEPT, 2 * HD), lambda s, i: (s, 0, 0))],
        [shape(prefix.shape, jnp.float32)],
        (flags, turned_all, query, grad, out, log_sums, prefix),
        received=(grad,),
    )


def attend_back(flags, turned_all, query, grad, out, log_sums, prefix, kv, rows_here, count):
    total = query.shape[0]
    pieces = SEG // rows_here
    return run(
        attend_back_kernel,
        (total // SEG, SEG // SPAN),
        attend_back_specs(rows_here)
        + [
            pl.BlockSpec((3 * HD, SEG), lambda s, i: (0, s)),
            pl.BlockSpec((SEG, 2 * HD), lambda s, i: (s, 0)),
        ],
        [
            pl.BlockSpec(
                (count, pieces, 3 * HD // count, rows_here), lambda s, i: (0, s, 0, 0)
            ),
            pl.BlockSpec((1, KEPT, 2 * HD), lambda s, i: (s, 0, 0)),
        ],
        [
            shape((count, total // rows_here, 3 * HD // count, rows_here), LOW),
            shape((total // SEG, KEPT, 2 * HD), jnp.float32),
        ],
        (flags, turned_all, query, grad, out, log_sums, prefix, turned_all, kv),
        received=(grad,),
        scratch=[pltpu.VMEM((SEG, 2 * HD), jnp.float32)],
    )


def returned_kernel(grads_ref, kept_ref, returned_ref, out_ref):
    out_ref[...] = grads_ref[...]
    part = (kept_ref[0] + returned_ref[0]).T.astype(LOW)
    store_shares(out_ref, 0, part, slice(out_ref.shape[3] - KEPT, None))


def add_returned(grads, kept, returned):
    count, places, feats, rows = grads.shape
    segs = kept.shape[0]
    last = places // segs
    grad_spec = pl.BlockSpec((count, 1, feats, rows), lambda s: (0, s * last + last - 1, 0, 0))
    kept_spec = pl.BlockSpec((1, KEPT, 2 * HD), lambda s: (s, 0, 0))
    return run(
        returned_kernel,
        (segs,),
        [grad_spec, kept_spec, kept_spec],
        [grad_spec],
        [shape(grads.shape, LOW)],
        (grads, kept, returned),
        aliases={0: 0},
    )[0]


def out_kernel(
    part_ref, weight_ref, tokens_ref, bias_ref, gain_ref, shift_ref, resid_ref, two_ref, total
):
    step = pl.program_id(0)
    rows = part_ref.shape[2]
    part = turned(part_ref[...].reshape(-1, rows)).astype(LOW)
    added = dot(part, weight_ref[...].reshape(part.shape[1], -1))

    @pl.when(step == 0)
    def _():
        total[...] = added

    @pl.when(step > 0)
    def _():
        total[...] += added

    @pl.when(step == pl.num_programs(0) - 1)
    def _():
        resid = tokens_ref[...].astype(jnp.float32) + total[...] + bias_ref[...]
        resid_ref[...] = resid
        two_ref[...] = layer_norm(resid, gain_ref[...], shift_ref[...]).astype(LOW)


def out_project(parts, gathered, at, tokens, bias, gain, shift, step=8):
    places, feats, rows = parts.shape
    width = gathered.shape[2]
    return run(
        out_kernel,
        (places // step,),
        [
            pl.BlockSpec((step, feats, rows), lambda i: (i, 0, 0)),
            pl.BlockSpec((step, feats, width), lambda i: (i, at, 0)),
            whole(tokens),
            whole(bias),
            whole(gain),
            whole(shift),
        ],
        [pl.BlockSpec((rows, width), lambda i: (0, 0))] * 2,
        [shape((rows, width), jnp.float32), shape((rows, width), LOW)],
        (parts, gathered, tokens, bias, gain, shift),
        received=(parts,),
        scratch=[pltpu.VMEM((rows, width), jnp.float32)],
    )


def owner_maps(chips, at):
    def of(core_step, chip):
        return lambda i, place: at((i * chips[1] + chip) * 2 + lax.rem(place[0] + core_step, 2))

    return [of(core_step, chip) for core_step in (0, 1) for chip in range(chips[1])]


def own_map(index):
    return lambda i, place: index(i)


def fixed(dims):
    return pl.BlockSpec(
        dims, own_map(lambda i: (0,) * len(dims)), pipeline_mode=pl.Buffered(buffer_count=1)
    )


def feed_run(
    body, chips, place, in_specs, out_specs, out_shape, operands, scratch, vmem, received=()
):
    return pl.pallas_call(
        body,
        grid_spec=pltpu.PrefetchScalarGridSpec(
            num_scalar_prefetch=1,
            grid=(chips[0],),
            in_specs=in_specs,
            out_specs=out_specs,
            scratch_shapes=scratch,
        ),
        out_shape=out_hbm(out_shape),
        compiler_params=pltpu.CompilerParams(
            dimension_semantics=("arbitrary",), vmem_limit_bytes=vmem * MIB
        ),
        cost_estimate=pl.CostEstimate(flops=COST, bytes_accessed=COST, transcendentals=0),
    )(place, *in_hbm(operands, received))


def stacked(refs, axis=0):
    return jnp.concatenate([ref[0] for ref in refs], axis=axis)


def pile(refs, into):
    rows = refs[0].shape[0]
    for at, ref in enumerate(refs):
        into[at * rows : (at + 1) * rows, :] = ref[...]


def spread(source, refs):
    rows = refs[0].shape[0]
    for at, ref in enumerate(refs):
        ref[...] = source[at * rows : (at + 1) * rows, :].astype(ref.dtype)


def take(refs, *counts):
    refs = list(refs)
    return [[refs.pop(0) for _ in range(count)] for count in counts] + [refs]


def d_act_kernel(count, owners, place_ref, *refs):
    cot_refs, weight_refs, (out_ref, cots) = take(refs, count, owners)

    @pl.when(pl.program_id(0) == 0)
    def _():
        pile(cot_refs, cots)

    out_ref[...] = dot_cols(cots[...], stacked(weight_refs))


def feed_d_act(place, chips, cots, weights):
    count = len(cots)
    rows, width = cots[0].shape
    places, both, _ = weights.shape
    units = both // 2
    total = count * rows
    owners = 2 * chips[1]
    step = owners * units
    return feed_run(
        partial(d_act_kernel, count, owners),
        chips,
        place,
        [fixed((rows, width))] * count
        + [
            pl.BlockSpec((1, units, width), at)
            for at in owner_maps(chips, lambda owner: (owner, 1, 0))
        ],
        [pl.BlockSpec((total, step), own_map(lambda i: (0, i))), fixed((total, width))],
        [shape((total, places * units), jnp.float32), shape((total, width), LOW)],
        (*cots, *[weights] * owners),
        [],
        32,
        received=cots[1:],
    )


def feed_kernel(count, chips, place_ref, *refs):
    owners = 2 * chips[1]
    norm_refs, weight_refs, bias_refs, (d_act_ref,), back_refs, refs = take(
        refs, count, owners, owners, 1, count
    )
    norms, kept_ref, sent_ref, bias_sum_ref, back = refs
    step = pl.program_id(0)

    @pl.when(step == 0)
    def _():
        pile(norm_refs, norms)
        back[...] = jnp.zeros_like(back)

    units = weight_refs[0].shape[1]
    half = owners // 2
    added = []
    for ref, first in ((kept_ref, 0), (sent_ref, half)):
        up = stacked(weight_refs[first : first + half])
        bias = stacked(bias_refs[first : first + half], axis=1)
        here = slice(first * units, (first + half) * units)
        pre = dot_cols(norms[...], up) + bias
        square = pre * pre
        bent = jnp.tanh(0.7978845608 * (pre + 0.044715 * (square * pre)))
        up_half = 0.5 * (1.0 + bent)
        slope = up_half + 0.5 * pre * (1.0 - bent * bent) * (
            0.7978845608 * (1.0 + 3.0 * 0.044715 * square)
        )
        d_pre = (d_act_ref[:, here] * slope).astype(LOW)
        ref[0] = (pre * up_half).astype(LOW)
        ref[1] = d_pre
        bias_sums = jnp.sum(d_pre.astype(jnp.float32), axis=0, keepdims=True)
        for at, index in enumerate(owner_maps(chips, lambda owner: owner)[first : first + half]):
            bias_sum_ref[index(step, place_ref)] = bias_sums[:, at * units : (at + 1) * units]
        added.append(dot(d_pre, up))
    back[...] += added[0] + added[1]

    @pl.when(step == pl.num_programs(0) - 1)
    def _():
        spread(back, back_refs)


def feed(place, chips, norms, weights, bias, d_act):
    count = len(norms)
    rows, width = norms[0].shape
    places, both, _ = weights.shape
    units = both // 2
    total = count * rows
    owners = 2 * chips[1]
    step = owners * units
    pair_spec = pl.BlockSpec((2, total, step // 2), own_map(lambda i: (0, 0, i)))
    results = feed_run(
        partial(feed_kernel, count, chips),
        chips,
        place,
        [fixed((rows, width))] * count
        + [
            pl.BlockSpec((1, units, width), at)
            for at in owner_maps(chips, lambda owner: (owner, 0, 0))
        ]
        + [
            pl.BlockSpec((1, 1, units), at)
            for at in owner_maps(chips, lambda owner: (owner, 0, 0))
        ]
        + [pl.BlockSpec((total, step), own_map(lambda i: (0, i)))],
        [pl.BlockSpec((rows, width), own_map(lambda i: (0, 0)))] * count
        + [fixed((total, width)), pair_spec, pair_spec, fixed((places, 1, units))],
        [shape((rows, width), LOW)] * count
        + [shape((total, width), LOW)]
        + [shape((2, total, places * units // 2), LOW)] * 2
        + [shape((places, 1, units), jnp.float32)],
        (*norms, *[weights] * owners, *[bias] * owners, d_act),
        [pltpu.VMEM((total, width), jnp.float32)],
        40,
        received=norms[1:],
    )
    return results[:count], results[count:]


def feed_grad_kernel(owners, place_ref, *refs):
    norm_refs, cot_refs, pair_refs, weight_refs, mixed_refs, (out_ref, mixed) = take(
        refs, 2, 2, 3, owners, 2
    )
    kept_ref, sent_ref, other_ref = pair_refs
    step = pl.program_id(0)
    units = weight_refs[0].shape[1]

    @pl.when(step == 0)
    def _():
        mixed[...] = jnp.zeros_like(mixed)

    act = jnp.concatenate([kept_ref[0], sent_ref[0]], axis=1)
    mixed[...] += dot(act, stacked(weight_refs))

    def grad(at, rows):
        total = dot(turned(kept_ref[at]).astype(LOW), rows[0][...])
        total += dot(turned(other_ref[at]).astype(LOW), rows[1][...])
        return total.astype(LOW).reshape(out_ref.shape[0], units, -1)

    out_ref[:, :units, :] = grad(1, norm_refs)
    out_ref[:, units:, :] = grad(0, cot_refs)

    @pl.when(step == pl.num_programs(0) - 1)
    def _():
        spread(mixed, mixed_refs)


def feed_grad(place, chips, norms, cots, kept, sent, other, weights):
    total, width = norms[0].shape
    rows = total // 2
    units = weights.shape[1] // 2
    owners = 2 * chips[1]
    pair_spec = pl.BlockSpec((2, total, owners * units // 2), own_map(lambda i: (0, 0, i)))
    results = feed_run(
        partial(feed_grad_kernel, owners),
        chips,
        place,
        [fixed((total, width))] * 4
        + [pair_spec] * 3
        + [
            pl.BlockSpec((1, units, width), at)
            for at in owner_maps(chips, lambda owner: (owner, 1, 0))
        ],
        [pl.BlockSpec((rows, width), own_map(lambda i: (0, 0)))] * 2
        + [pl.BlockSpec((chips[1], 2 * units, width), own_map(lambda i: (i, 0, 0)))],
        [shape((rows, width), LOW)] * 2
        + [shape((chips[0] * chips[1], 2 * units, width), LOW)],
        (*norms, *cots, kept, sent, other, *[weights] * owners),
        [pltpu.VMEM((total, width), jnp.float32)],
        48,
        received=(norms[1], cots[1], other),
    )
    return results


def branch_kernel(count, place_ref, *refs):
    (resid_ref, cot_ref, gain_ref, weight_ref, part_ref), back_refs, refs = take(refs, 5, count)
    (d_resid_ref, sums_ref, parts_ref), sent_refs, (d_branch_ref,) = take(refs, 3, count)
    step = pl.program_id(0)

    @pl.when(step == 0)
    def _():
        d_two = sum(ref[...].astype(jnp.float32) for ref in back_refs)
        normed, scale = norm_parts(resid_ref[...])
        cot = cot_ref[...].astype(jnp.float32)
        d_resid = cot + norm_back(d_two, normed, scale, gain_ref[...])
        d_branch = d_resid.astype(LOW)
        d_resid_ref[...] = d_resid
        d_branch_ref[...] = d_branch
        sums_ref[0:1, :] = jnp.sum(d_two * normed, axis=0, keepdims=True)
        sums_ref[1:2, :] = jnp.sum(d_two, axis=0, keepdims=True)
        sums_ref[2:3, :] = jnp.sum(d_branch.astype(jnp.float32), axis=0, keepdims=True)
        sums_ref[3:4, :] = jnp.sum(cot, axis=0, keepdims=True)

    width = weight_ref.shape[2]
    part = dot_cols(weight_ref[...].reshape(-1, width), d_branch_ref[...])
    parts_ref[...] = part.reshape(parts_ref.shape).astype(LOW)

    @pl.when(step == pl.num_programs(0) - 1)
    def _():
        places, feats, rows = part_ref.shape
        share = feats // count
        more = places * share * rows // width
        for at, ref in enumerate(sent_refs):
            first = lax.rem(place_ref[3] + at, count) * share
            taken = part_ref[:, pl.ds(pl.multiple_of(first, share), share), :]
            taken = taken.reshape(places * share, rows)
            ref[:rows, :] = d_branch_ref[...]
            ref[rows:, :] = jnp.concatenate(
                [taken[more * at : more * (at + 1)] for at in range(width // rows)], axis=1
            )


def branch_back(place, resid, cotangent, gain, gathered, at, attended, backs, step=8):
    rows, width = resid.shape
    places, feats, _ = attended.shape
    count = len(backs)
    row_spec = pl.BlockSpec((rows, width), lambda i: (0, 0))
    sent = shape((rows + places * feats // count * rows // width, width), LOW)
    results = run(
        partial(branch_kernel, count),
        (places // step,),
        [
            pl.BlockSpec(memory_space=pltpu.SMEM),
            row_spec,
            row_spec,
            whole(gain),
            pl.BlockSpec((step, feats, width), lambda i: (i, at, 0)),
            whole(attended),
        ]
        + [row_spec] * count,
        [
            row_spec,
            pl.BlockSpec((4, width), lambda i: (0, 0)),
            pl.BlockSpec((step, feats, rows), lambda i: (i, 0, 0)),
        ]
        + [whole(sent)] * count,
        [
            shape((rows, width), jnp.float32),
            shape((4, width), jnp.float32),
            shape((places, feats, rows), LOW),
        ]
        + [sent] * count,
        (place, resid, cotangent, gain, gathered, attended, *backs),
        received=backs[1:],
        scratch=[pltpu.VMEM((rows, width), LOW)],
    )
    return (*results[:3], results[3:])


SMALL = 8


def packed(small):
    rounded = small.astype(LOW)
    return jnp.concatenate([rounded, (small - rounded.astype(jnp.float32)).astype(LOW)], axis=0)


def unpacked(rows):
    rows = rows.astype(jnp.float32)
    return rows[:SMALL] + rows[SMALL:]


def even_sum(terms):
    return (terms[0] + terms[2]) + (terms[1] + terms[3])


def branch_grad_kernel(count, chips, rows, place_ref, *refs):
    sent_refs, small_refs, (own_ref, other_ref, small_ref, parts) = take(refs, count, 3)
    chips_x, chips_y = chips
    places, feats = parts.shape[1:3]
    for at, ref in enumerate(sent_refs):
        taken = ref[rows:, :]
        taken = [taken[:, rows * at : rows * (at + 1)] for at in range(taken.shape[1] // rows)]
        parts[at] = jnp.concatenate(taken, axis=0).reshape(places, feats, rows)
    grads = jnp.concatenate([ref[:rows, :] for ref in sent_refs], axis=0)

    def owner(at, core):
        x = lax.rem(place_ref[1] + at // chips_y, chips_x)
        y = lax.rem(place_ref[2] + at % chips_y, chips_y)
        return (x * chips_y + y) * 2 + core

    def grad(core):
        left = [
            jnp.concatenate([parts[step, owner(at, core)] for step in range(count)], axis=1)
            for at in range(chips_x * chips_y)
        ]
        return dot(jnp.concatenate(left, axis=0), grads).astype(LOW)

    total = own_ref.shape[0]
    small_ref[...] = jnp.zeros_like(small_ref)
    first = 0
    for ref in small_refs:
        small_ref[first : first + ref.shape[0], :] = ref[...]
        first += ref.shape[0]
    other_ref[:total, :] = grad(1 - place_ref[0])
    other_ref[total:, :] = packed(small_ref[...])
    own_ref[...] = grad(place_ref[0])


def branch_grad(place, chips, rows, sent, small):
    count = len(sent)
    places = 2 * chips[0] * chips[1]
    more, width = sent[0].shape
    feats = (more - rows) * width // rows // places
    total = places // 2 * feats
    out_shape = [
        shape((total, width), LOW),
        shape((total + 2 * SMALL, width), LOW),
        shape((SMALL, width), jnp.float32),
    ]
    return feed_run(
        partial(branch_grad_kernel, count, chips, rows),
        (1,),
        place,
        [fixed(sent[0].shape)] * count + [fixed(item.shape) for item in small],
        [fixed(item.shape) for item in out_shape],
        out_shape,
        (*sent, *small),
        [pltpu.VMEM((count, places, feats, rows), LOW)],
        32,
        received=sent[1:],
    )


def step_run(body, operands, out_shape, received):
    return run(
        body,
        (1,),
        [whole(item) for item in operands],
        [whole(item) for item in out_shape],
        out_shape,
        operands,
        received=received,
    )


def core_step_kernel(own_ref, other_ref, small_ref, *out_refs):
    total = own_ref.shape[0]
    rows = total // len(out_refs)
    out = own_ref[...].astype(jnp.float32) + other_ref[:total, :].astype(jnp.float32)
    out = out.astype(LOW)
    small = packed(small_ref[...] + unpacked(other_ref[total:, :]))
    for at, ref in enumerate(out_refs):
        ref[:rows, :] = out[at * rows : (at + 1) * rows]
        ref[rows:, :] = small


def core_step(own, other, small, count):
    rows, width = own.shape
    out = shape((rows // count + 2 * SMALL, width), LOW)
    return step_run(core_step_kernel, (own, other, small), [out] * count, (other,))


def chip_step_kernel(count, *refs):
    term_refs, out_refs = take(refs, count)
    total = term_refs[0].shape[0] - 2 * SMALL
    rows = total // len(out_refs)
    out = sum(ref[:total, :].astype(jnp.float32) for ref in term_refs).astype(LOW)
    small = packed(even_sum([unpacked(ref[total:, :]) for ref in term_refs]))
    for at, ref in enumerate(out_refs):
        ref[:rows, :] = out[at * rows : (at + 1) * rows]
        ref[rows:, :] = small


def chip_step(terms, count):
    rows, width = terms[0].shape
    out = shape(((rows - 2 * SMALL) // count + 2 * SMALL, width), LOW)
    return step_run(partial(chip_step_kernel, len(terms)), tuple(terms), [out] * count, terms[1:])


def item_step_kernel(count, *refs):
    term_refs, (bias_ref, out_ref) = take(refs, count)
    rows = term_refs[0].shape[0] - 2 * SMALL
    out = sum(ref[:rows, :].astype(jnp.float32) for ref in term_refs)
    small = even_sum([unpacked(ref[rows:, :]) for ref in term_refs])
    place = lax.broadcasted_iota(jnp.int32, small.shape, 0)
    small = jnp.where(place == SMALL - 1, bias_ref[...], small)
    out_ref[:rows, :] = out.astype(LOW)
    out_ref[rows:, :] = packed(small)


def item_step(terms, bias):
    out = shape(terms[0].shape, LOW)
    return step_run(partial(item_step_kernel, len(terms)), (*terms, bias), [out], terms[1:])[0]


def last_kernel(count, rows, place_ref, *refs):
    term_refs, (out_ref, small_ref, units_ref) = take(refs, count)
    small = []
    for at, ref in enumerate(term_refs):
        item = lax.rem(place_ref[3] + at, count)
        out_ref[pl.ds(pl.multiple_of(item * rows, rows), rows), :] = ref[:rows, :].astype(
            jnp.float32
        )
        small.append(unpacked(ref[rows:, :]))
        units_ref[item] = small[-1][0:1]
    small_ref[...] = even_sum(small)


def last_step(place, terms, rows):
    count = len(terms)
    width = terms[0].shape[1]
    out_shape = [
        shape((count * rows, width), jnp.float32),
        shape((SMALL, width), jnp.float32),
        shape((count, 1, width), jnp.float32),
    ]
    return run(
        partial(last_kernel, count, rows),
        (1,),
        [pl.BlockSpec(memory_space=pltpu.SMEM)] + [whole(item) for item in terms],
        [whole(item) for item in out_shape],
        out_shape,
        (place, *terms),
        received=terms[1:],
    )


def joint_grad_kernel(count, place_ref, *refs):
    (grad_ref, rows_ref, weight_ref, gain_ref, shift_ref), out_refs, refs = take(refs, 5, count)
    bias_ref, sums_ref, total, biases, bias_row = refs
    step = pl.program_id(0)
    grads = side_by_side(grad_ref)
    added = dot(grads, rows_ref[...].reshape(grads.shape[1], -1))
    summed = jnp.sum(grads.astype(jnp.float32), axis=1, keepdims=True)
    summed_row = dot_cols(jnp.ones((8, grads.shape[1]), LOW), grads)

    @pl.when(step == 0)
    def _():
        total[...] = added
        biases[...] = summed
        bias_row[...] = summed_row

    @pl.when(step > 0)
    def _():
        total[...] += added
        biases[...] += summed
        bias_row[...] += summed_row

    @pl.when(step == pl.num_programs(0) - 1)
    def _():
        rows = out_refs[0].shape[0]
        for at, ref in enumerate(out_refs):
            first = lax.rem(place_ref[3] + at, count) * rows
            ref[...] = total[pl.ds(pl.multiple_of(first, rows), rows), :].astype(LOW)
        bias_ref[...] = jnp.zeros_like(bias_ref)
        bias_ref[:, : bias_row.shape[1]] = bias_row[0:1, :]
        weight = weight_ref[...].astype(jnp.float32)
        shift_sum = jnp.sum(weight * biases[...], axis=0, keepdims=True)
        product = jnp.sum(weight * total[...], axis=0, keepdims=True)
        sums_ref[0:1, :] = (product - shift_sum * shift_ref[...]) / gain_ref[...]
        sums_ref[1:2, :] = shift_sum


def joint_grad(place, count, grads, gathered, weight, gain, shift, step=8):
    places, feats, rows = grads.shape
    width = gathered.shape[2]
    results = run(
        partial(joint_grad_kernel, count),
        (places // step,),
        [
            pl.BlockSpec(memory_space=pltpu.SMEM),
            pl.BlockSpec((step, feats, rows), lambda i: (i, 0, 0)),
            pl.BlockSpec((step, rows, width), lambda i: (i, 0, 0)),
            whole(weight),
            whole(gain),
            whole(shift),
        ],
        [pl.BlockSpec((feats // count, width), lambda i: (0, 0))] * count
        + [
            pl.BlockSpec((1, width), lambda i: (0, 0)),
            pl.BlockSpec((2, width), lambda i: (0, 0)),
        ],
        [shape((feats // count, width), LOW)] * count
        + [shape((1, width), jnp.float32), shape((2, width), jnp.float32)],
        (place, grads, gathered, weight, gain, shift),
        scratch=[
            pltpu.VMEM((feats, width), jnp.float32),
            pltpu.VMEM((feats, 1), jnp.float32),
            pltpu.VMEM((8, feats), jnp.float32),
        ],
    )
    return results[:count], *results[count:]


def input_kernel(part_ref, weight_ref, tokens_ref, gain_ref, d_resid_ref, out_ref, total):
    step = pl.program_id(0)
    added = dot(turned(part_ref[...]).astype(LOW), weight_ref[...])

    @pl.when(step == 0)
    def _():
        total[...] = added

    @pl.when(step > 0)
    def _():
        total[...] += added

    @pl.when(step == pl.num_programs(0) - 1)
    def _():
        normed, scale = norm_parts(tokens_ref[...].astype(jnp.float32))
        out_ref[...] = d_resid_ref[...] + norm_back(total[...], normed, scale, gain_ref[...])


def input_back(parts, weights, tokens, gain, d_resid, steps=4):
    feats, rows = parts.shape
    width = weights.shape[1]
    step = feats // steps
    return run(
        input_kernel,
        (steps,),
        [
            pl.BlockSpec((step, rows), lambda i: (i, 0)),
            pl.BlockSpec((step, width), lambda i: (i, 0)),
            whole(tokens),
            whole(gain),
            whole(d_resid),
        ],
        [pl.BlockSpec((rows, width), lambda i: (0, 0))],
        [shape((rows, width), jnp.float32)],
        (parts, weights, tokens, gain, d_resid),
        received=(parts,),
        scratch=[pltpu.VMEM((rows, width), jnp.float32)],
    )[0]


ITEM = "z"
HEAD = ("x", "y", "c")
CORE = "c"


def moved(value, axis, steps):
    count = lax.axis_size(axis)
    return lax.ppermute(value, axis, [(place, (place + steps) % count) for place in range(count)])


def shifted(value, axis, steps):
    count = lax.axis_size(axis)
    initial, last = (max(0, -steps), min(count, count - steps))
    return lax.ppermute(value, axis, [(source, source + steps) for source in range(initial, last)])


def around(value, axis):
    return [value] + [moved(value, axis, -step) for step in range(1, lax.axis_size(axis))]


def sum_back(values, axis):
    return [values[0]] + [
        moved(values[step], axis, step) for step in range(1, lax.axis_size(axis))
    ]


def both_halves(value, bit, axis, step):
    pairs = [(place, place ^ step) for place in range(lax.axis_size(axis))]
    other = lax.ppermute(value, axis, pairs)
    first = jnp.where(bit == 0, value, other)
    return jnp.concatenate([first, jnp.where(bit == 0, other, value)], axis=0)


def head_swap(value):
    return lax.all_to_all(value, HEAD, split_axis=0, concat_axis=0, tiled=True)


def segment_flags(seg_counts):
    total_segs = seg_counts.shape[0]
    openings = jnp.cumsum(seg_counts) - seg_counts
    places = jnp.arange(total_segs, dtype=jnp.int32)
    opens_here = jnp.any((openings[:, None] == places[None, :]) & (seg_counts[:, None] > 0), axis=0)
    opens_before = jnp.concatenate([jnp.ones((1,), dtype=bool), opens_here[:-1]])
    one_back = jnp.logical_not(opens_here)
    two_back = one_back & jnp.logical_not(opens_before)
    return (one_back, two_back)


def local(
    tokens,
    cotangent,
    seg_counts,
    query_weight,
    key_weight,
    value_weight,
    query_bias,
    value_bias,
    out_weight,
    out_bias,
    first_gain,
    first_shift,
    second_gain,
    second_shift,
    up_weight,
    up_bias,
    down_weight,
    down_bias,
):
    rows, width = tokens.shape
    heads = lax.axis_size(HEAD)
    item_place = lax.axis_index(ITEM)
    group_rows = rows * heads
    seg_local = group_rows // SEG
    feats = query_weight.shape[0]
    units = up_weight.shape[0]
    hidden_here = units * heads

    def row(vector):
        return vector.reshape(1, -1)

    first = first_norm(tokens, row(first_gain), row(first_shift), out_weight)
    gathered = lax.all_gather(first, HEAD, axis=0, tiled=True).reshape(heads, -1, width)
    second = jnp.concatenate([up_weight, down_weight], axis=0)
    feed_weights = lax.all_gather(second, HEAD, axis=0, tiled=True).reshape(heads, -1, width)
    cots = around(cotangent, ITEM)
    joint_weight = jnp.concatenate([query_weight, key_weight, value_weight], axis=0)
    joint_bias = jnp.concatenate([query_bias, jnp.zeros_like(query_bias), value_bias])

    one_back, two_back = segment_flags(seg_counts)
    flags = jnp.stack([two_back, one_back], axis=1).astype(jnp.int32)
    flags = lax.dynamic_slice_in_dim(flags, item_place * seg_local, seg_local).reshape(-1)

    gathered, cots = lax.optimization_barrier((gathered, cots))
    query, kv, turned_all = project(gathered, rows, joint_weight, row(joint_bias))
    own_kept = kv.reshape(seg_local, SEG, 2 * HD)[:, SEG - KEPT :]
    table = jnp.concatenate([shifted(own_kept, ITEM, 1), own_kept], axis=0)
    prefix = jnp.concatenate(
        [table[seg_local - 2 : 2 * seg_local - 2], table[seg_local - 1 : 2 * seg_local - 1]], axis=1
    )
    attended, log_sums = attend(flags, turned_all, kv, prefix, rows)
    attended_own = head_swap(attended)
    resid, inputs_two = out_project(
        attended_own, gathered, rows // feats, tokens, row(out_bias), row(second_gain), row(second_shift)
    )

    joint_turn = lax.optimization_barrier((joint_weight, resid))[0]
    joint_full = lax.all_gather(joint_turn, HEAD, axis=0, tiled=True)
    norms = around(inputs_two, ITEM)
    chips = (lax.axis_size("x"), lax.axis_size("y"))
    place = jnp.stack([lax.axis_index(axis) for axis in (CORE, "x", "y", ITEM)]).astype(jnp.int32)
    d_act, cots = feed_d_act(place, chips, cots, feed_weights)
    cots = [cots, moved(cots, CORE, 1)]
    bias_here = lax.dynamic_slice_in_dim(up_bias, item_place * hidden_here, hidden_here)
    backs, (norms, kept, sent, up_bias_part) = feed(
        place, chips, norms, feed_weights, bias_here.reshape(heads, 1, units), d_act
    )
    backs = sum_back(backs, ITEM)
    norms = [norms, moved(norms, CORE, 1)]
    near, far, feed_parts = feed_grad(
        place, chips, norms, cots, kept, sent, moved(sent, CORE, 1), feed_weights
    )
    backs, near, far = lax.optimization_barrier((backs, near, far))
    d_resid, sums_two, d_parts, sent = branch_back(
        place,
        resid,
        cotangent,
        row(second_gain),
        gathered,
        rows // feats,
        attended_own,
        backs,
    )
    sent = sum_back(sent, ITEM)
    d_attended = head_swap(d_parts)
    d_attended, far = lax.optimization_barrier((d_attended, moved(far, ITEM, 2)))
    feed_parts = lax.optimization_barrier((feed_parts, d_resid))[0]
    feed_grads = lax.psum_scatter(
        feed_parts.reshape(-1, width), ("x", "y"), scatter_dimension=0, tiled=True
    )
    d_prefix = prefix_back(
        flags, turned_all, query, d_attended, attended, log_sums, prefix, rows
    )[0]
    older, newer = d_prefix[:, :KEPT], d_prefix[:, KEPT:]
    spread = jnp.pad(older, ((seg_local - 2, 2), (0, 0), (0, 0)))
    spread = spread + jnp.pad(newer, ((seg_local - 1, 1), (0, 0), (0, 0)))
    returned = shifted(spread[:seg_local], ITEM, -1)
    joint_grads, kept_grads = attend_back(
        flags, turned_all, query, d_attended, attended, log_sums, prefix, kv, rows, 1
    )
    returned, kept_grads, joint_full = lax.optimization_barrier((returned, kept_grads, joint_full))
    joint_grads = add_returned(joint_grads, kept_grads, spread[seg_local:] + returned)
    grads_own = head_swap(joint_grads[0]).reshape(-1, rows)
    joint_parts, bias_part, sums_one = joint_grad(
        place,
        lax.axis_size(ITEM),
        joint_grads[0],
        gathered,
        joint_weight,
        row(first_gain),
        row(first_shift),
    )
    joint_parts, sums_one, sent, near, far = lax.optimization_barrier(
        (joint_parts, sums_one, sent, near, far)
    )
    out_own, out_other, small = branch_grad(
        place, chips, rows, sent, (row(up_bias_part), sums_two, sums_one)
    )
    joint_parts = sum_back(joint_parts, ITEM)
    near = (near.astype(jnp.float32) + far.astype(jnp.float32)).astype(LOW)
    terms = core_step(out_own, moved(out_other, CORE, 1), small, chips[0])
    grads_own, terms, joint_parts, near = lax.optimization_barrier(
        (grads_own, terms, joint_parts, near)
    )
    high, low = item_place // 2, item_place % 2
    terms = sum_back(terms, "x")
    mixed = moved(near[rows:], ITEM, 1)
    joint_sums = sum(part.astype(jnp.float32) for part in joint_parts).astype(LOW)
    joint_sums = both_halves(joint_sums, low, ITEM, 1)
    input_grad = input_back(grads_own, joint_full, tokens, row(first_gain), d_resid)
    input_grad, terms, mixed, joint_sums = lax.optimization_barrier(
        (input_grad, terms, mixed, joint_sums)
    )
    mixed = near[:rows].astype(jnp.float32) + mixed.astype(jnp.float32)
    terms = sum_back(chip_step(terms, chips[1]), "y")
    joint_sums = both_halves(joint_sums, high, ITEM, 2)
    terms, joint_sums, feed_grads = lax.optimization_barrier((terms, joint_sums, feed_grads))
    feed_grads = feed_grads.astype(jnp.float32)
    terms = around(item_step(terms, bias_part), ITEM)
    joint_sums = joint_sums.astype(jnp.float32)
    mixed_out = (resid + mixed + down_bias).astype(LOW)
    share = feats // lax.axis_size(ITEM)
    out_sum, small, up_bias_grad = last_step(place, terms, share)
    up_bias_grad = up_bias_grad.reshape(-1)
    bias_sums, early_rows, late = small[SMALL - 1, : 3 * feats], small[1:5], small[5:7]
    return (
        mixed_out,
        input_grad,
        joint_sums[:feats],
        joint_sums[feats : 2 * feats],
        joint_sums[2 * feats :],
        bias_sums[:feats],
        bias_sums[2 * feats : 3 * feats],
        out_sum,
        early_rows[2],
        late[0],
        late[1],
        early_rows[0],
        early_rows[1],
        feed_grads[:units],
        up_bias_grad,
        feed_grads[units:],
        early_rows[3],
    )


def solution(mesh):
    sizes = (mesh.shape["item"], 4, mesh.shape["head"] // 8, 2)
    fine = Mesh(mesh.devices.reshape(sizes), (ITEM, *HEAD))
    split = P((ITEM, *HEAD), None)
    by_head = P(HEAD, None)
    return jax.shard_map(
        local,
        mesh=fine,
        in_specs=(
            split,
            split,
            P(),
            by_head,
            by_head,
            by_head,
            P(HEAD),
            P(HEAD),
            by_head,
            P(),
            P(),
            P(),
            P(),
            P(),
            split,
            P(),
            split,
            P(),
        ),
        out_specs=(
            split,
            split,
            by_head,
            by_head,
            by_head,
            P(HEAD),
            P(HEAD),
            by_head,
            P(),
            P(),
            P(),
            P(),
            P(),
            split,
            P(),
            split,
            P(),
        ),
        check_vma=False,
    )
```
